32 devices in a mesh: groups: 2 (over x), row: 8 (over z, y), col: 2 (over core).
Axes of the slice: x: 2, y: 2, z: 4, core: 2. Of those that a mesh axis runs over, the one named last changes fastest.
Arguments:
- points_x: bfloat16 [32768, 96], P(('groups', 'row', 'col')), parts along dimension 0, may hold values from -24 to 24
- points_y: bfloat16 [2048, 96], P(('groups', 'col', 'row')), parts along dimension 0, may hold values from -6 to 6
- mass_x: bfloat16 [32768], P(('groups', 'row', 'col')), parts along dimension 0, may hold values from -1 to 1
- mass_y: bfloat16 [2048], P(('groups', 'col', 'row')), parts along dimension 0, may hold values from -1 to 1
Outputs:
- f_potential: float32 [32768], P(('groups', 'row', 'col')), parts along dimension 0
- g_potential: float32 [2048], P(('groups', 'col', 'row')), parts along dimension 0
- grad_x: float32 [32768, 96], P(('groups', 'row', 'col')), parts along dimension 0
- grad_y: float32 [2048, 96], P(('groups', 'col', 'row')), parts along dimension 0
The draws below stay inside these ranges and needn't reach their ends.
There are 2 independent parts, one for each index of `groups`. The reference program is written for one: setup_inputs(seed, part) draws one part's arguments, and reference() takes and returns one part's arrays. A program takes and returns all parts, laid end to end along the dimension named above; each array names one. Nothing has to cross between parts.
All inputs are finite; a program needn't handle non-finite values.
Results may differ from the reference program's by a relative error of at most 0.003.
Values may be sent and summed in bfloat16 or wider, within the bound.
No kernel may reach another device: no remote copies, remote signals or barrier semaphores. Data moves between devices by JAX's collectives and lax.ppermute only.
A program may use at most 64 MiB of HBM per device.

```python
import math
import jax
import jax.numpy as jnp
from jax import lax

F = 96
ITERS = 2
NX = 16384
NY = 1024


def draw_points_x(key, part):
    key = jax.random.fold_in(key, 1)
    base_key = jax.random.fold_in(key, 0)
    values = jnp.clip(jax.random.normal(base_key, (NX, F), jnp.float32), -6.0, 6.0)
    return values.astype(jnp.bfloat16)


def block_scale(own_key, dims, cuts, low, top_value):
    factor_of = 1.0
    for dim, shards_of in cuts:
        steps = jax.random.uniform(jax.random.fold_in(jax.random.fold_in(own_key, 6), dim), (shards_of,), jnp.float32, low / len(cuts), top_value / len(cuts))
        factor_of = factor_of * jnp.repeat(jnp.exp(steps), dims[dim] // shards_of).reshape((-1,) + (1,) * (len(dims) - 1 - dim))
    return factor_of


def noise(stream_key, shape, width, most, cuts=(), kind=jnp.bfloat16):
    drawn = width * jax.random.normal(stream_key, shape, jnp.float32)
    if cuts:
        drawn = drawn * block_scale(stream_key, shape, cuts, -0.22, 0.18)
    return jnp.clip(drawn, -most, most).astype(kind)


def setup_inputs(seed: int = 0, part: int = 0) -> dict:
    streams_of = jax.random.split(jax.random.key(seed), 5)
    part_splits = jax.random.split(jax.random.fold_in(streams_of[4], part), 5)
    points_x = draw_points_x(jax.random.fold_in(jax.random.fold_in(streams_of[4], part), 71), part)
    points_y = noise(part_splits[1], (NY, F), 1.0, 6.0, ((0, 16),))
    mass_x = jnp.clip(jax.random.uniform(part_splits[2], (NX,), jnp.float32, -1.0, 1.0) * block_scale(part_splits[2], (NX,), ((0, 16),), -0.4, 0.0), -1.0, 1.0).astype(jnp.bfloat16)
    mass_y = jnp.clip(jax.random.uniform(part_splits[3], (NY,), jnp.float32, -1.0, 1.0) * block_scale(part_splits[3], (NY,), ((0, 16),), -0.4, 0.0), -1.0, 1.0).astype(jnp.bfloat16)
    return dict(points_x=points_x, points_y=points_y, mass_x=mass_x, mass_y=mass_y)


epsilon = 0.02


def cost_block(xb, yv):
    xf = xb.astype(jnp.float32)
    yf = yv.astype(jnp.float32)
    xn = jnp.sum(xf * xf, axis=1)
    yn = jnp.sum(yf * yf, axis=1)
    cross = jnp.dot(xb, yv.T, preferred_element_type=jnp.float32)
    return (xn[:, None] + yn[None, :] - 2.0 * cross) * (1.0 / xb.shape[1])


def reference(points_x, points_y, mass_x, mass_y):
    rblock = min(1024, NX)
    count = NX // rblock
    log_a = mass_x.astype(jnp.float32) - math.log(NX)
    log_b = mass_y.astype(jnp.float32) - math.log(NY)
    xs = points_x.reshape(count, rblock, F)
    las = log_a.reshape(count, rblock)
    mxs = mass_x.astype(jnp.float32).reshape(count, rblock)
    g_pot = jnp.zeros((NY,), jnp.float32)
    f_pot = jnp.zeros((NX,), jnp.float32)
    for step in range(ITERS):
        def row_fn(xb):
            scores = log_b[None, :] + (g_pot[None, :] - cost_block(xb, points_y)) / epsilon
            peak = jnp.max(scores, axis=1)
            total = jnp.sum(jnp.exp(scores - peak[:, None]), axis=1)
            return -epsilon * (peak + jnp.log(total))
        f_pot = lax.map(row_fn, xs).reshape(NX)
        fs = f_pot.reshape(count, rblock)

        def col_fn(carry, item):
            peak, total = carry
            xb, lab, fb = item
            scores = lab[:, None] + (fb[:, None] - cost_block(xb, points_y)) / epsilon
            newpk = jnp.maximum(peak, jnp.max(scores, axis=0))
            total = total * jnp.exp(peak - newpk) + jnp.sum(jnp.exp(scores - newpk[None, :]), axis=0)
            return (newpk, total), None
        init = (jnp.full((NY,), -jnp.inf, jnp.float32), jnp.zeros((NY,), jnp.float32))
        (peak, total), unused = lax.scan(col_fn, init, (xs, las, fs))
        g_pot = -epsilon * (peak + jnp.log(total))
    fs = f_pot.reshape(count, rblock)
    yf = points_y.astype(jnp.float32)
    my = mass_y.astype(jnp.float32)

    def grad_fn(carry, item):
        xb, mb, fb = item
        cost = cost_block(xb, points_y)
        weight = jnp.exp(mb[:, None] + my[None, :] + (fb[:, None] + g_pot[None, :] - cost) / epsilon)
        wrows = jnp.sum(weight, axis=1)
        wcols = jnp.sum(weight, axis=0)
        wb = weight.astype(jnp.bfloat16)
        xf = xb.astype(jnp.float32)
        gx = (xf * wrows[:, None] - jnp.dot(wb, points_y, preferred_element_type=jnp.float32)) / NY
        carry = carry + yf * wcols[:, None] - jnp.dot(wb.T, xb, preferred_element_type=jnp.float32)
        return carry, gx
    gy_sum, gx = lax.scan(grad_fn, jnp.zeros((NY, F), jnp.float32), (xs, mxs, fs))
    return f_pot, g_pot, gx.reshape(NX, F), gy_sum / NX
```

```python
import functools
import math

import jax
import jax.numpy as jnp
from jax import lax
from jax.experimental import pallas as pl
from jax.experimental.pallas import tpu as pltpu
from jax.sharding import PartitionSpec as P

ITERS = 2
EPSILON = 0.02
LOG2E = math.log2(math.e)
AXES = ("row", "col")
TILE = 256
STEP = 32
EXT = 32
F32 = jnp.float32
BF16 = jnp.bfloat16


def kappa_of(width):
    return 2.0 / (width * EPSILON)


def pieces(value):
    high = value.astype(BF16).astype(F32)
    rest = value - high
    mid = rest.astype(BF16).astype(F32)
    return high, mid, rest - mid


def select(index, values):
    out = jnp.zeros(index.shape, F32)
    for k, value in values.items():
        out = jnp.where(index == k, value, out)
    return out


def extras_y(index, c_term, mass):
    high, mid, low = pieces(c_term)
    return select(index, {0: high, 1: mid, 2: low, 3: 1.0, 4: 1.0, 5: 1.0, 6: mass})


def extras_x(index, b_term):
    high, mid, low = pieces(b_term)
    return select(index, {0: 1.0, 1: 1.0, 2: 1.0, 3: high, 4: mid, 5: low})


def rows_index(columns):
    return lax.broadcasted_iota(jnp.int32, (EXT, columns), 0)


def to_column(row):
    size = row.shape[1]
    eye = lax.broadcasted_iota(jnp.int32, (size, size), 0) == lax.broadcasted_iota(jnp.int32, (size, size), 1)
    return jnp.sum(jnp.where(eye, row, 0.0), axis=1, keepdims=True)


def to_row(column):
    size = column.shape[0]
    eye = lax.broadcasted_iota(jnp.int32, (size, size), 0) == lax.broadcasted_iota(jnp.int32, (size, size), 1)
    return jnp.sum(jnp.where(eye, column, 0.0), axis=0, keepdims=True)


def for_tiles(total, body):
    count = total // TILE
    if count <= 4:
        for t in range(count):
            body(pl.ds(t * TILE, TILE))
    else:

        @pl.loop(0, count)
        def _(t):
            body(pl.ds(pl.multiple_of(t * TILE, TILE), TILE))


def max_down(z_ref, rows):
    peak = z_ref[0:STEP, :]
    for r in range(STEP, rows, STEP):
        peak = jnp.maximum(peak, z_ref[r : r + STEP, :])
    return jnp.max(peak, axis=0, keepdims=True)


def exp_down(z_ref, rows, scale, shift=None, keep=()):
    total = jnp.zeros((STEP, TILE), F32)
    for r in range(0, rows, STEP):
        z = z_ref[r : r + STEP, :]
        if shift is not None:
            z = z - shift
        value = jnp.exp2(z * scale)
        total = total + value
        if keep:
            high = value.astype(BF16)
            keep[0][r : r + STEP, :] = high
            if len(keep) > 1:
                keep[1][r : r + STEP, :] = (value - high.astype(F32)).astype(BF16)
    return jnp.sum(total, axis=0, keepdims=True)


def lse_down(z_ref, rows, scale):
    peak = max_down(z_ref, rows)
    total = exp_down(z_ref, rows, scale, peak)
    return scale * peak + jnp.log(total) * LOG2E


def prep_kernel(log_ny, y_ref, my_ref, out_ref):
    width = y_ref.shape[1]
    y = y_ref[...]
    yf = y.astype(F32)
    norm = jnp.sum(yf * yf, axis=1, keepdims=True)
    mass = to_column(my_ref[...].astype(F32))
    c_term = (mass - log_ny) / kappa_of(width) - 0.5 * norm
    index = lax.broadcasted_iota(jnp.int32, (y.shape[0], EXT), 1)
    out_ref[:, :width] = y
    out_ref[:, width:] = extras_y(index, c_term, mass).astype(BF16)


def first_kernel(nd, log_nx, *refs):
    xt_ref, mx_ref = refs[:2]
    y_refs = refs[2 : 2 + nd]
    ya_ref, b_ref, l_ref, xa_ref, z_ref, zc_ref = refs[2 + nd :]
    width, n = xt_ref.shape
    yd = y_refs[0].shape[0]
    ny = nd * yd
    scale = kappa_of(width) * LOG2E
    me = lax.axis_index("row") * lax.axis_size("col") + lax.axis_index("col")
    for k in range(nd):
        ya_ref[pl.ds(pl.multiple_of((me ^ k) * yd, yd), yd), :] = y_refs[k][...]
    la2 = (mx_ref[...].astype(F32) - log_nx) * LOG2E
    xa_ref[:width, :] = xt_ref[...]
    xa_ref[width:, :] = extras_x(rows_index(n), jnp.zeros((1, n), F32)).astype(BF16)

    def row_tile(t):
        z_ref[...] = jnp.dot(ya_ref[...], xa_ref[:, t], preferred_element_type=F32)
        b_ref[:, t] = -lse_down(z_ref, ny, scale)

    for_tiles(n, row_tile)
    b_term = (la2 + b_ref[...]) / scale
    b_ref[...] = b_term
    xa_ref[width:, :] = extras_x(rows_index(n), b_term).astype(BF16)
    x_rows = xa_ref[...].T

    def col_tile(t):
        zc_ref[...] = lax.dot_general(x_rows, ya_ref[t, :], (((1,), (1,)), ((), ())), preferred_element_type=F32)
        l_ref[:, :, t] = jnp.broadcast_to(lse_down(zc_ref, n, scale)[None], (nd, 1, TILE))

    for_tiles(ny, col_tile)


def update_y(log_ny, scale, width, yt_ref, ya_ref, lse2):
    ny = ya_ref.shape[0]
    old = yt_ref[width:, :].astype(F32)
    c_old = (old[0:1] + old[1:2]) + old[2:3]
    mass = old[6:7]
    lb2 = (mass - log_ny) * LOG2E
    c_term = c_old + (lb2 - lse2) / scale
    return c_term, mass


def second_kernel(
    nd, log_nx, log_ny, xt_ref, mx_ref, ya0_ref, b1_ref, l_ref,
    f_ref, s_ref, g_ref, xa_ref, ya_ref, yt_ref, z_ref, zc_ref, ph_ref, pw_ref, gt_ref,
):
    width, n = xt_ref.shape
    ny = ya0_ref.shape[0]
    yd = ny // nd
    kappa = kappa_of(width)
    scale = kappa * LOG2E
    l_all = l_ref[...]
    peak = jnp.max(l_all, axis=0)
    lse2 = peak + jnp.log(jnp.sum(jnp.exp2(l_all - peak[None]), axis=0)) * LOG2E
    yt_ref[...] = ya0_ref[...].T
    c_term, mass = update_y(log_ny, scale, width, yt_ref, ya0_ref, lse2)
    ext = extras_y(rows_index(ny), c_term, mass)
    yt_ref[width:, :] = ext.astype(BF16)
    ya_ref[:, :width] = ya0_ref[:, :width]
    ya_ref[:, width:] = ext.T.astype(BF16)
    xt = xt_ref[...]
    xa_ref[:width, :] = xt
    xa_ref[width:, :] = extras_x(rows_index(n), b1_ref[...]).astype(BF16)

    def row_tile(t):
        z_ref[...] = jnp.dot(ya_ref[...], xa_ref[:, t], preferred_element_type=F32)
        f_ref[:, t] = exp_down(z_ref, ny, scale)

    for_tiles(n, row_tile)
    log_a = mx_ref[...].astype(F32) - log_nx
    b_term = b1_ref[...] + (log_a - jnp.log(f_ref[...])) / kappa
    xf = xt.astype(F32)
    f_ref[...] = jnp.sum(xf * xf, axis=0, keepdims=True) / width - EPSILON * (log_a - kappa * b_term)
    xa_ref[width:, :] = extras_x(rows_index(n), b_term).astype(BF16)
    x_rows = xa_ref[...].T

    def col_tile(t):
        zc_ref[...] = jnp.dot(x_rows, yt_ref[:, t], preferred_element_type=F32)
        total = exp_down(zc_ref, n, scale, None, (ph_ref, pw_ref))
        s_ref[:, t] = total
        moment = jnp.dot(xt, ph_ref[...], preferred_element_type=F32) + jnp.dot(xt, pw_ref[...], preferred_element_type=F32)
        gt_ref[:width, t] = yt_ref[:width, t].astype(F32) * total - moment

    for_tiles(ny, col_tile)
    high, mid, low = pieces(s_ref[...])
    c_high, c_mid, c_low = pieces(c_term)
    gt_ref[width:, :] = select(rows_index(ny), {0: high, 1: mid, 2: low, 3: c_high, 4: c_mid, 5: c_low})
    g_ref[...] = gt_ref[...].T.astype(BF16).reshape(nd, yd, width + EXT)


def grad_x_kernel(nd, log_nx, log_ny, *refs):
    xa_ref, ya1_ref, yt1_ref = refs[:3]
    s_refs = refs[3 : 3 + nd]
    out_ref, ya_ref, z_ref, w_ref = refs[3 + nd :]
    width = out_ref.shape[0]
    ny = ya1_ref.shape[0]
    kappa = kappa_of(width)
    scale = kappa * LOG2E
    total = s_refs[0][...]
    for ref in s_refs[1:]:
        total = total + ref[...]
    c_term, mass = update_y(log_ny, scale, width, yt1_ref, ya1_ref, jnp.log(total) * LOG2E)
    ext = extras_y(rows_index(ny), c_term + (log_nx + log_ny) / kappa, mass)
    ya_ref[:, :width] = ya1_ref[:, :width]
    ya_ref[:, width:] = ext.T.astype(BF16)

    def row_tile(t):
        z_ref[...] = jnp.dot(ya_ref[...], xa_ref[:, t], preferred_element_type=F32)
        total = exp_down(z_ref, ny, scale, None, (w_ref,))
        moved = jnp.dot(yt1_ref[:width, :], w_ref[...], preferred_element_type=F32)
        out_ref[:, t] = (xa_ref[:width, t].astype(F32) * total - moved) * (1.0 / ny)

    for_tiles(out_ref.shape[1], row_tile)


def grad_y_kernel(nd, y_ref, my_ref, g_ref, out_ref, pot_ref):
    yd, width = y_ref.shape
    total = g_ref[0].astype(F32)
    for k in range(1, nd):
        total = total + g_ref[k].astype(F32)
    part = total[:, width:]
    colsum = (part[:, 0:1] + part[:, 1:2]) + part[:, 2:3]
    c_term = ((part[:, 3:4] + part[:, 4:5]) + part[:, 5:6]) * (1.0 / nd)
    mass = to_column(my_ref[...].astype(F32))
    out_ref[...] = total[:, :width] * (jnp.exp(mass) / colsum)
    yf = y_ref[...].astype(F32)
    norm = jnp.sum(yf * yf, axis=1, keepdims=True)
    pot = norm / width - EPSILON * (jnp.log(colsum) - kappa_of(width) * c_term)
    pot_ref[...] = to_row(pot)


def call(kernel, outs, scratch, *args):
    return pl.pallas_call(
        kernel,
        out_shape=outs,
        in_specs=[pl.BlockSpec(memory_space=pltpu.VMEM)] * len(args),
        out_specs=jax.tree.map(lambda _: pl.BlockSpec(memory_space=pltpu.VMEM), outs),
        scratch_shapes=scratch,
        compiler_params=pltpu.CompilerParams(vmem_limit_bytes=40 * 1024 * 1024),
    )(*args)


def shape(dims, dtype=F32):
    return jax.ShapeDtypeStruct(dims, dtype)


def everyone(value, nd):
    return [value] + [lax.ppermute(value, AXES, [(s, s ^ k) for s in range(nd)]) for k in range(1, nd)]


def on_device(points_x, points_y, mass_x, mass_y):
    n, width = points_x.shape
    yd = points_y.shape[0]
    nd = lax.axis_size("row") * lax.axis_size("col")
    ny = nd * yd
    log_nx, log_ny = math.log(n * nd), math.log(ny)
    depth = width + EXT
    xt = points_x.T
    mx = mass_x.reshape(1, n)
    my = mass_y.reshape(1, yd)
    y_own = call(functools.partial(prep_kernel, log_ny), shape((yd, depth), BF16), [], points_y, my)
    y_blocks = everyone(y_own, nd)
    ya, b1, lse = call(
        functools.partial(first_kernel, nd, log_nx),
        (shape((ny, depth), BF16), shape((1, n)), shape((nd, 1, ny))),
        [pltpu.VMEM((depth, n), BF16), pltpu.VMEM((ny, TILE), F32), pltpu.VMEM((n, TILE), F32)],
        xt, mx, *y_blocks,
    )
    lse = lax.all_to_all(lse, AXES, 0, 0, tiled=True)
    f_pot, sums, g_part, xa, ya, yt = call(
        functools.partial(second_kernel, nd, log_nx, log_ny),
        (
            shape((1, n)), shape((1, ny)), shape((nd, yd, depth), BF16),
            shape((depth, n), BF16), shape((ny, depth), BF16), shape((depth, ny), BF16),
        ),
        [
            pltpu.VMEM((ny, TILE), F32), pltpu.VMEM((n, TILE), F32),
            pltpu.VMEM((n, TILE), BF16), pltpu.VMEM((n, TILE), BF16), pltpu.VMEM((depth, ny), F32),
        ],
        xt, mx, ya, b1, lse,
    )
    all_sums = everyone(sums, nd)
    g_all = lax.all_to_all(g_part, AXES, 0, 0, tiled=True)
    grad_xt = call(
        functools.partial(grad_x_kernel, nd, log_nx, log_ny),
        shape((width, n)),
        [pltpu.VMEM((ny, depth), BF16), pltpu.VMEM((ny, TILE), F32), pltpu.VMEM((ny, TILE), BF16)],
        xa, ya, yt, *all_sums,
    )
    grad_y, g_pot = call(
        functools.partial(grad_y_kernel, nd), (shape((yd, width)), shape((1, yd))), [], points_y, my, g_all
    )
    return f_pot.reshape(n), g_pot.reshape(yd), grad_xt.T, grad_y


def solution(mesh):
    in_specs = (
        P(("groups", "row", "col"), None),
        P(("groups", "col", "row"), None),
        P(("groups", "row", "col")),
        P(("groups", "col", "row")),
    )
    out_specs = (
        P(("groups", "row", "col")),
        P(("groups", "col", "row")),
        P(("groups", "row", "col"), None),
        P(("groups", "col", "row"), None),
    )
    return jax.shard_map(
        on_device, mesh=mesh, in_specs=in_specs, out_specs=out_specs, check_vma=False
    )
```

```python
import functools
import math

import jax
import jax.numpy as jnp
from jax import lax
from jax.experimental import pallas as pl
from jax.experimental.pallas import tpu as pltpu
from jax.sharding import PartitionSpec as P

ITERS = 2
EPSILON = 0.02
LOG2E = math.log2(math.e)
AXES = ("row", "col")
TILE = 256
STEP = 32
EXT = 32
PAD = 16
F32 = jnp.float32
BF16 = jnp.bfloat16


def kappa_of(width):
    return 2.0 / (width * EPSILON)


def pieces(value):
    high = value.astype(BF16).astype(F32)
    rest = value - high
    mid = rest.astype(BF16).astype(F32)
    return high, mid, rest - mid


def select(index, values):
    out = jnp.zeros(index.shape, F32)
    for k, value in values.items():
        out = jnp.where(index == k, value, out)
    return out


def extras_y(index, c_term, mass):
    high, mid, low = pieces(c_term)
    return select(index, {0: high, 1: mid, 2: low, 3: 1.0, 4: 1.0, 5: 1.0, 6: mass})


def extras_x(index, b_term):
    high, mid, low = pieces(b_term)
    return select(index, {0: 1.0, 1: 1.0, 2: 1.0, 3: high, 4: mid, 5: low})


def rows_index(columns):
    return lax.broadcasted_iota(jnp.int32, (EXT, columns), 0)


def to_column(row):
    size = row.shape[1]
    eye = lax.broadcasted_iota(jnp.int32, (size, size), 0) == lax.broadcasted_iota(jnp.int32, (size, size), 1)
    return jnp.sum(jnp.where(eye, row, 0.0), axis=1, keepdims=True)


def to_row(column):
    size = column.shape[0]
    eye = lax.broadcasted_iota(jnp.int32, (size, size), 0) == lax.broadcasted_iota(jnp.int32, (size, size), 1)
    return jnp.sum(jnp.where(eye, column, 0.0), axis=0, keepdims=True)


def for_tiles(total, body):
    count = total // TILE
    if count <= 4:
        for t in range(count):
            body(pl.ds(t * TILE, TILE))
    else:

        @pl.loop(0, count)
        def _(t):
            body(pl.ds(pl.multiple_of(t * TILE, TILE), TILE))


def max_down(z_ref, rows):
    peak = z_ref[0:STEP, :]
    for r in range(STEP, rows, STEP):
        peak = jnp.maximum(peak, z_ref[r : r + STEP, :])
    return jnp.max(peak, axis=0, keepdims=True)


def exp_sum_down(z_ref, rows, scale, shift):
    total = jnp.zeros((STEP, TILE), F32)
    for r in range(0, rows, STEP):
        total = total + jnp.exp2((z_ref[r : r + STEP, :] - shift) * scale)
    return jnp.sum(total, axis=0, keepdims=True)


def prep_kernel(log_ny, y_ref, my_ref, out_ref):
    width = y_ref.shape[1]
    y = y_ref[...]
    yf = y.astype(F32)
    norm = jnp.sum(yf * yf, axis=1, keepdims=True)
    mass = to_column(my_ref[...].astype(F32))
    c_term = (mass - log_ny) / kappa_of(width) - 0.5 * norm
    index = lax.broadcasted_iota(jnp.int32, (y.shape[0], EXT), 1)
    ext = extras_y(index, c_term, mass).astype(BF16)
    for k in range(out_ref.shape[0]):
        out_ref[k, :, :width] = y
        out_ref[k, :, width:] = ext


def prep_x_kernel(xt_ref, xa_ref):
    width, n = xt_ref.shape
    xa_ref[:width, :] = xt_ref[...]
    xa_ref[width:, :] = extras_x(rows_index(n), jnp.zeros((1, n), F32)).astype(BF16)


def first_kernel(log_nx, xa0_ref, mx_ref, ya_ref, b_ref, l_ref, m_ref, rows_ref, xa_ref, z_ref, zc_ref):
    nd, yd, depth = ya_ref.shape
    n = mx_ref.shape[1]
    width = depth - EXT
    ny = nd * yd
    scale = kappa_of(width) * LOG2E
    la2 = (mx_ref[...].astype(F32) - log_nx) * LOG2E
    y_rows = ya_ref[...].reshape(ny, depth)

    def row_tile(t):
        z_ref[...] = jnp.dot(y_rows, xa0_ref[:, t], preferred_element_type=F32)
        peak = max_down(z_ref, ny)
        b_ref[:, t] = -peak - jnp.log(exp_sum_down(z_ref, ny, scale, peak)) * (LOG2E / scale)

    for_tiles(n, row_tile)
    b_term = b_ref[...] + la2 / scale
    b_ref[...] = b_term
    xa_ref[:width, :] = xa0_ref[:width, :]
    xa_ref[width:, :] = extras_x(rows_index(n), b_term).astype(BF16)
    rows_ref[...] = xa_ref[...].T
    y_tile = TILE // yd

    def col_tile(t):
        y_part = ya_ref[pl.ds(t.start // yd, y_tile)].reshape(TILE, depth)
        zc_ref[...] = lax.dot_general(
            rows_ref[...], y_part, (((1,), (1,)), ((), ())), preferred_element_type=F32
        )
        peak = max_down(zc_ref, n)
        m_ref[:, t] = peak
        lse = scale * peak + jnp.log(exp_sum_down(zc_ref, n, scale, peak)) * LOG2E
        l_ref[:, :, t] = jnp.broadcast_to(lse[None], (nd, 1, TILE))

    for_tiles(ny, col_tile)


def plan_kernel(rows_ref, ya_ref, m_ref, high_ref, low_ref, yt_ref, zc_ref):
    nd, yd, depth = ya_ref.shape
    n = rows_ref.shape[0]
    scale = kappa_of(depth - EXT) * LOG2E
    y_tile = TILE // yd

    def col_tile(t):
        y_part = ya_ref[pl.ds(t.start // yd, y_tile)].reshape(TILE, depth)
        yt_ref[:, t] = y_part.T
        zc_ref[...] = lax.dot_general(
            rows_ref[...], y_part, (((1,), (1,)), ((), ())), preferred_element_type=F32
        )
        peak = m_ref[:, t]
        for r in range(0, n, STEP):
            value = jnp.exp2((zc_ref[r : r + STEP, :] - peak) * scale)
            high = value.astype(BF16)
            high_ref[r : r + STEP, t] = high
            low_ref[r : r + STEP, t] = (value - high.astype(F32)).astype(BF16)

    for_tiles(nd * yd, col_tile)


def stack(out_ref, width, points, factor):
    moved = points.astype(F32) * factor
    high = moved.astype(BF16)
    out_ref[:width, :] = high
    out_ref[width : 2 * width, :] = (moved - high.astype(F32)).astype(BF16)
    one, two, three = pieces(factor)
    index = lax.broadcasted_iota(jnp.int32, (PAD, factor.shape[1]), 0)
    out_ref[2 * width :, :] = select(index, {0: one, 1: two, 2: three}).astype(BF16)


def unstack(product, width):
    ext = product[2 * width :]
    return product[:width] + product[width : 2 * width], (ext[0:1] + ext[1:2]) + ext[2:3]


def second_kernel(
    log_nx, log_ny, xt_ref, mx_ref, b_ref, l_ref, m_ref, yt_ref, high_ref, low_ref,
    f_ref, r_ref, v_ref, s_ref, g_ref, xs_ref, gt_ref,
):
    width, n = xt_ref.shape
    ny = m_ref.shape[1]
    nd, yd = g_ref.shape[:2]
    kappa = kappa_of(width)
    scale = kappa * LOG2E
    l_all = l_ref[...]
    peak = jnp.max(l_all, axis=0)
    lse2 = peak + jnp.log(jnp.sum(jnp.exp2(l_all - peak[None]), axis=0)) * LOG2E
    old = yt_ref[width:, :].astype(F32)
    c_old = (old[0:1] + old[1:2]) + old[2:3]
    lb2 = (old[6:7] - log_ny) * LOG2E
    c_term = c_old + (lb2 - lse2) / scale
    v = jnp.exp2(scale * m_ref[...] + (lb2 - lse2))
    v_ref[...] = v
    one, two, three = pieces(v)
    index = lax.broadcasted_iota(jnp.int32, (PAD, ny), 0)
    v_rows = select(index, {0: one, 1: two, 2: three}).astype(BF16)
    across = (((1,), (1,)), ((), ()))
    sums = lax.dot_general(v_rows, high_ref[...], across, preferred_element_type=F32) + lax.dot_general(
        v_rows, low_ref[...], across, preferred_element_type=F32
    )
    rowsum = (sums[0:1] + sums[1:2]) + sums[2:3]
    log_row = jnp.log(rowsum)
    xt = xt_ref[...]
    xf = xt.astype(F32)
    f_ref[...] = jnp.sum(xf * xf, axis=0, keepdims=True) / width + EPSILON * (kappa * b_ref[...] - log_row)
    r = jnp.exp(mx_ref[...].astype(F32) - log_nx - log_row)
    r_ref[...] = r
    stack(xs_ref, width, xt, r)
    high, mid, low = pieces(c_term)
    index = lax.broadcasted_iota(jnp.int32, (EXT, TILE), 0)
    for k in range(ny // TILE):
        t = slice(k * TILE, (k + 1) * TILE)
        product = jnp.dot(xs_ref[...], high_ref[:, t], preferred_element_type=F32) + jnp.dot(
            xs_ref[...], low_ref[:, t], preferred_element_type=F32
        )
        moment, total = unstack(product, width)
        total = total * v[:, t]
        s_ref[:, :, t] = jnp.broadcast_to(total[None], (nd, 1, TILE))
        gt_ref[:width, t] = yt_ref[:width, t].astype(F32) * total - moment * v[:, t]
        one, two, three = pieces(total)
        gt_ref[width:, t] = select(index, {0: one, 1: two, 2: three, 3: high[:, t], 4: mid[:, t], 5: low[:, t]})
    g_ref[...] = gt_ref[...].T.astype(BF16).reshape(nd, yd, width + EXT)


def grad_x_kernel(log_nx, log_ny, xt_ref, r_ref, v_ref, s_ref, yt_ref, high_ref, low_ref, out_ref, ys_ref):
    width, n = xt_ref.shape
    ny = v_ref.shape[1]
    mass = yt_ref[width:, :].astype(F32)[6:7]
    colsum = jnp.sum(s_ref[...], axis=0)
    q = v_ref[...] * jnp.exp(mass + log_nx - jnp.log(colsum))
    stack(ys_ref, width, yt_ref[:width, :], q)
    across = (((1,), (1,)), ((), ()))
    for k in range(n // TILE):
        t = slice(k * TILE, (k + 1) * TILE)
        product = lax.dot_general(
            ys_ref[...], high_ref[t, :], across, preferred_element_type=F32
        ) + lax.dot_general(ys_ref[...], low_ref[t, :], across, preferred_element_type=F32)
        moved, total = unstack(product, width)
        out_ref[:, t] = (xt_ref[:, t].astype(F32) * total - moved) * (r_ref[:, t] * (1.0 / ny))


def grad_y_kernel(y_ref, my_ref, g_ref, out_ref, pot_ref):
    yd, width = y_ref.shape
    nd = g_ref.shape[0]
    total = g_ref[0].astype(F32)
    for k in range(1, nd):
        total = total + g_ref[k].astype(F32)
    part = total[:, width:]
    colsum = (part[:, 0:1] + part[:, 1:2]) + part[:, 2:3]
    c_term = ((part[:, 3:4] + part[:, 4:5]) + part[:, 5:6]) * (1.0 / nd)
    mass = to_column(my_ref[...].astype(F32))
    out_ref[...] = total[:, :width] * (jnp.exp(mass) / colsum)
    yf = y_ref[...].astype(F32)
    norm = jnp.sum(yf * yf, axis=1, keepdims=True)
    pot = norm / width - EPSILON * (jnp.log(colsum) - kappa_of(width) * c_term)
    pot_ref[...] = to_row(pot)


def call(kernel, outs, scratch, limit, *args):
    return pl.pallas_call(
        kernel,
        out_shape=outs,
        in_specs=[pl.BlockSpec(memory_space=pltpu.VMEM)] * len(args),
        out_specs=jax.tree.map(lambda _: pl.BlockSpec(memory_space=pltpu.VMEM), outs),
        scratch_shapes=scratch,
        compiler_params=pltpu.CompilerParams(vmem_limit_bytes=limit),
    )(*args)


def shape(dims, dtype=F32):
    return jax.ShapeDtypeStruct(dims, dtype)


def on_device(points_x, points_y, mass_x, mass_y):
    n, width = points_x.shape
    yd = points_y.shape[0]
    nd = lax.axis_size("row") * lax.axis_size("col")
    ny = nd * yd
    log_nx, log_ny = math.log(n * nd), math.log(ny)
    depth = width + EXT
    limit = (8 + 24 * ny // 1024) * 1024 * 1024 if ny <= 1024 else 56 * 1024 * 1024
    run = functools.partial
    xt = points_x.T
    mx = mass_x.reshape(1, n)
    my = mass_y.reshape(1, yd)
    y_own = call(run(prep_kernel, log_ny), shape((nd, yd, depth), BF16), [], limit, points_y, my)
    ya = lax.all_to_all(y_own, AXES, 0, 0, tiled=True)
    xa = call(prep_x_kernel, shape((depth, n), BF16), [], limit, xt)
    b_term, lse, peak, rows = call(
        run(first_kernel, log_nx),
        (shape((1, n)), shape((nd, 1, ny)), shape((1, ny)), shape((n, depth), BF16)),
        [pltpu.VMEM((depth, n), BF16), pltpu.VMEM((ny, TILE), F32), pltpu.VMEM((n, TILE), F32)],
        limit, xa, mx, ya,
    )
    lse = lax.all_to_all(lse, AXES, 0, 0, tiled=True)
    high, low, yt = call(
        plan_kernel,
        (shape((n, ny), BF16), shape((n, ny), BF16), shape((depth, ny), BF16)),
        [pltpu.VMEM((n, TILE), F32)],
        limit, rows, ya, peak,
    )
    f_pot, r, v, sums, g_part = call(
        run(second_kernel, log_nx, log_ny),
        (shape((1, n)), shape((1, n)), shape((1, ny)), shape((nd, 1, ny)), shape((nd, yd, depth), BF16)),
        [pltpu.VMEM((2 * width + PAD, n), BF16), pltpu.VMEM((depth, ny), F32)],
        limit, xt, mx, b_term, lse, peak, yt, high, low,
    )
    sums = lax.all_to_all(sums, AXES, 0, 0, tiled=True)
    g_all = lax.all_to_all(g_part, AXES, 0, 0, tiled=True)
    grad_xt = call(
        run(grad_x_kernel, log_nx, log_ny),
        shape((width, n)),
        [pltpu.VMEM((2 * width + PAD, ny), BF16)],
        limit, xt, r, v, sums, yt, high, low,
    )
    grad_y, g_pot = call(
        grad_y_kernel, (shape((yd, width)), shape((1, yd))), [], limit, points_y, my, g_all
    )
    return f_pot.reshape(n), g_pot.reshape(yd), grad_xt.T, grad_y


def solution(mesh):
    in_specs = (
        P(("groups", "row", "col"), None),
        P(("groups", "col", "row"), None),
        P(("groups", "row", "col")),
        P(("groups", "col", "row")),
    )
    out_specs = (
        P(("groups", "row", "col")),
        P(("groups", "col", "row")),
        P(("groups", "row", "col"), None),
        P(("groups", "col", "row"), None),
    )
    return jax.shard_map(
        on_device, mesh=mesh, in_specs=in_specs, out_specs=out_specs, check_vma=False
    )
```

```python
import functools
import math

import jax
import jax.numpy as jnp
from jax import lax
from jax.experimental import pallas as pl
from jax.experimental.pallas import tpu as pltpu
from jax.sharding import PartitionSpec as P

ITERS = 2
EPSILON = 0.02
LOG2E = math.log2(math.e)
TILE = 256
STEP = 32
EXT = 32
PAD = 16
LANES = 128
F32 = jnp.float32
BF16 = jnp.bfloat16


def kappa_of(width):
    return 2.0 / (width * EPSILON)


def pieces(value):
    high = value.astype(BF16).astype(F32)
    rest = value - high
    mid = rest.astype(BF16).astype(F32)
    return high, mid, rest - mid


def select(index, values):
    out = jnp.zeros(index.shape, F32)
    for k, value in values.items():
        out = jnp.where(index == k, value, out)
    return out


def extras_y(index, c_term, mass):
    high, mid, low = pieces(c_term)
    return select(index, {0: high, 1: mid, 2: low, 3: 1.0, 4: 1.0, 5: 1.0, 6: mass})


def extras_x(index, b_term):
    high, mid, low = pieces(b_term)
    return select(index, {0: 1.0, 1: 1.0, 2: 1.0, 3: high, 4: mid, 5: low})


def rows_index(columns):
    return lax.broadcasted_iota(jnp.int32, (EXT, columns), 0)


def to_column(row):
    size = row.shape[1]
    eye = lax.broadcasted_iota(jnp.int32, (size, size), 0) == lax.broadcasted_iota(jnp.int32, (size, size), 1)
    return jnp.sum(jnp.where(eye, row, 0.0), axis=1, keepdims=True)


def to_row(column):
    size = column.shape[0]
    eye = lax.broadcasted_iota(jnp.int32, (size, size), 0) == lax.broadcasted_iota(jnp.int32, (size, size), 1)
    return jnp.sum(jnp.where(eye, column, 0.0), axis=0, keepdims=True)


def for_tiles(total, body):
    count = total // TILE
    if count <= 4:
        for t in range(count):
            body(pl.ds(t * TILE, TILE))
    else:

        @pl.loop(0, count)
        def _(t):
            body(pl.ds(pl.multiple_of(t * TILE, TILE), TILE))


def max_down(z_ref, rows):
    peak = z_ref[0:STEP, :]
    for r in range(STEP, rows, STEP):
        peak = jnp.maximum(peak, z_ref[r : r + STEP, :])
    return jnp.max(peak, axis=0, keepdims=True)


def exp_sum_down(z_ref, rows, scale, shift):
    total = jnp.zeros((STEP, TILE), F32)
    for r in range(0, rows, STEP):
        total = total + jnp.exp2((z_ref[r : r + STEP, :] - shift) * scale)
    return jnp.sum(total, axis=0, keepdims=True)


def prep_kernel(log_ny, y_ref, my_ref, out_ref):
    width = y_ref.shape[1]
    y = y_ref[...]
    yf = y.astype(F32)
    norm = jnp.sum(yf * yf, axis=1, keepdims=True)
    mass = to_column(my_ref[...].astype(F32))
    c_term = (mass - log_ny) / kappa_of(width) - 0.5 * norm
    index = lax.broadcasted_iota(jnp.int32, (y.shape[0], EXT), 1)
    ext = extras_y(index, c_term, mass).astype(BF16)
    for k in range(out_ref.shape[0]):
        out_ref[k, :, :width] = y
        out_ref[k, :, width:] = ext


def prep_x_kernel(xt_ref, xa_ref):
    width, n = xt_ref.shape
    xa_ref[:width, :] = xt_ref[...]
    xa_ref[width:, :] = extras_x(rows_index(n), jnp.zeros((1, n), F32)).astype(BF16)


def first_kernel(
    log_nx, xa0_ref, mx_ref, mine_ref, other_ref, ya_ref, b_ref, l_ref, m_ref, rows_ref, xa_ref, z_ref, zc_ref
):
    rows, yd, depth = mine_ref.shape
    n = mx_ref.shape[1]
    width = depth - EXT
    half = rows * yd
    ny = 2 * half
    scale = kappa_of(width) * LOG2E
    la2 = (mx_ref[...].astype(F32) - log_nx) * LOG2E
    col = lax.axis_index("col")
    ya_ref[pl.ds(pl.multiple_of(col * half, half), half), :] = mine_ref[...].reshape(half, depth)
    ya_ref[pl.ds(pl.multiple_of((1 - col) * half, half), half), :] = other_ref[...].reshape(half, depth)

    def row_tile(t):
        z_ref[...] = jnp.dot(ya_ref[...], xa0_ref[:, t], preferred_element_type=F32)
        peak = max_down(z_ref, ny)
        b_ref[:, t] = -peak - jnp.log(exp_sum_down(z_ref, ny, scale, peak)) * (LOG2E / scale)

    for_tiles(n, row_tile)
    b_term = b_ref[...] + la2 / scale
    b_ref[...] = b_term
    xa_ref[:width, :] = xa0_ref[:width, :]
    xa_ref[width:, :] = extras_x(rows_index(n), b_term).astype(BF16)
    rows_ref[...] = xa_ref[...].T

    def col_tile(t):
        zc_ref[...] = lax.dot_general(
            rows_ref[...], ya_ref[t, :], (((1,), (1,)), ((), ())), preferred_element_type=F32
        )
        peak = max_down(zc_ref, n)
        m_ref[:, t] = peak
        lse = scale * peak + jnp.log(exp_sum_down(zc_ref, n, scale, peak)) * LOG2E
        l_ref[:, :, t] = jnp.broadcast_to(lse[None], (l_ref.shape[0], 1, TILE))

    for_tiles(ny, col_tile)


def plan_kernel(rows_ref, ya_ref, m_ref, high_ref, low_ref, yt_ref, zc_ref):
    ny, depth = ya_ref.shape
    n = rows_ref.shape[0]
    scale = kappa_of(depth - EXT) * LOG2E

    def col_tile(t):
        y_part = ya_ref[t, :]
        yt_ref[:, t] = y_part.T
        zc_ref[...] = lax.dot_general(
            rows_ref[...], y_part, (((1,), (1,)), ((), ())), preferred_element_type=F32
        )
        peak = m_ref[:, t]
        for r in range(0, n, STEP):
            value = jnp.exp2((zc_ref[r : r + STEP, :] - peak) * scale)
            high = value.astype(BF16)
            high_ref[r : r + STEP, t] = high
            low_ref[r : r + STEP, t] = (value - high.astype(F32)).astype(BF16)

    for_tiles(ny, col_tile)


def stack(out_ref, width, points, factor):
    moved = points.astype(F32) * factor
    high = moved.astype(BF16)
    out_ref[:width, :] = high
    out_ref[width : 2 * width, :] = (moved - high.astype(F32)).astype(BF16)
    one, two, three = pieces(factor)
    index = lax.broadcasted_iota(jnp.int32, (PAD, factor.shape[1]), 0)
    out_ref[2 * width :, :] = select(index, {0: one, 1: two, 2: three}).astype(BF16)


def unstack(product, width):
    ext = product[2 * width :]
    return product[:width] + product[width : 2 * width], (ext[0:1] + ext[1:2]) + ext[2:3]


def to_lanes(row):
    return jnp.concatenate([row[:, k : k + LANES] for k in range(0, row.shape[1], LANES)], axis=0)


def from_lanes(block):
    return jnp.concatenate([block[k : k + 1] for k in range(block.shape[0])], axis=1)


def write_sums(ref, start, row):
    count = row.shape[1] // LANES
    for k, part in enumerate(pieces(row)):
        ref[start + k * count : start + (k + 1) * count, :] = to_lanes(part)


def sums_rows(ny):
    return -(-3 * ny // LANES // 16) * 16


def second_kernel(
    log_nx, log_ny, xt_ref, mx_ref, b_ref, l_ref, other_ref, m_ref, yt_ref, high_ref, low_ref,
    f_ref, r_ref, v_ref, c_ref, keep_ref, send_ref, xs_ref, gt_ref, sp_ref, part_ref,
):
    width, n = xt_ref.shape
    ny = m_ref.shape[1]
    half = ny // 2
    kappa = kappa_of(width)
    scale = kappa * LOG2E
    l_mine, l_other = l_ref[...], other_ref[...]
    peak = jnp.maximum(jnp.max(l_mine, axis=0), jnp.max(l_other, axis=0))
    total = jnp.sum(jnp.exp2(l_mine - peak[None]), axis=0) + jnp.sum(jnp.exp2(l_other - peak[None]), axis=0)
    lse2 = peak + jnp.log(total) * LOG2E
    old = yt_ref[width:, :].astype(F32)
    c_old = (old[0:1] + old[1:2]) + old[2:3]
    lb2 = (old[6:7] - log_ny) * LOG2E
    c_ref[...] = to_lanes(c_old + (lb2 - lse2) / scale)
    v = jnp.exp2(scale * m_ref[...] + (lb2 - lse2))
    v_ref[...] = v
    one, two, three = pieces(v)
    index = lax.broadcasted_iota(jnp.int32, (PAD, ny), 0)
    v_rows = select(index, {0: one, 1: two, 2: three}).astype(BF16)
    across = (((1,), (1,)), ((), ()))
    sums = lax.dot_general(v_rows, high_ref[...], across, preferred_element_type=F32) + lax.dot_general(
        v_rows, low_ref[...], across, preferred_element_type=F32
    )
    rowsum = (sums[0:1] + sums[1:2]) + sums[2:3]
    log_row = jnp.log(rowsum)
    xt = xt_ref[...]
    xf = xt.astype(F32)
    f_ref[...] = jnp.sum(xf * xf, axis=0, keepdims=True) / width + EPSILON * (kappa * b_ref[...] - log_row)
    r = jnp.exp(mx_ref[...].astype(F32) - log_nx - log_row)
    r_ref[...] = r
    stack(xs_ref, width, xt, r)
    totals = []
    for k in range(ny // TILE):
        t = slice(k * TILE, (k + 1) * TILE)
        product = jnp.dot(xs_ref[...], high_ref[:, t], preferred_element_type=F32) + jnp.dot(
            xs_ref[...], low_ref[:, t], preferred_element_type=F32
        )
        moment, total = unstack(product, width)
        total = total * v[:, t]
        totals.append(total)
        gt_ref[:width, t] = yt_ref[:width, t].astype(F32) * total - moment * v[:, t]
    gt_ref[width:, :] = jnp.zeros((EXT, ny), F32)
    sp_ref[...] = jnp.zeros(sp_ref.shape, F32)
    write_sums(sp_ref, 0, jnp.concatenate(totals, axis=1))
    part_ref[...] = gt_ref[...].T.astype(BF16)
    col = lax.axis_index("col")
    keep_ref[:half, :] = part_ref[pl.ds(pl.multiple_of(col * half, half), half), :]
    send_ref[:half, :] = part_ref[pl.ds(pl.multiple_of((1 - col) * half, half), half), :]
    sums = sp_ref[...].astype(BF16)
    keep_ref[half:, :] = sums
    send_ref[half:, :] = sums


def add_kernel(mine_ref, other_ref, out_ref, sp_ref):
    rows, block = out_ref.shape[:2]
    extra = sp_ref.shape[0]
    yd = block - extra
    ny = 2 * rows * yd
    count = ny // LANES
    total = mine_ref[...].astype(F32) + other_ref[...].astype(F32)
    ext = total[rows * yd :]
    whole = (ext[:count] + ext[count : 2 * count]) + ext[2 * count : 3 * count]
    sp_ref[...] = jnp.zeros(sp_ref.shape, F32)
    for k, part in enumerate(pieces(whole)):
        sp_ref[k * count : (k + 1) * count, :] = part
    sums = sp_ref[...].astype(BF16)
    for r in range(rows):
        out_ref[r, :yd, :] = total[r * yd : (r + 1) * yd].astype(BF16)
        out_ref[r, yd:, :] = sums


def own_part(ref, yd):
    block = lax.axis_index("col") * lax.axis_size("row") + lax.axis_index("row")
    fit = LANES // yd
    row = ref[pl.ds(block // fit, 1), :]
    out = row[:, :yd]
    for k in range(1, fit):
        out = jnp.where(block % fit == k, row[:, k * yd : (k + 1) * yd], out)
    return out


def last_kernel(
    log_nx, log_ny, xt_ref, r_ref, v_ref, c_ref, g_ref, yt_ref, high_ref, low_ref, y_ref, my_ref,
    gx_ref, gy_ref, pot_ref, ys_ref, sum_ref,
):
    width, n = xt_ref.shape
    ny = v_ref.shape[1]
    yd = y_ref.shape[0]
    count = ny // LANES
    total = g_ref[0].astype(F32)
    for k in range(1, g_ref.shape[0]):
        total = total + g_ref[k].astype(F32)
    ext = total[yd:]
    sum_ref[...] = (ext[:count] + ext[count : 2 * count]) + ext[2 * count : 3 * count]
    mass = yt_ref[width:, :].astype(F32)[6:7]
    q = v_ref[...] * jnp.exp(mass + log_nx - jnp.log(from_lanes(sum_ref[...])))
    stack(ys_ref, width, yt_ref[:width, :], q)
    across = (((1,), (1,)), ((), ()))
    for k in range(n // TILE):
        t = slice(k * TILE, (k + 1) * TILE)
        product = lax.dot_general(
            ys_ref[...], high_ref[t, :], across, preferred_element_type=F32
        ) + lax.dot_general(ys_ref[...], low_ref[t, :], across, preferred_element_type=F32)
        moved, weight = unstack(product, width)
        gx_ref[:, t] = (xt_ref[:, t].astype(F32) * weight - moved) * (r_ref[:, t] * (1.0 / ny))
    colsum = own_part(sum_ref, yd)
    c_term = own_part(c_ref, yd)
    gy_ref[...] = total[:yd, :width] * to_column(jnp.exp(my_ref[...].astype(F32)) / colsum)
    yf = y_ref[...].astype(F32)
    norm = to_row(jnp.sum(yf * yf, axis=1, keepdims=True))
    pot_ref[...] = norm / width - EPSILON * (jnp.log(colsum) - kappa_of(width) * c_term)


def call(kernel, outs, scratch, limit, *args):
    return pl.pallas_call(
        kernel,
        out_shape=outs,
        in_specs=[pl.BlockSpec(memory_space=pltpu.VMEM)] * len(args),
        out_specs=jax.tree.map(lambda _: pl.BlockSpec(memory_space=pltpu.VMEM), outs),
        scratch_shapes=scratch,
        compiler_params=pltpu.CompilerParams(vmem_limit_bytes=limit),
    )(*args)


def shape(dims, dtype=F32):
    return jax.ShapeDtypeStruct(dims, dtype)


def swap(value):
    return lax.ppermute(value, "col", [(0, 1), (1, 0)])


def on_device(points_x, points_y, mass_x, mass_y):
    n, width = points_x.shape
    yd = points_y.shape[0]
    nd = lax.axis_size("row") * lax.axis_size("col")
    ny = nd * yd
    log_nx, log_ny = math.log(n * nd), math.log(ny)
    depth = width + EXT
    limit = (12 if ny <= 1024 else 56) * 1024 * 1024
    rows = lax.axis_size("row")
    extra = sums_rows(ny)
    half = ny // 2
    run = functools.partial
    xt = points_x.T
    mx = mass_x.reshape(1, n)
    my = mass_y.reshape(1, yd)
    y_own = call(run(prep_kernel, log_ny), shape((rows, yd, depth), BF16), [], limit, points_y, my)
    y_mine = lax.all_to_all(y_own, "row", 0, 0, tiled=True)
    y_other = swap(y_mine)
    xa = call(prep_x_kernel, shape((depth, n), BF16), [], limit, xt)
    ya, b_term, lse, peak, x_rows = call(
        run(first_kernel, log_nx),
        (
            shape((ny, depth), BF16), shape((1, n)), shape((rows, 1, ny)), shape((1, ny)), shape((n, depth), BF16),
        ),
        [pltpu.VMEM((depth, n), BF16), pltpu.VMEM((ny, TILE), F32), pltpu.VMEM((n, TILE), F32)],
        limit, xa, mx, y_mine, y_other,
    )
    lse = lax.all_to_all(lse, "row", 0, 0, tiled=True)
    lse_other = swap(lse)
    high, low, yt = call(
        plan_kernel,
        (shape((n, ny), BF16), shape((n, ny), BF16), shape((depth, ny), BF16)),
        [pltpu.VMEM((n, TILE), F32)],
        limit, x_rows, ya, peak,
    )
    f_pot, r, v, c_term, keep, send = call(
        run(second_kernel, log_nx, log_ny),
        (
            shape((1, n)), shape((1, n)), shape((1, ny)), shape((ny // LANES, LANES)),
            shape((half + extra, depth), BF16), shape((half + extra, depth), BF16),
        ),
        [
            pltpu.VMEM((2 * width + PAD, n), BF16), pltpu.VMEM((depth, ny), F32), pltpu.VMEM((extra, LANES), F32),
            pltpu.VMEM((ny, depth), BF16),
        ],
        limit, xt, mx, b_term, lse, lse_other, peak, yt, high, low,
    )
    part = call(
        add_kernel, shape((rows, yd + extra, depth), BF16), [pltpu.VMEM((extra, LANES), F32)],
        limit, keep, swap(send),
    )
    part = lax.all_to_all(part, "row", 0, 0, tiled=True)
    grad_xt, grad_y, g_pot = call(
        run(last_kernel, log_nx, log_ny),
        (shape((width, n)), shape((yd, width)), shape((1, yd))),
        [pltpu.VMEM((2 * width + PAD, ny), BF16), pltpu.VMEM((ny // LANES, LANES), F32)],
        limit, xt, r, v, c_term, part, yt, high, low, points_y, my,
    )
    return f_pot.reshape(n), g_pot.reshape(yd), grad_xt.T, grad_y


def solution(mesh):
    in_specs = (
        P(("groups", "row", "col"), None),
        P(("groups", "col", "row"), None),
        P(("groups", "row", "col")),
        P(("groups", "col", "row")),
    )
    out_specs = (
        P(("groups", "row", "col")),
        P(("groups", "col", "row")),
        P(("groups", "row", "col"), None),
        P(("groups", "col", "row"), None),
    )
    return jax.shard_map(
        on_device, mesh=mesh, in_specs=in_specs, out_specs=out_specs, check_vma=False
    )
```

```python
import functools
import math

import jax
import jax.numpy as jnp
from jax import lax
from jax.experimental import pallas as pl
from jax.experimental.pallas import tpu as pltpu
from jax.sharding import PartitionSpec as P

ITERS = 2
EPSILON = 0.02
LOG2E = math.log2(math.e)
TILE = 256
STEP = 32
EXT = 32
PAD = 16
LANES = 128
F32 = jnp.float32
BF16 = jnp.bfloat16


def kappa_of(width):
    return 2.0 / (width * EPSILON)


def pieces(value):
    high = value.astype(BF16).astype(F32)
    rest = value - high
    mid = rest.astype(BF16).astype(F32)
    return high, mid, rest - mid


def select(index, values):
    out = jnp.zeros(index.shape, F32)
    for k, value in values.items():
        out = jnp.where(index == k, value, out)
    return out


def extras_y(index, c_term, mass):
    high, mid, low = pieces(c_term)
    return select(index, {0: high, 1: mid, 2: low, 3: 1.0, 4: 1.0, 5: 1.0, 6: mass})


def extras_x(index, b_term):
    high, mid, low = pieces(b_term)
    return select(index, {0: 1.0, 1: 1.0, 2: 1.0, 3: high, 4: mid, 5: low})


def rows_index(columns):
    return lax.broadcasted_iota(jnp.int32, (EXT, columns), 0)


def to_column(row):
    size = row.shape[1]
    eye = lax.broadcasted_iota(jnp.int32, (size, size), 0) == lax.broadcasted_iota(jnp.int32, (size, size), 1)
    return jnp.sum(jnp.where(eye, row, 0.0), axis=1, keepdims=True)


def to_row(column):
    size = column.shape[0]
    eye = lax.broadcasted_iota(jnp.int32, (size, size), 0) == lax.broadcasted_iota(jnp.int32, (size, size), 1)
    return jnp.sum(jnp.where(eye, column, 0.0), axis=0, keepdims=True)


def for_tiles(total, body):
    count = total // TILE
    if count <= 4:
        for t in range(count):
            body(pl.ds(t * TILE, TILE))
    else:

        @pl.loop(0, count)
        def _(t):
            body(pl.ds(pl.multiple_of(t * TILE, TILE), TILE))


def max_down(z_ref, rows):
    peak = z_ref[0:STEP, :]
    for r in range(STEP, rows, STEP):
        peak = jnp.maximum(peak, z_ref[r : r + STEP, :])
    return jnp.max(peak, axis=0, keepdims=True)


def exp_sum_down(z_ref, rows, scale, shift):
    total = jnp.zeros((STEP, TILE), F32)
    for r in range(0, rows, STEP):
        total = total + jnp.exp2((z_ref[r : r + STEP, :] - shift) * scale)
    return jnp.sum(total, axis=0, keepdims=True)


def to_lanes(row):
    return jnp.concatenate([row[:, k : k + LANES] for k in range(0, row.shape[1], LANES)], axis=0)


def from_lanes(block):
    return jnp.concatenate([block[k : k + 1] for k in range(block.shape[0])], axis=1)


def write_sums(ref, start, row):
    count = row.shape[1] // LANES
    for k, part in enumerate(pieces(row)):
        ref[start + k * count : start + (k + 1) * count, :] = to_lanes(part)


def sums_rows(ny):
    return -(-3 * ny // LANES // 16) * 16


def copies(sems, *pairs):
    moves = [pltpu.make_async_copy(a, b, sems.at[k]) for k, (a, b) in enumerate(pairs)]
    for move in moves:
        move.start()
    for move in moves:
        move.wait()


def prep_y_kernel(log_ny, y_hbm, my_hbm, out_ref, y_ref, my_ref, sems):
    copies(sems, (y_hbm, y_ref), (my_hbm, my_ref))
    width = y_ref.shape[1]
    y = y_ref[...]
    yf = y.astype(F32)
    norm = jnp.sum(yf * yf, axis=1, keepdims=True)
    mass = to_column(my_ref[...].astype(F32))
    c_term = (mass - log_ny) / kappa_of(width) - 0.5 * norm
    index = lax.broadcasted_iota(jnp.int32, (y.shape[0], EXT), 1)
    out_ref[:, :width] = y
    out_ref[:, width:] = extras_y(index, c_term, mass).astype(BF16)


def prep_x_kernel(xt_hbm, mx_hbm, xa_ref, mx_ref, norm_ref, mx_in, sems):
    width, n = xt_hbm.shape
    copies(sems, (xt_hbm, xa_ref.at[:width, :]), (mx_hbm, mx_in))
    xa_ref[width:, :] = extras_x(rows_index(n), jnp.zeros((1, n), F32)).astype(BF16)
    mx_ref[...] = from_lanes(mx_in[...].astype(F32))
    xf = xa_ref[:width, :].astype(F32)
    norm_ref[...] = jnp.sum(xf * xf, axis=0, keepdims=True)


def join_kernel(mine_ref, other_ref, out_ref):
    rows = mine_ref.shape[0]
    out_ref[:rows, :] = mine_ref[...]
    out_ref[rows:, :] = other_ref[...]


def lse_kernel(mine_ref, other_ref, out_ref):
    mine, other = mine_ref[...], other_ref[...]
    peak = jnp.maximum(mine, other)
    out_ref[...] = peak + jnp.log(jnp.exp2(mine - peak) + jnp.exp2(other - peak)) * LOG2E


def reverse_bits(value, count):
    return sum(((value >> k) & 1) << (count - 1 - k) for k in range(count))


def first_kernel(
    log_nx, rows, xa0_ref, mx_ref, mine_ref, other_ref, ya_ref, b_ref, l_ref, m_ref, rows_ref, xa_ref, z_ref, zc_ref,
    b2_ref,
):
    half, depth = mine_ref.shape
    yd = half // rows
    n = mx_ref.shape[1]
    width = depth - EXT
    ny = 2 * half
    row, col = lax.axis_index("row"), lax.axis_index("col")
    for k in range(rows):
        place = (row ^ reverse_bits(k, rows.bit_length() - 1)) * yd
        ya_ref[pl.ds(pl.multiple_of(col * half + place, yd), yd), :] = mine_ref[k * yd : (k + 1) * yd, :]
        ya_ref[pl.ds(pl.multiple_of((1 - col) * half + place, yd), yd), :] = other_ref[k * yd : (k + 1) * yd, :]
    scale = kappa_of(width) * LOG2E
    la2 = (mx_ref[...] - log_nx) * LOG2E

    def row_tile(t):
        z_ref[...] = jnp.dot(ya_ref[...], xa0_ref[:, t], preferred_element_type=F32)
        peak = max_down(z_ref, ny)
        b_ref[:, t] = -peak - jnp.log(exp_sum_down(z_ref, ny, scale, peak)) * (LOG2E / scale)

    for_tiles(n, row_tile)
    b_term = b_ref[...] + la2 / scale
    b_ref[...] = b_term
    xa_ref[:width, :] = xa0_ref[:width, :]
    xa_ref[width:, :] = extras_x(rows_index(n), b_term).astype(BF16)
    rows_ref[...] = xa_ref[...].T

    def col_tile(t):
        zc_ref[...] = lax.dot_general(
            rows_ref[...], ya_ref[t, :], (((1,), (1,)), ((), ())), preferred_element_type=F32
        )
        peak = max_down(zc_ref, n)
        m_ref[:, t] = peak
        b2_ref[:, t] = scale * peak + jnp.log(exp_sum_down(zc_ref, n, scale, peak)) * LOG2E

    for_tiles(ny, col_tile)
    l_ref[...] = to_lanes(b2_ref[...])


def plan_kernel(rows_ref, ya_ref, m_ref, high_ref, low_ref, yt_ref, zc_ref):
    ny, depth = ya_ref.shape
    n = rows_ref.shape[0]
    scale = kappa_of(depth - EXT) * LOG2E

    def col_tile(t):
        y_part = ya_ref[t, :]
        yt_ref[:, t] = y_part.T
        zc_ref[...] = lax.dot_general(
            rows_ref[...], y_part, (((1,), (1,)), ((), ())), preferred_element_type=F32
        )
        peak = m_ref[:, t]
        for r in range(0, n, STEP):
            value = jnp.exp2((zc_ref[r : r + STEP, :] - peak) * scale)
            high = value.astype(BF16)
            high_ref[r : r + STEP, t] = high
            low_ref[r : r + STEP, t] = (value - high.astype(F32)).astype(BF16)

    for_tiles(ny, col_tile)


def stack(out_ref, width, points, factor):
    moved = points.astype(F32) * factor
    high = moved.astype(BF16)
    out_ref[:width, :] = high
    out_ref[width : 2 * width, :] = (moved - high.astype(F32)).astype(BF16)
    one, two, three = pieces(factor)
    index = lax.broadcasted_iota(jnp.int32, (PAD, factor.shape[1]), 0)
    out_ref[2 * width :, :] = select(index, {0: one, 1: two, 2: three}).astype(BF16)


def unstack(product, width):
    ext = product[2 * width :]
    return product[:width] + product[width : 2 * width], (ext[0:1] + ext[1:2]) + ext[2:3]


def second_kernel(
    log_nx, log_ny, xa_ref, mx_ref, norm_ref, b_ref, l_ref, m_ref, yt_ref, high_ref, low_ref,
    f_ref, r_ref, v_ref, c_ref, keep_ref, sum_ref, send_ref, xs_ref, gt_ref, part_ref,
):
    width = xa_ref.shape[0] - EXT
    ny = m_ref.shape[1]
    kappa = kappa_of(width)
    scale = kappa * LOG2E
    lse2 = from_lanes(l_ref[...])
    old = yt_ref[width:, :].astype(F32)
    c_old = (old[0:1] + old[1:2]) + old[2:3]
    lb2 = (old[6:7] - log_ny) * LOG2E
    c_ref[...] = to_lanes(c_old + (lb2 - lse2) / scale)
    v = jnp.exp2(scale * m_ref[...] + (lb2 - lse2))
    v_ref[...] = v
    one, two, three = pieces(v)
    index = lax.broadcasted_iota(jnp.int32, (PAD, ny), 0)
    v_rows = select(index, {0: one, 1: two, 2: three}).astype(BF16)
    across = (((1,), (1,)), ((), ()))
    sums = lax.dot_general(v_rows, high_ref[...], across, preferred_element_type=F32) + lax.dot_general(
        v_rows, low_ref[...], across, preferred_element_type=F32
    )
    rowsum = (sums[0:1] + sums[1:2]) + sums[2:3]
    log_row = jnp.log(rowsum)
    f_ref[...] = norm_ref[...] / width + EPSILON * (kappa * b_ref[...] - log_row)
    r = jnp.exp(mx_ref[...] - log_nx - log_row)
    r_ref[...] = r
    stack(xs_ref, width, xa_ref[:width, :], r)
    totals = []
    for k in range(ny // TILE):
        t = slice(k * TILE, (k + 1) * TILE)
        product = jnp.dot(xs_ref[...], high_ref[:, t], preferred_element_type=F32) + jnp.dot(
            xs_ref[...], low_ref[:, t], preferred_element_type=F32
        )
        moment, total = unstack(product, width)
        total = total * v[:, t]
        totals.append(total)
        gt_ref[:width, t] = yt_ref[:width, t].astype(F32) * total - moment * v[:, t]
    gt_ref[width:, :] = jnp.zeros((EXT, ny), F32)
    part_ref[...] = gt_ref[...].T
    sum_ref[...] = to_lanes(jnp.concatenate(totals, axis=1))
    split(lax.axis_index("col"), part_ref, sum_ref[...], keep_ref, send_ref)


def split(bit, part_ref, sums, keep_ref, send_ref):
    half = keep_ref.shape[0]
    keep_ref[...] = part_ref[pl.ds(pl.multiple_of(bit * half, half), half), :]
    send_ref[:half, :] = part_ref[pl.ds(pl.multiple_of((1 - bit) * half, half), half), :].astype(BF16)
    used = 3 * sums.shape[0]
    spare = send_ref.shape[0] - half - used
    parts = list(pieces(sums)) + ([jnp.zeros((spare, LANES), F32)] if spare else [])
    send_ref[half:, :] = jnp.concatenate(parts, axis=0).astype(BF16)


def add_received(keep_ref, sum_ref, got_ref):
    half = keep_ref.shape[0]
    count = sum_ref.shape[0]
    ext = got_ref[half:, :].astype(F32)
    sums = sum_ref[...] + ((ext[:count] + ext[count : 2 * count]) + ext[2 * count : 3 * count])
    return keep_ref[...] + got_ref[:half, :].astype(F32), sums


def add_kernel(shift, old_ref, sum0_ref, got_ref, keep_ref, sum_ref, send_ref, part_ref):
    total, sums = add_received(old_ref, sum0_ref, got_ref)
    part_ref[...] = total
    sum_ref[...] = sums
    split((lax.axis_index("row") >> shift) & 1, part_ref, sums, keep_ref, send_ref)


def own_part(ref, yd):
    block = lax.axis_index("col") * lax.axis_size("row") + lax.axis_index("row")
    fit = LANES // yd
    row = ref[pl.ds(block // fit, 1), :]
    out = row[:, :yd]
    for k in range(1, fit):
        out = jnp.where(block % fit == k, row[:, k * yd : (k + 1) * yd], out)
    return out


def last_kernel(
    log_nx, log_ny, xa_ref, r_ref, v_ref, c_ref, keep_ref, sum0_ref, got_ref, yt_ref, high_ref, low_ref, y_ref,
    gx_ref, gy_ref, pot_ref, ys_ref, sum_ref,
):
    width, n = gx_ref.shape
    ny = v_ref.shape[1]
    yd = y_ref.shape[0]
    total, sums = add_received(keep_ref, sum0_ref, got_ref)
    sum_ref[...] = sums
    mass = yt_ref[width:, :].astype(F32)[6:7]
    q = v_ref[...] * jnp.exp(mass + log_nx - jnp.log(from_lanes(sums)))
    stack(ys_ref, width, yt_ref[:width, :], q)
    across = (((1,), (1,)), ((), ()))
    for k in range(n // TILE):
        t = slice(k * TILE, (k + 1) * TILE)
        product = lax.dot_general(
            ys_ref[...], high_ref[t, :], across, preferred_element_type=F32
        ) + lax.dot_general(ys_ref[...], low_ref[t, :], across, preferred_element_type=F32)
        moved, weight = unstack(product, width)
        gx_ref[:, t] = (xa_ref[:width, t].astype(F32) * weight - moved) * (r_ref[:, t] * (1.0 / ny))
    colsum = own_part(sum_ref, yd)
    c_term = own_part(c_ref, yd)
    own = y_ref[...].astype(F32)
    gy_ref[...] = total[:, :width] * (jnp.exp(own[:, width + 6 : width + 7]) * to_column(1.0 / colsum))
    norm = to_row(jnp.sum(own[:, :width] * own[:, :width], axis=1, keepdims=True))
    pot_ref[...] = norm / width - EPSILON * (jnp.log(colsum) - kappa_of(width) * c_term)


def call(kernel, outs, scratch, limit, *args, space=pltpu.VMEM):
    return pl.pallas_call(
        kernel,
        out_shape=outs,
        in_specs=[pl.BlockSpec(memory_space=space)] * len(args),
        out_specs=jax.tree.map(lambda _: pl.BlockSpec(memory_space=pltpu.VMEM), outs),
        scratch_shapes=scratch,
        compiler_params=pltpu.CompilerParams(vmem_limit_bytes=limit),
    )(*args)


def shape(dims, dtype=F32):
    return jax.ShapeDtypeStruct(dims, dtype)


def swap(value, axis, size, step):
    return lax.ppermute(value, axis, [(k, k ^ step) for k in range(size)])


def on_device(points_x, points_y, mass_x, mass_y):
    n, width = points_x.shape
    yd = points_y.shape[0]
    rows = lax.axis_size("row")
    ny = 2 * rows * yd
    half = ny // 2
    count = ny // LANES
    levels = rows.bit_length() - 1
    log_nx, log_ny = math.log(n * 2 * rows), math.log(ny)
    depth = width + EXT
    limit = (12 if ny <= 1024 else 56) * 1024 * 1024
    extra = sums_rows(ny)
    run = functools.partial
    vmem = pltpu.VMEM
    two_sems = pltpu.SemaphoreType.DMA((2,))

    y_own = call(
        run(prep_y_kernel, log_ny), shape((yd, depth), BF16),
        [vmem((yd, width), BF16), vmem((1, yd), BF16), two_sems],
        limit, points_y, mass_y.reshape(1, yd), space=pl.ANY,
    )
    xa, mx, norm = call(
        prep_x_kernel, (shape((depth, n), BF16), shape((1, n)), shape((1, n))),
        [vmem((n // LANES, LANES), BF16), two_sems],
        limit, points_x.T, mass_x.reshape(n // LANES, LANES), space=pl.ANY,
    )
    y_mine = y_own
    for k in reversed(range(levels)):
        got = swap(y_mine, "row", rows, 1 << k)
        y_mine = call(join_kernel, shape((2 * got.shape[0], depth), BF16), [], limit, y_mine, got)
    y_other = swap(y_mine, "col", 2, 1)
    ya, b_term, lse, peak, x_rows = call(
        run(first_kernel, log_nx, rows),
        (shape((ny, depth), BF16), shape((1, n)), shape((count, LANES)), shape((1, ny)), shape((n, depth), BF16)),
        [vmem((depth, n), BF16), vmem((ny, TILE), F32), vmem((n, TILE), F32), vmem((1, ny), F32)],
        limit, xa, mx, y_mine, y_other,
    )
    high, low, yt = call(
        plan_kernel,
        (shape((n, ny), BF16), shape((n, ny), BF16), shape((depth, ny), BF16)),
        [vmem((n, TILE), F32)],
        limit, x_rows, ya, peak,
    )
    for k in reversed(range(levels)):
        lse = call(lse_kernel, shape((count, LANES)), [], limit, lse, swap(lse, "row", rows, 1 << k))
    lse = call(lse_kernel, shape((count, LANES)), [], limit, lse, swap(lse, "col", 2, 1))
    f_pot, r, v, c_term, keep, sums, send = call(
        run(second_kernel, log_nx, log_ny),
        (
            shape((1, n)), shape((1, n)), shape((1, ny)), shape((count, LANES)),
            shape((half, depth)), shape((count, LANES)), shape((half + extra, depth), BF16),
        ),
        [vmem((2 * width + PAD, n), BF16), vmem((depth, ny), F32), vmem((ny, depth), F32)],
        limit, xa, mx, norm, b_term, lse, peak, yt, high, low,
    )
    got = swap(send, "col", 2, 1)
    for k in reversed(range(levels)):
        half = half // 2
        keep, sums, send = call(
            run(add_kernel, k),
            (shape((half, depth)), shape((count, LANES)), shape((half + extra, depth), BF16)),
            [vmem((2 * half, depth), F32)],
            limit, keep, sums, got,
        )
        got = swap(send, "row", rows, 1 << k)
    grad_xt, grad_y, g_pot = call(
        run(last_kernel, log_nx, log_ny),
        (shape((width, n)), shape((yd, width)), shape((1, yd))),
        [vmem((2 * width + PAD, ny), BF16), vmem((count, LANES), F32)],
        limit, xa, r, v, c_term, keep, sums, got, yt, high, low, y_own,
    )
    return f_pot.reshape(n), g_pot.reshape(yd), grad_xt.T, grad_y


def solution(mesh):
    in_specs = (
        P(("groups", "row", "col"), None),
        P(("groups", "col", "row"), None),
        P(("groups", "row", "col")),
        P(("groups", "col", "row")),
    )
    out_specs = (
        P(("groups", "row", "col")),
        P(("groups", "col", "row")),
        P(("groups", "row", "col"), None),
        P(("groups", "col", "row"), None),
    )
    return jax.shard_map(
        on_device, mesh=mesh, in_specs=in_specs, out_specs=out_specs, check_vma=False
    )
```

```python
import functools
import math

import jax
import jax.numpy as jnp
from jax import lax
from jax.experimental import pallas as pl
from jax.experimental.pallas import tpu as pltpu
from jax.sharding import PartitionSpec as P

ITERS = 2
EPSILON = 0.02
LOG2E = math.log2(math.e)
TILE = 256
STEP = 32
EXT = 32
PAD = 16
LANES = 128
F32 = jnp.float32
BF16 = jnp.bfloat16


def kappa_of(width):
    return 2.0 / (width * EPSILON)


def pieces(value):
    high = value.astype(BF16).astype(F32)
    rest = value - high
    mid = rest.astype(BF16).astype(F32)
    return high, mid, rest - mid


def select(index, values):
    out = jnp.zeros(index.shape, F32)
    for k, value in values.items():
        out = jnp.where(index == k, value, out)
    return out


def extras_y(index, c_term, mass):
    high, mid, low = pieces(c_term)
    return select(index, {0: high, 1: mid, 2: low, 3: 1.0, 4: 1.0, 5: 1.0, 6: mass})


def extras_x(index, b_term):
    high, mid, low = pieces(b_term)
    return select(index, {0: 1.0, 1: 1.0, 2: 1.0, 3: high, 4: mid, 5: low})


def rows_index(columns):
    return lax.broadcasted_iota(jnp.int32, (EXT, columns), 0)


def to_column(row):
    size = row.shape[1]
    eye = lax.broadcasted_iota(jnp.int32, (size, size), 0) == lax.broadcasted_iota(jnp.int32, (size, size), 1)
    return jnp.sum(jnp.where(eye, row, 0.0), axis=1, keepdims=True)


def to_row(column):
    size = column.shape[0]
    eye = lax.broadcasted_iota(jnp.int32, (size, size), 0) == lax.broadcasted_iota(jnp.int32, (size, size), 1)
    return jnp.sum(jnp.where(eye, column, 0.0), axis=0, keepdims=True)


def for_tiles(total, body):
    count = total // TILE
    if count <= 4:
        for t in range(count):
            body(pl.ds(t * TILE, TILE))
    else:

        @pl.loop(0, count)
        def _(t):
            body(pl.ds(pl.multiple_of(t * TILE, TILE), TILE))


def max_down(z_ref, rows):
    peak = z_ref[0:STEP, :]
    for r in range(STEP, rows, STEP):
        peak = jnp.maximum(peak, z_ref[r : r + STEP, :])
    return jnp.max(peak, axis=0, keepdims=True)


def exp_sum_down(z_ref, rows, scale, shift):
    total = jnp.zeros((STEP, TILE), F32)
    for r in range(0, rows, STEP):
        total = total + jnp.exp2((z_ref[r : r + STEP, :] - shift) * scale)
    return jnp.sum(total, axis=0, keepdims=True)


def to_lanes(row):
    return jnp.concatenate([row[:, k : k + LANES] for k in range(0, row.shape[1], LANES)], axis=0)


def from_lanes(block):
    return jnp.concatenate([block[k : k + 1] for k in range(block.shape[0])], axis=1)


def sums_rows(ny):
    return -(-2 * ny // LANES // 16) * 16


def sums_out(sums):
    high = sums.astype(BF16).astype(F32)
    spare = sums_rows(sums.size) - 2 * sums.shape[0]
    return jnp.concatenate([high, sums - high] + [jnp.zeros((spare, LANES), F32)] * (spare > 0), axis=0)


def sums_in(ext, count):
    return ext[:count] + ext[count : 2 * count]


def pack(block):
    rows, width = block.shape
    base = rows * width // LANES
    spare = LANES - width
    side = [block[base:, k : k + spare] for k in range(0, width, spare)]
    return jnp.concatenate([block[:base], jnp.concatenate(side, axis=0)], axis=1)


def unpack(block, rows, width):
    base = block.shape[0]
    rest = rows - base
    side = [block[k : k + rest, width:] for k in range(0, base, rest)]
    return jnp.concatenate([block[:, :width], jnp.concatenate(side, axis=1)], axis=0)


def prep_kernel(
    log_ny, xt_hbm, y_hbm, mx_hbm, my_hbm, ya_ref, xa_ref, mx_ref, y_ref, my_ref, mx_in, sems
):
    width, n = xt_hbm.shape
    pairs = ((y_hbm, y_ref), (my_hbm, my_ref), (xt_hbm, xa_ref.at[:width, :]), (mx_hbm, mx_in))
    moves = [pltpu.make_async_copy(a, b, sems.at[k]) for k, (a, b) in enumerate(pairs)]
    for move in moves:
        move.start()
    xa_ref[width:, :] = extras_x(rows_index(n), jnp.zeros((1, n), F32)).astype(BF16)
    moves[0].wait()
    moves[1].wait()
    y = y_ref[...]
    yf = y.astype(F32)
    norm = jnp.sum(yf * yf, axis=1, keepdims=True)
    mass = to_column(my_ref[...].astype(F32))
    c_term = (mass - log_ny) / kappa_of(width) - 0.5 * norm
    ext = extras_y(lax.broadcasted_iota(jnp.int32, (y.shape[0], EXT), 1), c_term, mass).astype(BF16)
    for k in range(ya_ref.shape[0]):
        ya_ref[k, :, :width] = y
        ya_ref[k, :, width:] = ext
    moves[2].wait()
    moves[3].wait()
    mx_ref[...] = from_lanes(mx_in[...].astype(F32))


def half_kernel(xa_ref, mine_ref, peak_ref, total_ref, z_ref):
    rows, yd, depth = mine_ref.shape
    half = rows * yd
    scale = kappa_of(depth - EXT) * LOG2E
    y_rows = mine_ref[...].reshape(half, depth)

    def row_tile(t):
        z_ref[...] = jnp.dot(y_rows, xa_ref[:, t], preferred_element_type=F32)
        peak = max_down(z_ref, half)
        peak_ref[:, t] = peak
        total_ref[:, t] = exp_sum_down(z_ref, half, scale, peak)

    for_tiles(xa_ref.shape[1], row_tile)


def first_kernel(
    log_nx, xa0_ref, mx_ref, mine_ref, other_ref, peak_ref, total_ref,
    ya_ref, b_ref, l_ref, m_ref, rows_ref, xa_ref, z_ref, zc_ref, b2_ref,
):
    rows, yd, depth = mine_ref.shape
    n = mx_ref.shape[1]
    width = depth - EXT
    half = rows * yd
    ny = 2 * half
    col = lax.axis_index("col")
    scale = kappa_of(width) * LOG2E
    other = other_ref[...].reshape(half, depth)
    ya_ref[pl.ds(pl.multiple_of(col * half, half), half), :] = mine_ref[...].reshape(half, depth)
    ya_ref[pl.ds(pl.multiple_of((1 - col) * half, half), half), :] = other

    def row_tile(t):
        z_ref[...] = jnp.dot(other, xa0_ref[:, t], preferred_element_type=F32)
        old = peak_ref[:, t]
        peak = jnp.maximum(max_down(z_ref, half), old)
        total = exp_sum_down(z_ref, half, scale, peak) + total_ref[:, t] * jnp.exp2((old - peak) * scale)
        b_ref[:, t] = -peak - jnp.log(total) * (LOG2E / scale)

    for_tiles(n, row_tile)
    b_term = b_ref[...] + (mx_ref[...] - log_nx) * (LOG2E / scale)
    b_ref[...] = b_term
    xa_ref[:width, :] = xa0_ref[:width, :]
    xa_ref[width:, :] = extras_x(rows_index(n), b_term).astype(BF16)
    rows_ref[...] = xa_ref[...].T

    def col_tile(t):
        zc_ref[...] = lax.dot_general(
            rows_ref[...], ya_ref[t, :], (((1,), (1,)), ((), ())), preferred_element_type=F32
        )
        peak = max_down(zc_ref, n)
        m_ref[:, t] = peak
        b2_ref[:, t] = scale * peak + jnp.log(exp_sum_down(zc_ref, n, scale, peak)) * LOG2E

    for_tiles(ny, col_tile)
    lse = to_lanes(b2_ref[...])
    for k in range(rows):
        l_ref[k] = lse


def plan_kernel(xa_ref, rows_ref, ya_ref, m_ref, t_ref, yt_ref, norm_ref, zc_ref):
    ny, depth = ya_ref.shape
    n = rows_ref.shape[0]
    scale = kappa_of(depth - EXT) * LOG2E

    def col_tile(t):
        y_part = ya_ref[t, :]
        yt_ref[:, t] = y_part.T
        zc_ref[...] = lax.dot_general(
            rows_ref[...], y_part, (((1,), (1,)), ((), ())), preferred_element_type=F32
        )
        peak = m_ref[:, t]
        for r in range(0, n, STEP):
            t_ref[r : r + STEP, t] = jnp.exp2((zc_ref[r : r + STEP, :] - peak) * scale).astype(BF16)

    for_tiles(ny, col_tile)
    xf = xa_ref[: depth - EXT, :].astype(F32)
    norm_ref[...] = jnp.sum(xf * xf, axis=0, keepdims=True)


def stack(out_ref, width, points, factor):
    moved = points.astype(F32) * factor
    high = moved.astype(BF16)
    out_ref[:width, :] = high
    out_ref[width : 2 * width, :] = (moved - high.astype(F32)).astype(BF16)
    one, two, three = pieces(factor)
    index = lax.broadcasted_iota(jnp.int32, (PAD, factor.shape[1]), 0)
    out_ref[2 * width :, :] = select(index, {0: one, 1: two, 2: three}).astype(BF16)


def unstack(product, width):
    ext = product[2 * width :]
    return product[:width] + product[width : 2 * width], (ext[0:1] + ext[1:2]) + ext[2:3]


def second_kernel(
    log_nx, log_ny, xa_ref, mx_ref, norm_ref, b_ref, l_ref, other_ref, m_ref, yt_ref, t_ref,
    f_ref, r_ref, v_ref, c_ref, keep_ref, sum_ref, send_ref, xs_ref, gt_ref, part_ref,
):
    width = xa_ref.shape[0] - EXT
    ny = m_ref.shape[1]
    kappa = kappa_of(width)
    scale = kappa * LOG2E
    l_mine, l_other = l_ref[...], other_ref[...]
    peak = jnp.maximum(jnp.max(l_mine, axis=0), jnp.max(l_other, axis=0))
    total = jnp.sum(jnp.exp2(l_mine - peak[None]), axis=0) + jnp.sum(jnp.exp2(l_other - peak[None]), axis=0)
    lse2 = from_lanes(peak + jnp.log(total) * LOG2E)
    old = yt_ref[width:, :].astype(F32)
    c_old = (old[0:1] + old[1:2]) + old[2:3]
    lb2 = (old[6:7] - log_ny) * LOG2E
    c_ref[...] = to_lanes(c_old + (lb2 - lse2) / scale)
    v = jnp.exp2(scale * m_ref[...] + (lb2 - lse2))
    v_ref[...] = v
    one, two, three = pieces(v)
    index = lax.broadcasted_iota(jnp.int32, (PAD, ny), 0)
    v_rows = select(index, {0: one, 1: two, 2: three}).astype(BF16)
    across = (((1,), (1,)), ((), ()))
    sums = lax.dot_general(v_rows, t_ref[...], across, preferred_element_type=F32)
    rowsum = (sums[0:1] + sums[1:2]) + sums[2:3]
    log_row = jnp.log(rowsum)
    f_ref[...] = norm_ref[...] / width + EPSILON * (kappa * b_ref[...] - log_row)
    r = jnp.exp(mx_ref[...] - log_nx - log_row)
    r_ref[...] = r
    stack(xs_ref, width, xa_ref[:width, :], r)
    totals = []
    for k in range(ny // TILE):
        t = slice(k * TILE, (k + 1) * TILE)
        product = jnp.dot(xs_ref[...], t_ref[:, t], preferred_element_type=F32)
        moment, total = unstack(product, width)
        total = total * v[:, t]
        totals.append(total)
        gt_ref[:width, t] = yt_ref[:width, t].astype(F32) * total - moment * v[:, t]
    gt_ref[width:, :] = jnp.zeros((EXT, ny), F32)
    part_ref[...] = gt_ref[...].T
    sums = to_lanes(jnp.concatenate(totals, axis=1))
    sum_ref[...] = sums
    col = lax.axis_index("col")
    half = keep_ref.shape[0]
    keep_ref[...] = part_ref[pl.ds(pl.multiple_of(col * half, half), half), :]
    send_ref[:half, :] = part_ref[pl.ds(pl.multiple_of((1 - col) * half, half), half), :].astype(BF16)
    send_ref[half:, :] = sums_out(sums).astype(BF16)


def add_kernel(width, keep_ref, sum_ref, got_ref, out_ref):
    half = keep_ref.shape[0]
    rows = out_ref.shape[0]
    yd = half // rows
    base = yd * width // LANES
    count = sum_ref.shape[0]
    sums = sums_out(sum_ref[...] + sums_in(got_ref[half:, :].astype(F32), count)).astype(BF16)
    for r in range(rows):
        part = slice(r * yd, (r + 1) * yd)
        total = keep_ref[part, :] + got_ref[part, :].astype(F32)
        out_ref[r, :base, :] = pack(total[:, :width]).astype(BF16)
        out_ref[r, base:, :] = sums


def own_part(ref, yd):
    block = lax.axis_index("col") * lax.axis_size("row") + lax.axis_index("row")
    fit = LANES // yd
    row = ref[pl.ds(block // fit, 1), :]
    out = row[:, :yd]
    for k in range(1, fit):
        out = jnp.where(block % fit == k, row[:, k * yd : (k + 1) * yd], out)
    return out


def last_kernel(
    log_nx, log_ny, xa_ref, r_ref, v_ref, c_ref, got_ref, yt_ref, t_ref, y_ref,
    gx_ref, gy_ref, pot_ref, ys_ref, sum_ref,
):
    width, n = gx_ref.shape
    ny = v_ref.shape[1]
    yd = y_ref.shape[1]
    base = yd * width // LANES
    total = got_ref[0].astype(F32)
    for k in range(1, got_ref.shape[0]):
        total = total + got_ref[k].astype(F32)
    sums = sums_in(total[base:], ny // LANES)
    sum_ref[...] = sums
    mass = yt_ref[width:, :].astype(F32)[6:7]
    q = v_ref[...] * jnp.exp(mass + log_nx - jnp.log(from_lanes(sums)))
    stack(ys_ref, width, yt_ref[:width, :], q)
    across = (((1,), (1,)), ((), ()))
    for k in range(n // TILE):
        t = slice(k * TILE, (k + 1) * TILE)
        product = lax.dot_general(ys_ref[...], t_ref[t, :], across, preferred_element_type=F32)
        moved, weight = unstack(product, width)
        gx_ref[:, t] = (xa_ref[:width, t].astype(F32) * weight - moved) * (r_ref[:, t] * (1.0 / ny))
    colsum = own_part(sum_ref, yd)
    c_term = own_part(c_ref, yd)
    own = y_ref[0].astype(F32)
    gy_ref[...] = unpack(total[:base], yd, width) * (jnp.exp(own[:, width + 6 : width + 7]) * to_column(1.0 / colsum))
    norm = to_row(jnp.sum(own[:, :width] * own[:, :width], axis=1, keepdims=True))
    pot_ref[...] = norm / width - EPSILON * (jnp.log(colsum) - kappa_of(width) * c_term)


def call(kernel, outs, scratch, limit, *args, space=pltpu.VMEM):
    return pl.pallas_call(
        kernel,
        out_shape=outs,
        in_specs=[pl.BlockSpec(memory_space=space)] * len(args),
        out_specs=jax.tree.map(lambda _: pl.BlockSpec(memory_space=pltpu.VMEM), outs),
        scratch_shapes=scratch,
        compiler_params=pltpu.CompilerParams(vmem_limit_bytes=limit),
    )(*args)


def shape(dims, dtype=F32):
    return jax.ShapeDtypeStruct(dims, dtype)


def swap(value):
    return lax.ppermute(value, "col", [(0, 1), (1, 0)])


def on_device(points_x, points_y, mass_x, mass_y):
    n, width = points_x.shape
    yd = points_y.shape[0]
    rows = lax.axis_size("row")
    ny = 2 * rows * yd
    half = ny // 2
    count = ny // LANES
    log_nx, log_ny = math.log(n * 2 * rows), math.log(ny)
    depth = width + EXT
    limit = (12 if ny <= 1024 else 56) * 1024 * 1024
    extra = sums_rows(ny)
    run = functools.partial
    vmem = pltpu.VMEM
    y_own, xa, mx = call(
        run(prep_kernel, log_ny),
        (shape((rows, yd, depth), BF16), shape((depth, n), BF16), shape((1, n))),
        [
            vmem((yd, width), BF16), vmem((1, yd), BF16), vmem((n // LANES, LANES), BF16),
            pltpu.SemaphoreType.DMA((4,)),
        ],
        58 * 1024 * 1024,
        points_x.T, points_y, mass_x.reshape(n // LANES, LANES), mass_y.reshape(1, yd), space=pl.ANY,
    )
    y_mine = lax.all_to_all(y_own, "row", 0, 0, tiled=True)
    y_other = swap(y_mine)
    peak, total = call(
        half_kernel, (shape((1, n)), shape((1, n))), [vmem((half, TILE), F32)], limit, xa, y_mine
    )
    ya, b_term, lse, peak, x_rows = call(
        run(first_kernel, log_nx),
        (
            shape((ny, depth), BF16), shape((1, n)), shape((rows, count, LANES)), shape((1, ny)),
            shape((n, depth), BF16),
        ),
        [vmem((depth, n), BF16), vmem((half, TILE), F32), vmem((n, TILE), F32), vmem((1, ny), F32)],
        limit, xa, mx, y_mine, y_other, peak, total,
    )
    lse = lax.all_to_all(lse, "row", 0, 0, tiled=True)
    lse_other = swap(lse)
    plan, yt, norm = call(
        plan_kernel,
        (shape((n, ny), BF16), shape((depth, ny), BF16), shape((1, n))),
        [vmem((n, TILE), F32)],
        limit, xa, x_rows, ya, peak,
    )
    f_pot, r, v, c_term, keep, sums, send = call(
        run(second_kernel, log_nx, log_ny),
        (
            shape((1, n)), shape((1, n)), shape((1, ny)), shape((count, LANES)),
            shape((half, depth)), shape((count, LANES)), shape((half + extra, depth), BF16),
        ),
        [vmem((2 * width + PAD, n), BF16), vmem((depth, ny), F32), vmem((ny, depth), F32)],
        limit, xa, mx, norm, b_term, lse, lse_other, peak, yt, plan,
    )
    part = call(
        run(add_kernel, width), shape((rows, yd * width // LANES + extra, LANES), BF16), [],
        limit, keep, sums, swap(send),
    )
    part = lax.all_to_all(part, "row", 0, 0, tiled=True)
    grad_xt, grad_y, g_pot = call(
        run(last_kernel, log_nx, log_ny),
        (shape((width, n)), shape((yd, width)), shape((1, yd))),
        [vmem((2 * width + PAD, ny), BF16), vmem((count, LANES), F32)],
        limit, xa, r, v, c_term, part, yt, plan, y_own,
    )
    return f_pot.reshape(n), g_pot.reshape(yd), grad_xt.T, grad_y


def solution(mesh):
    in_specs = (
        P(("groups", "row", "col"), None),
        P(("groups", "col", "row"), None),
        P(("groups", "row", "col")),
        P(("groups", "col", "row")),
    )
    out_specs = (
        P(("groups", "row", "col")),
        P(("groups", "col", "row")),
        P(("groups", "row", "col"), None),
        P(("groups", "col", "row"), None),
    )
    return jax.shard_map(
        on_device, mesh=mesh, in_specs=in_specs, out_specs=out_specs, check_vma=False
    )
```

```python
import functools
import math

import jax
import jax.numpy as jnp
from jax import lax
from jax.experimental import pallas as pl
from jax.experimental.pallas import tpu as pltpu
from jax.sharding import PartitionSpec as P

ITERS = 2
EPSILON = 0.02
LOG2E = math.log2(math.e)
TILE = 256
STEP = 32
EXT = 32
PAD = 16
LANES = 128
F32 = jnp.float32
BF16 = jnp.bfloat16


def kappa_of(width):
    return 2.0 / (width * EPSILON)


def pieces(value):
    high = value.astype(BF16).astype(F32)
    rest = value - high
    mid = rest.astype(BF16).astype(F32)
    return high, mid, rest - mid


def select(index, values):
    out = jnp.zeros(index.shape, F32)
    for k, value in values.items():
        out = jnp.where(index == k, value, out)
    return out


def extras_y(index, c_term, mass):
    high, mid, low = pieces(c_term)
    return select(index, {0: high, 1: mid, 2: low, 3: 1.0, 4: 1.0, 5: 1.0, 6: mass})


def extras_x(index, b_term, mass):
    high, mid, low = pieces(b_term)
    return select(index, {0: 1.0, 1: 1.0, 2: 1.0, 3: high, 4: mid, 5: low, 7: mass})


def rows_index(columns):
    return lax.broadcasted_iota(jnp.int32, (EXT, columns), 0)


def to_column(row):
    size = row.shape[1]
    eye = lax.broadcasted_iota(jnp.int32, (size, size), 0) == lax.broadcasted_iota(jnp.int32, (size, size), 1)
    return jnp.sum(jnp.where(eye, row, 0.0), axis=1, keepdims=True)


def to_row(column):
    size = column.shape[0]
    eye = lax.broadcasted_iota(jnp.int32, (size, size), 0) == lax.broadcasted_iota(jnp.int32, (size, size), 1)
    return jnp.sum(jnp.where(eye, column, 0.0), axis=0, keepdims=True)


def for_tiles(total, body):
    count = total // TILE
    if count <= 4:
        for t in range(count):
            body(pl.ds(t * TILE, TILE))
    else:

        @pl.loop(0, count)
        def _(t):
            body(pl.ds(pl.multiple_of(t * TILE, TILE), TILE))


def max_down(z_ref, rows):
    peak = z_ref[0:STEP, :]
    for r in range(STEP, rows, STEP):
        peak = jnp.maximum(peak, z_ref[r : r + STEP, :])
    return jnp.max(peak, axis=0, keepdims=True)


def exp_sum_down(z_ref, rows, scale, shift):
    total = jnp.zeros((STEP, TILE), F32)
    for r in range(0, rows, STEP):
        total = total + jnp.exp2((z_ref[r : r + STEP, :] - shift) * scale)
    return jnp.sum(total, axis=0, keepdims=True)


def to_lanes(row):
    return jnp.concatenate([row[:, k : k + LANES] for k in range(0, row.shape[1], LANES)], axis=0)


def from_lanes(block):
    return jnp.concatenate([block[k : k + 1] for k in range(block.shape[0])], axis=1)


def sums_rows(ny):
    return -(-2 * ny // LANES // 16) * 16


def sums_out(sums):
    high = sums.astype(BF16).astype(F32)
    spare = sums_rows(sums.size) - 2 * sums.shape[0]
    return jnp.concatenate([high, sums - high] + [jnp.zeros((spare, LANES), F32)] * (spare > 0), axis=0)


def sums_in(ext, count):
    return ext[:count] + ext[count : 2 * count]


def pack(block):
    rows, width = block.shape
    base = rows * width // LANES
    spare = LANES - width
    side = [block[base:, k : k + spare] for k in range(0, width, spare)]
    return jnp.concatenate([block[:base], jnp.concatenate(side, axis=0)], axis=1)


def unpack(block, rows, width):
    base = block.shape[0]
    rest = rows - base
    side = [block[k : k + rest, width:] for k in range(0, base, rest)]
    return jnp.concatenate([block[:, :width], jnp.concatenate(side, axis=1)], axis=0)


def prep_kernel(
    log_ny, xt_hbm, y_hbm, mx_hbm, my_hbm, ya_hbm, xa_hbm, y_ref, my_ref, mx_ref, ya_ref, ext_ref, sems
):
    width, n = xt_hbm.shape
    rows = ya_hbm.shape[0]
    move_y = pltpu.make_async_copy(y_hbm, y_ref, sems.at[0])
    move_my = pltpu.make_async_copy(my_hbm, my_ref, sems.at[1])
    move_mx = pltpu.make_async_copy(mx_hbm, mx_ref, sems.at[2])
    move_x = pltpu.make_async_copy(xt_hbm, xa_hbm.at[:width, :], sems.at[3])
    for move in (move_y, move_my, move_mx, move_x):
        move.start()
    move_y.wait()
    y = y_ref[...]
    yf = y.astype(F32)
    norm = jnp.sum(yf * yf, axis=1, keepdims=True)
    move_my.wait()
    mass = to_column(my_ref[...].astype(F32))
    c_term = (mass - log_ny) / kappa_of(width) - 0.5 * norm
    index = lax.broadcasted_iota(jnp.int32, (y.shape[0], EXT), 1)
    ya_ref[:, :width] = y
    ya_ref[:, width:] = extras_y(index, c_term, mass).astype(BF16)
    moves = [pltpu.make_async_copy(ya_ref, ya_hbm.at[k], sems.at[5 + k]) for k in range(rows)]
    for move in moves:
        move.start()
    move_mx.wait()
    mass = from_lanes(mx_ref[...].astype(F32))
    ext_ref[...] = extras_x(rows_index(n), jnp.zeros((1, n), F32), mass).astype(BF16)
    move_ext = pltpu.make_async_copy(ext_ref, xa_hbm.at[width:, :], sems.at[4])
    move_ext.start()
    for move in moves:
        move.wait()
    move_x.wait()
    move_ext.wait()


def half_kernel(xa_ref, mine_ref, peak_ref, total_ref, z_ref):
    rows, yd, depth = mine_ref.shape
    half = rows * yd
    scale = kappa_of(depth - EXT) * LOG2E
    y_rows = mine_ref[...].reshape(half, depth)

    def row_tile(t):
        z_ref[...] = jnp.dot(y_rows, xa_ref[:, t], preferred_element_type=F32)
        peak = max_down(z_ref, half)
        peak_ref[:, t] = peak
        total_ref[:, t] = exp_sum_down(z_ref, half, scale, peak)

    for_tiles(xa_ref.shape[1], row_tile)


def first_kernel(
    log_nx, xa0_ref, mine_ref, other_ref, peak_ref, total_ref,
    ya_ref, b_ref, l_ref, m_ref, rows_ref, xa_ref, z_ref, zc_ref, b2_ref,
):
    rows, yd, depth = mine_ref.shape
    n = xa0_ref.shape[1]
    width = depth - EXT
    half = rows * yd
    ny = 2 * half
    col = lax.axis_index("col")
    scale = kappa_of(width) * LOG2E
    other = other_ref[...].reshape(half, depth)
    ya_ref[pl.ds(pl.multiple_of(col * half, half), half), :] = mine_ref[...].reshape(half, depth)
    ya_ref[pl.ds(pl.multiple_of((1 - col) * half, half), half), :] = other

    def row_tile(t):
        z_ref[...] = jnp.dot(other, xa0_ref[:, t], preferred_element_type=F32)
        old = peak_ref[:, t]
        peak = jnp.maximum(max_down(z_ref, half), old)
        total = exp_sum_down(z_ref, half, scale, peak) + total_ref[:, t] * jnp.exp2((old - peak) * scale)
        b_ref[:, t] = -peak - jnp.log(total) * (LOG2E / scale)

    for_tiles(n, row_tile)
    mass = xa0_ref[width:, :].astype(F32)[7:8]
    b_term = b_ref[...] + (mass - log_nx) * (LOG2E / scale)
    b_ref[...] = b_term
    xa_ref[:width, :] = xa0_ref[:width, :]
    xa_ref[width:, :] = extras_x(rows_index(n), b_term, mass).astype(BF16)
    rows_ref[...] = xa_ref[...].T

    def col_tile(t):
        zc_ref[...] = lax.dot_general(
            rows_ref[...], ya_ref[t, :], (((1,), (1,)), ((), ())), preferred_element_type=F32
        )
        peak = max_down(zc_ref, n)
        m_ref[:, t] = peak
        b2_ref[:, t] = scale * peak + jnp.log(exp_sum_down(zc_ref, n, scale, peak)) * LOG2E

    for_tiles(ny, col_tile)
    lse = to_lanes(b2_ref[...])
    for k in range(rows):
        l_ref[k] = lse


def plan_kernel(xa_ref, rows_ref, ya_ref, m_ref, t_ref, yt_ref, norm_ref, zc_ref):
    ny, depth = ya_ref.shape
    n = rows_ref.shape[0]
    scale = kappa_of(depth - EXT) * LOG2E

    def col_tile(t):
        y_part = ya_ref[t, :]
        yt_ref[:, t] = y_part.T
        zc_ref[...] = lax.dot_general(
            rows_ref[...], y_part, (((1,), (1,)), ((), ())), preferred_element_type=F32
        )
        peak = m_ref[:, t]
        for r in range(0, n, STEP):
            t_ref[r : r + STEP, t] = jnp.exp2((zc_ref[r : r + STEP, :] - peak) * scale).astype(BF16)

    for_tiles(ny, col_tile)
    xf = xa_ref[: depth - EXT, :].astype(F32)
    norm_ref[...] = jnp.sum(xf * xf, axis=0, keepdims=True)


def stack(out_ref, width, points, factor):
    moved = points.astype(F32) * factor
    high = moved.astype(BF16)
    out_ref[:width, :] = high
    out_ref[width : 2 * width, :] = (moved - high.astype(F32)).astype(BF16)
    one, two, three = pieces(factor)
    index = lax.broadcasted_iota(jnp.int32, (PAD, factor.shape[1]), 0)
    out_ref[2 * width :, :] = select(index, {0: one, 1: two, 2: three}).astype(BF16)


def unstack(product, width):
    ext = product[2 * width :]
    return product[:width] + product[width : 2 * width], (ext[0:1] + ext[1:2]) + ext[2:3]


def second_kernel(
    log_nx, log_ny, xa_ref, norm_ref, b_ref, l_ref, other_ref, m_ref, yt_ref, t_ref,
    f_ref, r_ref, v_ref, c_ref, keep_ref, sum_ref, send_ref, xs_ref, gt_ref, part_ref,
):
    width = xa_ref.shape[0] - EXT
    ny = m_ref.shape[1]
    kappa = kappa_of(width)
    scale = kappa * LOG2E
    l_mine, l_other = l_ref[...], other_ref[...]
    peak = jnp.maximum(jnp.max(l_mine, axis=0), jnp.max(l_other, axis=0))
    total = jnp.sum(jnp.exp2(l_mine - peak[None]), axis=0) + jnp.sum(jnp.exp2(l_other - peak[None]), axis=0)
    lse2 = from_lanes(peak + jnp.log(total) * LOG2E)
    old = yt_ref[width:, :].astype(F32)
    c_old = (old[0:1] + old[1:2]) + old[2:3]
    lb2 = (old[6:7] - log_ny) * LOG2E
    c_ref[...] = to_lanes(c_old + (lb2 - lse2) / scale)
    v = jnp.exp2(scale * m_ref[...] + (lb2 - lse2))
    v_ref[...] = v
    one, two, three = pieces(v)
    index = lax.broadcasted_iota(jnp.int32, (PAD, ny), 0)
    v_rows = select(index, {0: one, 1: two, 2: three}).astype(BF16)
    across = (((1,), (1,)), ((), ()))
    sums = lax.dot_general(v_rows, t_ref[...], across, preferred_element_type=F32)
    rowsum = (sums[0:1] + sums[1:2]) + sums[2:3]
    log_row = jnp.log(rowsum)
    f_ref[...] = norm_ref[...] / width + EPSILON * (kappa * b_ref[...] - log_row)
    mass = xa_ref[width:, :].astype(F32)[7:8]
    r = jnp.exp(mass - log_nx - log_row)
    r_ref[...] = r
    stack(xs_ref, width, xa_ref[:width, :], r)
    totals = []
    for k in range(ny // TILE):
        t = slice(k * TILE, (k + 1) * TILE)
        product = jnp.dot(xs_ref[...], t_ref[:, t], preferred_element_type=F32)
        moment, total = unstack(product, width)
        total = total * v[:, t]
        totals.append(total)
        gt_ref[:width, t] = yt_ref[:width, t].astype(F32) * total - moment * v[:, t]
    gt_ref[width:, :] = jnp.zeros((EXT, ny), F32)
    part_ref[...] = gt_ref[...].T
    sums = to_lanes(jnp.concatenate(totals, axis=1))
    sum_ref[...] = sums
    col = lax.axis_index("col")
    half = keep_ref.shape[0]
    keep_ref[...] = part_ref[pl.ds(pl.multiple_of(col * half, half), half), :]
    send_ref[:half, :] = part_ref[pl.ds(pl.multiple_of((1 - col) * half, half), half), :].astype(BF16)
    send_ref[half:, :] = sums_out(sums).astype(BF16)


def add_kernel(width, keep_ref, sum_ref, got_ref, out_ref):
    half = keep_ref.shape[0]
    rows = out_ref.shape[0]
    yd = half // rows
    base = yd * width // LANES
    count = sum_ref.shape[0]
    sums = sums_out(sum_ref[...] + sums_in(got_ref[half:, :].astype(F32), count)).astype(BF16)
    for r in range(rows):
        part = slice(r * yd, (r + 1) * yd)
        total = keep_ref[part, :] + got_ref[part, :].astype(F32)
        out_ref[r, :base, :] = pack(total[:, :width]).astype(BF16)
        out_ref[r, base:, :] = sums


def own_part(ref, yd):
    block = lax.axis_index("col") * lax.axis_size("row") + lax.axis_index("row")
    fit = LANES // yd
    row = ref[pl.ds(block // fit, 1), :]
    out = row[:, :yd]
    for k in range(1, fit):
        out = jnp.where(block % fit == k, row[:, k * yd : (k + 1) * yd], out)
    return out


def last_kernel(
    log_nx, log_ny, xa_ref, r_ref, v_ref, c_ref, got_ref, yt_ref, t_ref, y_ref,
    gx_ref, gy_ref, pot_ref, ys_ref, sum_ref,
):
    width, n = gx_ref.shape
    ny = v_ref.shape[1]
    yd = y_ref.shape[1]
    base = yd * width // LANES
    total = got_ref[0].astype(F32)
    for k in range(1, got_ref.shape[0]):
        total = total + got_ref[k].astype(F32)
    sums = sums_in(total[base:], ny // LANES)
    sum_ref[...] = sums
    mass = yt_ref[width:, :].astype(F32)[6:7]
    q = v_ref[...] * jnp.exp(mass + log_nx - jnp.log(from_lanes(sums)))
    moved = yt_ref[:width, :].astype(F32) * q
    high = moved.astype(BF16)
    ys_ref[:width, :] = high
    ys_ref[LANES : LANES + width, :] = (moved - high.astype(F32)).astype(BF16)
    one, two, three = pieces(q)
    ys_ref[width:LANES, :] = select(rows_index(ny), {0: one, 1: two, 2: three}).astype(BF16)
    ys_ref[LANES + width :, :] = jnp.zeros((EXT, ny), BF16)
    right = ys_ref[...].T
    for k in range(n // TILE):
        t = slice(k * TILE, (k + 1) * TILE)
        product = jnp.dot(t_ref[t, :], right, preferred_element_type=F32)
        product = (product[:, :LANES] + product[:, LANES:]).T
        ext = product[width:]
        weight = (ext[0:1] + ext[1:2]) + ext[2:3]
        gx_ref[:, t] = (xa_ref[:width, t].astype(F32) * weight - product[:width]) * (r_ref[:, t] * (1.0 / ny))
    colsum = own_part(sum_ref, yd)
    c_term = own_part(c_ref, yd)
    own = y_ref[0].astype(F32)
    gy_ref[...] = unpack(total[:base], yd, width) * (jnp.exp(own[:, width + 6 : width + 7]) * to_column(1.0 / colsum))
    norm = to_row(jnp.sum(own[:, :width] * own[:, :width], axis=1, keepdims=True))
    pot_ref[...] = norm / width - EPSILON * (jnp.log(colsum) - kappa_of(width) * c_term)


def call(kernel, outs, scratch, limit, *args, space=pltpu.VMEM):
    return pl.pallas_call(
        kernel,
        out_shape=outs,
        in_specs=[pl.BlockSpec(memory_space=space)] * len(args),
        out_specs=jax.tree.map(lambda _: pl.BlockSpec(memory_space=space), outs),
        scratch_shapes=scratch,
        compiler_params=pltpu.CompilerParams(vmem_limit_bytes=limit),
    )(*args)


def shape(dims, dtype=F32):
    return jax.ShapeDtypeStruct(dims, dtype)


def swap(value):
    return lax.ppermute(value, "col", [(0, 1), (1, 0)])


def on_device(points_x, points_y, mass_x, mass_y):
    n, width = points_x.shape
    yd = points_y.shape[0]
    rows = lax.axis_size("row")
    ny = 2 * rows * yd
    half = ny // 2
    count = ny // LANES
    log_nx, log_ny = math.log(n * 2 * rows), math.log(ny)
    depth = width + EXT
    limit = (12 if ny <= 1024 else 56) * 1024 * 1024
    extra = sums_rows(ny)
    run = functools.partial
    vmem = pltpu.VMEM
    y_own, xa = call(
        run(prep_kernel, log_ny),
        (shape((rows, yd, depth), BF16), shape((depth, n), BF16)),
        [
            vmem((yd, width), BF16), vmem((1, yd), BF16), vmem((n // LANES, LANES), BF16),
            vmem((yd, depth), BF16), vmem((EXT, n), BF16), pltpu.SemaphoreType.DMA((5 + rows,)),
        ],
        58 * 1024 * 1024,
        points_x.T, points_y, mass_x.reshape(n // LANES, LANES), mass_y.reshape(1, yd), space=pl.ANY,
    )
    y_mine = lax.all_to_all(y_own, "row", 0, 0, tiled=True)
    y_other = swap(y_mine)
    peak, total = call(
        half_kernel, (shape((1, n)), shape((1, n))), [vmem((half, TILE), F32)], limit, xa, y_mine
    )
    ya, b_term, lse, peak, x_rows = call(
        run(first_kernel, log_nx),
        (
            shape((ny, depth), BF16), shape((1, n)), shape((rows, count, LANES)), shape((1, ny)),
            shape((n, depth), BF16),
        ),
        [vmem((depth, n), BF16), vmem((half, TILE), F32), vmem((n, TILE), F32), vmem((1, ny), F32)],
        limit, xa, y_mine, y_other, peak, total,
    )
    lse = lax.all_to_all(lse, "row", 0, 0, tiled=True)
    lse_other = swap(lse)
    plan, yt, norm = call(
        plan_kernel,
        (shape((n, ny), BF16), shape((depth, ny), BF16), shape((1, n))),
        [vmem((n, TILE), F32)],
        limit, xa, x_rows, ya, peak,
    )
    f_pot, r, v, c_term, keep, sums, send = call(
        run(second_kernel, log_nx, log_ny),
        (
            shape((1, n)), shape((1, n)), shape((1, ny)), shape((count, LANES)),
            shape((half, depth)), shape((count, LANES)), shape((half + extra, depth), BF16),
        ),
        [vmem((2 * width + PAD, n), BF16), vmem((depth, ny), F32), vmem((ny, depth), F32)],
        limit, xa, norm, b_term, lse, lse_other, peak, yt, plan,
    )
    part = call(
        run(add_kernel, width), shape((rows, yd * width // LANES + extra, LANES), BF16), [],
        limit, keep, sums, swap(send),
    )
    part = lax.all_to_all(part, "row", 0, 0, tiled=True)
    grad_xt, grad_y, g_pot = call(
        run(last_kernel, log_nx, log_ny),
        (shape((width, n)), shape((yd, width)), shape((1, yd))),
        [vmem((2 * LANES, ny), BF16), vmem((count, LANES), F32)],
        limit, xa, r, v, c_term, part, yt, plan, y_own,
    )
    return f_pot.reshape(n), g_pot.reshape(yd), grad_xt.T, grad_y


def solution(mesh):
    in_specs = (
        P(("groups", "row", "col"), None),
        P(("groups", "col", "row"), None),
        P(("groups", "row", "col")),
        P(("groups", "col", "row")),
    )
    out_specs = (
        P(("groups", "row", "col")),
        P(("groups", "col", "row")),
        P(("groups", "row", "col"), None),
        P(("groups", "col", "row"), None),
    )
    return jax.shard_map(
        on_device, mesh=mesh, in_specs=in_specs, out_specs=out_specs, check_vma=False
    )
```

```python
import functools
import math

import jax
import jax.numpy as jnp
from jax import lax
from jax.experimental import pallas as pl
from jax.experimental.pallas import tpu as pltpu
from jax.sharding import PartitionSpec as P

ITERS = 2
EPSILON = 0.02
LOG2E = math.log2(math.e)
TILE = 256
STEP = 32
EXT = 32
PAD = 16
LANES = 128
F32 = jnp.float32
BF16 = jnp.bfloat16


def kappa_of(width):
    return 2.0 / (width * EPSILON)


def pieces(value):
    high = value.astype(BF16).astype(F32)
    rest = value - high
    mid = rest.astype(BF16).astype(F32)
    return high, mid, rest - mid


def select(index, values):
    out = jnp.zeros(index.shape, F32)
    for k, value in values.items():
        out = jnp.where(index == k, value, out)
    return out


def extras_y(index, c_term, mass):
    high, mid, low = pieces(c_term)
    return select(index, {0: high, 1: mid, 2: low, 3: 1.0, 4: 1.0, 5: 1.0, 6: mass})


def extras_x(index, b_term, mass):
    high, mid, low = pieces(b_term)
    return select(index, {0: 1.0, 1: 1.0, 2: 1.0, 3: high, 4: mid, 5: low, 7: mass})


def rows_index(columns):
    return lax.broadcasted_iota(jnp.int32, (EXT, columns), 0)


def to_column(row):
    size = row.shape[1]
    eye = lax.broadcasted_iota(jnp.int32, (size, size), 0) == lax.broadcasted_iota(jnp.int32, (size, size), 1)
    return jnp.sum(jnp.where(eye, row, 0.0), axis=1, keepdims=True)


def to_row(column):
    size = column.shape[0]
    eye = lax.broadcasted_iota(jnp.int32, (size, size), 0) == lax.broadcasted_iota(jnp.int32, (size, size), 1)
    return jnp.sum(jnp.where(eye, column, 0.0), axis=0, keepdims=True)


def for_tiles(total, body):
    count = total // TILE
    if count <= 4:
        for t in range(count):
            body(pl.ds(t * TILE, TILE))
    else:

        @pl.loop(0, count)
        def _(t):
            body(pl.ds(pl.multiple_of(t * TILE, TILE), TILE))


def max_down(z_ref, rows):
    peak = z_ref[0:STEP, :]
    for r in range(STEP, rows, STEP):
        peak = jnp.maximum(peak, z_ref[r : r + STEP, :])
    return jnp.max(peak, axis=0, keepdims=True)


def exp_sum_down(z_ref, rows, scale, shift):
    total = jnp.zeros((STEP, TILE), F32)
    for r in range(0, rows, STEP):
        total = total + jnp.exp2((z_ref[r : r + STEP, :] - shift) * scale)
    return jnp.sum(total, axis=0, keepdims=True)


def to_lanes(row):
    return jnp.concatenate([row[:, k : k + LANES] for k in range(0, row.shape[1], LANES)], axis=0)


def from_lanes(block):
    return jnp.concatenate([block[k : k + 1] for k in range(block.shape[0])], axis=1)


def sums_rows(ny):
    return -(-2 * ny // LANES // 16) * 16


def sums_out(sums):
    high = sums.astype(BF16).astype(F32)
    spare = sums_rows(sums.size) - 2 * sums.shape[0]
    return jnp.concatenate([high, sums - high] + [jnp.zeros((spare, LANES), F32)] * (spare > 0), axis=0)


def pack(block):
    rows, width = block.shape
    base = rows * width // LANES
    spare = LANES - width
    side = [block[base:, k : k + spare] for k in range(0, width, spare)]
    return jnp.concatenate([block[:base], jnp.concatenate(side, axis=0)], axis=1)


def unpack(block, rows, width):
    base = block.shape[0]
    rest = rows - base
    side = [block[k : k + rest, width:] for k in range(0, base, rest)]
    return jnp.concatenate([block[:, :width], jnp.concatenate(side, axis=1)], axis=0)


def prep_kernel(
    log_ny, xt_hbm, y_hbm, mx_hbm, my_hbm, ya_hbm, xa_hbm, y_ref, my_ref, mx_ref, ya_ref, xa_ref, sems
):
    width, n = xt_hbm.shape
    rows = ya_hbm.shape[0]
    move_y = pltpu.make_async_copy(y_hbm, y_ref, sems.at[0])
    move_my = pltpu.make_async_copy(my_hbm, my_ref, sems.at[1])
    move_mx = pltpu.make_async_copy(mx_hbm, mx_ref, sems.at[2])
    move_x = pltpu.make_async_copy(xt_hbm, xa_ref.at[:width, :], sems.at[3])
    for move in (move_y, move_my, move_x, move_mx):
        move.start()
    move_y.wait()
    y = y_ref[...]
    yf = y.astype(F32)
    norm = jnp.sum(yf * yf, axis=1, keepdims=True)
    move_my.wait()
    mass = to_column(my_ref[...].astype(F32))
    c_term = (mass - log_ny) / kappa_of(width) - 0.5 * norm
    index = lax.broadcasted_iota(jnp.int32, (y.shape[0], EXT), 1)
    ya_ref[:, :width] = y
    ya_ref[:, width:] = extras_y(index, c_term, mass).astype(BF16)
    moves = [pltpu.make_async_copy(ya_ref, ya_hbm.at[k], sems.at[5 + k]) for k in range(rows)]
    for move in moves:
        move.start()
    move_mx.wait()
    mass = from_lanes(mx_ref[...].astype(F32))
    xa_ref[width:, :] = extras_x(rows_index(n), jnp.zeros((1, n), F32), mass).astype(BF16)
    move_x.wait()
    move_out = pltpu.make_async_copy(xa_ref, xa_hbm, sems.at[4])
    move_out.start()
    for move in moves:
        move.wait()
    move_out.wait()


def half_kernel(xa_ref, mine_ref, peak_ref, total_ref, z_ref):
    rows, yd, depth = mine_ref.shape
    half = rows * yd
    scale = kappa_of(depth - EXT) * LOG2E
    y_rows = mine_ref[...].reshape(half, depth)

    def row_tile(t):
        z_ref[...] = jnp.dot(y_rows, xa_ref[:, t], preferred_element_type=F32)
        peak = max_down(z_ref, half)
        peak_ref[:, t] = peak
        total_ref[:, t] = exp_sum_down(z_ref, half, scale, peak)

    for_tiles(xa_ref.shape[1], row_tile)


def first_kernel(
    log_nx, xa0_ref, mine_ref, other_ref, peak_ref, total_ref,
    ya_ref, b_ref, l_ref, m_ref, rows_ref, xa_ref, z_ref, zc_ref, b2_ref,
):
    rows, yd, depth = mine_ref.shape
    n = xa0_ref.shape[1]
    width = depth - EXT
    half = rows * yd
    ny = 2 * half
    col = lax.axis_index("col")
    scale = kappa_of(width) * LOG2E
    other = other_ref[...].reshape(half, depth)
    ya_ref[pl.ds(pl.multiple_of(col * half, half), half), :] = mine_ref[...].reshape(half, depth)
    ya_ref[pl.ds(pl.multiple_of((1 - col) * half, half), half), :] = other

    def row_tile(t):
        z_ref[...] = jnp.dot(other, xa0_ref[:, t], preferred_element_type=F32)
        old = peak_ref[:, t]
        peak = jnp.maximum(max_down(z_ref, half), old)
        total = exp_sum_down(z_ref, half, scale, peak) + total_ref[:, t] * jnp.exp2((old - peak) * scale)
        b_ref[:, t] = -peak - jnp.log(total) * (LOG2E / scale)

    for_tiles(n, row_tile)
    mass = xa0_ref[width:, :].astype(F32)[7:8]
    b_term = b_ref[...] + (mass - log_nx) * (LOG2E / scale)
    b_ref[...] = b_term
    xa_ref[:width, :] = xa0_ref[:width, :]
    xa_ref[width:, :] = extras_x(rows_index(n), b_term, mass).astype(BF16)
    rows_ref[...] = xa_ref[...].T

    def col_tile(t):
        zc_ref[...] = lax.dot_general(
            rows_ref[...], ya_ref[t, :], (((1,), (1,)), ((), ())), preferred_element_type=F32
        )
        peak = max_down(zc_ref, n)
        m_ref[:, t] = peak
        b2_ref[:, t] = scale * peak + jnp.log(exp_sum_down(zc_ref, n, scale, peak)) * LOG2E

    for_tiles(ny, col_tile)
    lse = to_lanes(b2_ref[...])
    for k in range(rows):
        l_ref[k] = lse


def plan_kernel(xa_ref, rows_ref, ya_ref, m_ref, t_ref, yt_ref, norm_ref, zc_ref):
    ny, depth = ya_ref.shape
    n = rows_ref.shape[0]
    scale = kappa_of(depth - EXT) * LOG2E

    def col_tile(t):
        y_part = ya_ref[t, :]
        yt_ref[:, t] = y_part.T
        zc_ref[...] = lax.dot_general(
            rows_ref[...], y_part, (((1,), (1,)), ((), ())), preferred_element_type=F32
        )
        peak = m_ref[:, t]
        for r in range(0, n, STEP):
            t_ref[r : r + STEP, t] = jnp.exp2((zc_ref[r : r + STEP, :] - peak) * scale).astype(BF16)

    for_tiles(ny, col_tile)
    xf = xa_ref[: depth - EXT, :].astype(F32)
    norm_ref[...] = jnp.sum(xf * xf, axis=0, keepdims=True)


def stack(out_ref, width, points, factor):
    moved = points.astype(F32) * factor
    high = moved.astype(BF16)
    out_ref[:width, :] = high
    out_ref[width : 2 * width, :] = (moved - high.astype(F32)).astype(BF16)
    one, two, three = pieces(factor)
    index = lax.broadcasted_iota(jnp.int32, (PAD, factor.shape[1]), 0)
    out_ref[2 * width :, :] = select(index, {0: one, 1: two, 2: three}).astype(BF16)


def unstack(product, width):
    ext = product[2 * width :]
    return product[:width] + product[width : 2 * width], (ext[0:1] + ext[1:2]) + ext[2:3]


def second_kernel(
    log_nx, log_ny, xa_ref, b_ref, l_ref, other_ref, m_ref, yt_ref, t_ref,
    r_ref, v_ref, c_ref, xs_ref, sum_ref, send_ref,
):
    width = xa_ref.shape[0] - EXT
    ny = m_ref.shape[1]
    half = ny // 2
    kappa = kappa_of(width)
    scale = kappa * LOG2E
    l_mine, l_other = l_ref[...], other_ref[...]
    peak = jnp.maximum(jnp.max(l_mine, axis=0), jnp.max(l_other, axis=0))
    total = jnp.sum(jnp.exp2(l_mine - peak[None]), axis=0) + jnp.sum(jnp.exp2(l_other - peak[None]), axis=0)
    lse2 = from_lanes(peak + jnp.log(total) * LOG2E)
    old = yt_ref[width:, :].astype(F32)
    c_old = (old[0:1] + old[1:2]) + old[2:3]
    lb2 = (old[6:7] - log_ny) * LOG2E
    c_ref[...] = to_lanes(c_old + (lb2 - lse2) / scale)
    v = jnp.exp2(scale * m_ref[...] + (lb2 - lse2))
    v_ref[...] = v
    one, two, three = pieces(v)
    index = lax.broadcasted_iota(jnp.int32, (PAD, ny), 0)
    v_rows = select(index, {0: one, 1: two, 2: three}).astype(BF16)
    across = (((1,), (1,)), ((), ()))
    sums = lax.dot_general(v_rows, t_ref[...], across, preferred_element_type=F32)
    rowsum = (sums[0:1] + sums[1:2]) + sums[2:3]
    mass = xa_ref[width:, :].astype(F32)[7:8]
    r = jnp.exp(mass - log_nx) / rowsum
    r_ref[...] = r
    stack(xs_ref, width, xa_ref[:width, :], r)
    col = lax.axis_index("col")
    for k in range(half // TILE):
        t = pl.ds(pl.multiple_of((1 - col) * half + k * TILE, TILE), TILE)
        product = jnp.dot(xs_ref[...], t_ref[:, t], preferred_element_type=F32)
        moment, total = unstack(product, width)
        total = total * v_ref[:, t]
        sum_ref[:, t] = total
        part = yt_ref[:width, t].astype(F32) * total - moment * v_ref[:, t]
        send_ref[:width, k * TILE : (k + 1) * TILE] = part.astype(BF16)
        t = pl.ds(pl.multiple_of(col * half + k * TILE, TILE), TILE)
        ext = jnp.dot(xs_ref[2 * width :, :], t_ref[:, t], preferred_element_type=F32)
        sum_ref[:, t] = ((ext[0:1] + ext[1:2]) + ext[2:3]) * v_ref[:, t]
    sums = sum_ref[...]
    high = sums.astype(BF16).astype(F32)
    low = sums - high
    index = lax.broadcasted_iota(jnp.int32, (PAD, half), 0)
    ext = select(index, {0: high[:, :half], 1: high[:, half:], 2: low[:, :half], 3: low[:, half:]})
    send_ref[width:, :] = ext.astype(BF16)


def keep_kernel(xs_ref, v_ref, sum_ref, yt_ref, t_ref, keep_ref):
    width, half = keep_ref.shape
    col = lax.axis_index("col")
    for k in range(half // TILE):
        t = pl.ds(pl.multiple_of(col * half + k * TILE, TILE), TILE)
        product = jnp.dot(xs_ref[: 2 * width, :], t_ref[:, t], preferred_element_type=F32)
        moment = product[:width] + product[width:]
        part = yt_ref[:width, t].astype(F32) * sum_ref[:, t] - moment * v_ref[:, t]
        keep_ref[:, k * TILE : (k + 1) * TILE] = part


def add_kernel(keep_ref, sum_ref, got_ref, out_ref):
    width, half = keep_ref.shape
    rows = out_ref.shape[0]
    yd = half // rows
    base = yd * width // LANES
    ext = got_ref[width:, :].astype(F32)
    other = jnp.concatenate([ext[0:1] + ext[2:3], ext[1:2] + ext[3:4]], axis=1)
    sums = sums_out(to_lanes(sum_ref[...] + other)).astype(BF16)
    total = (keep_ref[...] + got_ref[:width, :].astype(F32)).T
    for r in range(rows):
        out_ref[r, :base, :] = pack(total[r * yd : (r + 1) * yd, :]).astype(BF16)
        out_ref[r, base:, :] = sums


def own_part(ref, yd):
    block = lax.axis_index("col") * lax.axis_size("row") + lax.axis_index("row")
    fit = LANES // yd
    row = ref[pl.ds(block // fit, 1), :]
    out = row[:, :yd]
    for k in range(1, fit):
        out = jnp.where(block % fit == k, row[:, k * yd : (k + 1) * yd], out)
    return out


def last_kernel(
    log_nx, log_ny, xa_ref, norm_ref, b_ref, r_ref, v_ref, c_ref, got_ref, yt_ref, t_ref, y_ref,
    f_hbm, pot_hbm, gx_hbm, gy_hbm, f_ref, pot_ref, gx_ref, gy_ref, ys_ref, sum_ref, sems,
):
    width, n = gx_ref.shape
    ny = v_ref.shape[1]
    yd = y_ref.shape[1]
    base = yd * width // LANES
    count = ny // LANES
    kappa = kappa_of(width)
    moves = []

    def leave(source, target):
        move = pltpu.make_async_copy(source, target, sems.at[len(moves)])
        move.start()
        moves.append(move)

    mass = xa_ref[width:, :].astype(F32)[7:8]
    log_row = mass - log_nx - jnp.log(r_ref[...])
    f_ref[...] = norm_ref[...] / width + EPSILON * (kappa * b_ref[...] - log_row)
    leave(f_ref, f_hbm)
    total = got_ref[0].astype(F32)
    for k in range(1, got_ref.shape[0]):
        total = total + got_ref[k].astype(F32)
    sums = total[base : base + count] + total[base + count : base + 2 * count]
    sum_ref[...] = sums
    colsum = own_part(sum_ref, yd)
    c_term = own_part(c_ref, yd)
    own = y_ref[0].astype(F32)
    gy_ref[...] = unpack(total[:base], yd, width) * (
        jnp.exp(own[:, width + 6 : width + 7]) * to_column(1.0 / colsum)
    )
    leave(gy_ref, gy_hbm)
    norm = to_row(jnp.sum(own[:, :width] * own[:, :width], axis=1, keepdims=True))
    pot_ref[...] = norm / width - EPSILON * (jnp.log(colsum) - kappa * c_term)
    leave(pot_ref, pot_hbm)
    mass = yt_ref[width:, :].astype(F32)[6:7]
    q = v_ref[...] * jnp.exp(mass + log_nx - jnp.log(from_lanes(sums)))
    stack(ys_ref, width, yt_ref[:width, :], q)
    across = (((1,), (1,)), ((), ()))
    for k in range(n // TILE):
        t = slice(k * TILE, (k + 1) * TILE)
        product = lax.dot_general(ys_ref[...], t_ref[t, :], across, preferred_element_type=F32)
        moved, weight = unstack(product, width)
        gx_ref[:, t] = (xa_ref[:width, t].astype(F32) * weight - moved) * (r_ref[:, t] * (1.0 / ny))
        leave(gx_ref.at[:, t], gx_hbm.at[:, t])
    for move in moves:
        move.wait()


def call(kernel, outs, scratch, limit, *args, space=pltpu.VMEM, out_space=pltpu.VMEM):
    return pl.pallas_call(
        kernel,
        out_shape=outs,
        in_specs=[pl.BlockSpec(memory_space=space)] * len(args),
        out_specs=jax.tree.map(lambda _: pl.BlockSpec(memory_space=out_space), outs),
        scratch_shapes=scratch,
        compiler_params=pltpu.CompilerParams(vmem_limit_bytes=limit),
    )(*args)


def shape(dims, dtype=F32):
    return jax.ShapeDtypeStruct(dims, dtype)


def swap(value):
    return lax.ppermute(value, "col", [(0, 1), (1, 0)])


def on_device(points_x, points_y, mass_x, mass_y):
    n, width = points_x.shape
    yd = points_y.shape[0]
    rows = lax.axis_size("row")
    ny = 2 * rows * yd
    half = ny // 2
    count = ny // LANES
    log_nx, log_ny = math.log(n * 2 * rows), math.log(ny)
    depth = width + EXT
    limit = (12 if ny <= 1024 else 56) * 1024 * 1024
    extra = sums_rows(ny)
    run = functools.partial
    vmem = pltpu.VMEM
    y_own, xa = call(
        run(prep_kernel, log_ny),
        (shape((rows, yd, depth), BF16), shape((depth, n), BF16)),
        [
            vmem((yd, width), BF16), vmem((1, yd), BF16), vmem((n // LANES, LANES), BF16),
            vmem((yd, depth), BF16), vmem((depth, n), BF16), pltpu.SemaphoreType.DMA((5 + rows,)),
        ],
        58 * 1024 * 1024,
        points_x.T, points_y, mass_x.reshape(n // LANES, LANES), mass_y.reshape(1, yd), space=pl.ANY, out_space=pl.ANY,
    )
    y_mine = lax.all_to_all(y_own, "row", 0, 0, tiled=True)
    y_other = swap(y_mine)
    peak, total = call(
        half_kernel, (shape((1, n)), shape((1, n))), [vmem((half, TILE), F32)], limit, xa, y_mine
    )
    ya, b_term, lse, peak, x_rows = call(
        run(first_kernel, log_nx),
        (
            shape((ny, depth), BF16), shape((1, n)), shape((rows, count, LANES)), shape((1, ny)),
            shape((n, depth), BF16),
        ),
        [vmem((depth, n), BF16), vmem((half, TILE), F32), vmem((n, TILE), F32), vmem((1, ny), F32)],
        limit, xa, y_mine, y_other, peak, total,
    )
    lse = lax.all_to_all(lse, "row", 0, 0, tiled=True)
    lse_other = swap(lse)
    plan, yt, norm = call(
        plan_kernel,
        (shape((n, ny), BF16), shape((depth, ny), BF16), shape((1, n))),
        [vmem((n, TILE), F32)],
        limit, xa, x_rows, ya, peak,
    )
    r, v, c_term, xs, sums, send = call(
        run(second_kernel, log_nx, log_ny),
        (
            shape((1, n)), shape((1, ny)), shape((count, LANES)), shape((2 * width + PAD, n), BF16),
            shape((1, ny)), shape((width + PAD, half), BF16),
        ),
        [], limit, xa, b_term, lse, lse_other, peak, yt, plan,
    )
    got = swap(send)
    keep = call(keep_kernel, shape((width, half)), [], limit, xs, v, sums, yt, plan)
    part = call(
        add_kernel, shape((rows, yd * width // LANES + extra, LANES), BF16), [], limit, keep, sums, got
    )
    part = lax.all_to_all(part, "row", 0, 0, tiled=True)
    f_pot, g_pot, grad_xt, grad_y = call(
        run(last_kernel, log_nx, log_ny),
        (shape((1, n)), shape((1, yd)), shape((width, n)), shape((yd, width))),
        [
            vmem((1, n), F32), vmem((1, yd), F32), vmem((width, n), F32), vmem((yd, width), F32),
            vmem((2 * width + PAD, ny), BF16), vmem((count, LANES), F32),
            pltpu.SemaphoreType.DMA((3 + n // TILE,)),
        ],
        limit, xa, norm, b_term, r, v, c_term, part, yt, plan, y_own, out_space=pl.ANY,
    )
    return f_pot.reshape(n), g_pot.reshape(yd), grad_xt.T, grad_y


def solution(mesh):
    in_specs = (
        P(("groups", "row", "col"), None),
        P(("groups", "col", "row"), None),
        P(("groups", "row", "col")),
        P(("groups", "col", "row")),
    )
    out_specs = (
        P(("groups", "row", "col")),
        P(("groups", "col", "row")),
        P(("groups", "row", "col"), None),
        P(("groups", "col", "row"), None),
    )
    return jax.shard_map(
        on_device, mesh=mesh, in_specs=in_specs, out_specs=out_specs, check_vma=False
    )
```

```python
import functools
import math

import jax
import jax.numpy as jnp
from jax import lax
from jax.experimental import pallas as pl
from jax.experimental.pallas import tpu as pltpu
from jax.sharding import PartitionSpec as P

ITERS = 2
EPSILON = 0.02
LOG2E = math.log2(math.e)
TILE = 256
STEP = 32
EXT = 32
PAD = 16
LANES = 128
AXES = ("row", "col")
F32 = jnp.float32
BF16 = jnp.bfloat16


def kappa_of(width):
    return 2.0 / (width * EPSILON)


def pieces(value):
    high = value.astype(BF16).astype(F32)
    rest = value - high
    mid = rest.astype(BF16).astype(F32)
    return high, mid, rest - mid


def select(index, values):
    out = jnp.zeros(index.shape, F32)
    for k, value in values.items():
        out = jnp.where(index == k, value, out)
    return out


def extras_x(index, b_term, mass):
    high, mid, low = pieces(b_term)
    return select(index, {0: 1.0, 1: 1.0, 2: 1.0, 3: high, 4: mid, 5: low, 7: mass})


def rows_index(columns):
    return lax.broadcasted_iota(jnp.int32, (EXT, columns), 0)


def to_column(row):
    size = row.shape[1]
    eye = lax.broadcasted_iota(jnp.int32, (size, size), 0) == lax.broadcasted_iota(jnp.int32, (size, size), 1)
    return jnp.sum(jnp.where(eye, row, 0.0), axis=1, keepdims=True)


def to_row(column):
    size = column.shape[0]
    eye = lax.broadcasted_iota(jnp.int32, (size, size), 0) == lax.broadcasted_iota(jnp.int32, (size, size), 1)
    return jnp.sum(jnp.where(eye, column, 0.0), axis=0, keepdims=True)


def for_tiles(total, product, z_ref, use):
    count = total // TILE
    slots = z_ref.shape[0]
    if count <= slots:
        for t in range(count):
            z_ref[t] = product(pl.ds(t * TILE, TILE))
        for t in range(count):
            use(pl.ds(t * TILE, TILE), z_ref.at[t])
    else:

        @pl.loop(0, count)
        def _(t):
            tile = pl.ds(pl.multiple_of(t * TILE, TILE), TILE)
            z_ref[0] = product(tile)
            use(tile, z_ref.at[0])


def max_down(z_ref, rows):
    peak = z_ref[0:STEP, :]
    for r in range(STEP, rows, STEP):
        peak = jnp.maximum(peak, z_ref[r : r + STEP, :])
    return jnp.max(peak, axis=0, keepdims=True)


def exp_sum_down(z_ref, rows, scale, shift, keep=None):
    total = jnp.zeros((STEP, TILE), F32)
    for r in range(0, rows, STEP):
        value = jnp.exp2((z_ref[r : r + STEP, :] - shift) * scale)
        total = total + value
        if keep is not None:
            keep(r, value.astype(BF16))
    return jnp.sum(total, axis=0, keepdims=True)


def to_lanes(row):
    return jnp.concatenate([row[:, k : k + LANES] for k in range(0, row.shape[1], LANES)], axis=0)


def from_lanes(block):
    return jnp.concatenate([block[k : k + 1] for k in range(block.shape[0])], axis=1)


def sums_rows(ny):
    return -(-2 * ny // LANES // 16) * 16


def sums_out(sums):
    high = sums.astype(BF16).astype(F32)
    spare = sums_rows(sums.size) - 2 * sums.shape[0]
    return jnp.concatenate([high, sums - high] + [jnp.zeros((spare, LANES), F32)] * (spare > 0), axis=0)


def pack(block):
    rows, width = block.shape
    base = rows * width // LANES
    spare = LANES - width
    side = [block[base:, k : k + spare] for k in range(0, width, spare)]
    return jnp.concatenate([block[:base], jnp.concatenate(side, axis=0)], axis=1)


def unpack(block, rows, width):
    base = block.shape[0]
    rest = rows - base
    side = [block[k : k + rest, width:] for k in range(0, base, rest)]
    return jnp.concatenate([block[:, :width], jnp.concatenate(side, axis=1)], axis=0)


def ones_kernel(ext_ref):
    index = lax.broadcasted_iota(jnp.int32, ext_ref.shape, 1)
    ext_ref[...] = select(index, {3: 1.0, 4: 1.0, 5: 1.0})


def prep_kernel(log_ny, y_ref, my_ref, ones_ref, ya_ref):
    width = y_ref.shape[1]
    y = y_ref[...]
    yf = y.astype(F32)
    norm = jnp.sum(yf * yf, axis=1, keepdims=True)
    mass = to_column(my_ref[...].astype(F32))
    c_term = (mass - log_ny) / kappa_of(width) - 0.5 * norm
    high, mid, low = pieces(c_term)
    index = lax.broadcasted_iota(jnp.int32, ones_ref.shape, 1)
    ext = (ones_ref[...] + select(index, {0: high, 1: mid, 2: low, 6: mass})).astype(BF16)
    for k in range(ya_ref.shape[0]):
        ya_ref[k, :, :width] = y
        ya_ref[k, :, width:] = ext


def half_kernel(xt_ref, mx_ref, mine_ref, xa_ref, peak_ref, total_ref, z_ref):
    rows, yd, depth = mine_ref.shape
    width, n = xt_ref.shape
    half = rows * yd
    scale = kappa_of(width) * LOG2E
    mass = from_lanes(mx_ref[...].astype(F32))
    xa_ref[:width, :] = xt_ref[...]
    xa_ref[width:, :] = extras_x(rows_index(n), jnp.zeros((1, n), F32), mass).astype(BF16)
    y_rows = mine_ref[...].reshape(half, depth)

    def product(t):
        return jnp.dot(y_rows, xa_ref[:, t], preferred_element_type=F32)

    def use(t, z):
        peak = max_down(z, half)
        peak_ref[:, t] = peak
        total_ref[:, t] = exp_sum_down(z, half, scale, peak)

    for_tiles(n, product, z_ref, use)


def first_kernel(
    log_nx, xa0_ref, mine_ref, other_ref, peak_ref, total_ref,
    yt_ref, b_ref, l_ref, m_ref, t_ref, xa_ref, ya_ref, z_ref, zc_ref, b2_ref,
):
    rows, yd, depth = mine_ref.shape
    n = xa0_ref.shape[1]
    width = depth - EXT
    half = rows * yd
    ny = 2 * half
    col = lax.axis_index("col")
    scale = kappa_of(width) * LOG2E
    other = other_ref[...].reshape(half, depth)

    def product(t):
        return jnp.dot(other, xa0_ref[:, t], preferred_element_type=F32)

    def use(t, z):
        old = peak_ref[:, t]
        peak = jnp.maximum(max_down(z, half), old)
        total = exp_sum_down(z, half, scale, peak) + total_ref[:, t] * jnp.exp2((old - peak) * scale)
        b_ref[:, t] = -peak - jnp.log(total) * (LOG2E / scale)

    for_tiles(n, product, z_ref, use)
    ya_ref[pl.ds(pl.multiple_of(col * half, half), half), :] = mine_ref[...].reshape(half, depth)
    ya_ref[pl.ds(pl.multiple_of((1 - col) * half, half), half), :] = other
    yt_ref[...] = ya_ref[...].T
    mass = xa0_ref[width:, :].astype(F32)[7:8]
    b_term = b_ref[...] + (mass - log_nx) * (LOG2E / scale)
    b_ref[...] = b_term
    xa_ref[:width, :] = xa0_ref[:width, :]
    xa_ref[width:, :] = extras_x(rows_index(n), b_term, mass).astype(BF16)
    x_rows = xa_ref[...].T

    def product(t):
        return jnp.dot(x_rows, yt_ref[:, t], preferred_element_type=F32)

    def use(t, z):
        def keep(r, value):
            t_ref[r : r + STEP, t] = value

        peak = max_down(z, n)
        m_ref[:, t] = peak
        b2_ref[:, t] = scale * peak + jnp.log(exp_sum_down(z, n, scale, peak, keep)) * LOG2E

    for_tiles(ny, product, zc_ref, use)
    lse = to_lanes(b2_ref[...])
    for k in range(2 * rows):
        l_ref[k] = lse


def stack(out_ref, width, points, factor):
    moved = points.astype(F32) * factor
    high = moved.astype(BF16)
    out_ref[:width, :] = high
    out_ref[width : 2 * width, :] = (moved - high.astype(F32)).astype(BF16)
    one, two, three = pieces(factor)
    index = lax.broadcasted_iota(jnp.int32, (PAD, factor.shape[1]), 0)
    out_ref[2 * width :, :] = select(index, {0: one, 1: two, 2: three}).astype(BF16)


def unstack(product, width):
    ext = product[2 * width :]
    return product[:width] + product[width : 2 * width], (ext[0:1] + ext[1:2]) + ext[2:3]


def second_kernel(
    log_nx, log_ny, xa_ref, b_ref, l_ref, m_ref, yt_ref, t_ref,
    r_ref, v_ref, c_ref, xs_ref, sum_ref, send_ref,
):
    width = xa_ref.shape[0] - EXT
    ny = m_ref.shape[1]
    half = ny // 2
    kappa = kappa_of(width)
    scale = kappa * LOG2E
    l_all = l_ref[...]
    peak = jnp.max(l_all, axis=0)
    total = jnp.sum(jnp.exp2(l_all - peak[None]), axis=0)
    lse2 = from_lanes(peak + jnp.log(total) * LOG2E)
    old = yt_ref[width:, :].astype(F32)
    c_old = (old[0:1] + old[1:2]) + old[2:3]
    lb2 = (old[6:7] - log_ny) * LOG2E
    c_ref[...] = to_lanes(c_old + (lb2 - lse2) / scale)
    v = jnp.exp2(scale * m_ref[...] + (lb2 - lse2))
    v_ref[...] = v
    one, two, three = pieces(v)
    index = lax.broadcasted_iota(jnp.int32, (PAD, ny), 0)
    v_rows = select(index, {0: one, 1: two, 2: three}).astype(BF16)
    across = (((1,), (1,)), ((), ()))
    sums = lax.dot_general(v_rows, t_ref[...], across, preferred_element_type=F32)
    rowsum = (sums[0:1] + sums[1:2]) + sums[2:3]
    mass = xa_ref[width:, :].astype(F32)[7:8]
    r = jnp.exp(mass - log_nx) / rowsum
    r_ref[...] = r
    stack(xs_ref, width, xa_ref[:width, :], r)
    col = lax.axis_index("col")
    for k in range(half // TILE):
        t = pl.ds(pl.multiple_of((1 - col) * half + k * TILE, TILE), TILE)
        product = jnp.dot(xs_ref[...], t_ref[:, t], preferred_element_type=F32)
        moment, total = unstack(product, width)
        total = total * v_ref[:, t]
        sum_ref[:, t] = total
        part = yt_ref[:width, t].astype(F32) * total - moment * v_ref[:, t]
        send_ref[:width, k * TILE : (k + 1) * TILE] = part.astype(BF16)
        t = pl.ds(pl.multiple_of(col * half + k * TILE, TILE), TILE)
        ext = jnp.dot(xs_ref[2 * width :, :], t_ref[:, t], preferred_element_type=F32)
        sum_ref[:, t] = ((ext[0:1] + ext[1:2]) + ext[2:3]) * v_ref[:, t]
    sums = sum_ref[...]
    high = sums.astype(BF16).astype(F32)
    low = sums - high
    index = lax.broadcasted_iota(jnp.int32, (PAD, half), 0)
    ext = select(index, {0: high[:, :half], 1: high[:, half:], 2: low[:, :half], 3: low[:, half:]})
    send_ref[width:, :] = ext.astype(BF16)


def keep_kernel(xa_ref, xs_ref, v_ref, sum_ref, yt_ref, t_ref, keep_ref, norm_ref):
    width, half = keep_ref.shape
    col = lax.axis_index("col")
    for k in range(half // TILE):
        t = pl.ds(pl.multiple_of(col * half + k * TILE, TILE), TILE)
        product = jnp.dot(xs_ref[: 2 * width, :], t_ref[:, t], preferred_element_type=F32)
        moment = product[:width] + product[width:]
        part = yt_ref[:width, t].astype(F32) * sum_ref[:, t] - moment * v_ref[:, t]
        keep_ref[:, k * TILE : (k + 1) * TILE] = part
    xf = xa_ref[:width, :].astype(F32)
    norm_ref[...] = jnp.sum(xf * xf, axis=0, keepdims=True)


def add_kernel(keep_ref, sum_ref, got_ref, out_ref):
    width, half = keep_ref.shape
    rows = out_ref.shape[0]
    yd = half // rows
    base = yd * width // LANES
    ext = got_ref[width:, :].astype(F32)
    other = jnp.concatenate([ext[0:1] + ext[2:3], ext[1:2] + ext[3:4]], axis=1)
    sums = sums_out(to_lanes(sum_ref[...] + other)).astype(BF16)
    total = (keep_ref[...] + got_ref[:width, :].astype(F32)).T
    for r in range(rows):
        out_ref[r, :base, :] = pack(total[r * yd : (r + 1) * yd, :]).astype(BF16)
        out_ref[r, base:, :] = sums


def own_part(ref, yd):
    block = lax.axis_index("col") * lax.axis_size("row") + lax.axis_index("row")
    fit = LANES // yd
    row = ref[pl.ds(block // fit, 1), :]
    out = row[:, :yd]
    for k in range(1, fit):
        out = jnp.where(block % fit == k, row[:, k * yd : (k + 1) * yd], out)
    return out


def last_kernel(
    log_nx, log_ny, xa_ref, norm_ref, b_ref, r_ref, v_ref, c_ref, got_ref, yt_ref, t_ref, y_ref,
    f_hbm, pot_hbm, gx_hbm, gy_hbm, f_ref, pot_ref, gx_ref, gy_ref, ys_ref, sum_ref, sems,
):
    width, n = gx_ref.shape
    ny = v_ref.shape[1]
    yd = y_ref.shape[1]
    base = yd * width // LANES
    count = ny // LANES
    kappa = kappa_of(width)
    moves = []

    def leave(source, target):
        move = pltpu.make_async_copy(source, target, sems.at[len(moves)])
        move.start()
        moves.append(move)

    mass = xa_ref[width:, :].astype(F32)[7:8]
    log_row = mass - log_nx - jnp.log(r_ref[...])
    f_ref[...] = norm_ref[...] / width + EPSILON * (kappa * b_ref[...] - log_row)
    leave(f_ref, f_hbm)
    total = got_ref[0].astype(F32)
    for k in range(1, got_ref.shape[0]):
        total = total + got_ref[k].astype(F32)
    sums = total[base : base + count] + total[base + count : base + 2 * count]
    sum_ref[...] = sums
    colsum = own_part(sum_ref, yd)
    c_term = own_part(c_ref, yd)
    own = y_ref[0].astype(F32)
    gy_ref[...] = unpack(total[:base], yd, width) * (
        jnp.exp(own[:, width + 6 : width + 7]) * to_column(1.0 / colsum)
    )
    leave(gy_ref, gy_hbm)
    norm = to_row(jnp.sum(own[:, :width] * own[:, :width], axis=1, keepdims=True))
    pot_ref[...] = norm / width - EPSILON * (jnp.log(colsum) - kappa * c_term)
    leave(pot_ref, pot_hbm)
    mass = yt_ref[width:, :].astype(F32)[6:7]
    q = v_ref[...] * jnp.exp(mass + log_nx - jnp.log(from_lanes(sums)))
    stack(ys_ref, width, yt_ref[:width, :], q)
    across = (((1,), (1,)), ((), ()))
    for k in range(n // TILE):
        t = slice(k * TILE, (k + 1) * TILE)
        product = lax.dot_general(ys_ref[...], t_ref[t, :], across, preferred_element_type=F32)
        moved, weight = unstack(product, width)
        gx_ref[:, t] = (xa_ref[:width, t].astype(F32) * weight - moved) * (r_ref[:, t] * (1.0 / ny))
        leave(gx_ref.at[:, t], gx_hbm.at[:, t])
    for move in moves:
        move.wait()


def call(kernel, outs, scratch, limit, *args, space=pltpu.VMEM, out_space=pltpu.VMEM, cost=None):
    return pl.pallas_call(
        kernel,
        out_shape=outs,
        in_specs=[pl.BlockSpec(memory_space=space)] * len(args),
        out_specs=jax.tree.map(lambda _: pl.BlockSpec(memory_space=out_space), outs),
        scratch_shapes=scratch,
        cost_estimate=cost,
        compiler_params=pltpu.CompilerParams(vmem_limit_bytes=limit),
    )(*args)


def shape(dims, dtype=F32):
    return jax.ShapeDtypeStruct(dims, dtype)


def swap(value):
    return lax.ppermute(value, "col", [(0, 1), (1, 0)])


def on_device(points_x, points_y, mass_x, mass_y):
    n, width = points_x.shape
    yd = points_y.shape[0]
    rows = lax.axis_size("row")
    ny = 2 * rows * yd
    half = ny // 2
    count = ny // LANES
    log_nx, log_ny = math.log(n * 2 * rows), math.log(ny)
    depth = width + EXT
    limit = (20 if ny <= 1024 else 56) * 1024 * 1024
    extra = sums_rows(ny)
    run = functools.partial
    vmem = pltpu.VMEM
    slots = 4 if ny <= 1024 else 1
    ones = call(
        ones_kernel, shape((yd, EXT)), [], limit,
        cost=pl.CostEstimate(flops=4 * 10**9, bytes_accessed=10000, transcendentals=0),
    )
    y_own = call(
        run(prep_kernel, log_ny), shape((rows, yd, depth), BF16), [], limit, points_y, mass_y.reshape(1, yd), ones,
        cost=pl.CostEstimate(flops=4 * 10**9, bytes_accessed=400000, transcendentals=0),
    )
    y_mine = lax.all_to_all(y_own, "row", 0, 0, tiled=True)
    y_other = swap(y_mine)
    xa, peak, total = call(
        half_kernel, (shape((depth, n), BF16), shape((1, n)), shape((1, n))), [vmem((slots, half, TILE), F32)],
        limit, points_x.T, mass_x.reshape(n // LANES, LANES), y_mine,
    )
    yt, b_term, lse, peak, plan = call(
        run(first_kernel, log_nx),
        (
            shape((depth, ny), BF16), shape((1, n)), shape((2 * rows, count, LANES)), shape((1, ny)),
            shape((n, ny), BF16),
        ),
        [
            vmem((depth, n), BF16), vmem((ny, depth), BF16), vmem((slots, half, TILE), F32),
            vmem((slots, n, TILE), F32), vmem((1, ny), F32),
        ],
        limit, xa, y_mine, y_other, peak, total,
    )
    lse = lax.all_to_all(lse, AXES, 0, 0, tiled=True)
    r, v, c_term, xs, sums, send = call(
        run(second_kernel, log_nx, log_ny),
        (
            shape((1, n)), shape((1, ny)), shape((count, LANES)), shape((2 * width + PAD, n), BF16),
            shape((1, ny)), shape((width + PAD, half), BF16),
        ),
        [], limit, xa, b_term, lse, peak, yt, plan,
    )
    got = swap(send)
    keep, norm = call(
        keep_kernel, (shape((width, half)), shape((1, n))), [], limit, xa, xs, v, sums, yt, plan
    )
    part = call(
        add_kernel, shape((rows, yd * width // LANES + extra, LANES), BF16), [], limit, keep, sums, got
    )
    part = lax.all_to_all(part, "row", 0, 0, tiled=True)
    f_pot, g_pot, grad_xt, grad_y = call(
        run(last_kernel, log_nx, log_ny),
        (shape((1, n)), shape((1, yd)), shape((width, n)), shape((yd, width))),
        [
            vmem((1, n), F32), vmem((1, yd), F32), vmem((width, n), F32), vmem((yd, width), F32),
            vmem((2 * width + PAD, ny), BF16), vmem((count, LANES), F32),
            pltpu.SemaphoreType.DMA((3 + n // TILE,)),
        ],
        limit, xa, norm, b_term, r, v, c_term, part, yt, plan, y_own, out_space=pl.ANY,
    )
    return f_pot.reshape(n), g_pot.reshape(yd), grad_xt.T, grad_y


def solution(mesh):
    in_specs = (
        P(("groups", "row", "col"), None),
        P(("groups", "col", "row"), None),
        P(("groups", "row", "col")),
        P(("groups", "col", "row")),
    )
    out_specs = (
        P(("groups", "row", "col")),
        P(("groups", "col", "row")),
        P(("groups", "row", "col"), None),
        P(("groups", "col", "row"), None),
    )
    return jax.shard_map(
        on_device, mesh=mesh, in_specs=in_specs, out_specs=out_specs, check_vma=False
    )
```

```python
import functools
import math

import jax
import jax.numpy as jnp
from jax import lax
from jax.experimental import pallas as pl
from jax.experimental.pallas import tpu as pltpu
from jax.sharding import PartitionSpec as P

ITERS = 2
EPSILON = 0.02
LOG2E = math.log2(math.e)
TILE = 256
STEP = 8
WIDE = 1024
EXT = 32
PAD = 16
LANES = 128
AXES = ("row", "col")
F32 = jnp.float32
BF16 = jnp.bfloat16


def kappa_of(width):
    return 2.0 / (width * EPSILON)


def pieces(value):
    high = value.astype(BF16).astype(F32)
    rest = value - high
    mid = rest.astype(BF16).astype(F32)
    return high, mid, rest - mid


def select(index, values):
    out = jnp.zeros(index.shape, F32)
    for k, value in values.items():
        out = jnp.where(index == k, value, out)
    return out


def extras_x(index, b_term, mass):
    high, mid, low = pieces(b_term)
    return select(index, {0: 1.0, 1: 1.0, 2: 1.0, 3: high, 4: mid, 5: low, 7: mass})


def rows_index(columns):
    return lax.broadcasted_iota(jnp.int32, (EXT, columns), 0)


def to_column(row):
    size = row.shape[1]
    eye = lax.broadcasted_iota(jnp.int32, (size, size), 0) == lax.broadcasted_iota(jnp.int32, (size, size), 1)
    return jnp.sum(jnp.where(eye, row, 0.0), axis=1, keepdims=True)


def to_row(column):
    size = column.shape[0]
    eye = lax.broadcasted_iota(jnp.int32, (size, size), 0) == lax.broadcasted_iota(jnp.int32, (size, size), 1)
    return jnp.sum(jnp.where(eye, column, 0.0), axis=0, keepdims=True)


def max_down(z_ref):
    rows, columns = z_ref.shape
    peak = z_ref[0:STEP, :]
    for r in range(STEP, rows, STEP):
        peak = jnp.maximum(peak, z_ref[r : r + STEP, :])
    return jnp.max(peak, axis=0, keepdims=True)


def exp_sum_down(z_ref, scale, shift):
    rows, columns = z_ref.shape
    total = jnp.zeros((STEP, columns), F32)
    for r in range(0, rows, STEP):
        total = total + jnp.exp2((z_ref[r : r + STEP, :] - shift) * scale)
    return jnp.sum(total, axis=0, keepdims=True)


def to_lanes(row):
    return jnp.concatenate([row[:, k : k + LANES] for k in range(0, row.shape[1], LANES)], axis=0)


def from_lanes(block):
    return jnp.concatenate([block[k : k + 1] for k in range(block.shape[0])], axis=1)


def sums_rows(ny):
    return -(-2 * ny // LANES // 16) * 16


def sums_out(sums):
    high = sums.astype(BF16).astype(F32)
    spare = sums_rows(sums.size) - 2 * sums.shape[0]
    return jnp.concatenate([high, sums - high] + [jnp.zeros((spare, LANES), F32)] * (spare > 0), axis=0)


def pack(block):
    rows, width = block.shape
    base = rows * width // LANES
    spare = LANES - width
    side = [block[base:, k : k + spare] for k in range(0, width, spare)]
    return jnp.concatenate([block[:base], jnp.concatenate(side, axis=0)], axis=1)


def unpack(block, rows, width):
    base = block.shape[0]
    rest = rows - base
    side = [block[k : k + rest, width:] for k in range(0, base, rest)]
    return jnp.concatenate([block[:, :width], jnp.concatenate(side, axis=1)], axis=0)


def ones_kernel(ext_ref):
    index = lax.broadcasted_iota(jnp.int32, ext_ref.shape, 1)
    ext_ref[...] = select(index, {3: 1.0, 4: 1.0, 5: 1.0})


def prep_kernel(log_ny, y_ref, my_ref, ones_ref, ya_ref):
    width = y_ref.shape[1]
    y = y_ref[...]
    yf = y.astype(F32)
    norm = jnp.sum(yf * yf, axis=1, keepdims=True)
    mass = to_column(my_ref[...].astype(F32))
    c_term = (mass - log_ny) / kappa_of(width) - 0.5 * norm
    high, mid, low = pieces(c_term)
    index = lax.broadcasted_iota(jnp.int32, ones_ref.shape, 1)
    ext = (ones_ref[...] + select(index, {0: high, 1: mid, 2: low, 6: mass})).astype(BF16)
    for k in range(ya_ref.shape[0]):
        ya_ref[k, :, :width] = y
        ya_ref[k, :, width:] = ext


def half_kernel(xt_ref, mx_ref, mine_ref, xa_ref, rows_ref, yt_ref, peak_ref, total_ref, z_ref):
    rows, yd, depth = mine_ref.shape
    width, n = xt_ref.shape
    half = rows * yd
    scale = kappa_of(width) * LOG2E
    mass = from_lanes(mx_ref[...].astype(F32))
    xa_ref[:width, :] = xt_ref[...]
    xa_ref[width:, :] = extras_x(rows_index(n), jnp.zeros((1, n), F32), mass).astype(BF16)
    mine = mine_ref[...].reshape(half, depth)
    z_ref[...] = jnp.dot(mine, xa_ref[...], preferred_element_type=F32)
    peak = max_down(z_ref)
    peak_ref[...] = peak
    total_ref[...] = exp_sum_down(z_ref, scale, peak)
    rows_ref[...] = xa_ref[...].T
    yt_ref[...] = mine.T


def first_kernel(
    log_nx, xa0_ref, rows0_ref, mine_ref, other_ref, peak_ref, total_ref,
    yt_ref, b_ref, l_ref, m_ref, t_ref, z_ref, zc_ref, b2_ref,
):
    rows, yd, depth = other_ref.shape
    n = xa0_ref.shape[1]
    width = depth - EXT
    half = rows * yd
    ny = 2 * half
    col = lax.axis_index("col")
    scale = kappa_of(width) * LOG2E
    other = other_ref[...].reshape(half, depth)
    z_ref[...] = jnp.dot(other, xa0_ref[...], preferred_element_type=F32)
    yt_ref[:, pl.ds(pl.multiple_of(col * half, half), half)] = mine_ref[...]
    yt_ref[:, pl.ds(pl.multiple_of((1 - col) * half, half), half)] = other.T
    old = peak_ref[...]
    peak = jnp.maximum(max_down(z_ref), old)
    total = exp_sum_down(z_ref, scale, peak) + total_ref[...] * jnp.exp2((old - peak) * scale)
    mass = xa0_ref[width:, :].astype(F32)[7:8]
    b_term = -peak + (mass - log_nx - jnp.log(total)) * (LOG2E / scale)
    b_ref[...] = b_term
    ext = extras_x(rows_index(n), b_term, mass).T.astype(BF16)
    x_rows = jnp.concatenate([rows0_ref[:, :width], ext], axis=1)
    wide = min(WIDE, ny)

    def columns(t):
        zc_ref[...] = jnp.dot(x_rows, yt_ref[:, t], preferred_element_type=F32)
        peak = max_down(zc_ref)
        m_ref[:, t] = peak
        total = jnp.zeros((2 * STEP, wide), F32)
        for r in range(0, n, 2 * STEP):
            value = jnp.exp2((zc_ref[r : r + 2 * STEP, :] - peak) * scale)
            total = total + value
            t_ref[r : r + 2 * STEP, t] = value.astype(BF16)
        total = jnp.sum(total, axis=0, keepdims=True)
        b2_ref[:, t] = scale * peak + jnp.log(total) * LOG2E

    if ny == wide:
        columns(slice(0, ny))
    else:

        @pl.loop(0, ny // wide)
        def _(t):
            columns(pl.ds(pl.multiple_of(t * wide, wide), wide))

    lse = to_lanes(b2_ref[...])
    for k in range(2 * rows):
        l_ref[k] = lse


def stack(out_ref, width, points, factor):
    moved = points.astype(F32) * factor
    high = moved.astype(BF16)
    out_ref[:width, :] = high
    out_ref[width : 2 * width, :] = (moved - high.astype(F32)).astype(BF16)
    one, two, three = pieces(factor)
    index = lax.broadcasted_iota(jnp.int32, (PAD, factor.shape[1]), 0)
    out_ref[2 * width :, :] = select(index, {0: one, 1: two, 2: three}).astype(BF16)


def unstack(product, width):
    ext = product[2 * width :]
    return product[:width] + product[width : 2 * width], (ext[0:1] + ext[1:2]) + ext[2:3]


def second_kernel(
    log_nx, log_ny, xa_ref, b_ref, l_ref, m_ref, yt_ref, t_ref,
    r_ref, v_ref, c_ref, xs_ref, sum_ref, send_ref,
):
    width = xa_ref.shape[0] - EXT
    ny = m_ref.shape[1]
    half = ny // 2
    kappa = kappa_of(width)
    scale = kappa * LOG2E
    l_all = l_ref[...]
    peak = jnp.max(l_all, axis=0)
    total = jnp.sum(jnp.exp2(l_all - peak[None]), axis=0)
    lse2 = from_lanes(peak + jnp.log(total) * LOG2E)
    old = yt_ref[width:, :].astype(F32)
    c_old = (old[0:1] + old[1:2]) + old[2:3]
    lb2 = (old[6:7] - log_ny) * LOG2E
    c_ref[...] = to_lanes(c_old + (lb2 - lse2) / scale)
    v = jnp.exp2(scale * m_ref[...] + (lb2 - lse2))
    v_ref[...] = v
    one, two, three = pieces(v)
    index = lax.broadcasted_iota(jnp.int32, (PAD, ny), 0)
    v_rows = select(index, {0: one, 1: two, 2: three}).astype(BF16)
    across = (((1,), (1,)), ((), ()))
    sums = lax.dot_general(v_rows, t_ref[...], across, preferred_element_type=F32)
    rowsum = (sums[0:1] + sums[1:2]) + sums[2:3]
    mass = xa_ref[width:, :].astype(F32)[7:8]
    r = jnp.exp(mass - log_nx) / rowsum
    r_ref[...] = r
    stack(xs_ref, width, xa_ref[:width, :], r)
    col = lax.axis_index("col")
    for k in range(half // TILE):
        t = pl.ds(pl.multiple_of((1 - col) * half + k * TILE, TILE), TILE)
        product = jnp.dot(xs_ref[...], t_ref[:, t], preferred_element_type=F32)
        moment, total = unstack(product, width)
        total = total * v_ref[:, t]
        sum_ref[:, t] = total
        part = yt_ref[:width, t].astype(F32) * total - moment * v_ref[:, t]
        send_ref[:width, k * TILE : (k + 1) * TILE] = part.astype(BF16)
        t = pl.ds(pl.multiple_of(col * half + k * TILE, TILE), TILE)
        ext = jnp.dot(xs_ref[2 * width :, :], t_ref[:, t], preferred_element_type=F32)
        sum_ref[:, t] = ((ext[0:1] + ext[1:2]) + ext[2:3]) * v_ref[:, t]
    sums = sum_ref[...]
    high = sums.astype(BF16).astype(F32)
    low = sums - high
    index = lax.broadcasted_iota(jnp.int32, (PAD, half), 0)
    ext = select(index, {0: high[:, :half], 1: high[:, half:], 2: low[:, :half], 3: low[:, half:]})
    send_ref[width:, :] = ext.astype(BF16)


def keep_kernel(xa_ref, xs_ref, v_ref, sum_ref, yt_ref, t_ref, keep_ref, norm_ref):
    width, half = keep_ref.shape
    col = lax.axis_index("col")
    for k in range(half // TILE):
        t = pl.ds(pl.multiple_of(col * half + k * TILE, TILE), TILE)
        product = jnp.dot(xs_ref[: 2 * width, :], t_ref[:, t], preferred_element_type=F32)
        moment = product[:width] + product[width:]
        part = yt_ref[:width, t].astype(F32) * sum_ref[:, t] - moment * v_ref[:, t]
        keep_ref[:, k * TILE : (k + 1) * TILE] = part
    xf = xa_ref[:width, :].astype(F32)
    norm_ref[...] = jnp.sum(xf * xf, axis=0, keepdims=True)


def add_kernel(keep_ref, sum_ref, got_ref, out_ref):
    width, half = keep_ref.shape
    rows = out_ref.shape[0]
    yd = half // rows
    base = yd * width // LANES
    ext = got_ref[width:, :].astype(F32)
    other = jnp.concatenate([ext[0:1] + ext[2:3], ext[1:2] + ext[3:4]], axis=1)
    sums = sums_out(to_lanes(sum_ref[...] + other)).astype(BF16)
    total = (keep_ref[...] + got_ref[:width, :].astype(F32)).T
    for r in range(rows):
        out_ref[r, :base, :] = pack(total[r * yd : (r + 1) * yd, :]).astype(BF16)
        out_ref[r, base:, :] = sums


def own_part(ref, yd):
    block = lax.axis_index("col") * lax.axis_size("row") + lax.axis_index("row")
    fit = LANES // yd
    row = ref[pl.ds(block // fit, 1), :]
    out = row[:, :yd]
    for k in range(1, fit):
        out = jnp.where(block % fit == k, row[:, k * yd : (k + 1) * yd], out)
    return out


def last_kernel(
    log_nx, log_ny, xa_ref, norm_ref, b_ref, r_ref, v_ref, c_ref, got_ref, yt_ref, t_ref, y_ref,
    f_hbm, pot_hbm, gx_hbm, gy_hbm, f_ref, pot_ref, gx_ref, gy_ref, ys_ref, sum_ref, sems,
):
    width, n = gx_ref.shape
    ny = v_ref.shape[1]
    yd = y_ref.shape[1]
    base = yd * width // LANES
    count = ny // LANES
    kappa = kappa_of(width)
    moves = []

    def leave(source, target):
        move = pltpu.make_async_copy(source, target, sems.at[len(moves)])
        move.start()
        moves.append(move)

    mass = xa_ref[width:, :].astype(F32)[7:8]
    log_row = mass - log_nx - jnp.log(r_ref[...])
    f_ref[...] = norm_ref[...] / width + EPSILON * (kappa * b_ref[...] - log_row)
    leave(f_ref, f_hbm)
    total = got_ref[0].astype(F32)
    for k in range(1, got_ref.shape[0]):
        total = total + got_ref[k].astype(F32)
    sums = total[base : base + count] + total[base + count : base + 2 * count]
    sum_ref[...] = sums
    colsum = own_part(sum_ref, yd)
    c_term = own_part(c_ref, yd)
    own = y_ref[0].astype(F32)
    gy_ref[...] = unpack(total[:base], yd, width) * (
        jnp.exp(own[:, width + 6 : width + 7]) * to_column(1.0 / colsum)
    )
    leave(gy_ref, gy_hbm)
    norm = to_row(jnp.sum(own[:, :width] * own[:, :width], axis=1, keepdims=True))
    pot_ref[...] = norm / width - EPSILON * (jnp.log(colsum) - kappa * c_term)
    leave(pot_ref, pot_hbm)
    mass = yt_ref[width:, :].astype(F32)[6:7]
    q = v_ref[...] * jnp.exp(mass + log_nx - jnp.log(from_lanes(sums)))
    stack(ys_ref, width, yt_ref[:width, :], q)
    across = (((1,), (1,)), ((), ()))
    for k in range(n // TILE):
        t = slice(k * TILE, (k + 1) * TILE)
        product = lax.dot_general(ys_ref[...], t_ref[t, :], across, preferred_element_type=F32)
        moved, weight = unstack(product, width)
        gx_ref[:, t] = (xa_ref[:width, t].astype(F32) * weight - moved) * (r_ref[:, t] * (1.0 / ny))
        leave(gx_ref.at[:, t], gx_hbm.at[:, t])
    for move in moves:
        move.wait()


def call(kernel, outs, scratch, limit, *args, space=pltpu.VMEM, out_space=pltpu.VMEM, cost=None):
    return pl.pallas_call(
        kernel,
        out_shape=outs,
        in_specs=[pl.BlockSpec(memory_space=space)] * len(args),
        out_specs=jax.tree.map(lambda _: pl.BlockSpec(memory_space=out_space), outs),
        scratch_shapes=scratch,
        cost_estimate=cost,
        compiler_params=pltpu.CompilerParams(vmem_limit_bytes=limit),
    )(*args)


def shape(dims, dtype=F32):
    return jax.ShapeDtypeStruct(dims, dtype)


def swap(value):
    return lax.ppermute(value, "col", [(0, 1), (1, 0)])


def on_device(points_x, points_y, mass_x, mass_y):
    n, width = points_x.shape
    yd = points_y.shape[0]
    rows = lax.axis_size("row")
    ny = 2 * rows * yd
    half = ny // 2
    count = ny // LANES
    log_nx, log_ny = math.log(n * 2 * rows), math.log(ny)
    depth = width + EXT
    limit = (20 if ny <= 1024 else 56) * 1024 * 1024
    extra = sums_rows(ny)
    run = functools.partial
    vmem = pltpu.VMEM
    ones = call(
        ones_kernel, shape((yd, EXT)), [], limit,
        cost=pl.CostEstimate(flops=4 * 10**9, bytes_accessed=10000, transcendentals=0),
    )
    y_own = call(
        run(prep_kernel, log_ny), shape((rows, yd, depth), BF16), [], limit, points_y, mass_y.reshape(1, yd), ones,
        cost=pl.CostEstimate(flops=4 * 10**9, bytes_accessed=400000, transcendentals=0),
    )
    y_mine = lax.all_to_all(y_own, "row", 0, 0, tiled=True)
    y_other = swap(y_mine)
    xa, x_rows, yt_mine, peak, total = call(
        half_kernel,
        (
            shape((depth, n), BF16), shape((n, depth), BF16), shape((depth, half), BF16), shape((1, n)),
            shape((1, n)),
        ),
        [vmem((half, n), F32)],
        limit, points_x.T, mass_x.reshape(n // LANES, LANES), y_mine,
    )
    yt, b_term, lse, peak, plan = call(
        run(first_kernel, log_nx),
        (
            shape((depth, ny), BF16), shape((1, n)), shape((2 * rows, count, LANES)), shape((1, ny)),
            shape((n, ny), BF16),
        ),
        [vmem((half, n), F32), vmem((n, min(WIDE, ny)), F32), vmem((1, ny), F32)],
        limit, xa, x_rows, yt_mine, y_other, peak, total,
    )
    lse = lax.all_to_all(lse, AXES, 0, 0, tiled=True)
    r, v, c_term, xs, sums, send = call(
        run(second_kernel, log_nx, log_ny),
        (
            shape((1, n)), shape((1, ny)), shape((count, LANES)), shape((2 * width + PAD, n), BF16),
            shape((1, ny)), shape((width + PAD, half), BF16),
        ),
        [], limit, xa, b_term, lse, peak, yt, plan,
    )
    got = swap(send)
    keep, norm = call(
        keep_kernel, (shape((width, half)), shape((1, n))), [], limit, xa, xs, v, sums, yt, plan
    )
    part = call(
        add_kernel, shape((rows, yd * width // LANES + extra, LANES), BF16), [], limit, keep, sums, got
    )
    part = lax.all_to_all(part, "row", 0, 0, tiled=True)
    f_pot, g_pot, grad_xt, grad_y = call(
        run(last_kernel, log_nx, log_ny),
        (shape((1, n)), shape((1, yd)), shape((width, n)), shape((yd, width))),
        [
            vmem((1, n), F32), vmem((1, yd), F32), vmem((width, n), F32), vmem((yd, width), F32),
            vmem((2 * width + PAD, ny), BF16), vmem((count, LANES), F32),
            pltpu.SemaphoreType.DMA((3 + n // TILE,)),
        ],
        limit, xa, norm, b_term, r, v, c_term, part, yt, plan, y_own, out_space=pl.ANY,
    )
    return f_pot.reshape(n), g_pot.reshape(yd), grad_xt.T, grad_y


def solution(mesh):
    in_specs = (
        P(("groups", "row", "col"), None),
        P(("groups", "col", "row"), None),
        P(("groups", "row", "col")),
        P(("groups", "col", "row")),
    )
    out_specs = (
        P(("groups", "row", "col")),
        P(("groups", "col", "row")),
        P(("groups", "row", "col"), None),
        P(("groups", "col", "row"), None),
    )
    return jax.shard_map(
        on_device, mesh=mesh, in_specs=in_specs, out_specs=out_specs, check_vma=False
    )
```

```python
import functools
import math

import jax
import jax.numpy as jnp
from jax import lax
from jax.experimental import pallas as pl
from jax.experimental.pallas import tpu as pltpu
from jax.sharding import PartitionSpec as P

ITERS = 2
EPSILON = 0.02
LOG2E = math.log2(math.e)
TILE = 256
STEP = 32
EXT = 32
PAD = 16
LANES = 128
AXES = ("row", "col")
F32 = jnp.float32
BF16 = jnp.bfloat16


def kappa_of(width):
    return 2.0 / (width * EPSILON)


def pieces(value):
    high = value.astype(BF16).astype(F32)
    rest = value - high
    mid = rest.astype(BF16).astype(F32)
    return high, mid, rest - mid


def select(index, values):
    out = jnp.zeros(index.shape, F32)
    for k, value in values.items():
        out = jnp.where(index == k, value, out)
    return out


def extras_x(index, b_term, mass):
    high, mid, low = pieces(b_term)
    return select(index, {0: 1.0, 1: 1.0, 2: 1.0, 3: high, 4: mid, 5: low, 7: mass})


def rows_index(columns):
    return lax.broadcasted_iota(jnp.int32, (EXT, columns), 0)


def to_column(row):
    size = row.shape[1]
    eye = lax.broadcasted_iota(jnp.int32, (size, size), 0) == lax.broadcasted_iota(jnp.int32, (size, size), 1)
    return jnp.sum(jnp.where(eye, row, 0.0), axis=1, keepdims=True)


def to_row(column):
    size = column.shape[0]
    eye = lax.broadcasted_iota(jnp.int32, (size, size), 0) == lax.broadcasted_iota(jnp.int32, (size, size), 1)
    return jnp.sum(jnp.where(eye, column, 0.0), axis=0, keepdims=True)


def for_tiles(total, product, z_ref, use):
    count = total // TILE
    slots = z_ref.shape[0]
    if count <= slots:
        for t in range(count + 1):
            if t < count:
                z_ref[t] = product(pl.ds(t * TILE, TILE))
            if t > 0:
                use(pl.ds((t - 1) * TILE, TILE), z_ref.at[t - 1])
    else:

        @pl.loop(0, count)
        def _(t):
            tile = pl.ds(pl.multiple_of(t * TILE, TILE), TILE)
            z_ref[0] = product(tile)
            use(tile, z_ref.at[0])


def max_down(z_ref):
    peak = z_ref[0:STEP, :]
    for r in range(STEP, z_ref.shape[0], STEP):
        peak = jnp.maximum(peak, z_ref[r : r + STEP, :])
    return jnp.max(peak, axis=0, keepdims=True)


def exp_sum_down(z_ref, scale, shift, keep=None):
    total = jnp.zeros((STEP, TILE), F32)
    for r in range(0, z_ref.shape[0], STEP):
        value = jnp.exp2((z_ref[r : r + STEP, :] - shift) * scale)
        total = total + value
        if keep is not None:
            keep(r, value.astype(BF16))
    return jnp.sum(total, axis=0, keepdims=True)


def to_lanes(row):
    return jnp.concatenate([row[:, k : k + LANES] for k in range(0, row.shape[1], LANES)], axis=0)


def from_lanes(block):
    return jnp.concatenate([block[k : k + 1] for k in range(block.shape[0])], axis=1)


def sums_rows(ny):
    return -(-2 * ny // LANES // 16) * 16


def sums_out(sums):
    high = sums.astype(BF16).astype(F32)
    spare = sums_rows(sums.size) - 2 * sums.shape[0]
    return jnp.concatenate([high, sums - high] + [jnp.zeros((spare, LANES), F32)] * (spare > 0), axis=0)


def pack(block):
    rows, width = block.shape
    base = rows * width // LANES
    spare = LANES - width
    side = [block[base:, k : k + spare] for k in range(0, width, spare)]
    return jnp.concatenate([block[:base], jnp.concatenate(side, axis=0)], axis=1)


def unpack(block, rows, width):
    base = block.shape[0]
    rest = rows - base
    side = [block[k : k + rest, width:] for k in range(0, base, rest)]
    return jnp.concatenate([block[:, :width], jnp.concatenate(side, axis=1)], axis=0)


def ones_kernel(ext_ref):
    index = lax.broadcasted_iota(jnp.int32, ext_ref.shape, 1)
    ext_ref[...] = select(index, {3: 1.0, 4: 1.0, 5: 1.0})


def prep_kernel(log_ny, y_ref, my_ref, ones_ref, ya_ref):
    width = y_ref.shape[1]
    y = y_ref[...]
    yf = y.astype(F32)
    norm = jnp.sum(yf * yf, axis=1, keepdims=True)
    mass = to_column(my_ref[...].astype(F32))
    c_term = (mass - log_ny) / kappa_of(width) - 0.5 * norm
    high, mid, low = pieces(c_term)
    index = lax.broadcasted_iota(jnp.int32, ones_ref.shape, 1)
    ext = (ones_ref[...] + select(index, {0: high, 1: mid, 2: low, 6: mass})).astype(BF16)
    for k in range(ya_ref.shape[0]):
        ya_ref[k, :, :width] = y
        ya_ref[k, :, width:] = ext


def half_kernel(xt_ref, mx_ref, mine_ref, xa_ref, rows_ref, yt_ref, peak_ref, total_ref, z_ref):
    rows, yd, depth = mine_ref.shape
    width, n = xt_ref.shape
    half = rows * yd
    scale = kappa_of(width) * LOG2E
    mass = from_lanes(mx_ref[...].astype(F32))
    xa_ref[:width, :] = xt_ref[...]
    xa_ref[width:, :] = extras_x(rows_index(n), jnp.zeros((1, n), F32), mass).astype(BF16)
    mine = mine_ref[...].reshape(half, depth)

    def product(t):
        return jnp.dot(mine, xa_ref[:, t], preferred_element_type=F32)

    def use(t, z):
        peak = max_down(z)
        peak_ref[:, t] = peak
        total_ref[:, t] = exp_sum_down(z, scale, peak)

    for_tiles(n, product, z_ref, use)
    rows_ref[...] = xa_ref[...].T
    yt_ref[...] = mine.T


def first_kernel(
    log_nx, xa0_ref, rows0_ref, mine_ref, other_ref, peak_ref, total_ref,
    yt_ref, b_ref, l_ref, m_ref, t_ref, z_ref, zc_ref, b2_ref,
):
    rows, yd, depth = other_ref.shape
    n = xa0_ref.shape[1]
    width = depth - EXT
    half = rows * yd
    ny = 2 * half
    col = lax.axis_index("col")
    scale = kappa_of(width) * LOG2E
    other = other_ref[...].reshape(half, depth)
    yt_ref[:, pl.ds(pl.multiple_of(col * half, half), half)] = mine_ref[...]
    yt_ref[:, pl.ds(pl.multiple_of((1 - col) * half, half), half)] = other.T

    def product(t):
        return jnp.dot(other, xa0_ref[:, t], preferred_element_type=F32)

    def use(t, z):
        old = peak_ref[:, t]
        peak = jnp.maximum(max_down(z), old)
        total = exp_sum_down(z, scale, peak) + total_ref[:, t] * jnp.exp2((old - peak) * scale)
        b_ref[:, t] = -peak - jnp.log(total) * (LOG2E / scale)

    for_tiles(n, product, z_ref, use)
    mass = xa0_ref[width:, :].astype(F32)[7:8]
    b_term = b_ref[...] + (mass - log_nx) * (LOG2E / scale)
    b_ref[...] = b_term
    ext = extras_x(rows_index(n), b_term, mass).T.astype(BF16)
    x_rows = jnp.concatenate([rows0_ref[:, :width], ext], axis=1)

    def product(t):
        return jnp.dot(x_rows, yt_ref[:, t], preferred_element_type=F32)

    def use(t, z):
        def keep(r, value):
            t_ref[r : r + STEP, t] = value

        peak = max_down(z)
        m_ref[:, t] = peak
        b2_ref[:, t] = scale * peak + jnp.log(exp_sum_down(z, scale, peak, keep)) * LOG2E

    for_tiles(ny, product, zc_ref, use)
    lse = to_lanes(b2_ref[...])
    for k in range(2 * rows):
        l_ref[k] = lse


def stack(out_ref, width, points, factor):
    moved = points.astype(F32) * factor
    high = moved.astype(BF16)
    out_ref[:width, :] = high
    out_ref[width : 2 * width, :] = (moved - high.astype(F32)).astype(BF16)
    one, two, three = pieces(factor)
    index = lax.broadcasted_iota(jnp.int32, (PAD, factor.shape[1]), 0)
    out_ref[2 * width :, :] = select(index, {0: one, 1: two, 2: three}).astype(BF16)


def unstack(product, width):
    ext = product[2 * width :]
    return product[:width] + product[width : 2 * width], (ext[0:1] + ext[1:2]) + ext[2:3]


def second_kernel(
    log_nx, log_ny, xa_ref, b_ref, l_ref, m_ref, yt_ref, t_ref,
    r_ref, v_ref, c_ref, xs_ref, sum_ref, send_ref,
):
    width = xa_ref.shape[0] - EXT
    ny = m_ref.shape[1]
    half = ny // 2
    kappa = kappa_of(width)
    scale = kappa * LOG2E
    l_all = l_ref[...]
    peak = jnp.max(l_all, axis=0)
    total = jnp.sum(jnp.exp2(l_all - peak[None]), axis=0)
    lse2 = from_lanes(peak + jnp.log(total) * LOG2E)
    old = yt_ref[width:, :].astype(F32)
    c_old = (old[0:1] + old[1:2]) + old[2:3]
    lb2 = (old[6:7] - log_ny) * LOG2E
    c_ref[...] = to_lanes(c_old + (lb2 - lse2) / scale)
    v = jnp.exp2(scale * m_ref[...] + (lb2 - lse2))
    v_ref[...] = v
    one, two, three = pieces(v)
    index = lax.broadcasted_iota(jnp.int32, (PAD, ny), 0)
    v_rows = select(index, {0: one, 1: two, 2: three}).astype(BF16)
    across = (((1,), (1,)), ((), ()))
    sums = lax.dot_general(v_rows, t_ref[...], across, preferred_element_type=F32)
    rowsum = (sums[0:1] + sums[1:2]) + sums[2:3]
    mass = xa_ref[width:, :].astype(F32)[7:8]
    r = jnp.exp(mass - log_nx) / rowsum
    r_ref[...] = r
    stack(xs_ref, width, xa_ref[:width, :], r)
    col = lax.axis_index("col")
    for k in range(half // TILE):
        t = pl.ds(pl.multiple_of((1 - col) * half + k * TILE, TILE), TILE)
        product = jnp.dot(xs_ref[...], t_ref[:, t], preferred_element_type=F32)
        moment, total = unstack(product, width)
        total = total * v_ref[:, t]
        sum_ref[:, t] = total
        part = yt_ref[:width, t].astype(F32) * total - moment * v_ref[:, t]
        send_ref[:width, k * TILE : (k + 1) * TILE] = part.astype(BF16)
        t = pl.ds(pl.multiple_of(col * half + k * TILE, TILE), TILE)
        ext = jnp.dot(xs_ref[2 * width :, :], t_ref[:, t], preferred_element_type=F32)
        sum_ref[:, t] = ((ext[0:1] + ext[1:2]) + ext[2:3]) * v_ref[:, t]
    sums = sum_ref[...]
    high = sums.astype(BF16).astype(F32)
    low = sums - high
    index = lax.broadcasted_iota(jnp.int32, (PAD, half), 0)
    ext = select(index, {0: high[:, :half], 1: high[:, half:], 2: low[:, :half], 3: low[:, half:]})
    send_ref[width:, :] = ext.astype(BF16)


def keep_kernel(xa_ref, xs_ref, v_ref, sum_ref, yt_ref, t_ref, keep_ref, norm_ref):
    width, half = keep_ref.shape
    col = lax.axis_index("col")
    for k in range(half // TILE):
        t = pl.ds(pl.multiple_of(col * half + k * TILE, TILE), TILE)
        product = jnp.dot(xs_ref[: 2 * width, :], t_ref[:, t], preferred_element_type=F32)
        moment = product[:width] + product[width:]
        part = yt_ref[:width, t].astype(F32) * sum_ref[:, t] - moment * v_ref[:, t]
        keep_ref[:, k * TILE : (k + 1) * TILE] = part
    xf = xa_ref[:width, :].astype(F32)
    norm_ref[...] = jnp.sum(xf * xf, axis=0, keepdims=True)


def add_kernel(keep_ref, sum_ref, got_ref, out_ref):
    width, half = keep_ref.shape
    rows = out_ref.shape[0]
    yd = half // rows
    base = yd * width // LANES
    ext = got_ref[width:, :].astype(F32)
    other = jnp.concatenate([ext[0:1] + ext[2:3], ext[1:2] + ext[3:4]], axis=1)
    sums = sums_out(to_lanes(sum_ref[...] + other)).astype(BF16)
    total = (keep_ref[...] + got_ref[:width, :].astype(F32)).T
    for r in range(rows):
        out_ref[r, :base, :] = pack(total[r * yd : (r + 1) * yd, :]).astype(BF16)
        out_ref[r, base:, :] = sums


def own_part(ref, yd):
    block = lax.axis_index("col") * lax.axis_size("row") + lax.axis_index("row")
    fit = LANES // yd
    row = ref[pl.ds(block // fit, 1), :]
    out = row[:, :yd]
    for k in range(1, fit):
        out = jnp.where(block % fit == k, row[:, k * yd : (k + 1) * yd], out)
    return out


def last_kernel(
    log_nx, log_ny, xa_ref, norm_ref, b_ref, r_ref, v_ref, c_ref, got_ref, yt_ref, t_ref, y_ref,
    f_hbm, pot_hbm, gx_hbm, gy_hbm, f_ref, pot_ref, gx_ref, gy_ref, ys_ref, sum_ref, sems,
):
    width, n = gx_ref.shape
    ny = v_ref.shape[1]
    yd = y_ref.shape[1]
    base = yd * width // LANES
    count = ny // LANES
    kappa = kappa_of(width)
    moves = []

    def leave(source, target):
        move = pltpu.make_async_copy(source, target, sems.at[len(moves)])
        move.start()
        moves.append(move)

    mass = xa_ref[width:, :].astype(F32)[7:8]
    log_row = mass - log_nx - jnp.log(r_ref[...])
    f_ref[...] = norm_ref[...] / width + EPSILON * (kappa * b_ref[...] - log_row)
    leave(f_ref, f_hbm)
    total = got_ref[0].astype(F32)
    for k in range(1, got_ref.shape[0]):
        total = total + got_ref[k].astype(F32)
    sums = total[base : base + count] + total[base + count : base + 2 * count]
    sum_ref[...] = sums
    colsum = own_part(sum_ref, yd)
    c_term = own_part(c_ref, yd)
    own = y_ref[0].astype(F32)
    gy_ref[...] = unpack(total[:base], yd, width) * (
        jnp.exp(own[:, width + 6 : width + 7]) * to_column(1.0 / colsum)
    )
    leave(gy_ref, gy_hbm)
    norm = to_row(jnp.sum(own[:, :width] * own[:, :width], axis=1, keepdims=True))
    pot_ref[...] = norm / width - EPSILON * (jnp.log(colsum) - kappa * c_term)
    leave(pot_ref, pot_hbm)
    mass = yt_ref[width:, :].astype(F32)[6:7]
    q = v_ref[...] * jnp.exp(mass + log_nx - jnp.log(from_lanes(sums)))
    stack(ys_ref, width, yt_ref[:width, :], q)
    across = (((1,), (1,)), ((), ()))
    for k in range(n // TILE):
        t = slice(k * TILE, (k + 1) * TILE)
        product = lax.dot_general(ys_ref[...], t_ref[t, :], across, preferred_element_type=F32)
        moved, weight = unstack(product, width)
        gx_ref[:, t] = (xa_ref[:width, t].astype(F32) * weight - moved) * (r_ref[:, t] * (1.0 / ny))
        leave(gx_ref.at[:, t], gx_hbm.at[:, t])
    for move in moves:
        move.wait()


def call(kernel, outs, scratch, limit, *args, space=pltpu.VMEM, out_space=pltpu.VMEM, cost=None):
    return pl.pallas_call(
        kernel,
        out_shape=outs,
        in_specs=[pl.BlockSpec(memory_space=space)] * len(args),
        out_specs=jax.tree.map(lambda _: pl.BlockSpec(memory_space=out_space), outs),
        scratch_shapes=scratch,
        cost_estimate=cost,
        compiler_params=pltpu.CompilerParams(vmem_limit_bytes=limit),
    )(*args)


def shape(dims, dtype=F32):
    return jax.ShapeDtypeStruct(dims, dtype)


def swap(value):
    return lax.ppermute(value, "col", [(0, 1), (1, 0)])


def on_device(points_x, points_y, mass_x, mass_y):
    n, width = points_x.shape
    yd = points_y.shape[0]
    rows = lax.axis_size("row")
    ny = 2 * rows * yd
    half = ny // 2
    count = ny // LANES
    log_nx, log_ny = math.log(n * 2 * rows), math.log(ny)
    depth = width + EXT
    limit = (20 if ny <= 1024 else 56) * 1024 * 1024
    extra = sums_rows(ny)
    run = functools.partial
    vmem = pltpu.VMEM
    slots = 4 if ny <= 1024 else 1
    ones = call(
        ones_kernel, shape((yd, EXT)), [], limit,
        cost=pl.CostEstimate(flops=4 * 10**9, bytes_accessed=10000, transcendentals=0),
    )
    y_own = call(
        run(prep_kernel, log_ny), shape((rows, yd, depth), BF16), [], limit, points_y, mass_y.reshape(1, yd), ones,
        cost=pl.CostEstimate(flops=4 * 10**9, bytes_accessed=400000, transcendentals=0),
    )
    y_mine = lax.all_to_all(y_own, "row", 0, 0, tiled=True)
    y_other = swap(y_mine)
    xa, x_rows, yt_mine, peak, total = call(
        half_kernel,
        (
            shape((depth, n), BF16), shape((n, depth), BF16), shape((depth, half), BF16), shape((1, n)),
            shape((1, n)),
        ),
        [vmem((slots, half, TILE), F32)],
        limit, points_x.T, mass_x.reshape(n // LANES, LANES), y_mine,
    )
    yt, b_term, lse, peak, plan = call(
        run(first_kernel, log_nx),
        (
            shape((depth, ny), BF16), shape((1, n)), shape((2 * rows, count, LANES)), shape((1, ny)),
            shape((n, ny), BF16),
        ),
        [vmem((slots, half, TILE), F32), vmem((slots, n, TILE), F32), vmem((1, ny), F32)],
        limit, xa, x_rows, yt_mine, y_other, peak, total,
    )
    lse = lax.all_to_all(lse, AXES, 0, 0, tiled=True)
    r, v, c_term, xs, sums, send = call(
        run(second_kernel, log_nx, log_ny),
        (
            shape((1, n)), shape((1, ny)), shape((count, LANES)), shape((2 * width + PAD, n), BF16),
            shape((1, ny)), shape((width + PAD, half), BF16),
        ),
        [], limit, xa, b_term, lse, peak, yt, plan,
    )
    got = swap(send)
    keep, norm = call(
        keep_kernel, (shape((width, half)), shape((1, n))), [], limit, xa, xs, v, sums, yt, plan
    )
    part = call(
        add_kernel, shape((rows, yd * width // LANES + extra, LANES), BF16), [], limit, keep, sums, got
    )
    part = lax.all_to_all(part, "row", 0, 0, tiled=True)
    f_pot, g_pot, grad_xt, grad_y = call(
        run(last_kernel, log_nx, log_ny),
        (shape((1, n)), shape((1, yd)), shape((width, n)), shape((yd, width))),
        [
            vmem((1, n), F32), vmem((1, yd), F32), vmem((width, n), F32), vmem((yd, width), F32),
            vmem((2 * width + PAD, ny), BF16), vmem((count, LANES), F32),
            pltpu.SemaphoreType.DMA((3 + n // TILE,)),
        ],
        limit, xa, norm, b_term, r, v, c_term, part, yt, plan, y_own, out_space=pl.ANY,
    )
    return f_pot.reshape(n), g_pot.reshape(yd), grad_xt.T, grad_y


def solution(mesh):
    in_specs = (
        P(("groups", "row", "col"), None),
        P(("groups", "col", "row"), None),
        P(("groups", "row", "col")),
        P(("groups", "col", "row")),
    )
    out_specs = (
        P(("groups", "row", "col")),
        P(("groups", "col", "row")),
        P(("groups", "row", "col"), None),
        P(("groups", "col", "row"), None),
    )
    return jax.shard_map(
        on_device, mesh=mesh, in_specs=in_specs, out_specs=out_specs, check_vma=False
    )
```

```python
import functools
import math

import jax
import jax.numpy as jnp
from jax import lax
from jax.experimental import pallas as pl
from jax.experimental.pallas import tpu as pltpu
from jax.sharding import PartitionSpec as P

ITERS = 2
EPSILON = 0.02
LOG2E = math.log2(math.e)
TILE = 256
EXT = 32
PAD = 16
LANES = 128
AXES = ("row", "col")
F32 = jnp.float32
BF16 = jnp.bfloat16


def kappa_of(width):
    return 2.0 / (width * EPSILON)


def pieces(value):
    high = value.astype(BF16).astype(F32)
    rest = value - high
    mid = rest.astype(BF16).astype(F32)
    return high, mid, rest - mid


def select(index, values):
    out = jnp.zeros(index.shape, F32)
    for k, value in values.items():
        out = jnp.where(index == k, value, out)
    return out


def extras_x(index, b_term, mass):
    high, mid, low = pieces(b_term)
    return select(index, {0: 1.0, 1: 1.0, 2: 1.0, 3: high, 4: mid, 5: low, 7: mass})


def rows_index(columns):
    return lax.broadcasted_iota(jnp.int32, (EXT, columns), 0)


def to_column(row):
    size = row.shape[1]
    eye = lax.broadcasted_iota(jnp.int32, (size, size), 0) == lax.broadcasted_iota(jnp.int32, (size, size), 1)
    return jnp.sum(jnp.where(eye, row, 0.0), axis=1, keepdims=True)


def to_row(column):
    size = column.shape[0]
    eye = lax.broadcasted_iota(jnp.int32, (size, size), 0) == lax.broadcasted_iota(jnp.int32, (size, size), 1)
    return jnp.sum(jnp.where(eye, column, 0.0), axis=0, keepdims=True)


def for_tiles(total, body):
    count = total // TILE
    if count <= 4:
        for t in range(count):
            body(pl.ds(t * TILE, TILE))
    else:

        @pl.loop(0, count)
        def _(t):
            body(pl.ds(pl.multiple_of(t * TILE, TILE), TILE))


def to_lanes(row):
    return jnp.concatenate([row[:, k : k + LANES] for k in range(0, row.shape[1], LANES)], axis=0)


def from_lanes(block):
    return jnp.concatenate([block[k : k + 1] for k in range(block.shape[0])], axis=1)


def sums_rows(ny):
    return -(-2 * ny // LANES // 16) * 16


def sums_out(sums):
    high = sums.astype(BF16).astype(F32)
    spare = sums_rows(sums.size) - 2 * sums.shape[0]
    return jnp.concatenate([high, sums - high] + [jnp.zeros((spare, LANES), F32)] * (spare > 0), axis=0)


def pack(block):
    rows, width = block.shape
    base = rows * width // LANES
    spare = LANES - width
    side = [block[base:, k : k + spare] for k in range(0, width, spare)]
    return jnp.concatenate([block[:base], jnp.concatenate(side, axis=0)], axis=1)


def unpack(block, rows, width):
    base = block.shape[0]
    rest = rows - base
    side = [block[k : k + rest, width:] for k in range(0, base, rest)]
    return jnp.concatenate([block[:, :width], jnp.concatenate(side, axis=1)], axis=0)


def ones_kernel(ext_ref):
    index = lax.broadcasted_iota(jnp.int32, ext_ref.shape, 1)
    ext_ref[...] = select(index, {3: 1.0, 4: 1.0, 5: 1.0})


def prep_kernel(log_ny, y_ref, my_ref, ones_ref, ya_ref):
    width = y_ref.shape[1]
    y = y_ref[...]
    yf = y.astype(F32)
    norm = jnp.sum(yf * yf, axis=1, keepdims=True)
    mass = to_column(my_ref[...].astype(F32))
    c_term = (mass - log_ny) / kappa_of(width) - 0.5 * norm
    high, mid, low = pieces(c_term)
    index = lax.broadcasted_iota(jnp.int32, ones_ref.shape, 1)
    ext = (ones_ref[...] + select(index, {0: high, 1: mid, 2: low, 6: mass})).astype(BF16)
    for k in range(ya_ref.shape[0]):
        ya_ref[k, :, :width] = y
        ya_ref[k, :, width:] = ext


def half_kernel(xt_ref, mx_ref, mine_ref, xa_ref, yt_ref, peak_ref, total_ref):
    rows, yd, depth = mine_ref.shape
    width, n = xt_ref.shape
    half = rows * yd
    scale = kappa_of(width) * LOG2E
    mass = from_lanes(mx_ref[...].astype(F32))
    xa_ref[:width, :] = xt_ref[...]
    xa_ref[width:, :] = extras_x(rows_index(n), jnp.zeros((1, n), F32), mass).astype(BF16)
    mine = mine_ref[...].reshape(half, depth)

    def row_tile(t):
        z = jnp.dot(mine, xa_ref[:, t], preferred_element_type=F32)
        peak = jnp.max(z, axis=0, keepdims=True)
        peak_ref[:, t] = peak
        total_ref[:, t] = jnp.sum(jnp.exp2((z - peak) * scale), axis=0, keepdims=True)

    for_tiles(n, row_tile)
    yt_ref[...] = mine.T


def first_kernel(
    log_nx, xa0_ref, mine_ref, other_ref, peak_ref, total_ref,
    yt_ref, b_ref, l_ref, m_ref, t_ref, xa_ref, b2_ref,
):
    rows, yd, depth = other_ref.shape
    n = xa0_ref.shape[1]
    width = depth - EXT
    half = rows * yd
    ny = 2 * half
    col = lax.axis_index("col")
    scale = kappa_of(width) * LOG2E
    other = other_ref[...].reshape(half, depth)
    yt_ref[:, pl.ds(pl.multiple_of(col * half, half), half)] = mine_ref[...]
    yt_ref[:, pl.ds(pl.multiple_of((1 - col) * half, half), half)] = other.T

    def row_tile(t):
        z = jnp.dot(other, xa0_ref[:, t], preferred_element_type=F32)
        old = peak_ref[:, t]
        peak = jnp.maximum(jnp.max(z, axis=0, keepdims=True), old)
        total = jnp.sum(jnp.exp2((z - peak) * scale), axis=0, keepdims=True)
        total = total + total_ref[:, t] * jnp.exp2((old - peak) * scale)
        b_ref[:, t] = -peak - jnp.log(total) * (LOG2E / scale)

    for_tiles(n, row_tile)
    mass = xa0_ref[width:, :].astype(F32)[7:8]
    b_term = b_ref[...] + (mass - log_nx) * (LOG2E / scale)
    b_ref[...] = b_term
    xa_ref[:width, :] = xa0_ref[:width, :]
    xa_ref[width:, :] = extras_x(rows_index(n), b_term, mass).astype(BF16)
    x_rows = xa_ref[...].T

    def col_tile(t):
        z = jnp.dot(x_rows, yt_ref[:, t], preferred_element_type=F32)
        peak = jnp.max(z, axis=0, keepdims=True)
        m_ref[:, t] = peak
        value = jnp.exp2((z - peak) * scale)
        t_ref[:, t] = value.astype(BF16)
        b2_ref[:, t] = scale * peak + jnp.log(jnp.sum(value, axis=0, keepdims=True)) * LOG2E

    for_tiles(ny, col_tile)
    lse = to_lanes(b2_ref[...])
    for k in range(2 * rows):
        l_ref[k] = lse


def stack(out_ref, width, points, factor):
    moved = points.astype(F32) * factor
    high = moved.astype(BF16)
    out_ref[:width, :] = high
    out_ref[width : 2 * width, :] = (moved - high.astype(F32)).astype(BF16)
    one, two, three = pieces(factor)
    index = lax.broadcasted_iota(jnp.int32, (PAD, factor.shape[1]), 0)
    out_ref[2 * width :, :] = select(index, {0: one, 1: two, 2: three}).astype(BF16)


def unstack(product, width):
    ext = product[2 * width :]
    return product[:width] + product[width : 2 * width], (ext[0:1] + ext[1:2]) + ext[2:3]


def second_kernel(
    log_nx, log_ny, xa_ref, b_ref, l_ref, m_ref, yt_ref, t_ref,
    r_ref, v_ref, c_ref, xs_ref, sum_ref, send_ref,
):
    width = xa_ref.shape[0] - EXT
    ny = m_ref.shape[1]
    half = ny // 2
    kappa = kappa_of(width)
    scale = kappa * LOG2E
    l_all = l_ref[...]
    peak = jnp.max(l_all, axis=0)
    total = jnp.sum(jnp.exp2(l_all - peak[None]), axis=0)
    lse2 = from_lanes(peak + jnp.log(total) * LOG2E)
    old = yt_ref[width:, :].astype(F32)
    c_old = (old[0:1] + old[1:2]) + old[2:3]
    lb2 = (old[6:7] - log_ny) * LOG2E
    c_ref[...] = to_lanes(c_old + (lb2 - lse2) / scale)
    v = jnp.exp2(scale * m_ref[...] + (lb2 - lse2))
    v_ref[...] = v
    one, two, three = pieces(v)
    index = lax.broadcasted_iota(jnp.int32, (PAD, ny), 0)
    v_rows = select(index, {0: one, 1: two, 2: three}).astype(BF16)
    across = (((1,), (1,)), ((), ()))
    sums = lax.dot_general(v_rows, t_ref[...], across, preferred_element_type=F32)
    rowsum = (sums[0:1] + sums[1:2]) + sums[2:3]
    mass = xa_ref[width:, :].astype(F32)[7:8]
    r = jnp.exp(mass - log_nx) / rowsum
    r_ref[...] = r
    stack(xs_ref, width, xa_ref[:width, :], r)
    col = lax.axis_index("col")
    for k in range(half // TILE):
        t = pl.ds(pl.multiple_of((1 - col) * half + k * TILE, TILE), TILE)
        product = jnp.dot(xs_ref[...], t_ref[:, t], preferred_element_type=F32)
        moment, total = unstack(product, width)
        total = total * v_ref[:, t]
        sum_ref[:, t] = total
        part = yt_ref[:width, t].astype(F32) * total - moment * v_ref[:, t]
        send_ref[:width, k * TILE : (k + 1) * TILE] = part.astype(BF16)
        t = pl.ds(pl.multiple_of(col * half + k * TILE, TILE), TILE)
        ext = jnp.dot(xs_ref[2 * width :, :], t_ref[:, t], preferred_element_type=F32)
        sum_ref[:, t] = ((ext[0:1] + ext[1:2]) + ext[2:3]) * v_ref[:, t]
    sums = sum_ref[...]
    high = sums.astype(BF16).astype(F32)
    low = sums - high
    index = lax.broadcasted_iota(jnp.int32, (PAD, half), 0)
    ext = select(index, {0: high[:, :half], 1: high[:, half:], 2: low[:, :half], 3: low[:, half:]})
    send_ref[width:, :] = ext.astype(BF16)


def keep_kernel(xa_ref, xs_ref, v_ref, sum_ref, yt_ref, t_ref, keep_ref, norm_ref):
    width, half = keep_ref.shape
    col = lax.axis_index("col")
    for k in range(half // TILE):
        t = pl.ds(pl.multiple_of(col * half + k * TILE, TILE), TILE)
        product = jnp.dot(xs_ref[: 2 * width, :], t_ref[:, t], preferred_element_type=F32)
        moment = product[:width] + product[width:]
        part = yt_ref[:width, t].astype(F32) * sum_ref[:, t] - moment * v_ref[:, t]
        keep_ref[:, k * TILE : (k + 1) * TILE] = part
    xf = xa_ref[:width, :].astype(F32)
    norm_ref[...] = jnp.sum(xf * xf, axis=0, keepdims=True)


def add_kernel(keep_ref, sum_ref, got_ref, out_ref):
    width, half = keep_ref.shape
    rows = out_ref.shape[0]
    yd = half // rows
    base = yd * width // LANES
    ext = got_ref[width:, :].astype(F32)
    other = jnp.concatenate([ext[0:1] + ext[2:3], ext[1:2] + ext[3:4]], axis=1)
    sums = sums_out(to_lanes(sum_ref[...] + other)).astype(BF16)
    total = (keep_ref[...] + got_ref[:width, :].astype(F32)).T
    for r in range(rows):
        out_ref[r, :base, :] = pack(total[r * yd : (r + 1) * yd, :]).astype(BF16)
        out_ref[r, base:, :] = sums


def own_part(ref, yd):
    block = lax.axis_index("col") * lax.axis_size("row") + lax.axis_index("row")
    fit = LANES // yd
    row = ref[pl.ds(block // fit, 1), :]
    out = row[:, :yd]
    for k in range(1, fit):
        out = jnp.where(block % fit == k, row[:, k * yd : (k + 1) * yd], out)
    return out


def last_kernel(
    log_nx, log_ny, xa_ref, norm_ref, b_ref, r_ref, v_ref, c_ref, got_ref, yt_ref, t_ref, y_ref,
    f_hbm, pot_hbm, gx_hbm, gy_hbm, f_ref, pot_ref, gx_ref, gy_ref, ys_ref, sum_ref, sems,
):
    width, n = gx_ref.shape
    ny = v_ref.shape[1]
    yd = y_ref.shape[1]
    base = yd * width // LANES
    count = ny // LANES
    kappa = kappa_of(width)
    moves = []

    def leave(source, target):
        move = pltpu.make_async_copy(source, target, sems.at[len(moves)])
        move.start()
        moves.append(move)

    mass = xa_ref[width:, :].astype(F32)[7:8]
    log_row = mass - log_nx - jnp.log(r_ref[...])
    f_ref[...] = norm_ref[...] / width + EPSILON * (kappa * b_ref[...] - log_row)
    leave(f_ref, f_hbm)
    total = got_ref[0].astype(F32)
    for k in range(1, got_ref.shape[0]):
        total = total + got_ref[k].astype(F32)
    sums = total[base : base + count] + total[base + count : base + 2 * count]
    sum_ref[...] = sums
    colsum = own_part(sum_ref, yd)
    c_term = own_part(c_ref, yd)
    own = y_ref[0].astype(F32)
    gy_ref[...] = unpack(total[:base], yd, width) * (
        jnp.exp(own[:, width + 6 : width + 7]) * to_column(1.0 / colsum)
    )
    leave(gy_ref, gy_hbm)
    norm = to_row(jnp.sum(own[:, :width] * own[:, :width], axis=1, keepdims=True))
    pot_ref[...] = norm / width - EPSILON * (jnp.log(colsum) - kappa * c_term)
    leave(pot_ref, pot_hbm)
    mass = yt_ref[width:, :].astype(F32)[6:7]
    q = v_ref[...] * jnp.exp(mass + log_nx - jnp.log(from_lanes(sums)))
    stack(ys_ref, width, yt_ref[:width, :], q)
    across = (((1,), (1,)), ((), ()))
    for k in range(n // TILE):
        t = slice(k * TILE, (k + 1) * TILE)
        product = lax.dot_general(ys_ref[...], t_ref[t, :], across, preferred_element_type=F32)
        moved, weight = unstack(product, width)
        gx_ref[:, t] = (xa_ref[:width, t].astype(F32) * weight - moved) * (r_ref[:, t] * (1.0 / ny))
        leave(gx_ref.at[:, t], gx_hbm.at[:, t])
    for move in moves:
        move.wait()


def call(kernel, outs, scratch, limit, *args, space=pltpu.VMEM, out_space=pltpu.VMEM, cost=None):
    return pl.pallas_call(
        kernel,
        out_shape=outs,
        in_specs=[pl.BlockSpec(memory_space=space)] * len(args),
        out_specs=jax.tree.map(lambda _: pl.BlockSpec(memory_space=out_space), outs),
        scratch_shapes=scratch,
        cost_estimate=cost,
        compiler_params=pltpu.CompilerParams(vmem_limit_bytes=limit),
    )(*args)


def shape(dims, dtype=F32):
    return jax.ShapeDtypeStruct(dims, dtype)


def swap(value):
    return lax.ppermute(value, "col", [(0, 1), (1, 0)])


def on_device(points_x, points_y, mass_x, mass_y):
    n, width = points_x.shape
    yd = points_y.shape[0]
    rows = lax.axis_size("row")
    ny = 2 * rows * yd
    half = ny // 2
    count = ny // LANES
    log_nx, log_ny = math.log(n * 2 * rows), math.log(ny)
    depth = width + EXT
    limit = (20 if ny <= 1024 else 56) * 1024 * 1024
    extra = sums_rows(ny)
    run = functools.partial
    vmem = pltpu.VMEM
    ones = call(
        ones_kernel, shape((yd, EXT)), [], limit,
        cost=pl.CostEstimate(flops=4 * 10**9, bytes_accessed=10000, transcendentals=0),
    )
    y_own = call(
        run(prep_kernel, log_ny), shape((rows, yd, depth), BF16), [], limit, points_y, mass_y.reshape(1, yd), ones,
        cost=pl.CostEstimate(flops=4 * 10**9, bytes_accessed=400000, transcendentals=0),
    )
    y_mine = lax.all_to_all(y_own, "row", 0, 0, tiled=True)
    y_other = swap(y_mine)
    xa, yt_mine, peak, total = call(
        half_kernel,
        (
            shape((depth, n), BF16), shape((depth, half), BF16), shape((1, n)), shape((1, n)),
        ),
        [],
        limit, points_x.T, mass_x.reshape(n // LANES, LANES), y_mine,
    )
    yt, b_term, lse, peak, plan = call(
        run(first_kernel, log_nx),
        (
            shape((depth, ny), BF16), shape((1, n)), shape((2 * rows, count, LANES)), shape((1, ny)),
            shape((n, ny), BF16),
        ),
        [vmem((depth, n), BF16), vmem((1, ny), F32)],
        limit, xa, yt_mine, y_other, peak, total,
    )
    lse = lax.all_to_all(lse, AXES, 0, 0, tiled=True)
    r, v, c_term, xs, sums, send = call(
        run(second_kernel, log_nx, log_ny),
        (
            shape((1, n)), shape((1, ny)), shape((count, LANES)), shape((2 * width + PAD, n), BF16),
            shape((1, ny)), shape((width + PAD, half), BF16),
        ),
        [], limit, xa, b_term, lse, peak, yt, plan,
    )
    got = swap(send)
    keep, norm = call(
        keep_kernel, (shape((width, half)), shape((1, n))), [], limit, xa, xs, v, sums, yt, plan
    )
    part = call(
        add_kernel, shape((rows, yd * width // LANES + extra, LANES), BF16), [], limit, keep, sums, got
    )
    part = lax.all_to_all(part, "row", 0, 0, tiled=True)
    f_pot, g_pot, grad_xt, grad_y = call(
        run(last_kernel, log_nx, log_ny),
        (shape((1, n)), shape((1, yd)), shape((width, n)), shape((yd, width))),
        [
            vmem((1, n), F32), vmem((1, yd), F32), vmem((width, n), F32), vmem((yd, width), F32),
            vmem((2 * width + PAD, ny), BF16), vmem((count, LANES), F32),
            pltpu.SemaphoreType.DMA((3 + n // TILE,)),
        ],
        limit, xa, norm, b_term, r, v, c_term, part, yt, plan, y_own, out_space=pl.ANY,
    )
    return f_pot.reshape(n), g_pot.reshape(yd), grad_xt.T, grad_y


def solution(mesh):
    in_specs = (
        P(("groups", "row", "col"), None),
        P(("groups", "col", "row"), None),
        P(("groups", "row", "col")),
        P(("groups", "col", "row")),
    )
    out_specs = (
        P(("groups", "row", "col")),
        P(("groups", "col", "row")),
        P(("groups", "row", "col"), None),
        P(("groups", "col", "row"), None),
    )
    return jax.shard_map(
        on_device, mesh=mesh, in_specs=in_specs, out_specs=out_specs, check_vma=False
    )
```

```python
import functools
import math

import jax
import jax.numpy as jnp
from jax import lax
from jax.experimental import pallas as pl
from jax.experimental.pallas import tpu as pltpu
from jax.sharding import PartitionSpec as P

ITERS = 2
EPSILON = 0.02
LOG2E = math.log2(math.e)
TILE = 256
STEP = 8
WIDE = 1024
EXT = 32
PAD = 16
LANES = 128
AXES = ("row", "col")
F32 = jnp.float32
BF16 = jnp.bfloat16


def kappa_of(width):
    return 2.0 / (width * EPSILON)


def pieces(value):
    high = value.astype(BF16).astype(F32)
    rest = value - high
    mid = rest.astype(BF16).astype(F32)
    return high, mid, rest - mid


def select(index, values):
    out = jnp.zeros(index.shape, F32)
    for k, value in values.items():
        out = jnp.where(index == k, value, out)
    return out


def extras_x(index, b_term, mass):
    high, mid, low = pieces(b_term)
    return select(index, {0: 1.0, 1: 1.0, 2: 1.0, 3: high, 4: mid, 5: low, 7: mass})


def rows_index(columns):
    return lax.broadcasted_iota(jnp.int32, (EXT, columns), 0)


def to_column(row):
    size = row.shape[1]
    eye = lax.broadcasted_iota(jnp.int32, (size, size), 0) == lax.broadcasted_iota(jnp.int32, (size, size), 1)
    return jnp.sum(jnp.where(eye, row, 0.0), axis=1, keepdims=True)


def to_row(column):
    size = column.shape[0]
    eye = lax.broadcasted_iota(jnp.int32, (size, size), 0) == lax.broadcasted_iota(jnp.int32, (size, size), 1)
    return jnp.sum(jnp.where(eye, column, 0.0), axis=0, keepdims=True)


def max_down(z_ref):
    rows, columns = z_ref.shape
    peak = z_ref[0:STEP, :]
    for r in range(STEP, rows, STEP):
        peak = jnp.maximum(peak, z_ref[r : r + STEP, :])
    return jnp.max(peak, axis=0, keepdims=True)


def exp_sum_down(z_ref, scale, shift):
    rows, columns = z_ref.shape
    total = jnp.zeros((STEP, columns), F32)
    for r in range(0, rows, STEP):
        total = total + jnp.exp2((z_ref[r : r + STEP, :] - shift) * scale)
    return jnp.sum(total, axis=0, keepdims=True)


def to_lanes(row):
    return jnp.concatenate([row[:, k : k + LANES] for k in range(0, row.shape[1], LANES)], axis=0)


def from_lanes(block):
    return jnp.concatenate([block[k : k + 1] for k in range(block.shape[0])], axis=1)


def sums_rows(ny):
    return -(-2 * ny // LANES // 16) * 16


def sums_out(sums):
    high = sums.astype(BF16).astype(F32)
    spare = sums_rows(sums.size) - 2 * sums.shape[0]
    return jnp.concatenate([high, sums - high] + [jnp.zeros((spare, LANES), F32)] * (spare > 0), axis=0)


def pack(block):
    rows, width = block.shape
    base = rows * width // LANES
    spare = LANES - width
    side = [block[base:, k : k + spare] for k in range(0, width, spare)]
    return jnp.concatenate([block[:base], jnp.concatenate(side, axis=0)], axis=1)


def unpack(block, rows, width):
    base = block.shape[0]
    rest = rows - base
    side = [block[k : k + rest, width:] for k in range(0, base, rest)]
    return jnp.concatenate([block[:, :width], jnp.concatenate(side, axis=1)], axis=0)


def ones_kernel(ext_ref):
    index = lax.broadcasted_iota(jnp.int32, ext_ref.shape, 1)
    ext_ref[...] = select(index, {3: 1.0, 4: 1.0, 5: 1.0})


def prep_kernel(log_ny, y_ref, my_ref, ones_ref, ya_ref):
    width = y_ref.shape[1]
    y = y_ref[...]
    yf = y.astype(F32)
    norm = jnp.sum(yf * yf, axis=1, keepdims=True)
    mass = to_column(my_ref[...].astype(F32))
    c_term = (mass - log_ny) / kappa_of(width) - 0.5 * norm
    high, mid, low = pieces(c_term)
    index = lax.broadcasted_iota(jnp.int32, ones_ref.shape, 1)
    ext = (ones_ref[...] + select(index, {0: high, 1: mid, 2: low, 6: mass})).astype(BF16)
    for k in range(ya_ref.shape[0]):
        ya_ref[k, :, :width] = y
        ya_ref[k, :, width:] = ext


def half_kernel(xt_ref, mx_ref, mine_ref, xa_ref, yt_ref, peak_ref, total_ref, z_ref):
    rows, yd, depth = mine_ref.shape
    width, n = xt_ref.shape
    half = rows * yd
    scale = kappa_of(width) * LOG2E
    mass = from_lanes(mx_ref[...].astype(F32))
    xa_ref[:width, :] = xt_ref[...]
    xa_ref[width:, :] = extras_x(rows_index(n), jnp.zeros((1, n), F32), mass).astype(BF16)
    mine = mine_ref[...].reshape(half, depth)
    z_ref[...] = jnp.dot(mine, xa_ref[...], preferred_element_type=F32)
    peak = max_down(z_ref)
    peak_ref[...] = peak
    total_ref[...] = exp_sum_down(z_ref, scale, peak)
    yt_ref[...] = mine.T


def by_core(half, body):
    halves = (slice(0, half), slice(half, 2 * half))
    col = lax.axis_index("col")

    @pl.when(col == 0)
    def _():
        body(halves[0], halves[1])

    @pl.when(col == 1)
    def _():
        body(halves[1], halves[0])


def tiles_of(part):
    return [slice(k, k + TILE) for k in range(part.start, part.stop, TILE)]


def first_kernel(
    log_nx, xa0_ref, mine_ref, other_ref, peak_ref, total_ref,
    yt_ref, b_ref, l_ref, m_ref, t_ref, xa_ref, z_ref, zc_ref, b2_ref,
):
    rows, yd, depth = other_ref.shape
    n = xa0_ref.shape[1]
    width = depth - EXT
    half = rows * yd
    ny = 2 * half
    scale = kappa_of(width) * LOG2E
    other = other_ref[...].reshape(half, depth)
    z_ref[...] = jnp.dot(other, xa0_ref[...], preferred_element_type=F32)

    def place(mine, theirs):
        yt_ref[:, mine] = mine_ref[...]
        yt_ref[:, theirs] = other.T

    by_core(half, place)
    old = peak_ref[...]
    peak = jnp.maximum(max_down(z_ref), old)
    total = exp_sum_down(z_ref, scale, peak) + total_ref[...] * jnp.exp2((old - peak) * scale)
    mass = xa0_ref[width:, :].astype(F32)[7:8]
    b_term = -peak + (mass - log_nx - jnp.log(total)) * (LOG2E / scale)
    b_ref[...] = b_term
    xa_ref[:width, :] = xa0_ref[:width, :]
    xa_ref[width:, :] = extras_x(rows_index(n), b_term, mass).astype(BF16)
    x_rows = xa_ref[...].T
    wide = min(WIDE, ny)

    def columns(t):
        zc_ref[...] = jnp.dot(x_rows, yt_ref[:, t], preferred_element_type=F32)
        peak = max_down(zc_ref)
        m_ref[:, t] = peak
        total = jnp.zeros((2 * STEP, wide), F32)
        for r in range(0, n, 2 * STEP):
            value = jnp.exp2((zc_ref[r : r + 2 * STEP, :] - peak) * scale)
            total = total + value
            t_ref[r : r + 2 * STEP, t] = value.astype(BF16)
        total = jnp.sum(total, axis=0, keepdims=True)
        b2_ref[:, t] = scale * peak + jnp.log(total) * LOG2E

    if ny == wide:
        columns(slice(0, ny))
    else:

        @pl.loop(0, ny // wide)
        def _(t):
            columns(pl.ds(pl.multiple_of(t * wide, wide), wide))

    lse = to_lanes(b2_ref[...])
    for k in range(2 * rows):
        l_ref[k] = lse


def stack(out_ref, width, points, factor):
    moved = points.astype(F32) * factor
    high = moved.astype(BF16)
    out_ref[:width, :] = high
    out_ref[width : 2 * width, :] = (moved - high.astype(F32)).astype(BF16)
    one, two, three = pieces(factor)
    index = lax.broadcasted_iota(jnp.int32, (PAD, factor.shape[1]), 0)
    out_ref[2 * width :, :] = select(index, {0: one, 1: two, 2: three}).astype(BF16)


def unstack(product, width):
    ext = product[2 * width :]
    return product[:width] + product[width : 2 * width], (ext[0:1] + ext[1:2]) + ext[2:3]


def second_kernel(
    log_nx, log_ny, xa_ref, b_ref, l_ref, m_ref, yt_ref, t_ref,
    r_ref, v_ref, c_ref, xs_ref, sum_ref, send_ref,
):
    width = xa_ref.shape[0] - EXT
    ny = m_ref.shape[1]
    half = ny // 2
    kappa = kappa_of(width)
    scale = kappa * LOG2E
    l_all = l_ref[...]
    peak = jnp.max(l_all, axis=0)
    total = jnp.sum(jnp.exp2(l_all - peak[None]), axis=0)
    lse2 = from_lanes(peak + jnp.log(total) * LOG2E)
    old = yt_ref[width:, :].astype(F32)
    c_old = (old[0:1] + old[1:2]) + old[2:3]
    lb2 = (old[6:7] - log_ny) * LOG2E
    c_ref[...] = to_lanes(c_old + (lb2 - lse2) / scale)
    v = jnp.exp2(scale * m_ref[...] + (lb2 - lse2))
    v_ref[...] = v
    one, two, three = pieces(v)
    index = lax.broadcasted_iota(jnp.int32, (PAD, ny), 0)
    v_rows = select(index, {0: one, 1: two, 2: three}).astype(BF16)
    across = (((1,), (1,)), ((), ()))
    sums = lax.dot_general(v_rows, t_ref[...], across, preferred_element_type=F32)
    rowsum = (sums[0:1] + sums[1:2]) + sums[2:3]
    mass = xa_ref[width:, :].astype(F32)[7:8]
    r = jnp.exp(mass - log_nx) / rowsum
    r_ref[...] = r
    stack(xs_ref, width, xa_ref[:width, :], r)

    def products(mine, theirs):
        for t in tiles_of(theirs):
            product = jnp.dot(xs_ref[...], t_ref[:, t], preferred_element_type=F32)
            moment, total = unstack(product, width)
            total = total * v[:, t]
            sum_ref[:, t] = total
            part = yt_ref[:width, t].astype(F32) * total - moment * v[:, t]
            send_ref[:width, t.start - theirs.start : t.stop - theirs.start] = part.astype(BF16)
        for t in tiles_of(mine):
            ext = jnp.dot(xs_ref[2 * width :, :], t_ref[:, t], preferred_element_type=F32)
            sum_ref[:, t] = ((ext[0:1] + ext[1:2]) + ext[2:3]) * v[:, t]

    by_core(half, products)
    sums = sum_ref[...]
    high = sums.astype(BF16).astype(F32)
    low = sums - high
    index = lax.broadcasted_iota(jnp.int32, (PAD, half), 0)
    ext = select(index, {0: high[:, :half], 1: high[:, half:], 2: low[:, :half], 3: low[:, half:]})
    send_ref[width:, :] = ext.astype(BF16)


def keep_kernel(xa_ref, xs_ref, v_ref, sum_ref, yt_ref, t_ref, keep_ref, norm_ref):
    width, half = keep_ref.shape

    def products(mine, theirs):
        for t in tiles_of(mine):
            product = jnp.dot(xs_ref[: 2 * width, :], t_ref[:, t], preferred_element_type=F32)
            moment = product[:width] + product[width:]
            part = yt_ref[:width, t].astype(F32) * sum_ref[:, t] - moment * v_ref[:, t]
            keep_ref[:, t.start - mine.start : t.stop - mine.start] = part

    by_core(half, products)
    xf = xa_ref[:width, :].astype(F32)
    norm_ref[...] = jnp.sum(xf * xf, axis=0, keepdims=True)


def add_kernel(keep_ref, sum_ref, got_ref, out_ref):
    width, half = keep_ref.shape
    rows = out_ref.shape[0]
    yd = half // rows
    base = yd * width // LANES
    ext = got_ref[width:, :].astype(F32)
    other = jnp.concatenate([ext[0:1] + ext[2:3], ext[1:2] + ext[3:4]], axis=1)
    sums = sums_out(to_lanes(sum_ref[...] + other)).astype(BF16)
    total = (keep_ref[...] + got_ref[:width, :].astype(F32)).T
    for r in range(rows):
        out_ref[r, :base, :] = pack(total[r * yd : (r + 1) * yd, :]).astype(BF16)
        out_ref[r, base:, :] = sums


def own_part(ref, yd):
    block = lax.axis_index("col") * lax.axis_size("row") + lax.axis_index("row")
    fit = LANES // yd
    row = ref[pl.ds(block // fit, 1), :]
    out = row[:, :yd]
    for k in range(1, fit):
        out = jnp.where(block % fit == k, row[:, k * yd : (k + 1) * yd], out)
    return out


def last_kernel(
    log_nx, log_ny, xa_ref, norm_ref, b_ref, r_ref, v_ref, c_ref, got_ref, yt_ref, t_ref, y_ref,
    f_hbm, pot_hbm, gx_hbm, gy_hbm, f_ref, pot_ref, gx_ref, gy_ref, ys_ref, sum_ref, sems,
):
    width, n = gx_ref.shape
    ny = v_ref.shape[1]
    yd = y_ref.shape[1]
    base = yd * width // LANES
    count = ny // LANES
    kappa = kappa_of(width)
    moves = []

    def leave(source, target):
        move = pltpu.make_async_copy(source, target, sems.at[len(moves)])
        move.start()
        moves.append(move)

    mass = xa_ref[width:, :].astype(F32)[7:8]
    log_row = mass - log_nx - jnp.log(r_ref[...])
    f_ref[...] = norm_ref[...] / width + EPSILON * (kappa * b_ref[...] - log_row)
    leave(f_ref, f_hbm)
    total = got_ref[0].astype(F32)
    for k in range(1, got_ref.shape[0]):
        total = total + got_ref[k].astype(F32)
    sums = total[base : base + count] + total[base + count : base + 2 * count]
    sum_ref[...] = sums
    colsum = own_part(sum_ref, yd)
    c_term = own_part(c_ref, yd)
    own = y_ref[0].astype(F32)
    gy_ref[...] = unpack(total[:base], yd, width) * (
        jnp.exp(own[:, width + 6 : width + 7]) * to_column(1.0 / colsum)
    )
    leave(gy_ref, gy_hbm)
    norm = to_row(jnp.sum(own[:, :width] * own[:, :width], axis=1, keepdims=True))
    pot_ref[...] = norm / width - EPSILON * (jnp.log(colsum) - kappa * c_term)
    leave(pot_ref, pot_hbm)
    mass = yt_ref[width:, :].astype(F32)[6:7]
    q = v_ref[...] * jnp.exp(mass + log_nx - jnp.log(from_lanes(sums)))
    stack(ys_ref, width, yt_ref[:width, :], q)
    across = (((1,), (1,)), ((), ()))
    for k in range(n // TILE):
        t = slice(k * TILE, (k + 1) * TILE)
        product = lax.dot_general(ys_ref[...], t_ref[t, :], across, preferred_element_type=F32)
        moved, weight = unstack(product, width)
        gx_ref[:, t] = (xa_ref[:width, t].astype(F32) * weight - moved) * (r_ref[:, t] * (1.0 / ny))
        leave(gx_ref.at[:, t], gx_hbm.at[:, t])
    for move in moves:
        move.wait()


def call(kernel, outs, scratch, limit, *args, space=pltpu.VMEM, out_space=pltpu.VMEM, cost=None):
    return pl.pallas_call(
        kernel,
        out_shape=outs,
        in_specs=[pl.BlockSpec(memory_space=space)] * len(args),
        out_specs=jax.tree.map(lambda _: pl.BlockSpec(memory_space=out_space), outs),
        scratch_shapes=scratch,
        cost_estimate=cost,
        compiler_params=pltpu.CompilerParams(vmem_limit_bytes=limit),
    )(*args)


def shape(dims, dtype=F32):
    return jax.ShapeDtypeStruct(dims, dtype)


def swap(value):
    return lax.ppermute(value, "col", [(0, 1), (1, 0)])


def on_device(points_x, points_y, mass_x, mass_y):
    n, width = points_x.shape
    yd = points_y.shape[0]
    rows = lax.axis_size("row")
    ny = 2 * rows * yd
    half = ny // 2
    count = ny // LANES
    log_nx, log_ny = math.log(n * 2 * rows), math.log(ny)
    depth = width + EXT
    limit = (20 if ny <= 1024 else 56) * 1024 * 1024
    extra = sums_rows(ny)
    run = functools.partial
    vmem = pltpu.VMEM
    ones = call(
        ones_kernel, shape((yd, EXT)), [], limit,
        cost=pl.CostEstimate(flops=4 * 10**9, bytes_accessed=10000, transcendentals=0),
    )
    y_own = call(
        run(prep_kernel, log_ny), shape((rows, yd, depth), BF16), [], limit, points_y, mass_y.reshape(1, yd), ones,
        cost=pl.CostEstimate(flops=4 * 10**9, bytes_accessed=400000, transcendentals=0),
    )
    y_mine = lax.all_to_all(y_own, "row", 0, 0, tiled=True)
    y_other = swap(y_mine)
    xa, yt_mine, peak, total = call(
        half_kernel,
        (
            shape((depth, n), BF16), shape((depth, half), BF16), shape((1, n)), shape((1, n)),
        ),
        [vmem((half, n), F32)],
        limit, points_x.T, mass_x.reshape(n // LANES, LANES), y_mine,
    )
    yt, b_term, lse, peak, plan = call(
        run(first_kernel, log_nx),
        (
            shape((depth, ny), BF16), shape((1, n)), shape((2 * rows, count, LANES)), shape((1, ny)),
            shape((n, ny), BF16),
        ),
        [vmem((depth, n), BF16), vmem((half, n), F32), vmem((n, min(WIDE, ny)), F32), vmem((1, ny), F32)],
        limit, xa, yt_mine, y_other, peak, total,
    )
    lse = lax.all_to_all(lse, AXES, 0, 0, tiled=True)
    r, v, c_term, xs, sums, send = call(
        run(second_kernel, log_nx, log_ny),
        (
            shape((1, n)), shape((1, ny)), shape((count, LANES)), shape((2 * width + PAD, n), BF16),
            shape((1, ny)), shape((width + PAD, half), BF16),
        ),
        [], limit, xa, b_term, lse, peak, yt, plan,
    )
    got = swap(send)
    keep, norm = call(
        keep_kernel, (shape((width, half)), shape((1, n))), [], limit, xa, xs, v, sums, yt, plan
    )
    part = call(
        add_kernel, shape((rows, yd * width // LANES + extra, LANES), BF16), [], limit, keep, sums, got
    )
    part = lax.all_to_all(part, "row", 0, 0, tiled=True)
    f_pot, g_pot, grad_xt, grad_y = call(
        run(last_kernel, log_nx, log_ny),
        (shape((1, n)), shape((1, yd)), shape((width, n)), shape((yd, width))),
        [
            vmem((1, n), F32), vmem((1, yd), F32), vmem((width, n), F32), vmem((yd, width), F32),
            vmem((2 * width + PAD, ny), BF16), vmem((count, LANES), F32),
            pltpu.SemaphoreType.DMA((3 + n // TILE,)),
        ],
        limit, xa, norm, b_term, r, v, c_term, part, yt, plan, y_own, out_space=pl.ANY,
    )
    return f_pot.reshape(n), g_pot.reshape(yd), grad_xt.T, grad_y


def solution(mesh):
    in_specs = (
        P(("groups", "row", "col"), None),
        P(("groups", "col", "row"), None),
        P(("groups", "row", "col")),
        P(("groups", "col", "row")),
    )
    out_specs = (
        P(("groups", "row", "col")),
        P(("groups", "col", "row")),
        P(("groups", "row", "col"), None),
        P(("groups", "col", "row"), None),
    )
    return jax.shard_map(
        on_device, mesh=mesh, in_specs=in_specs, out_specs=out_specs, check_vma=False
    )
```

```python
import functools
import math

import jax
import jax.numpy as jnp
from jax import lax
from jax.experimental import pallas as pl
from jax.experimental.pallas import tpu as pltpu
from jax.sharding import PartitionSpec as P

ITERS = 2
EPSILON = 0.02
LOG2E = math.log2(math.e)
TILE = 256
STEP = 32
EXT = 32
PAD = 16
LANES = 128
TINY = 1e-25
ACROSS = (((1,), (1,)), ((), ()))
AXES = ("row", "col")
F32 = jnp.float32
BF16 = jnp.bfloat16


def kappa_of(width):
    return 2.0 / (width * EPSILON)


def pieces(value):
    high = value.astype(BF16).astype(F32)
    rest = value - high
    mid = rest.astype(BF16).astype(F32)
    return high, mid, rest - mid


def select(index, values):
    out = jnp.zeros(index.shape, F32)
    for k, value in values.items():
        out = jnp.where(index == k, value, out)
    return out


def extras_x(index, b_term, mass):
    high, mid, low = pieces(b_term)
    return select(index, {0: 1.0, 1: 1.0, 2: 1.0, 3: high, 4: mid, 5: low, 7: mass})


def rows_index(columns):
    return lax.broadcasted_iota(jnp.int32, (EXT, columns), 0)


def to_column(row):
    size = row.shape[1]
    eye = lax.broadcasted_iota(jnp.int32, (size, size), 0) == lax.broadcasted_iota(jnp.int32, (size, size), 1)
    return jnp.sum(jnp.where(eye, row, 0.0), axis=1, keepdims=True)


def to_row(column):
    size = column.shape[0]
    eye = lax.broadcasted_iota(jnp.int32, (size, size), 0) == lax.broadcasted_iota(jnp.int32, (size, size), 1)
    return jnp.sum(jnp.where(eye, column, 0.0), axis=0, keepdims=True)


def for_tiles(total, product, z_ref, use):
    count = total // TILE
    slots = z_ref.shape[0]
    if count <= slots:
        for t in range(count):
            z_ref[t] = product(pl.ds(t * TILE, TILE))
        for t in range(count):
            use(pl.ds(t * TILE, TILE), z_ref.at[t])
    else:

        @pl.loop(0, count)
        def _(t):
            tile = pl.ds(pl.multiple_of(t * TILE, TILE), TILE)
            z_ref[0] = product(tile)
            use(tile, z_ref.at[0])


def max_down(z_ref, rows):
    peak = z_ref[0:STEP, :]
    for r in range(STEP, rows, STEP):
        peak = jnp.maximum(peak, z_ref[r : r + STEP, :])
    return jnp.max(peak, axis=0, keepdims=True)


def exp_sum_down(z_ref, rows, scale, shift, keep=None):
    total = jnp.zeros((STEP, TILE), F32)
    for r in range(0, rows, STEP):
        value = jnp.exp2((z_ref[r : r + STEP, :] - shift) * scale)
        total = total + value
        if keep is not None:
            keep(r, value)
    return jnp.sum(total, axis=0, keepdims=True)


def to_lanes(row):
    return jnp.concatenate([row[:, k : k + LANES] for k in range(0, row.shape[1], LANES)], axis=0)


def from_lanes(block):
    return jnp.concatenate([block[k : k + 1] for k in range(block.shape[0])], axis=1)


def sums_rows(ny):
    return -(-2 * ny // LANES // 16) * 16


def sums_out(sums):
    high = sums.astype(BF16).astype(F32)
    spare = sums_rows(sums.size) - 2 * sums.shape[0]
    return jnp.concatenate([high, sums - high] + [jnp.zeros((spare, LANES), F32)] * (spare > 0), axis=0)


def pack(block):
    rows, width = block.shape
    base = rows * width // LANES
    spare = LANES - width
    side = [block[base:, k : k + spare] for k in range(0, width, spare)]
    return jnp.concatenate([block[:base], jnp.concatenate(side, axis=0)], axis=1)


def unpack(block, rows, width):
    base = block.shape[0]
    rest = rows - base
    side = [block[k : k + rest, width:] for k in range(0, base, rest)]
    return jnp.concatenate([block[:, :width], jnp.concatenate(side, axis=1)], axis=0)


def ones_kernel(ext_ref):
    index = lax.broadcasted_iota(jnp.int32, ext_ref.shape, 1)
    ext_ref[...] = select(index, {3: 1.0, 4: 1.0, 5: 1.0})


def prep_kernel(log_ny, y_ref, my_ref, ones_ref, ya_ref):
    width = y_ref.shape[1]
    y = y_ref[...]
    yf = y.astype(F32)
    norm = jnp.sum(yf * yf, axis=1, keepdims=True)
    mass = to_column(my_ref[...].astype(F32))
    c_term = (mass - log_ny) / kappa_of(width) - 0.5 * norm
    high, mid, low = pieces(c_term)
    index = lax.broadcasted_iota(jnp.int32, ones_ref.shape, 1)
    ext = (ones_ref[...] + select(index, {0: high, 1: mid, 2: low, 6: mass})).astype(BF16)
    for k in range(ya_ref.shape[0]):
        ya_ref[k, :, :width] = y
        ya_ref[k, :, width:] = ext


def halves(row):
    half = row.shape[1] // 2
    return row[:, :half], row[:, half:]


def other_order(row):
    mine, other = halves(row)
    return jnp.where(lax.axis_index("col") == 0, row, jnp.concatenate([other, mine], axis=1))


def piece_rows(row):
    one, two, three = pieces(row)
    index = lax.broadcasted_iota(jnp.int32, (PAD, row.shape[1]), 0)
    return select(index, {0: one, 1: two, 2: three}).astype(BF16)


def sum_pieces(block):
    return (block[0:1] + block[1:2]) + block[2:3]


def half_kernel(xt_ref, mx_ref, mine_ref, xa_ref, yt_ref, peak_ref, total_ref, e_ref, z_ref):
    rows, yd, depth = mine_ref.shape
    width, n = xt_ref.shape
    half = rows * yd
    scale = kappa_of(width) * LOG2E
    mass = from_lanes(mx_ref[...].astype(F32))
    xa_ref[:width, :] = xt_ref[...]
    xa_ref[width:, :] = extras_x(rows_index(n), jnp.zeros((1, n), F32), mass).astype(BF16)
    mine = mine_ref[...].reshape(half, depth)

    def product(t):
        return jnp.dot(mine, xa_ref[:, t], preferred_element_type=F32)

    def use(t, z):
        def keep(r, value):
            e_ref[r : r + STEP, t] = value

        peak = max_down(z, half)
        peak_ref[:, t] = peak
        total_ref[:, t] = exp_sum_down(z, half, scale, peak, keep)

    for_tiles(n, product, z_ref, use)
    yt_ref[...] = mine.T


def first_kernel(
    log_nx, xa_ref, mine_ref, other_ref, peak_ref, total_ref, e_ref,
    yt_ref, km_ref, ko_ref, b_ref, omega_ref, mu_ref, l_ref, xb_ref, z_ref, sum_ref, lse_ref,
):
    rows, yd, depth = other_ref.shape
    n = xa_ref.shape[1]
    width = depth - EXT
    half = rows * yd
    scale = kappa_of(width) * LOG2E
    other = other_ref[...].reshape(half, depth)

    def product(t):
        return jnp.dot(other, xa_ref[:, t], preferred_element_type=F32)

    def use(t, z):
        def keep(r, value):
            ko_ref[r : r + STEP, t] = value.astype(BF16)

        old = peak_ref[:, t]
        peak = jnp.maximum(max_down(z, half), old)
        down = jnp.exp2((old - peak) * scale)
        total = exp_sum_down(z, half, scale, peak, keep) + total_ref[:, t] * down
        sum_ref[:, t] = total
        b_ref[:, t] = -peak - jnp.log(total) * (LOG2E / scale)
        for r in range(0, half, STEP):
            km_ref[r : r + STEP, t] = (e_ref[r : r + STEP, t] * down).astype(BF16)

    for_tiles(n, product, z_ref, use)
    yt_ref[...] = other.T
    mass = xa_ref[width:, :].astype(F32)[7:8]
    b_ref[...] = b_ref[...] + (mass - log_nx) * (LOG2E / scale)
    omega = jnp.exp(mass - log_nx) / sum_ref[...]
    omega_ref[...] = omega
    left = piece_rows(omega)
    sums = jnp.concatenate(
        [
            sum_pieces(lax.dot_general(left, ref[...], ACROSS, preferred_element_type=F32))
            for ref in (km_ref, ko_ref)
        ],
        axis=1,
    )
    lse_ref[...] = jnp.log(sums) * LOG2E
    mu_ref[...] = jnp.zeros(mu_ref.shape, F32)

    @pl.when(jnp.min(sums) < TINY)
    def _():
        xb_ref[:width, :] = xa_ref[:width, :]
        xb_ref[width:, :] = extras_x(rows_index(n), b_ref[...], mass).astype(BF16)
        omega_ref[...] = jnp.ones((1, n), F32)
        step = LANES // yd
        for k, (y_ref, k_ref) in enumerate(((mine_ref, km_ref), (other_ref, ko_ref))):

            @pl.loop(0, rows // step)
            def _(t):
                y = y_ref[pl.ds(t * step, step)].reshape(LANES, depth)
                z = jnp.dot(y, xb_ref[...], preferred_element_type=F32)
                peak = jnp.max(z, axis=1, keepdims=True)
                value = jnp.exp2((z - peak) * scale)
                k_ref[pl.ds(pl.multiple_of(t * LANES, LANES), LANES), :] = value.astype(BF16)
                place = pl.ds(pl.multiple_of(k * half + t * LANES, LANES), LANES)
                mu_ref[:, place] = to_row(scale * peak)
                lse_ref[:, place] = to_row(scale * peak + jnp.log(jnp.sum(value, axis=1, keepdims=True)) * LOG2E)

    lse = to_lanes(other_order(lse_ref[...]))
    for k in range(2 * rows):
        l_ref[k] = lse


def stack(out_ref, width, points, factor):
    moved = points.astype(F32) * factor
    high = moved.astype(BF16)
    out_ref[:width, :] = high
    out_ref[width : 2 * width, :] = (moved - high.astype(F32)).astype(BF16)
    one, two, three = pieces(factor)
    index = lax.broadcasted_iota(jnp.int32, (PAD, factor.shape[1]), 0)
    out_ref[2 * width :, :] = select(index, {0: one, 1: two, 2: three}).astype(BF16)


def unstack(product, width):
    ext = product[2 * width :]
    return product[:width] + product[width : 2 * width], (ext[0:1] + ext[1:2]) + ext[2:3]


def second_kernel(
    log_nx, log_ny, xa_ref, omega_ref, mu_ref, l_ref, ym_ref, yo_ref, km_ref, ko_ref,
    r_ref, wr_ref, v_ref, c_ref, xs_ref, sum_ref, send_ref,
):
    width = xa_ref.shape[0] - EXT
    half = ym_ref.shape[1]
    kappa = kappa_of(width)
    scale = kappa * LOG2E
    l_all = l_ref[...]
    peak = jnp.max(l_all, axis=0)
    total = jnp.sum(jnp.exp2(l_all - peak[None]), axis=0)
    lse2 = other_order(from_lanes(peak + jnp.log(total) * LOG2E))
    old = jnp.concatenate([ym_ref[width:, :], yo_ref[width:, :]], axis=1).astype(F32)
    lb2 = (old[6:7] - log_ny) * LOG2E
    c_ref[...] = to_lanes(sum_pieces(old) + (lb2 - lse2) / scale)
    v = jnp.exp2(mu_ref[...] + (lb2 - lse2))
    v_ref[...] = v
    v_mine, v_other = halves(v)
    left = piece_rows(v)
    rowsum = jnp.dot(left[:, :half], km_ref[...], preferred_element_type=F32) + jnp.dot(
        left[:, half:], ko_ref[...], preferred_element_type=F32
    )
    omega = omega_ref[...]
    rowsum = sum_pieces(rowsum) * omega
    mass = xa_ref[width:, :].astype(F32)[7:8]
    r = jnp.exp(mass - log_nx) / rowsum
    r_ref[...] = r
    wr_ref[...] = r * omega
    stack(xs_ref, width, xa_ref[:width, :], r * omega)
    totals = []
    for k in range(half // TILE):
        t = slice(k * TILE, (k + 1) * TILE)
        product = lax.dot_general(xs_ref[...], ko_ref[t, :], ACROSS, preferred_element_type=F32)
        moment, total = unstack(product, width)
        total = total * v_other[:, t]
        totals.append(total)
        part = yo_ref[:width, t].astype(F32) * total - moment * v_other[:, t]
        send_ref[:width, t] = part.astype(BF16)
    s_other = jnp.concatenate(totals, axis=1)
    ext = lax.dot_general(xs_ref[2 * width :, :], km_ref[...], ACROSS, preferred_element_type=F32)
    s_mine = sum_pieces(ext) * v_mine
    sum_ref[...] = jnp.concatenate([s_mine, s_other], axis=1)
    high_m, high_o = s_mine.astype(BF16).astype(F32), s_other.astype(BF16).astype(F32)
    index = lax.broadcasted_iota(jnp.int32, (PAD, half), 0)
    ext = select(index, {0: high_m, 1: high_o, 2: s_mine - high_m, 3: s_other - high_o})
    send_ref[width:, :] = ext.astype(BF16)


def keep_kernel(xa_ref, xs_ref, v_ref, sum_ref, ym_ref, km_ref, keep_ref, norm_ref):
    width, half = keep_ref.shape
    for k in range(half // TILE):
        t = slice(k * TILE, (k + 1) * TILE)
        product = lax.dot_general(xs_ref[: 2 * width, :], km_ref[t, :], ACROSS, preferred_element_type=F32)
        moment = product[:width] + product[width:]
        keep_ref[:, t] = ym_ref[:width, t].astype(F32) * sum_ref[:, t] - moment * v_ref[:, t]
    xf = xa_ref[:width, :].astype(F32)
    norm_ref[...] = jnp.sum(xf * xf, axis=0, keepdims=True)


def add_kernel(keep_ref, sum_ref, got_ref, out_ref):
    width, half = keep_ref.shape
    rows = out_ref.shape[0]
    yd = half // rows
    base = yd * width // LANES
    ext = got_ref[width:, :].astype(F32)
    other = jnp.concatenate([ext[1:2] + ext[3:4], ext[0:1] + ext[2:3]], axis=1)
    sums = sums_out(to_lanes(sum_ref[...] + other)).astype(BF16)
    total = (keep_ref[...] + got_ref[:width, :].astype(F32)).T
    for r in range(rows):
        out_ref[r, :base, :] = pack(total[r * yd : (r + 1) * yd, :]).astype(BF16)
        out_ref[r, base:, :] = sums


def own_part(ref, yd):
    block = lax.axis_index("row")
    fit = LANES // yd
    row = ref[pl.ds(block // fit, 1), :]
    out = row[:, :yd]
    for k in range(1, fit):
        out = jnp.where(block % fit == k, row[:, k * yd : (k + 1) * yd], out)
    return out


def last_kernel(
    log_nx, log_ny, xa_ref, norm_ref, b_ref, r_ref, wr_ref, v_ref, c_ref, got_ref, ym_ref, yo_ref, km_ref, ko_ref, y_ref,
    f_hbm, pot_hbm, gx_hbm, gy_hbm, f_ref, pot_ref, gx_ref, gy_ref, ys_ref, sum_ref, sems,
):
    width, n = gx_ref.shape
    ny = v_ref.shape[1]
    yd = y_ref.shape[1]
    base = yd * width // LANES
    count = ny // LANES
    kappa = kappa_of(width)
    moves = []

    def leave(source, target):
        move = pltpu.make_async_copy(source, target, sems.at[len(moves)])
        move.start()
        moves.append(move)

    mass = xa_ref[width:, :].astype(F32)[7:8]
    log_row = mass - log_nx - jnp.log(r_ref[...])
    f_ref[...] = norm_ref[...] / width + EPSILON * (kappa * b_ref[...] - log_row)
    leave(f_ref, f_hbm)
    total = got_ref[0].astype(F32)
    for k in range(1, got_ref.shape[0]):
        total = total + got_ref[k].astype(F32)
    sums = total[base : base + count] + total[base + count : base + 2 * count]
    sum_ref[...] = sums
    colsum = own_part(sum_ref, yd)
    c_term = own_part(c_ref, yd)
    own = y_ref[0].astype(F32)
    gy_ref[...] = unpack(total[:base], yd, width) * (
        jnp.exp(own[:, width + 6 : width + 7]) * to_column(1.0 / colsum)
    )
    leave(gy_ref, gy_hbm)
    norm = to_row(jnp.sum(own[:, :width] * own[:, :width], axis=1, keepdims=True))
    pot_ref[...] = norm / width - EPSILON * (jnp.log(colsum) - kappa * c_term)
    leave(pot_ref, pot_hbm)
    half = ny // 2
    yt = jnp.concatenate([ym_ref[...], yo_ref[...]], axis=1)
    mass = yt[width:].astype(F32)[6:7]
    q = v_ref[...] * jnp.exp(mass + log_nx - jnp.log(from_lanes(sums)))
    stack(ys_ref, width, yt[:width], q)
    for k in range(n // TILE):
        t = slice(k * TILE, (k + 1) * TILE)
        product = jnp.dot(ys_ref[:, :half], km_ref[:, t], preferred_element_type=F32) + jnp.dot(
            ys_ref[:, half:], ko_ref[:, t], preferred_element_type=F32
        )
        moved, weight = unstack(product, width)
        gx_ref[:, t] = (xa_ref[:width, t].astype(F32) * weight - moved) * (wr_ref[:, t] * (1.0 / ny))
        leave(gx_ref.at[:, t], gx_hbm.at[:, t])
    for move in moves:
        move.wait()


def call(kernel, outs, scratch, limit, *args, space=pltpu.VMEM, out_space=pltpu.VMEM, cost=None):
    return pl.pallas_call(
        kernel,
        out_shape=outs,
        in_specs=[pl.BlockSpec(memory_space=space)] * len(args),
        out_specs=jax.tree.map(lambda _: pl.BlockSpec(memory_space=out_space), outs),
        scratch_shapes=scratch,
        cost_estimate=cost,
        compiler_params=pltpu.CompilerParams(vmem_limit_bytes=limit),
    )(*args)


def shape(dims, dtype=F32):
    return jax.ShapeDtypeStruct(dims, dtype)


def swap(value):
    return lax.ppermute(value, "col", [(0, 1), (1, 0)])


def on_device(points_x, points_y, mass_x, mass_y):
    n, width = points_x.shape
    yd = points_y.shape[0]
    rows = lax.axis_size("row")
    ny = 2 * rows * yd
    half = ny // 2
    count = ny // LANES
    log_nx, log_ny = math.log(n * 2 * rows), math.log(ny)
    depth = width + EXT
    limit = (20 if ny <= 1024 else 56) * 1024 * 1024
    extra = sums_rows(ny)
    run = functools.partial
    vmem = pltpu.VMEM
    slots = 4 if ny <= 1024 else 1
    ones = call(
        ones_kernel, shape((yd, EXT)), [], limit,
        cost=pl.CostEstimate(flops=4 * 10**9, bytes_accessed=10000, transcendentals=0),
    )
    y_own = call(
        run(prep_kernel, log_ny), shape((rows, yd, depth), BF16), [], limit, points_y, mass_y.reshape(1, yd), ones,
        cost=pl.CostEstimate(flops=4 * 10**9, bytes_accessed=400000, transcendentals=0),
    )
    y_mine = lax.all_to_all(y_own, "row", 0, 0, tiled=True)
    y_other = swap(y_mine)
    xa, yt_mine, peak, total, exps = call(
        half_kernel,
        (
            shape((depth, n), BF16), shape((depth, half), BF16), shape((1, n)), shape((1, n)), shape((half, n)),
        ),
        [vmem((slots, half, TILE), F32)],
        limit, points_x.T, mass_x.reshape(n // LANES, LANES), y_mine,
    )
    yt_other, kept_mine, kept_other, b_term, omega, mu, lse = call(
        run(first_kernel, log_nx),
        (
            shape((depth, half), BF16), shape((half, n), BF16), shape((half, n), BF16), shape((1, n)),
            shape((1, n)), shape((1, ny)), shape((2 * rows, count, LANES)),
        ),
        [vmem((depth, n), BF16), vmem((slots, half, TILE), F32), vmem((1, n), F32), vmem((1, ny), F32)],
        limit, xa, y_mine, y_other, peak, total, exps,
    )
    lse = lax.all_to_all(lse, AXES, 0, 0, tiled=True)
    r, wr, v, c_term, xs, sums, send = call(
        run(second_kernel, log_nx, log_ny),
        (
            shape((1, n)), shape((1, n)), shape((1, ny)), shape((count, LANES)),
            shape((2 * width + PAD, n), BF16), shape((1, ny)), shape((width + PAD, half), BF16),
        ),
        [], limit, xa, omega, mu, lse, yt_mine, yt_other, kept_mine, kept_other,
    )
    got = swap(send)
    keep, norm = call(
        keep_kernel, (shape((width, half)), shape((1, n))), [], limit, xa, xs, v, sums, yt_mine, kept_mine
    )
    part = call(
        add_kernel, shape((rows, yd * width // LANES + extra, LANES), BF16), [], limit, keep, sums, got
    )
    part = lax.all_to_all(part, "row", 0, 0, tiled=True)
    f_pot, g_pot, grad_xt, grad_y = call(
        run(last_kernel, log_nx, log_ny),
        (shape((1, n)), shape((1, yd)), shape((width, n)), shape((yd, width))),
        [
            vmem((1, n), F32), vmem((1, yd), F32), vmem((width, n), F32), vmem((yd, width), F32),
            vmem((2 * width + PAD, ny), BF16), vmem((count, LANES), F32),
            pltpu.SemaphoreType.DMA((3 + n // TILE,)),
        ],
        limit, xa, norm, b_term, r, wr, v, c_term, part, yt_mine, yt_other, kept_mine, kept_other, y_own,
        out_space=pl.ANY,
    )
    return f_pot.reshape(n), g_pot.reshape(yd), grad_xt.T, grad_y


def solution(mesh):
    in_specs = (
        P(("groups", "row", "col"), None),
        P(("groups", "col", "row"), None),
        P(("groups", "row", "col")),
        P(("groups", "col", "row")),
    )
    out_specs = (
        P(("groups", "row", "col")),
        P(("groups", "col", "row")),
        P(("groups", "row", "col"), None),
        P(("groups", "col", "row"), None),
    )
    return jax.shard_map(
        on_device, mesh=mesh, in_specs=in_specs, out_specs=out_specs, check_vma=False
    )
```

```python
import functools
import math

import jax
import jax.numpy as jnp
from jax import lax
from jax.experimental import pallas as pl
from jax.experimental.pallas import tpu as pltpu
from jax.sharding import PartitionSpec as P

ITERS = 2
EPSILON = 0.02
LOG2E = math.log2(math.e)
TILE = 256
STEP = 32
EXT = 32
PAD = 16
LANES = 128
LIFT = 40.0
TINY = 1e-31
HUGE = 1e35
ACROSS = (((1,), (1,)), ((), ()))
AXES = ("row", "col")
F32 = jnp.float32
BF16 = jnp.bfloat16


def kappa_of(width):
    return 2.0 / (width * EPSILON)


def pieces(value):
    high = value.astype(BF16).astype(F32)
    rest = value - high
    mid = rest.astype(BF16).astype(F32)
    return high, mid, rest - mid


def select(index, values):
    out = jnp.zeros(index.shape, F32)
    for k, value in values.items():
        out = jnp.where(index == k, value, out)
    return out


def extras_x(index, b_term, mass):
    high, mid, low = pieces(b_term)
    return select(index, {0: 1.0, 1: 1.0, 2: 1.0, 3: high, 4: mid, 5: low, 7: mass})


def rows_index(columns):
    return lax.broadcasted_iota(jnp.int32, (EXT, columns), 0)


def to_column(row):
    size = row.shape[1]
    eye = lax.broadcasted_iota(jnp.int32, (size, size), 0) == lax.broadcasted_iota(jnp.int32, (size, size), 1)
    return jnp.sum(jnp.where(eye, row, 0.0), axis=1, keepdims=True)


def to_row(column):
    size = column.shape[0]
    eye = lax.broadcasted_iota(jnp.int32, (size, size), 0) == lax.broadcasted_iota(jnp.int32, (size, size), 1)
    return jnp.sum(jnp.where(eye, column, 0.0), axis=0, keepdims=True)


def for_tiles(total, product, z_ref, use):
    count = total // TILE
    slots = z_ref.shape[0]
    if count <= slots:
        for t in range(count):
            z_ref[t] = product(pl.ds(t * TILE, TILE))
        for t in range(count):
            use(pl.ds(t * TILE, TILE), z_ref.at[t])
    else:

        @pl.loop(0, count)
        def _(t):
            tile = pl.ds(pl.multiple_of(t * TILE, TILE), TILE)
            z_ref[0] = product(tile)
            use(tile, z_ref.at[0])


def max_down(z_ref, rows):
    peak = z_ref[0:STEP, :]
    for r in range(STEP, rows, STEP):
        peak = jnp.maximum(peak, z_ref[r : r + STEP, :])
    return jnp.max(peak, axis=0, keepdims=True)


def exp_sum_down(z_ref, rows, scale, shift, keep=None):
    total = jnp.zeros((STEP, TILE), F32)
    for r in range(0, rows, STEP):
        value = jnp.exp2((z_ref[r : r + STEP, :] - shift) * scale)
        total = total + value
        if keep is not None:
            keep(r, value)
    return jnp.sum(total, axis=0, keepdims=True)


def to_lanes(row):
    return jnp.concatenate([row[:, k : k + LANES] for k in range(0, row.shape[1], LANES)], axis=0)


def from_lanes(block):
    return jnp.concatenate([block[k : k + 1] for k in range(block.shape[0])], axis=1)


def sums_rows(ny):
    return -(-2 * ny // LANES // 16) * 16


def sums_out(sums):
    high = sums.astype(BF16).astype(F32)
    spare = sums_rows(sums.size) - 2 * sums.shape[0]
    return jnp.concatenate([high, sums - high] + [jnp.zeros((spare, LANES), F32)] * (spare > 0), axis=0)


def pack(block):
    rows, width = block.shape
    base = rows * width // LANES
    spare = LANES - width
    side = [block[base:, k : k + spare] for k in range(0, width, spare)]
    return jnp.concatenate([block[:base], jnp.concatenate(side, axis=0)], axis=1)


def unpack(block, rows, width):
    base = block.shape[0]
    rest = rows - base
    side = [block[k : k + rest, width:] for k in range(0, base, rest)]
    return jnp.concatenate([block[:, :width], jnp.concatenate(side, axis=1)], axis=0)


def ones_kernel(ext_ref):
    index = lax.broadcasted_iota(jnp.int32, ext_ref.shape, 1)
    ext_ref[...] = select(index, {3: 1.0, 4: 1.0, 5: 1.0})


def prep_kernel(log_ny, y_ref, my_ref, ones_ref, ya_ref):
    width = y_ref.shape[1]
    y = y_ref[...]
    yf = y.astype(F32)
    norm = jnp.sum(yf * yf, axis=1, keepdims=True)
    mass = to_column(my_ref[...].astype(F32))
    c_term = (mass - log_ny) / kappa_of(width) - 0.5 * norm
    high, mid, low = pieces(c_term)
    index = lax.broadcasted_iota(jnp.int32, ones_ref.shape, 1)
    ext = (ones_ref[...] + select(index, {0: high, 1: mid, 2: low, 6: mass})).astype(BF16)
    for k in range(ya_ref.shape[0]):
        ya_ref[k, :, :width] = y
        ya_ref[k, :, width:] = ext


def halves(row):
    half = row.shape[1] // 2
    return row[:, :half], row[:, half:]


def other_order(row):
    mine, other = halves(row)
    return jnp.where(lax.axis_index("col") == 0, row, jnp.concatenate([other, mine], axis=1))


def piece_rows(row):
    one, two, three = pieces(row)
    index = lax.broadcasted_iota(jnp.int32, (PAD, row.shape[1]), 0)
    return select(index, {0: one, 1: two, 2: three}).astype(BF16)


def sum_pieces(block):
    return (block[0:1] + block[1:2]) + block[2:3]


def half_kernel(xt_ref, mx_ref, mine_ref, xa_ref, yt_ref, base_ref, total_ref, k_ref, z_ref):
    rows, yd, depth = mine_ref.shape
    width, n = xt_ref.shape
    half = rows * yd
    scale = kappa_of(width) * LOG2E
    mass = from_lanes(mx_ref[...].astype(F32))
    xa_ref[:width, :] = xt_ref[...]
    xa_ref[width:, :] = extras_x(rows_index(n), jnp.zeros((1, n), F32), mass).astype(BF16)
    mine = mine_ref[...].reshape(half, depth)

    def product(t):
        return jnp.dot(mine, xa_ref[:, t], preferred_element_type=F32)

    def use(t, z):
        def keep(r, value):
            k_ref[r : r + STEP, t] = value.astype(BF16)

        base = max_down(z, half) - LIFT / scale
        base_ref[:, t] = base
        total_ref[:, t] = exp_sum_down(z, half, scale, base, keep)

    for_tiles(n, product, z_ref, use)
    yt_ref[...] = mine.T


def first_kernel(
    log_nx, xa_ref, mine_ref, other_ref, base_ref, total_ref, km0_ref,
    yt_ref, km_ref, ko_ref, b_ref, omega_ref, mu_ref, l_ref, xb_ref, z_ref, sum_ref, lse_ref, sem,
):
    rows, yd, depth = other_ref.shape
    n = xa_ref.shape[1]
    width = depth - EXT
    half = rows * yd
    scale = kappa_of(width) * LOG2E
    other = other_ref[...].reshape(half, depth)
    move = pltpu.make_async_copy(km0_ref, km_ref, sem)
    move.start()

    def product(t):
        return jnp.dot(other, xa_ref[:, t], preferred_element_type=F32)

    def use(t, z):
        def keep(r, value):
            ko_ref[r : r + STEP, t] = value.astype(BF16)

        sum_ref[:, t] = exp_sum_down(z, half, scale, base_ref[:, t], keep) + total_ref[:, t]

    for_tiles(n, product, z_ref, use)
    yt_ref[...] = other.T
    mass = xa_ref[width:, :].astype(F32)[7:8]
    total = sum_ref[...]
    b_ref[...] = (mass - log_nx - jnp.log(total)) * (LOG2E / scale) - base_ref[...]
    omega = jnp.exp(mass - log_nx) * (2.0**LIFT / total)
    omega_ref[...] = omega
    left = piece_rows(omega)
    move.wait()
    sums = jnp.concatenate(
        [
            sum_pieces(lax.dot_general(left, ref[...], ACROSS, preferred_element_type=F32))
            for ref in (km_ref, ko_ref)
        ],
        axis=1,
    )
    lse_ref[...] = jnp.log(sums) * LOG2E - LIFT
    mu_ref[...] = jnp.full(mu_ref.shape, -LIFT, F32)

    @pl.when(jnp.logical_not((jnp.max(total) < HUGE) & (jnp.min(sums) > TINY)))
    def _():
        step = LANES // yd
        sides = ((0, mine_ref, km_ref), (1, other_ref, ko_ref))

        def scores(y_ref, x_ref, t):
            y = y_ref[pl.ds(t * step, step)].reshape(LANES, depth)
            return jnp.dot(y, x_ref[...], preferred_element_type=F32)

        b_ref[...] = jnp.full((1, n), -jnp.inf, F32)
        for k, y_ref, k_ref in sides:

            @pl.loop(0, rows // step)
            def _(t):
                b_ref[...] = jnp.maximum(b_ref[...], jnp.max(scores(y_ref, xa_ref, t), axis=0, keepdims=True))

        sum_ref[...] = jnp.zeros((1, n), F32)
        for k, y_ref, k_ref in sides:

            @pl.loop(0, rows // step)
            def _(t):
                value = jnp.exp2((scores(y_ref, xa_ref, t) - b_ref[...]) * scale)
                sum_ref[...] = sum_ref[...] + jnp.sum(value, axis=0, keepdims=True)

        b_ref[...] = (mass - log_nx - jnp.log(sum_ref[...])) * (LOG2E / scale) - b_ref[...]
        xb_ref[:width, :] = xa_ref[:width, :]
        xb_ref[width:, :] = extras_x(rows_index(n), b_ref[...], mass).astype(BF16)
        omega_ref[...] = jnp.ones((1, n), F32)
        for k, y_ref, k_ref in sides:

            @pl.loop(0, rows // step)
            def _(t):
                z = scores(y_ref, xb_ref, t)
                peak = jnp.max(z, axis=1, keepdims=True)
                value = jnp.exp2((z - peak) * scale)
                k_ref[pl.ds(pl.multiple_of(t * LANES, LANES), LANES), :] = value.astype(BF16)
                place = pl.ds(pl.multiple_of(k * half + t * LANES, LANES), LANES)
                mu_ref[:, place] = to_row(scale * peak)
                lse_ref[:, place] = to_row(scale * peak + jnp.log(jnp.sum(value, axis=1, keepdims=True)) * LOG2E)

    lse = to_lanes(other_order(lse_ref[...]))
    for k in range(2 * rows):
        l_ref[k] = lse


def stack(out_ref, width, points, factor):
    moved = points.astype(F32) * factor
    high = moved.astype(BF16)
    out_ref[:width, :] = high
    out_ref[width : 2 * width, :] = (moved - high.astype(F32)).astype(BF16)
    one, two, three = pieces(factor)
    index = lax.broadcasted_iota(jnp.int32, (PAD, factor.shape[1]), 0)
    out_ref[2 * width :, :] = select(index, {0: one, 1: two, 2: three}).astype(BF16)


def unstack(product, width):
    ext = product[2 * width :]
    return product[:width] + product[width : 2 * width], (ext[0:1] + ext[1:2]) + ext[2:3]


def second_kernel(
    log_nx, log_ny, xa_ref, omega_ref, mu_ref, l_ref, ym_ref, yo_ref, km_ref, ko_ref,
    r_ref, wr_ref, v_ref, c_ref, xs_ref, sum_ref, send_ref,
):
    width = xa_ref.shape[0] - EXT
    half = ym_ref.shape[1]
    kappa = kappa_of(width)
    scale = kappa * LOG2E
    l_all = l_ref[...]
    peak = jnp.max(l_all, axis=0)
    total = jnp.sum(jnp.exp2(l_all - peak[None]), axis=0)
    lse2 = other_order(from_lanes(peak + jnp.log(total) * LOG2E))
    old = jnp.concatenate([ym_ref[width:, :], yo_ref[width:, :]], axis=1).astype(F32)
    lb2 = (old[6:7] - log_ny) * LOG2E
    c_ref[...] = to_lanes(sum_pieces(old) + (lb2 - lse2) / scale)
    v = jnp.exp2(mu_ref[...] + (lb2 - lse2))
    v_ref[...] = v
    v_mine, v_other = halves(v)
    left = piece_rows(v)
    rowsum = jnp.dot(left[:, :half], km_ref[...], preferred_element_type=F32) + jnp.dot(
        left[:, half:], ko_ref[...], preferred_element_type=F32
    )
    omega = omega_ref[...]
    rowsum = sum_pieces(rowsum) * omega
    mass = xa_ref[width:, :].astype(F32)[7:8]
    r = jnp.exp(mass - log_nx) / rowsum
    r_ref[...] = r
    wr_ref[...] = r * omega
    stack(xs_ref, width, xa_ref[:width, :], r * omega)
    totals = []
    for k in range(half // TILE):
        t = slice(k * TILE, (k + 1) * TILE)
        product = lax.dot_general(xs_ref[...], ko_ref[t, :], ACROSS, preferred_element_type=F32)
        moment, total = unstack(product, width)
        total = total * v_other[:, t]
        totals.append(total)
        part = yo_ref[:width, t].astype(F32) * total - moment * v_other[:, t]
        send_ref[:width, t] = part.astype(BF16)
    s_other = jnp.concatenate(totals, axis=1)
    ext = lax.dot_general(xs_ref[2 * width :, :], km_ref[...], ACROSS, preferred_element_type=F32)
    s_mine = sum_pieces(ext) * v_mine
    sum_ref[...] = jnp.concatenate([s_mine, s_other], axis=1)
    high_m, high_o = s_mine.astype(BF16).astype(F32), s_other.astype(BF16).astype(F32)
    index = lax.broadcasted_iota(jnp.int32, (PAD, half), 0)
    ext = select(index, {0: high_m, 1: high_o, 2: s_mine - high_m, 3: s_other - high_o})
    send_ref[width:, :] = ext.astype(BF16)


def keep_kernel(xa_ref, xs_ref, v_ref, sum_ref, ym_ref, km_ref, keep_ref, norm_ref):
    width, half = keep_ref.shape
    for k in range(half // TILE):
        t = slice(k * TILE, (k + 1) * TILE)
        product = lax.dot_general(xs_ref[: 2 * width, :], km_ref[t, :], ACROSS, preferred_element_type=F32)
        moment = product[:width] + product[width:]
        keep_ref[:, t] = ym_ref[:width, t].astype(F32) * sum_ref[:, t] - moment * v_ref[:, t]
    xf = xa_ref[:width, :].astype(F32)
    norm_ref[...] = jnp.sum(xf * xf, axis=0, keepdims=True)


def add_kernel(keep_ref, sum_ref, got_ref, out_ref):
    width, half = keep_ref.shape
    rows = out_ref.shape[0]
    yd = half // rows
    base = yd * width // LANES
    ext = got_ref[width:, :].astype(F32)
    other = jnp.concatenate([ext[1:2] + ext[3:4], ext[0:1] + ext[2:3]], axis=1)
    sums = sums_out(to_lanes(sum_ref[...] + other)).astype(BF16)
    total = (keep_ref[...] + got_ref[:width, :].astype(F32)).T
    for r in range(rows):
        out_ref[r, :base, :] = pack(total[r * yd : (r + 1) * yd, :]).astype(BF16)
        out_ref[r, base:, :] = sums


def own_part(ref, yd):
    block = lax.axis_index("row")
    fit = LANES // yd
    row = ref[pl.ds(block // fit, 1), :]
    out = row[:, :yd]
    for k in range(1, fit):
        out = jnp.where(block % fit == k, row[:, k * yd : (k + 1) * yd], out)
    return out


def last_kernel(
    log_nx, log_ny, xa_ref, norm_ref, b_ref, r_ref, wr_ref, v_ref, c_ref, got_ref, ym_ref, yo_ref, km_ref, ko_ref, y_ref,
    f_hbm, pot_hbm, gx_hbm, gy_hbm, f_ref, pot_ref, gx_ref, gy_ref, ys_ref, sum_ref, sems,
):
    width, n = gx_ref.shape
    ny = v_ref.shape[1]
    yd = y_ref.shape[1]
    base = yd * width // LANES
    count = ny // LANES
    kappa = kappa_of(width)
    moves = []

    def leave(source, target):
        move = pltpu.make_async_copy(source, target, sems.at[len(moves)])
        move.start()
        moves.append(move)

    mass = xa_ref[width:, :].astype(F32)[7:8]
    log_row = mass - log_nx - jnp.log(r_ref[...])
    f_ref[...] = norm_ref[...] / width + EPSILON * (kappa * b_ref[...] - log_row)
    leave(f_ref, f_hbm)
    total = got_ref[0].astype(F32)
    for k in range(1, got_ref.shape[0]):
        total = total + got_ref[k].astype(F32)
    sums = total[base : base + count] + total[base + count : base + 2 * count]
    sum_ref[...] = sums
    colsum = own_part(sum_ref, yd)
    c_term = own_part(c_ref, yd)
    own = y_ref[0].astype(F32)
    gy_ref[...] = unpack(total[:base], yd, width) * (
        jnp.exp(own[:, width + 6 : width + 7]) * to_column(1.0 / colsum)
    )
    leave(gy_ref, gy_hbm)
    norm = to_row(jnp.sum(own[:, :width] * own[:, :width], axis=1, keepdims=True))
    pot_ref[...] = norm / width - EPSILON * (jnp.log(colsum) - kappa * c_term)
    leave(pot_ref, pot_hbm)
    half = ny // 2
    yt = jnp.concatenate([ym_ref[...], yo_ref[...]], axis=1)
    mass = yt[width:].astype(F32)[6:7]
    q = v_ref[...] * jnp.exp(mass + log_nx - jnp.log(from_lanes(sums)))
    stack(ys_ref, width, yt[:width], q)
    for k in range(n // TILE):
        t = slice(k * TILE, (k + 1) * TILE)
        product = jnp.dot(ys_ref[:, :half], km_ref[:, t], preferred_element_type=F32) + jnp.dot(
            ys_ref[:, half:], ko_ref[:, t], preferred_element_type=F32
        )
        moved, weight = unstack(product, width)
        gx_ref[:, t] = (xa_ref[:width, t].astype(F32) * weight - moved) * (wr_ref[:, t] * (1.0 / ny))
        leave(gx_ref.at[:, t], gx_hbm.at[:, t])
    for move in moves:
        move.wait()


def call(kernel, outs, scratch, limit, *args, space=pltpu.VMEM, out_space=pltpu.VMEM, cost=None):
    return pl.pallas_call(
        kernel,
        out_shape=outs,
        in_specs=[pl.BlockSpec(memory_space=space)] * len(args),
        out_specs=jax.tree.map(lambda _: pl.BlockSpec(memory_space=out_space), outs),
        scratch_shapes=scratch,
        cost_estimate=cost,
        compiler_params=pltpu.CompilerParams(vmem_limit_bytes=limit),
    )(*args)


def shape(dims, dtype=F32):
    return jax.ShapeDtypeStruct(dims, dtype)


def swap(value):
    return lax.ppermute(value, "col", [(0, 1), (1, 0)])


def on_device(points_x, points_y, mass_x, mass_y):
    n, width = points_x.shape
    yd = points_y.shape[0]
    rows = lax.axis_size("row")
    ny = 2 * rows * yd
    half = ny // 2
    count = ny // LANES
    log_nx, log_ny = math.log(n * 2 * rows), math.log(ny)
    depth = width + EXT
    limit = (20 if ny <= 1024 else 56) * 1024 * 1024
    extra = sums_rows(ny)
    run = functools.partial
    vmem = pltpu.VMEM
    slots = 4 if ny <= 1024 else 1
    ones = call(
        ones_kernel, shape((yd, EXT)), [], limit,
        cost=pl.CostEstimate(flops=4 * 10**9, bytes_accessed=10000, transcendentals=0),
    )
    y_own = call(
        run(prep_kernel, log_ny), shape((rows, yd, depth), BF16), [], limit, points_y, mass_y.reshape(1, yd), ones,
        cost=pl.CostEstimate(flops=4 * 10**9, bytes_accessed=400000, transcendentals=0),
    )
    y_mine = lax.all_to_all(y_own, "row", 0, 0, tiled=True)
    y_other = swap(y_mine)
    xa, yt_mine, base, total, kept_mine = call(
        half_kernel,
        (
            shape((depth, n), BF16), shape((depth, half), BF16), shape((1, n)), shape((1, n)),
            shape((half, n), BF16),
        ),
        [vmem((slots, half, TILE), F32)],
        limit, points_x.T, mass_x.reshape(n // LANES, LANES), y_mine,
    )
    yt_other, kept_mine, kept_other, b_term, omega, mu, lse = call(
        run(first_kernel, log_nx),
        (
            shape((depth, half), BF16), shape((half, n), BF16), shape((half, n), BF16), shape((1, n)),
            shape((1, n)), shape((1, ny)), shape((2 * rows, count, LANES)),
        ),
        [vmem((depth, n), BF16), vmem((slots, half, TILE), F32), vmem((1, n), F32), vmem((1, ny), F32), pltpu.SemaphoreType.DMA],
        limit, xa, y_mine, y_other, base, total, kept_mine,
    )
    lse = lax.all_to_all(lse, AXES, 0, 0, tiled=True)
    r, wr, v, c_term, xs, sums, send = call(
        run(second_kernel, log_nx, log_ny),
        (
            shape((1, n)), shape((1, n)), shape((1, ny)), shape((count, LANES)),
            shape((2 * width + PAD, n), BF16), shape((1, ny)), shape((width + PAD, half), BF16),
        ),
        [], limit, xa, omega, mu, lse, yt_mine, yt_other, kept_mine, kept_other,
    )
    got = swap(send)
    keep, norm = call(
        keep_kernel, (shape((width, half)), shape((1, n))), [], limit, xa, xs, v, sums, yt_mine, kept_mine
    )
    part = call(
        add_kernel, shape((rows, yd * width // LANES + extra, LANES), BF16), [], limit, keep, sums, got
    )
    part = lax.all_to_all(part, "row", 0, 0, tiled=True)
    f_pot, g_pot, grad_xt, grad_y = call(
        run(last_kernel, log_nx, log_ny),
        (shape((1, n)), shape((1, yd)), shape((width, n)), shape((yd, width))),
        [
            vmem((1, n), F32), vmem((1, yd), F32), vmem((width, n), F32), vmem((yd, width), F32),
            vmem((2 * width + PAD, ny), BF16), vmem((count, LANES), F32),
            pltpu.SemaphoreType.DMA((3 + n // TILE,)),
        ],
        limit, xa, norm, b_term, r, wr, v, c_term, part, yt_mine, yt_other, kept_mine, kept_other, y_own,
        out_space=pl.ANY,
    )
    return f_pot.reshape(n), g_pot.reshape(yd), grad_xt.T, grad_y


def solution(mesh):
    in_specs = (
        P(("groups", "row", "col"), None),
        P(("groups", "col", "row"), None),
        P(("groups", "row", "col")),
        P(("groups", "col", "row")),
    )
    out_specs = (
        P(("groups", "row", "col")),
        P(("groups", "col", "row")),
        P(("groups", "row", "col"), None),
        P(("groups", "col", "row"), None),
    )
    return jax.shard_map(
        on_device, mesh=mesh, in_specs=in_specs, out_specs=out_specs, check_vma=False
    )
```

```python
import functools
import math

import jax
import jax.numpy as jnp
from jax import lax
from jax.experimental import pallas as pl
from jax.experimental.pallas import tpu as pltpu
from jax.sharding import PartitionSpec as P

ITERS = 2
EPSILON = 0.02
LOG2E = math.log2(math.e)
TILE = 256
STEP = 32
EXT = 32
PAD = 16
LANES = 128
LIFT = 40.0
TINY = 1e-31
HUGE = 1e35
ACROSS = (((1,), (1,)), ((), ()))
AXES = ("row", "col")
F32 = jnp.float32
BF16 = jnp.bfloat16


def kappa_of(width):
    return 2.0 / (width * EPSILON)


def pieces(value):
    high = value.astype(BF16).astype(F32)
    rest = value - high
    mid = rest.astype(BF16).astype(F32)
    return high, mid, rest - mid


def select(index, values):
    out = jnp.zeros(index.shape, F32)
    for k, value in values.items():
        out = jnp.where(index == k, value, out)
    return out


def extras_x(index, b_term):
    high, mid, low = pieces(b_term)
    return select(index, {0: 1.0, 1: 1.0, 2: 1.0, 3: high, 4: mid, 5: low})


def rows_index(columns):
    return lax.broadcasted_iota(jnp.int32, (EXT, columns), 0)


def to_column(row):
    size = row.shape[1]
    eye = lax.broadcasted_iota(jnp.int32, (size, size), 0) == lax.broadcasted_iota(jnp.int32, (size, size), 1)
    return jnp.sum(jnp.where(eye, row, 0.0), axis=1, keepdims=True)


def to_row(column):
    size = column.shape[0]
    eye = lax.broadcasted_iota(jnp.int32, (size, size), 0) == lax.broadcasted_iota(jnp.int32, (size, size), 1)
    return jnp.sum(jnp.where(eye, column, 0.0), axis=0, keepdims=True)


def for_tiles(total, product, z_ref, use):
    count = total // TILE
    slots = z_ref.shape[0]
    if count <= slots:
        for t in range(count):
            z_ref[t] = product(pl.ds(t * TILE, TILE))
        for t in range(count):
            use(pl.ds(t * TILE, TILE), z_ref.at[t])
    else:

        @pl.loop(0, count)
        def _(t):
            tile = pl.ds(pl.multiple_of(t * TILE, TILE), TILE)
            z_ref[0] = product(tile)
            use(tile, z_ref.at[0])


def max_down(z_ref, rows):
    peak = z_ref[0:STEP, :]
    for r in range(STEP, rows, STEP):
        peak = jnp.maximum(peak, z_ref[r : r + STEP, :])
    return jnp.max(peak, axis=0, keepdims=True)


def exp_sum_down(z_ref, rows, scale, shift, keep=None):
    total = jnp.zeros((STEP, TILE), F32)
    for r in range(0, rows, STEP):
        value = jnp.exp2((z_ref[r : r + STEP, :] - shift) * scale)
        total = total + value
        if keep is not None:
            keep(r, value)
    return jnp.sum(total, axis=0, keepdims=True)


def to_lanes(row):
    return jnp.concatenate([row[:, k : k + LANES] for k in range(0, row.shape[1], LANES)], axis=0)


def from_lanes(block):
    return jnp.concatenate([block[k : k + 1] for k in range(block.shape[0])], axis=1)


def sums_rows(ny):
    return -(-2 * ny // LANES // 16) * 16


def sums_out(sums):
    high = sums.astype(BF16).astype(F32)
    spare = sums_rows(sums.size) - 2 * sums.shape[0]
    return jnp.concatenate([high, sums - high] + [jnp.zeros((spare, LANES), F32)] * (spare > 0), axis=0)


def pack(block):
    rows, width = block.shape
    base = rows * width // LANES
    spare = LANES - width
    side = [block[base:, k : k + spare] for k in range(0, width, spare)]
    return jnp.concatenate([block[:base], jnp.concatenate(side, axis=0)], axis=1)


def unpack(block, rows, width):
    base = block.shape[0]
    rest = rows - base
    side = [block[k : k + rest, width:] for k in range(0, base, rest)]
    return jnp.concatenate([block[:, :width], jnp.concatenate(side, axis=1)], axis=0)


def ones_kernel(ext_ref):
    index = lax.broadcasted_iota(jnp.int32, ext_ref.shape, 1)
    ext_ref[...] = select(index, {3: 1.0, 4: 1.0, 5: 1.0})


def prep_kernel(log_nx, log_ny, y_ref, my_ref, mx_ref, ones_ref, ya_ref, la_ref):
    la_ref[...] = from_lanes(mx_ref[...].astype(F32)) - log_nx
    width = y_ref.shape[1]
    y = y_ref[...]
    yf = y.astype(F32)
    norm = jnp.sum(yf * yf, axis=1, keepdims=True)
    mass = to_column(my_ref[...].astype(F32))
    c_term = (mass - log_ny) / kappa_of(width) - 0.5 * norm
    high, mid, low = pieces(c_term)
    index = lax.broadcasted_iota(jnp.int32, ones_ref.shape, 1)
    ext = (ones_ref[...] + select(index, {0: high, 1: mid, 2: low, 6: mass})).astype(BF16)
    for k in range(ya_ref.shape[0]):
        ya_ref[k, :, :width] = y
        ya_ref[k, :, width:] = ext


def halves(row):
    half = row.shape[1] // 2
    return row[:, :half], row[:, half:]


def other_order(row):
    mine, other = halves(row)
    return jnp.where(lax.axis_index("col") == 0, row, jnp.concatenate([other, mine], axis=1))


def piece_rows(row):
    one, two, three = pieces(row)
    index = lax.broadcasted_iota(jnp.int32, (PAD, row.shape[1]), 0)
    return select(index, {0: one, 1: two, 2: three}).astype(BF16)


def sum_pieces(block):
    return (block[0:1] + block[1:2]) + block[2:3]


def half_kernel(xt_ref, mine_ref, xa_ref, yt_ref, base_ref, total_ref, k_ref, z_ref):
    rows, yd, depth = mine_ref.shape
    width, n = xt_ref.shape
    half = rows * yd
    scale = kappa_of(width) * LOG2E
    xa_ref[:width, :] = xt_ref[...]
    xa_ref[width:, :] = extras_x(rows_index(n), jnp.zeros((1, n), F32)).astype(BF16)
    mine = mine_ref[...].reshape(half, depth)

    def product(t):
        return jnp.dot(mine, xa_ref[:, t], preferred_element_type=F32)

    def use(t, z):
        def keep(r, value):
            k_ref[r : r + STEP, t] = value.astype(BF16)

        base = max_down(z, half) - LIFT / scale
        base_ref[:, t] = base
        total_ref[:, t] = exp_sum_down(z, half, scale, base, keep)

    for_tiles(n, product, z_ref, use)
    yt_ref[...] = mine.T


def first_kernel(
    xa_ref, la_ref, mine_ref, other_ref, base_ref, total_ref, km0_ref,
    yt_ref, km_ref, ko_ref, b_ref, omega_ref, mu_ref, l_ref, xb_ref, z_ref, sum_ref, lse_ref, sem,
):
    rows, yd, depth = other_ref.shape
    n = xa_ref.shape[1]
    width = depth - EXT
    half = rows * yd
    scale = kappa_of(width) * LOG2E
    other = other_ref[...].reshape(half, depth)
    move = pltpu.make_async_copy(km0_ref, km_ref, sem)
    move.start()

    def product(t):
        return jnp.dot(other, xa_ref[:, t], preferred_element_type=F32)

    def use(t, z):
        def keep(r, value):
            ko_ref[r : r + STEP, t] = value.astype(BF16)

        sum_ref[:, t] = exp_sum_down(z, half, scale, base_ref[:, t], keep) + total_ref[:, t]

    for_tiles(n, product, z_ref, use)
    yt_ref[...] = other.T
    log_a = la_ref[...]
    total = sum_ref[...]
    b_ref[...] = (log_a - jnp.log(total)) * (LOG2E / scale) - base_ref[...]
    omega = jnp.exp(log_a) * (2.0**LIFT / total)
    omega_ref[...] = omega
    left = piece_rows(omega)
    move.wait()
    sums = jnp.concatenate(
        [
            sum_pieces(lax.dot_general(left, ref[...], ACROSS, preferred_element_type=F32))
            for ref in (km_ref, ko_ref)
        ],
        axis=1,
    )
    lse_ref[...] = jnp.log(sums) * LOG2E - LIFT
    mu_ref[...] = jnp.full(mu_ref.shape, -LIFT, F32)

    @pl.when(jnp.logical_not((jnp.max(total) < HUGE) & (jnp.min(sums) > TINY)))
    def _():
        step = LANES // yd
        sides = ((0, mine_ref, km_ref), (1, other_ref, ko_ref))

        def scores(y_ref, x_ref, t):
            y = y_ref[pl.ds(t * step, step)].reshape(LANES, depth)
            return jnp.dot(y, x_ref[...], preferred_element_type=F32)

        b_ref[...] = jnp.full((1, n), -jnp.inf, F32)
        for k, y_ref, k_ref in sides:

            @pl.loop(0, rows // step)
            def _(t):
                b_ref[...] = jnp.maximum(b_ref[...], jnp.max(scores(y_ref, xa_ref, t), axis=0, keepdims=True))

        sum_ref[...] = jnp.zeros((1, n), F32)
        for k, y_ref, k_ref in sides:

            @pl.loop(0, rows // step)
            def _(t):
                value = jnp.exp2((scores(y_ref, xa_ref, t) - b_ref[...]) * scale)
                sum_ref[...] = sum_ref[...] + jnp.sum(value, axis=0, keepdims=True)

        b_ref[...] = (log_a - jnp.log(sum_ref[...])) * (LOG2E / scale) - b_ref[...]
        xb_ref[:width, :] = xa_ref[:width, :]
        xb_ref[width:, :] = extras_x(rows_index(n), b_ref[...]).astype(BF16)
        omega_ref[...] = jnp.ones((1, n), F32)
        for k, y_ref, k_ref in sides:

            @pl.loop(0, rows // step)
            def _(t):
                z = scores(y_ref, xb_ref, t)
                peak = jnp.max(z, axis=1, keepdims=True)
                value = jnp.exp2((z - peak) * scale)
                k_ref[pl.ds(pl.multiple_of(t * LANES, LANES), LANES), :] = value.astype(BF16)
                place = pl.ds(pl.multiple_of(k * half + t * LANES, LANES), LANES)
                mu_ref[:, place] = to_row(scale * peak)
                lse_ref[:, place] = to_row(scale * peak + jnp.log(jnp.sum(value, axis=1, keepdims=True)) * LOG2E)

    lse = to_lanes(other_order(lse_ref[...]))
    for k in range(2 * rows):
        l_ref[k] = lse


def stack(out_ref, width, points, factor):
    moved = points.astype(F32) * factor
    high = moved.astype(BF16)
    out_ref[:width, :] = high
    out_ref[width : 2 * width, :] = (moved - high.astype(F32)).astype(BF16)
    one, two, three = pieces(factor)
    index = lax.broadcasted_iota(jnp.int32, (PAD, factor.shape[1]), 0)
    out_ref[2 * width :, :] = select(index, {0: one, 1: two, 2: three}).astype(BF16)


def unstack(product, width):
    ext = product[2 * width :]
    return product[:width] + product[width : 2 * width], (ext[0:1] + ext[1:2]) + ext[2:3]


def second_kernel(
    log_ny, xa_ref, la_ref, omega_ref, mu_ref, l_ref, ym_ref, yo_ref, km_ref, ko_ref,
    r_ref, wr_ref, v_ref, c_ref, xs_ref, sum_ref, send_ref,
):
    width = xa_ref.shape[0] - EXT
    half = ym_ref.shape[1]
    kappa = kappa_of(width)
    scale = kappa * LOG2E
    l_all = l_ref[...]
    peak = jnp.max(l_all, axis=0)
    total = jnp.sum(jnp.exp2(l_all - peak[None]), axis=0)
    lse2 = other_order(from_lanes(peak + jnp.log(total) * LOG2E))
    old = jnp.concatenate([ym_ref[width:, :], yo_ref[width:, :]], axis=1).astype(F32)
    lb2 = (old[6:7] - log_ny) * LOG2E
    c_ref[...] = to_lanes(sum_pieces(old) + (lb2 - lse2) / scale)
    v = jnp.exp2(mu_ref[...] + (lb2 - lse2))
    v_ref[...] = v
    v_mine, v_other = halves(v)
    left = piece_rows(v)
    rowsum = jnp.dot(left[:, :half], km_ref[...], preferred_element_type=F32) + jnp.dot(
        left[:, half:], ko_ref[...], preferred_element_type=F32
    )
    omega = omega_ref[...]
    rowsum = sum_pieces(rowsum) * omega
    r = jnp.exp(la_ref[...]) / rowsum
    r_ref[...] = r
    wr_ref[...] = r * omega
    stack(xs_ref, width, xa_ref[:width, :], r * omega)
    totals = []
    for k in range(half // TILE):
        t = slice(k * TILE, (k + 1) * TILE)
        product = lax.dot_general(xs_ref[...], ko_ref[t, :], ACROSS, preferred_element_type=F32)
        moment, total = unstack(product, width)
        total = total * v_other[:, t]
        totals.append(total)
        part = yo_ref[:width, t].astype(F32) * total - moment * v_other[:, t]
        send_ref[:width, t] = part.astype(BF16)
    s_other = jnp.concatenate(totals, axis=1)
    ext = lax.dot_general(xs_ref[2 * width :, :], km_ref[...], ACROSS, preferred_element_type=F32)
    s_mine = sum_pieces(ext) * v_mine
    sum_ref[...] = jnp.concatenate([s_mine, s_other], axis=1)
    high_m, high_o = s_mine.astype(BF16).astype(F32), s_other.astype(BF16).astype(F32)
    index = lax.broadcasted_iota(jnp.int32, (PAD, half), 0)
    ext = select(index, {0: high_m, 1: high_o, 2: s_mine - high_m, 3: s_other - high_o})
    send_ref[width:, :] = ext.astype(BF16)


def keep_kernel(xa_ref, xs_ref, v_ref, sum_ref, ym_ref, km_ref, keep_ref, norm_ref):
    width, half = keep_ref.shape
    for k in range(half // TILE):
        t = slice(k * TILE, (k + 1) * TILE)
        product = lax.dot_general(xs_ref[: 2 * width, :], km_ref[t, :], ACROSS, preferred_element_type=F32)
        moment = product[:width] + product[width:]
        keep_ref[:, t] = ym_ref[:width, t].astype(F32) * sum_ref[:, t] - moment * v_ref[:, t]
    xf = xa_ref[:width, :].astype(F32)
    norm_ref[...] = jnp.sum(xf * xf, axis=0, keepdims=True)


def add_kernel(keep_ref, sum_ref, got_ref, out_ref):
    width, half = keep_ref.shape
    rows = out_ref.shape[0]
    yd = half // rows
    base = yd * width // LANES
    ext = got_ref[width:, :].astype(F32)
    other = jnp.concatenate([ext[1:2] + ext[3:4], ext[0:1] + ext[2:3]], axis=1)
    sums = sums_out(to_lanes(sum_ref[...] + other)).astype(BF16)
    total = (keep_ref[...] + got_ref[:width, :].astype(F32)).T
    for r in range(rows):
        out_ref[r, :base, :] = pack(total[r * yd : (r + 1) * yd, :]).astype(BF16)
        out_ref[r, base:, :] = sums


def own_part(ref, yd):
    block = lax.axis_index("row")
    fit = LANES // yd
    row = ref[pl.ds(block // fit, 1), :]
    out = row[:, :yd]
    for k in range(1, fit):
        out = jnp.where(block % fit == k, row[:, k * yd : (k + 1) * yd], out)
    return out


def last_kernel(
    log_nx, xa_ref, la_ref, norm_ref, b_ref, r_ref, wr_ref, v_ref, c_ref, got_ref, ym_ref, yo_ref, km_ref, ko_ref, y_ref,
    f_hbm, pot_hbm, gx_hbm, gy_hbm, f_ref, pot_ref, gx_ref, gy_ref, ys_ref, sum_ref, sems,
):
    width, n = gx_ref.shape
    ny = v_ref.shape[1]
    yd = y_ref.shape[1]
    base = yd * width // LANES
    count = ny // LANES
    kappa = kappa_of(width)
    moves = []

    def leave(source, target):
        move = pltpu.make_async_copy(source, target, sems.at[len(moves)])
        move.start()
        moves.append(move)

    log_row = la_ref[...] - jnp.log(r_ref[...])
    f_ref[...] = norm_ref[...] / width + EPSILON * (kappa * b_ref[...] - log_row)
    leave(f_ref, f_hbm)
    total = got_ref[0].astype(F32)
    for k in range(1, got_ref.shape[0]):
        total = total + got_ref[k].astype(F32)
    sums = total[base : base + count] + total[base + count : base + 2 * count]
    sum_ref[...] = sums
    colsum = own_part(sum_ref, yd)
    c_term = own_part(c_ref, yd)
    own = y_ref[0].astype(F32)
    gy_ref[...] = unpack(total[:base], yd, width) * (
        jnp.exp(own[:, width + 6 : width + 7]) * to_column(1.0 / colsum)
    )
    leave(gy_ref, gy_hbm)
    norm = to_row(jnp.sum(own[:, :width] * own[:, :width], axis=1, keepdims=True))
    pot_ref[...] = norm / width - EPSILON * (jnp.log(colsum) - kappa * c_term)
    leave(pot_ref, pot_hbm)
    half = ny // 2
    yt = jnp.concatenate([ym_ref[...], yo_ref[...]], axis=1)
    mass = yt[width:].astype(F32)[6:7]
    q = v_ref[...] * jnp.exp(mass + log_nx - jnp.log(from_lanes(sums)))
    stack(ys_ref, width, yt[:width], q)
    for k in range(n // TILE):
        t = slice(k * TILE, (k + 1) * TILE)
        product = jnp.dot(ys_ref[:, :half], km_ref[:, t], preferred_element_type=F32) + jnp.dot(
            ys_ref[:, half:], ko_ref[:, t], preferred_element_type=F32
        )
        moved, weight = unstack(product, width)
        gx_ref[:, t] = (xa_ref[:width, t].astype(F32) * weight - moved) * (wr_ref[:, t] * (1.0 / ny))
        leave(gx_ref.at[:, t], gx_hbm.at[:, t])
    for move in moves:
        move.wait()


def call(kernel, outs, scratch, limit, *args, space=pltpu.VMEM, out_space=pltpu.VMEM, cost=None):
    return pl.pallas_call(
        kernel,
        out_shape=outs,
        in_specs=[pl.BlockSpec(memory_space=space)] * len(args),
        out_specs=jax.tree.map(lambda _: pl.BlockSpec(memory_space=out_space), outs),
        scratch_shapes=scratch,
        cost_estimate=cost,
        compiler_params=pltpu.CompilerParams(vmem_limit_bytes=limit),
    )(*args)


def shape(dims, dtype=F32):
    return jax.ShapeDtypeStruct(dims, dtype)


def swap(value):
    return lax.ppermute(value, "col", [(0, 1), (1, 0)])


def on_device(points_x, points_y, mass_x, mass_y):
    n, width = points_x.shape
    yd = points_y.shape[0]
    rows = lax.axis_size("row")
    ny = 2 * rows * yd
    half = ny // 2
    count = ny // LANES
    log_nx, log_ny = math.log(n * 2 * rows), math.log(ny)
    depth = width + EXT
    limit = (20 if ny <= 1024 else 56) * 1024 * 1024
    extra = sums_rows(ny)
    run = functools.partial
    vmem = pltpu.VMEM
    slots = 4 if ny <= 1024 else 1
    ones = call(
        ones_kernel, shape((yd, EXT)), [], limit,
        cost=pl.CostEstimate(flops=4 * 10**9, bytes_accessed=10000, transcendentals=0),
    )
    y_own, log_a = call(
        run(prep_kernel, log_nx, log_ny), (shape((rows, yd, depth), BF16), shape((1, n))), [], limit,
        points_y, mass_y.reshape(1, yd), mass_x.reshape(n // LANES, LANES), ones,
        cost=pl.CostEstimate(flops=4 * 10**9, bytes_accessed=400000, transcendentals=0),
    )
    y_mine = lax.all_to_all(y_own, "row", 0, 0, tiled=True)
    y_other = swap(y_mine)
    xa, yt_mine, base, total, kept_mine = call(
        half_kernel,
        (
            shape((depth, n), BF16), shape((depth, half), BF16), shape((1, n)), shape((1, n)),
            shape((half, n), BF16),
        ),
        [vmem((slots, half, TILE), F32)],
        limit, points_x.T, y_mine,
    )
    yt_other, kept_mine, kept_other, b_term, omega, mu, lse = call(
        first_kernel,
        (
            shape((depth, half), BF16), shape((half, n), BF16), shape((half, n), BF16), shape((1, n)),
            shape((1, n)), shape((1, ny)), shape((2 * rows, count, LANES)),
        ),
        [vmem((depth, n), BF16), vmem((slots, half, TILE), F32), vmem((1, n), F32), vmem((1, ny), F32), pltpu.SemaphoreType.DMA],
        limit, xa, log_a, y_mine, y_other, base, total, kept_mine,
    )
    lse = lax.all_to_all(lse, AXES, 0, 0, tiled=True)
    r, wr, v, c_term, xs, sums, send = call(
        run(second_kernel, log_ny),
        (
            shape((1, n)), shape((1, n)), shape((1, ny)), shape((count, LANES)),
            shape((2 * width + PAD, n), BF16), shape((1, ny)), shape((width + PAD, half), BF16),
        ),
        [], limit, xa, log_a, omega, mu, lse, yt_mine, yt_other, kept_mine, kept_other,
    )
    got = swap(send)
    keep, norm = call(
        keep_kernel, (shape((width, half)), shape((1, n))), [], limit, xa, xs, v, sums, yt_mine, kept_mine
    )
    part = call(
        add_kernel, shape((rows, yd * width // LANES + extra, LANES), BF16), [], limit, keep, sums, got
    )
    part = lax.all_to_all(part, "row", 0, 0, tiled=True)
    f_pot, g_pot, grad_xt, grad_y = call(
        run(last_kernel, log_nx),
        (shape((1, n)), shape((1, yd)), shape((width, n)), shape((yd, width))),
        [
            vmem((1, n), F32), vmem((1, yd), F32), vmem((width, n), F32), vmem((yd, width), F32),
            vmem((2 * width + PAD, ny), BF16), vmem((count, LANES), F32),
            pltpu.SemaphoreType.DMA((3 + n // TILE,)),
        ],
        limit, xa, log_a, norm, b_term, r, wr, v, c_term, part, yt_mine, yt_other, kept_mine, kept_other, y_own,
        out_space=pl.ANY,
    )
    return f_pot.reshape(n), g_pot.reshape(yd), grad_xt.T, grad_y


def solution(mesh):
    in_specs = (
        P(("groups", "row", "col"), None),
        P(("groups", "col", "row"), None),
        P(("groups", "row", "col")),
        P(("groups", "col", "row")),
    )
    out_specs = (
        P(("groups", "row", "col")),
        P(("groups", "col", "row")),
        P(("groups", "row", "col"), None),
        P(("groups", "col", "row"), None),
    )
    return jax.shard_map(
        on_device, mesh=mesh, in_specs=in_specs, out_specs=out_specs, check_vma=False
    )
```

```python
import functools
import math

import jax
import jax.numpy as jnp
from jax import lax
from jax.experimental import pallas as pl
from jax.experimental.pallas import tpu as pltpu
from jax.sharding import PartitionSpec as P

ITERS = 2
EPSILON = 0.02
LOG2E = math.log2(math.e)
TILE = 256
STEP = 32
EXT = 32
PAD = 16
LANES = 128
LIFT = 52.0
TINY = 1e-24
HUGE = 5e33
ACROSS = (((1,), (1,)), ((), ()))
AXES = ("row", "col")
F32 = jnp.float32
BF16 = jnp.bfloat16


def kappa_of(width):
    return 2.0 / (width * EPSILON)


def pieces(value):
    high = value.astype(BF16).astype(F32)
    rest = value - high
    mid = rest.astype(BF16).astype(F32)
    return high, mid, rest - mid


def select(index, values):
    out = jnp.zeros(index.shape, F32)
    for k, value in values.items():
        out = jnp.where(index == k, value, out)
    return out


def extras_x(index, b_term):
    high, mid, low = pieces(b_term)
    return select(index, {0: 1.0, 1: 1.0, 2: 1.0, 3: high, 4: mid, 5: low})


def rows_index(columns):
    return lax.broadcasted_iota(jnp.int32, (EXT, columns), 0)


def to_column(row):
    size = row.shape[1]
    eye = lax.broadcasted_iota(jnp.int32, (size, size), 0) == lax.broadcasted_iota(jnp.int32, (size, size), 1)
    return jnp.sum(jnp.where(eye, row, 0.0), axis=1, keepdims=True)


def to_row(column):
    size = column.shape[0]
    eye = lax.broadcasted_iota(jnp.int32, (size, size), 0) == lax.broadcasted_iota(jnp.int32, (size, size), 1)
    return jnp.sum(jnp.where(eye, column, 0.0), axis=0, keepdims=True)


def for_tiles(total, product, z_ref, use):
    count = total // TILE
    slots = z_ref.shape[0]
    if count <= slots:
        for t in range(count):
            z_ref[t] = product(pl.ds(t * TILE, TILE))
        for t in range(count):
            use(pl.ds(t * TILE, TILE), z_ref.at[t])
    else:

        @pl.loop(0, count)
        def _(t):
            tile = pl.ds(pl.multiple_of(t * TILE, TILE), TILE)
            z_ref[0] = product(tile)
            use(tile, z_ref.at[0])


def max_down(z_ref, rows):
    peak = z_ref[0:STEP, :]
    for r in range(STEP, rows, STEP):
        peak = jnp.maximum(peak, z_ref[r : r + STEP, :])
    return jnp.max(peak, axis=0, keepdims=True)


def exp_sum_down(z_ref, rows, scale, shift, keep=None):
    total = jnp.zeros((STEP, TILE), F32)
    for r in range(0, rows, STEP):
        value = jnp.exp2((z_ref[r : r + STEP, :] - shift) * scale)
        total = total + value
        if keep is not None:
            keep(r, value)
    return jnp.sum(total, axis=0, keepdims=True)


def to_lanes(row):
    return jnp.concatenate([row[:, k : k + LANES] for k in range(0, row.shape[1], LANES)], axis=0)


def from_lanes(block):
    return jnp.concatenate([block[k : k + 1] for k in range(block.shape[0])], axis=1)


def sums_rows(ny):
    return -(-2 * ny // LANES // 16) * 16


def sums_out(sums):
    high = sums.astype(BF16).astype(F32)
    spare = sums_rows(sums.size) - 2 * sums.shape[0]
    return jnp.concatenate([high, sums - high] + [jnp.zeros((spare, LANES), F32)] * (spare > 0), axis=0)


def pack(block):
    width, yd = block.shape
    base = width * yd // LANES
    return jnp.concatenate([block[k : k + base] for k in range(0, width, base)], axis=1)


def unpack(block, yd):
    return jnp.concatenate([block[:, k : k + yd] for k in range(0, LANES, yd)], axis=0)


def ones_kernel(ext_ref):
    index = lax.broadcasted_iota(jnp.int32, ext_ref.shape, 1)
    ext_ref[...] = select(index, {3: 1.0, 4: 1.0, 5: 1.0})


def prep_kernel(log_nx, log_ny, y_ref, my_ref, mx_ref, ones_ref, ya_ref, la_ref):
    la_ref[...] = from_lanes(mx_ref[...].astype(F32)) - log_nx
    width = y_ref.shape[1]
    y = y_ref[...]
    yf = y.astype(F32)
    norm = jnp.sum(yf * yf, axis=1, keepdims=True)
    mass = to_column(my_ref[...].astype(F32))
    c_term = (mass - log_ny) / kappa_of(width) - 0.5 * norm
    high, mid, low = pieces(c_term)
    index = lax.broadcasted_iota(jnp.int32, ones_ref.shape, 1)
    ext = (ones_ref[...] + select(index, {0: high, 1: mid, 2: low, 6: mass})).astype(BF16)
    for k in range(ya_ref.shape[0]):
        ya_ref[k, :, :width] = y
        ya_ref[k, :, width:] = ext


def halves(row):
    half = row.shape[1] // 2
    return row[:, :half], row[:, half:]


def other_order(row):
    mine, other = halves(row)
    return jnp.where(lax.axis_index("col") == 0, row, jnp.concatenate([other, mine], axis=1))


def piece_rows(row):
    one, two, three = pieces(row)
    index = lax.broadcasted_iota(jnp.int32, (PAD, row.shape[1]), 0)
    return select(index, {0: one, 1: two, 2: three}).astype(BF16)


def sum_pieces(block):
    return (block[0:1] + block[1:2]) + block[2:3]


def half_kernel(xt_ref, mine_ref, xa_ref, yt_ref, base_ref, total_ref, k_ref, z_ref):
    rows, yd, depth = mine_ref.shape
    width, n = xt_ref.shape
    half = rows * yd
    scale = kappa_of(width) * LOG2E
    xa_ref[:width, :] = xt_ref[...]
    xa_ref[width:, :] = extras_x(rows_index(n), jnp.zeros((1, n), F32)).astype(BF16)
    mine = mine_ref[...].reshape(half, depth)

    def product(t):
        return jnp.dot(mine, xa_ref[:, t], preferred_element_type=F32)

    def use(t, z):
        def keep(r, value):
            k_ref[r : r + STEP, t] = value.astype(BF16)

        base = max_down(z, half) - LIFT / scale
        base_ref[:, t] = base
        total_ref[:, t] = exp_sum_down(z, half, scale, base, keep)

    for_tiles(n, product, z_ref, use)
    yt_ref[...] = mine.T


def first_kernel(
    xa_ref, la_ref, mine_ref, other_ref, base_ref, total_ref, km0_ref,
    yt_ref, km_ref, ko_ref, b_ref, omega_ref, mu_ref, l_ref, xb_ref, z_ref, sum_ref, lse_ref, sem,
):
    rows, yd, depth = other_ref.shape
    n = xa_ref.shape[1]
    width = depth - EXT
    half = rows * yd
    scale = kappa_of(width) * LOG2E
    other = other_ref[...].reshape(half, depth)
    move = pltpu.make_async_copy(km0_ref, km_ref, sem)
    move.start()

    def product(t):
        return jnp.dot(other, xa_ref[:, t], preferred_element_type=F32)

    def use(t, z):
        def keep(r, value):
            ko_ref[r : r + STEP, t] = value.astype(BF16)

        sum_ref[:, t] = exp_sum_down(z, half, scale, base_ref[:, t], keep) + total_ref[:, t]

    for_tiles(n, product, z_ref, use)
    yt_ref[...] = other.T
    log_a = la_ref[...]
    total = sum_ref[...]
    b_ref[...] = (log_a - jnp.log(total)) * (LOG2E / scale) - base_ref[...]
    omega = jnp.exp(log_a) * (2.0**LIFT / total)
    omega_ref[...] = omega
    left = piece_rows(omega)
    move.wait()
    sums = jnp.concatenate(
        [
            sum_pieces(lax.dot_general(left, ref[...], ACROSS, preferred_element_type=F32))
            for ref in (km_ref, ko_ref)
        ],
        axis=1,
    )
    lse_ref[...] = jnp.log(sums) * LOG2E - LIFT
    mu_ref[...] = jnp.full(mu_ref.shape, -LIFT, F32)

    @pl.when(jnp.logical_not((jnp.max(total) < HUGE) & (jnp.min(sums) > TINY)))
    def _():
        step = LANES // yd
        sides = ((0, mine_ref, km_ref), (1, other_ref, ko_ref))

        def scores(y_ref, x_ref, t):
            y = y_ref[pl.ds(t * step, step)].reshape(LANES, depth)
            return jnp.dot(y, x_ref[...], preferred_element_type=F32)

        b_ref[...] = jnp.full((1, n), -jnp.inf, F32)
        for k, y_ref, k_ref in sides:

            @pl.loop(0, rows // step)
            def _(t):
                b_ref[...] = jnp.maximum(b_ref[...], jnp.max(scores(y_ref, xa_ref, t), axis=0, keepdims=True))

        sum_ref[...] = jnp.zeros((1, n), F32)
        for k, y_ref, k_ref in sides:

            @pl.loop(0, rows // step)
            def _(t):
                value = jnp.exp2((scores(y_ref, xa_ref, t) - b_ref[...]) * scale)
                sum_ref[...] = sum_ref[...] + jnp.sum(value, axis=0, keepdims=True)

        b_ref[...] = (log_a - jnp.log(sum_ref[...])) * (LOG2E / scale) - b_ref[...]
        xb_ref[:width, :] = xa_ref[:width, :]
        xb_ref[width:, :] = extras_x(rows_index(n), b_ref[...]).astype(BF16)
        omega_ref[...] = jnp.ones((1, n), F32)
        for k, y_ref, k_ref in sides:

            @pl.loop(0, rows // step)
            def _(t):
                z = scores(y_ref, xb_ref, t)
                peak = jnp.max(z, axis=1, keepdims=True)
                value = jnp.exp2((z - peak) * scale)
                k_ref[pl.ds(pl.multiple_of(t * LANES, LANES), LANES), :] = value.astype(BF16)
                place = pl.ds(pl.multiple_of(k * half + t * LANES, LANES), LANES)
                mu_ref[:, place] = to_row(scale * peak)
                lse_ref[:, place] = to_row(scale * peak + jnp.log(jnp.sum(value, axis=1, keepdims=True)) * LOG2E)

    lse = to_lanes(other_order(lse_ref[...]))
    for k in range(2 * rows):
        l_ref[k] = lse


def stack(out_ref, width, points, factor):
    moved = points.astype(F32) * factor
    high = moved.astype(BF16)
    out_ref[:width, :] = high
    out_ref[width : 2 * width, :] = (moved - high.astype(F32)).astype(BF16)
    one, two, three = pieces(factor)
    index = lax.broadcasted_iota(jnp.int32, (PAD, factor.shape[1]), 0)
    out_ref[2 * width :, :] = select(index, {0: one, 1: two, 2: three}).astype(BF16)


def unstack(product, width):
    ext = product[2 * width :]
    return product[:width] + product[width : 2 * width], (ext[0:1] + ext[1:2]) + ext[2:3]


def second_kernel(
    log_ny, xa_ref, la_ref, omega_ref, mu_ref, l_ref, ym_ref, yo_ref, km_ref, ko_ref,
    r_ref, wr_ref, v_ref, c_ref, xs_ref, sum_ref, send_ref,
):
    width = xa_ref.shape[0] - EXT
    half = ym_ref.shape[1]
    kappa = kappa_of(width)
    scale = kappa * LOG2E
    l_all = l_ref[...]
    peak = jnp.max(l_all, axis=0)
    total = jnp.sum(jnp.exp2(l_all - peak[None]), axis=0)
    lse2 = other_order(from_lanes(peak + jnp.log(total) * LOG2E))
    old = jnp.concatenate([ym_ref[width:, :], yo_ref[width:, :]], axis=1).astype(F32)
    lb2 = (old[6:7] - log_ny) * LOG2E
    c_ref[...] = to_lanes(sum_pieces(old) + (lb2 - lse2) / scale)
    v = jnp.exp2(mu_ref[...] + (lb2 - lse2))
    v_ref[...] = v
    v_mine, v_other = halves(v)
    left = piece_rows(v)
    rowsum = jnp.dot(left[:, :half], km_ref[...], preferred_element_type=F32) + jnp.dot(
        left[:, half:], ko_ref[...], preferred_element_type=F32
    )
    omega = omega_ref[...]
    rowsum = sum_pieces(rowsum) * omega
    r = jnp.exp(la_ref[...]) / rowsum
    r_ref[...] = r
    wr_ref[...] = r * omega
    stack(xs_ref, width, xa_ref[:width, :], r * omega)
    totals = []
    for k in range(half // TILE):
        t = slice(k * TILE, (k + 1) * TILE)
        product = lax.dot_general(xs_ref[...], ko_ref[t, :], ACROSS, preferred_element_type=F32)
        moment, total = unstack(product, width)
        total = total * v_other[:, t]
        totals.append(total)
        part = yo_ref[:width, t].astype(F32) * total - moment * v_other[:, t]
        send_ref[:width, t] = part.astype(BF16)
    s_other = jnp.concatenate(totals, axis=1)
    ext = lax.dot_general(xs_ref[2 * width :, :], km_ref[...], ACROSS, preferred_element_type=F32)
    s_mine = sum_pieces(ext) * v_mine
    sum_ref[...] = jnp.concatenate([s_mine, s_other], axis=1)
    high_m, high_o = s_mine.astype(BF16).astype(F32), s_other.astype(BF16).astype(F32)
    index = lax.broadcasted_iota(jnp.int32, (PAD, half), 0)
    ext = select(index, {0: high_m, 1: high_o, 2: s_mine - high_m, 3: s_other - high_o})
    send_ref[width:, :] = ext.astype(BF16)


def keep_kernel(log_nx, xa_ref, xs_ref, v_ref, sum_ref, ym_ref, yo_ref, km_ref, keep_ref, norm_ref, q_ref):
    width, half = keep_ref.shape
    for k in range(half // TILE):
        t = slice(k * TILE, (k + 1) * TILE)
        product = lax.dot_general(xs_ref[: 2 * width, :], km_ref[t, :], ACROSS, preferred_element_type=F32)
        moment = product[:width] + product[width:]
        keep_ref[:, t] = ym_ref[:width, t].astype(F32) * sum_ref[:, t] - moment * v_ref[:, t]
    xf = xa_ref[:width, :].astype(F32)
    norm_ref[...] = jnp.sum(xf * xf, axis=0, keepdims=True)
    mass = jnp.concatenate([ym_ref[width:, :], yo_ref[width:, :]], axis=1).astype(F32)[6:7]
    q_ref[...] = v_ref[...] * jnp.exp(mass + log_nx)


def add_kernel(keep_ref, sum_ref, got_ref, out_ref):
    width, half = keep_ref.shape
    rows = out_ref.shape[0]
    yd = half // rows
    base = yd * width // LANES
    ext = got_ref[width:, :].astype(F32)
    other = jnp.concatenate([ext[1:2] + ext[3:4], ext[0:1] + ext[2:3]], axis=1)
    sums = sums_out(to_lanes(sum_ref[...] + other)).astype(BF16)
    total = keep_ref[...] + got_ref[:width, :].astype(F32)
    for r in range(rows):
        out_ref[r, :base, :] = pack(total[:, r * yd : (r + 1) * yd]).astype(BF16)
        out_ref[r, base:, :] = sums


def own_part(ref, yd):
    block = lax.axis_index("row")
    fit = LANES // yd
    row = ref[pl.ds(block // fit, 1), :]
    out = row[:, :yd]
    for k in range(1, fit):
        out = jnp.where(block % fit == k, row[:, k * yd : (k + 1) * yd], out)
    return out


def last_kernel(
    xa_ref, la_ref, norm_ref, b_ref, r_ref, wr_ref, q_ref, c_ref, got_ref, ym_ref, yo_ref, km_ref, ko_ref, y_ref,
    f_hbm, pot_hbm, gx_hbm, gy_hbm, f_ref, pot_ref, gx_ref, gy_ref, ys_ref, sum_ref, sems,
):
    width, n = gx_ref.shape
    ny = q_ref.shape[1]
    yd = y_ref.shape[1]
    base = yd * width // LANES
    count = ny // LANES
    kappa = kappa_of(width)
    moves = []

    def leave(source, target):
        move = pltpu.make_async_copy(source, target, sems.at[len(moves)])
        move.start()
        moves.append(move)

    log_row = la_ref[...] - jnp.log(r_ref[...])
    f_ref[...] = norm_ref[...] / width + EPSILON * (kappa * b_ref[...] - log_row)
    leave(f_ref, f_hbm)
    total = got_ref[0].astype(F32)
    for k in range(1, got_ref.shape[0]):
        total = total + got_ref[k].astype(F32)
    sums = total[base : base + count] + total[base + count : base + 2 * count]
    sum_ref[...] = sums
    colsum = own_part(sum_ref, yd)
    c_term = own_part(c_ref, yd)
    own = y_ref[0].astype(F32)
    gy_ref[...] = unpack(total[:base], yd).T * (
        jnp.exp(own[:, width + 6 : width + 7]) * to_column(1.0 / colsum)
    )
    leave(gy_ref, gy_hbm)
    norm = to_row(jnp.sum(own[:, :width] * own[:, :width], axis=1, keepdims=True))
    pot_ref[...] = norm / width - EPSILON * (jnp.log(colsum) - kappa * c_term)
    leave(pot_ref, pot_hbm)
    half = ny // 2
    yt = jnp.concatenate([ym_ref[:width, :], yo_ref[:width, :]], axis=1)
    stack(ys_ref, width, yt, q_ref[...] / from_lanes(sums))
    for k in range(n // TILE):
        t = slice(k * TILE, (k + 1) * TILE)
        product = jnp.dot(ys_ref[:, :half], km_ref[:, t], preferred_element_type=F32) + jnp.dot(
            ys_ref[:, half:], ko_ref[:, t], preferred_element_type=F32
        )
        moved, weight = unstack(product, width)
        gx_ref[:, t] = (xa_ref[:width, t].astype(F32) * weight - moved) * (wr_ref[:, t] * (1.0 / ny))
        leave(gx_ref.at[:, t], gx_hbm.at[:, t])
    for move in moves:
        move.wait()


def call(kernel, outs, scratch, limit, *args, space=pltpu.VMEM, out_space=pltpu.VMEM, cost=None):
    return pl.pallas_call(
        kernel,
        out_shape=outs,
        in_specs=[pl.BlockSpec(memory_space=space)] * len(args),
        out_specs=jax.tree.map(lambda _: pl.BlockSpec(memory_space=out_space), outs),
        scratch_shapes=scratch,
        cost_estimate=cost,
        compiler_params=pltpu.CompilerParams(vmem_limit_bytes=limit),
    )(*args)


def shape(dims, dtype=F32):
    return jax.ShapeDtypeStruct(dims, dtype)


def swap(value):
    return lax.ppermute(value, "col", [(0, 1), (1, 0)])


def on_device(points_x, points_y, mass_x, mass_y):
    n, width = points_x.shape
    yd = points_y.shape[0]
    rows = lax.axis_size("row")
    ny = 2 * rows * yd
    half = ny // 2
    count = ny // LANES
    log_nx, log_ny = math.log(n * 2 * rows), math.log(ny)
    depth = width + EXT
    limit = (20 if ny <= 1024 else 56) * 1024 * 1024
    extra = sums_rows(ny)
    run = functools.partial
    vmem = pltpu.VMEM
    slots = 4 if ny <= 1024 else 1
    ones = call(
        ones_kernel, shape((yd, EXT)), [], limit,
        cost=pl.CostEstimate(flops=4 * 10**9, bytes_accessed=10000, transcendentals=0),
    )
    y_own, log_a = call(
        run(prep_kernel, log_nx, log_ny), (shape((rows, yd, depth), BF16), shape((1, n))), [], limit,
        points_y, mass_y.reshape(1, yd), mass_x.reshape(n // LANES, LANES), ones,
        cost=pl.CostEstimate(flops=4 * 10**9, bytes_accessed=400000, transcendentals=0),
    )
    y_mine = lax.all_to_all(y_own, "row", 0, 0, tiled=True)
    y_other = swap(y_mine)
    xa, yt_mine, base, total, kept_mine = call(
        half_kernel,
        (
            shape((depth, n), BF16), shape((depth, half), BF16), shape((1, n)), shape((1, n)),
            shape((half, n), BF16),
        ),
        [vmem((slots, half, TILE), F32)],
        limit, points_x.T, y_mine,
    )
    yt_other, kept_mine, kept_other, b_term, omega, mu, lse = call(
        first_kernel,
        (
            shape((depth, half), BF16), shape((half, n), BF16), shape((half, n), BF16), shape((1, n)),
            shape((1, n)), shape((1, ny)), shape((2 * rows, count, LANES)),
        ),
        [vmem((depth, n), BF16), vmem((slots, half, TILE), F32), vmem((1, n), F32), vmem((1, ny), F32), pltpu.SemaphoreType.DMA],
        limit, xa, log_a, y_mine, y_other, base, total, kept_mine,
    )
    lse = lax.all_to_all(lse, AXES, 0, 0, tiled=True)
    r, wr, v, c_term, xs, sums, send = call(
        run(second_kernel, log_ny),
        (
            shape((1, n)), shape((1, n)), shape((1, ny)), shape((count, LANES)),
            shape((2 * width + PAD, n), BF16), shape((1, ny)), shape((width + PAD, half), BF16),
        ),
        [], limit, xa, log_a, omega, mu, lse, yt_mine, yt_other, kept_mine, kept_other,
    )
    got = swap(send)
    keep, norm, q = call(
        run(keep_kernel, log_nx), (shape((width, half)), shape((1, n)), shape((1, ny))), [],
        limit, xa, xs, v, sums, yt_mine, yt_other, kept_mine,
    )
    part = call(
        add_kernel, shape((rows, yd * width // LANES + extra, LANES), BF16), [], limit, keep, sums, got
    )
    part = lax.all_to_all(part, "row", 0, 0, tiled=True)
    f_pot, g_pot, grad_xt, grad_y = call(
        last_kernel,
        (shape((1, n)), shape((1, yd)), shape((width, n)), shape((yd, width))),
        [
            vmem((1, n), F32), vmem((1, yd), F32), vmem((width, n), F32), vmem((yd, width), F32),
            vmem((2 * width + PAD, ny), BF16), vmem((count, LANES), F32),
            pltpu.SemaphoreType.DMA((3 + n // TILE,)),
        ],
        limit, xa, log_a, norm, b_term, r, wr, q, c_term, part, yt_mine, yt_other, kept_mine, kept_other, y_own,
        out_space=pl.ANY,
    )
    return f_pot.reshape(n), g_pot.reshape(yd), grad_xt.T, grad_y


def solution(mesh):
    in_specs = (
        P(("groups", "row", "col"), None),
        P(("groups", "col", "row"), None),
        P(("groups", "row", "col")),
        P(("groups", "col", "row")),
    )
    out_specs = (
        P(("groups", "row", "col")),
        P(("groups", "col", "row")),
        P(("groups", "row", "col"), None),
        P(("groups", "col", "row"), None),
    )
    return jax.shard_map(
        on_device, mesh=mesh, in_specs=in_specs, out_specs=out_specs, check_vma=False
    )
```

```python
import functools
import math

import jax
import jax.numpy as jnp
from jax import lax
from jax.experimental import pallas as pl
from jax.experimental.pallas import tpu as pltpu
from jax.sharding import PartitionSpec as P

ITERS = 2
EPSILON = 0.02
LOG2E = math.log2(math.e)
TILE = 512
STEP = 16
EXT = 32
PAD = 16
LANES = 128
LIFT = 52.0
TINY = 1e-24
HUGE = 5e33
ACROSS = (((1,), (1,)), ((), ()))
AXES = ("row", "col")
F32 = jnp.float32
BF16 = jnp.bfloat16


def kappa_of(width):
    return 2.0 / (width * EPSILON)


def pieces(value):
    high = value.astype(BF16).astype(F32)
    rest = value - high
    mid = rest.astype(BF16).astype(F32)
    return high, mid, rest - mid


def select(index, values):
    out = jnp.zeros(index.shape, F32)
    for k, value in values.items():
        out = jnp.where(index == k, value, out)
    return out


def extras_x(index, b_term):
    high, mid, low = pieces(b_term)
    return select(index, {0: 1.0, 1: 1.0, 2: 1.0, 3: high, 4: mid, 5: low})


def rows_index(columns):
    return lax.broadcasted_iota(jnp.int32, (EXT, columns), 0)


def to_column(row):
    size = row.shape[1]
    eye = lax.broadcasted_iota(jnp.int32, (size, size), 0) == lax.broadcasted_iota(jnp.int32, (size, size), 1)
    return jnp.sum(jnp.where(eye, row, 0.0), axis=1, keepdims=True)


def to_row(column):
    size = column.shape[0]
    eye = lax.broadcasted_iota(jnp.int32, (size, size), 0) == lax.broadcasted_iota(jnp.int32, (size, size), 1)
    return jnp.sum(jnp.where(eye, column, 0.0), axis=0, keepdims=True)


def for_tiles(total, product, z_ref, use):
    count = total // TILE
    slots = z_ref.shape[0]
    if count <= slots:
        for t in range(count):
            z_ref[t] = product(pl.ds(t * TILE, TILE))
        for t in range(count):
            use(pl.ds(t * TILE, TILE), z_ref.at[t])
    else:

        @pl.loop(0, count)
        def _(t):
            tile = pl.ds(pl.multiple_of(t * TILE, TILE), TILE)
            z_ref[0] = product(tile)
            use(tile, z_ref.at[0])


def max_down(z_ref, rows):
    peak = z_ref[0:STEP, :]
    for r in range(STEP, rows, STEP):
        peak = jnp.maximum(peak, z_ref[r : r + STEP, :])
    return jnp.max(peak, axis=0, keepdims=True)


def exp_sum_down(z_ref, rows, scale, shift, keep=None):
    total = jnp.zeros((STEP, TILE), F32)
    for r in range(0, rows, STEP):
        value = jnp.exp2((z_ref[r : r + STEP, :] - shift) * scale)
        total = total + value
        if keep is not None:
            keep(r, value)
    return jnp.sum(total, axis=0, keepdims=True)


def to_lanes(row):
    return jnp.concatenate([row[:, k : k + LANES] for k in range(0, row.shape[1], LANES)], axis=0)


def from_lanes(block):
    return jnp.concatenate([block[k : k + 1] for k in range(block.shape[0])], axis=1)


def sums_rows(ny):
    return -(-2 * ny // LANES // 16) * 16


def sums_out(sums):
    high = sums.astype(BF16).astype(F32)
    spare = sums_rows(sums.size) - 2 * sums.shape[0]
    return jnp.concatenate([high, sums - high] + [jnp.zeros((spare, LANES), F32)] * (spare > 0), axis=0)


def pack(block):
    width, yd = block.shape
    base = width * yd // LANES
    return jnp.concatenate([block[k : k + base] for k in range(0, width, base)], axis=1)


def unpack(block, yd):
    return jnp.concatenate([block[:, k : k + yd] for k in range(0, LANES, yd)], axis=0)


def ones_kernel(ext_ref):
    index = lax.broadcasted_iota(jnp.int32, ext_ref.shape, 1)
    ext_ref[...] = select(index, {3: 1.0, 4: 1.0, 5: 1.0})


def prep_kernel(log_nx, log_ny, y_ref, my_ref, mx_ref, ones_ref, ya_ref, la_ref):
    la_ref[...] = from_lanes(mx_ref[...].astype(F32)) - log_nx
    width = y_ref.shape[1]
    y = y_ref[...]
    yf = y.astype(F32)
    norm = jnp.sum(yf * yf, axis=1, keepdims=True)
    mass = to_column(my_ref[...].astype(F32))
    c_term = (mass - log_ny) / kappa_of(width) - 0.5 * norm
    high, mid, low = pieces(c_term)
    index = lax.broadcasted_iota(jnp.int32, ones_ref.shape, 1)
    ext = (ones_ref[...] + select(index, {0: high, 1: mid, 2: low, 6: mass})).astype(BF16)
    for k in range(ya_ref.shape[0]):
        ya_ref[k, :, :width] = y
        ya_ref[k, :, width:] = ext


def halves(row):
    half = row.shape[1] // 2
    return row[:, :half], row[:, half:]


def other_order(row):
    mine, other = halves(row)
    return jnp.where(lax.axis_index("col") == 0, row, jnp.concatenate([other, mine], axis=1))


def piece_rows(row):
    one, two, three = pieces(row)
    index = lax.broadcasted_iota(jnp.int32, (PAD, row.shape[1]), 0)
    return select(index, {0: one, 1: two, 2: three}).astype(BF16)


def sum_pieces(block):
    return (block[0:1] + block[1:2]) + block[2:3]


def half_kernel(xt_ref, mine_ref, xa_ref, yt_ref, base_ref, total_ref, k_ref, z_ref):
    rows, yd, depth = mine_ref.shape
    width, n = xt_ref.shape
    half = rows * yd
    scale = kappa_of(width) * LOG2E
    xa_ref[:width, :] = xt_ref[...]
    xa_ref[width:, :] = extras_x(rows_index(n), jnp.zeros((1, n), F32)).astype(BF16)
    mine = mine_ref[...].reshape(half, depth)

    def product(t):
        return jnp.dot(mine, xa_ref[:, t], preferred_element_type=F32)

    def use(t, z):
        def keep(r, value):
            k_ref[r : r + STEP, t] = value.astype(BF16)

        base = max_down(z, half) - LIFT / scale
        base_ref[:, t] = base
        total_ref[:, t] = exp_sum_down(z, half, scale, base, keep)

    for_tiles(n, product, z_ref, use)
    yt_ref[...] = mine.T


def first_kernel(
    xa_ref, la_ref, mine_ref, other_ref, base_ref, total_ref, km0_ref,
    yt_ref, km_ref, ko_ref, b_ref, omega_ref, mu_ref, l_ref, xb_ref, z_ref, sum_ref, lse_ref, sem,
):
    rows, yd, depth = other_ref.shape
    n = xa_ref.shape[1]
    width = depth - EXT
    half = rows * yd
    scale = kappa_of(width) * LOG2E
    other = other_ref[...].reshape(half, depth)
    move = pltpu.make_async_copy(km0_ref, km_ref, sem)
    move.start()

    def product(t):
        return jnp.dot(other, xa_ref[:, t], preferred_element_type=F32)

    def use(t, z):
        def keep(r, value):
            ko_ref[r : r + STEP, t] = value.astype(BF16)

        sum_ref[:, t] = exp_sum_down(z, half, scale, base_ref[:, t], keep) + total_ref[:, t]

    for_tiles(n, product, z_ref, use)
    yt_ref[...] = other.T
    log_a = la_ref[...]
    total = sum_ref[...]
    b_ref[...] = (log_a - jnp.log(total)) * (LOG2E / scale) - base_ref[...]
    omega = jnp.exp(log_a) * (2.0**LIFT / total)
    omega_ref[...] = omega
    left = piece_rows(omega)
    move.wait()
    sums = jnp.concatenate(
        [
            sum_pieces(lax.dot_general(left, ref[...], ACROSS, preferred_element_type=F32))
            for ref in (km_ref, ko_ref)
        ],
        axis=1,
    )
    lse_ref[...] = jnp.log(sums) * LOG2E - LIFT
    mu_ref[...] = jnp.full(mu_ref.shape, -LIFT, F32)

    @pl.when(jnp.logical_not((jnp.max(total) < HUGE) & (jnp.min(sums) > TINY)))
    def _():
        step = LANES // yd
        sides = ((0, mine_ref, km_ref), (1, other_ref, ko_ref))

        def scores(y_ref, x_ref, t):
            y = y_ref[pl.ds(t * step, step)].reshape(LANES, depth)
            return jnp.dot(y, x_ref[...], preferred_element_type=F32)

        b_ref[...] = jnp.full((1, n), -jnp.inf, F32)
        for k, y_ref, k_ref in sides:

            @pl.loop(0, rows // step)
            def _(t):
                b_ref[...] = jnp.maximum(b_ref[...], jnp.max(scores(y_ref, xa_ref, t), axis=0, keepdims=True))

        sum_ref[...] = jnp.zeros((1, n), F32)
        for k, y_ref, k_ref in sides:

            @pl.loop(0, rows // step)
            def _(t):
                value = jnp.exp2((scores(y_ref, xa_ref, t) - b_ref[...]) * scale)
                sum_ref[...] = sum_ref[...] + jnp.sum(value, axis=0, keepdims=True)

        b_ref[...] = (log_a - jnp.log(sum_ref[...])) * (LOG2E / scale) - b_ref[...]
        xb_ref[:width, :] = xa_ref[:width, :]
        xb_ref[width:, :] = extras_x(rows_index(n), b_ref[...]).astype(BF16)
        omega_ref[...] = jnp.ones((1, n), F32)
        for k, y_ref, k_ref in sides:

            @pl.loop(0, rows // step)
            def _(t):
                z = scores(y_ref, xb_ref, t)
                peak = jnp.max(z, axis=1, keepdims=True)
                value = jnp.exp2((z - peak) * scale)
                k_ref[pl.ds(pl.multiple_of(t * LANES, LANES), LANES), :] = value.astype(BF16)
                place = pl.ds(pl.multiple_of(k * half + t * LANES, LANES), LANES)
                mu_ref[:, place] = to_row(scale * peak)
                lse_ref[:, place] = to_row(scale * peak + jnp.log(jnp.sum(value, axis=1, keepdims=True)) * LOG2E)

    lse = to_lanes(other_order(lse_ref[...]))
    for k in range(2 * rows):
        l_ref[k] = lse


def stack(out_ref, width, points, factor):
    moved = points.astype(F32) * factor
    high = moved.astype(BF16)
    out_ref[:width, :] = high
    out_ref[width : 2 * width, :] = (moved - high.astype(F32)).astype(BF16)
    one, two, three = pieces(factor)
    index = lax.broadcasted_iota(jnp.int32, (PAD, factor.shape[1]), 0)
    out_ref[2 * width :, :] = select(index, {0: one, 1: two, 2: three}).astype(BF16)


def unstack(product, width):
    ext = product[2 * width :]
    return product[:width] + product[width : 2 * width], (ext[0:1] + ext[1:2]) + ext[2:3]


def second_kernel(
    log_ny, xa_ref, la_ref, omega_ref, mu_ref, l_ref, ym_ref, yo_ref, km_ref, ko_ref,
    r_ref, wr_ref, v_ref, c_ref, xs_ref, sum_ref, send_ref,
):
    width = xa_ref.shape[0] - EXT
    half = ym_ref.shape[1]
    kappa = kappa_of(width)
    scale = kappa * LOG2E
    l_all = l_ref[...]
    peak = jnp.max(l_all, axis=0)
    total = jnp.sum(jnp.exp2(l_all - peak[None]), axis=0)
    lse2 = other_order(from_lanes(peak + jnp.log(total) * LOG2E))
    old = jnp.concatenate([ym_ref[width:, :], yo_ref[width:, :]], axis=1).astype(F32)
    lb2 = (old[6:7] - log_ny) * LOG2E
    c_ref[...] = to_lanes(sum_pieces(old) + (lb2 - lse2) / scale)
    v = jnp.exp2(mu_ref[...] + (lb2 - lse2))
    v_ref[...] = v
    v_mine, v_other = halves(v)
    left = piece_rows(v)
    rowsum = jnp.dot(left[:, :half], km_ref[...], preferred_element_type=F32) + jnp.dot(
        left[:, half:], ko_ref[...], preferred_element_type=F32
    )
    omega = omega_ref[...]
    rowsum = sum_pieces(rowsum) * omega
    r = jnp.exp(la_ref[...]) / rowsum
    r_ref[...] = r
    wr_ref[...] = r * omega
    stack(xs_ref, width, xa_ref[:width, :], r * omega)
    totals = []
    for k in range(half // TILE):
        t = slice(k * TILE, (k + 1) * TILE)
        product = lax.dot_general(xs_ref[...], ko_ref[t, :], ACROSS, preferred_element_type=F32)
        moment, total = unstack(product, width)
        total = total * v_other[:, t]
        totals.append(total)
        part = yo_ref[:width, t].astype(F32) * total - moment * v_other[:, t]
        send_ref[:width, t] = part.astype(BF16)
    s_other = jnp.concatenate(totals, axis=1)
    ext = lax.dot_general(xs_ref[2 * width :, :], km_ref[...], ACROSS, preferred_element_type=F32)
    s_mine = sum_pieces(ext) * v_mine
    sum_ref[...] = jnp.concatenate([s_mine, s_other], axis=1)
    high_m, high_o = s_mine.astype(BF16).astype(F32), s_other.astype(BF16).astype(F32)
    index = lax.broadcasted_iota(jnp.int32, (PAD, half), 0)
    ext = select(index, {0: high_m, 1: high_o, 2: s_mine - high_m, 3: s_other - high_o})
    send_ref[width:, :] = ext.astype(BF16)


def keep_kernel(log_nx, xa_ref, xs_ref, v_ref, sum_ref, ym_ref, yo_ref, km_ref, keep_ref, norm_ref, q_ref):
    width, half = keep_ref.shape
    for k in range(half // TILE):
        t = slice(k * TILE, (k + 1) * TILE)
        product = lax.dot_general(xs_ref[: 2 * width, :], km_ref[t, :], ACROSS, preferred_element_type=F32)
        moment = product[:width] + product[width:]
        keep_ref[:, t] = ym_ref[:width, t].astype(F32) * sum_ref[:, t] - moment * v_ref[:, t]
    xf = xa_ref[:width, :].astype(F32)
    norm_ref[...] = jnp.sum(xf * xf, axis=0, keepdims=True)
    mass = jnp.concatenate([ym_ref[width:, :], yo_ref[width:, :]], axis=1).astype(F32)[6:7]
    q_ref[...] = v_ref[...] * jnp.exp(mass + log_nx)


def add_kernel(keep_ref, sum_ref, got_ref, out_ref):
    width, half = keep_ref.shape
    rows = out_ref.shape[0]
    yd = half // rows
    base = yd * width // LANES
    ext = got_ref[width:, :].astype(F32)
    other = jnp.concatenate([ext[1:2] + ext[3:4], ext[0:1] + ext[2:3]], axis=1)
    sums = sums_out(to_lanes(sum_ref[...] + other)).astype(BF16)
    total = keep_ref[...] + got_ref[:width, :].astype(F32)
    for r in range(rows):
        out_ref[r, :base, :] = pack(total[:, r * yd : (r + 1) * yd]).astype(BF16)
        out_ref[r, base:, :] = sums


def own_part(ref, yd):
    block = lax.axis_index("row")
    fit = LANES // yd
    row = ref[pl.ds(block // fit, 1), :]
    out = row[:, :yd]
    for k in range(1, fit):
        out = jnp.where(block % fit == k, row[:, k * yd : (k + 1) * yd], out)
    return out


def last_kernel(
    xa_ref, la_ref, norm_ref, b_ref, r_ref, wr_ref, q_ref, c_ref, got_ref, ym_ref, yo_ref, km_ref, ko_ref, y_ref,
    f_hbm, pot_hbm, gx_hbm, gy_hbm, f_ref, pot_ref, gx_ref, gy_ref, ys_ref, sum_ref, sems,
):
    width, n = gx_ref.shape
    ny = q_ref.shape[1]
    yd = y_ref.shape[1]
    base = yd * width // LANES
    count = ny // LANES
    kappa = kappa_of(width)
    moves = []

    def leave(source, target):
        move = pltpu.make_async_copy(source, target, sems.at[len(moves)])
        move.start()
        moves.append(move)

    log_row = la_ref[...] - jnp.log(r_ref[...])
    f_ref[...] = norm_ref[...] / width + EPSILON * (kappa * b_ref[...] - log_row)
    leave(f_ref, f_hbm)
    total = got_ref[0].astype(F32)
    for k in range(1, got_ref.shape[0]):
        total = total + got_ref[k].astype(F32)
    sums = total[base : base + count] + total[base + count : base + 2 * count]
    sum_ref[...] = sums
    colsum = own_part(sum_ref, yd)
    c_term = own_part(c_ref, yd)
    own = y_ref[0].astype(F32)
    gy_ref[...] = unpack(total[:base], yd).T * (
        jnp.exp(own[:, width + 6 : width + 7]) * to_column(1.0 / colsum)
    )
    leave(gy_ref, gy_hbm)
    norm = to_row(jnp.sum(own[:, :width] * own[:, :width], axis=1, keepdims=True))
    pot_ref[...] = norm / width - EPSILON * (jnp.log(colsum) - kappa * c_term)
    leave(pot_ref, pot_hbm)
    half = ny // 2
    yt = jnp.concatenate([ym_ref[:width, :], yo_ref[:width, :]], axis=1)
    stack(ys_ref, width, yt, q_ref[...] / from_lanes(sums))
    for k in range(n // TILE):
        t = slice(k * TILE, (k + 1) * TILE)
        product = jnp.dot(ys_ref[:, :half], km_ref[:, t], preferred_element_type=F32) + jnp.dot(
            ys_ref[:, half:], ko_ref[:, t], preferred_element_type=F32
        )
        moved, weight = unstack(product, width)
        gx_ref[:, t] = (xa_ref[:width, t].astype(F32) * weight - moved) * (wr_ref[:, t] * (1.0 / ny))
        leave(gx_ref.at[:, t], gx_hbm.at[:, t])
    for move in moves:
        move.wait()


def call(kernel, outs, scratch, limit, *args, space=pltpu.VMEM, out_space=pltpu.VMEM, cost=None):
    return pl.pallas_call(
        kernel,
        out_shape=outs,
        in_specs=[pl.BlockSpec(memory_space=space)] * len(args),
        out_specs=jax.tree.map(lambda _: pl.BlockSpec(memory_space=out_space), outs),
        scratch_shapes=scratch,
        cost_estimate=cost,
        compiler_params=pltpu.CompilerParams(vmem_limit_bytes=limit),
    )(*args)


def shape(dims, dtype=F32):
    return jax.ShapeDtypeStruct(dims, dtype)


def swap(value):
    return lax.ppermute(value, "col", [(0, 1), (1, 0)])


def on_device(points_x, points_y, mass_x, mass_y):
    n, width = points_x.shape
    yd = points_y.shape[0]
    rows = lax.axis_size("row")
    ny = 2 * rows * yd
    half = ny // 2
    count = ny // LANES
    log_nx, log_ny = math.log(n * 2 * rows), math.log(ny)
    depth = width + EXT
    limit = (20 if ny <= 1024 else 56) * 1024 * 1024
    extra = sums_rows(ny)
    run = functools.partial
    vmem = pltpu.VMEM
    slots = 4 if ny <= 1024 else 1
    ones = call(
        ones_kernel, shape((yd, EXT)), [], limit,
        cost=pl.CostEstimate(flops=4 * 10**9, bytes_accessed=10000, transcendentals=0),
    )
    y_own, log_a = call(
        run(prep_kernel, log_nx, log_ny), (shape((rows, yd, depth), BF16), shape((1, n))), [], limit,
        points_y, mass_y.reshape(1, yd), mass_x.reshape(n // LANES, LANES), ones,
        cost=pl.CostEstimate(flops=4 * 10**9, bytes_accessed=400000, transcendentals=0),
    )
    y_mine = lax.all_to_all(y_own, "row", 0, 0, tiled=True)
    y_other = swap(y_mine)
    xa, yt_mine, base, total, kept_mine = call(
        half_kernel,
        (
            shape((depth, n), BF16), shape((depth, half), BF16), shape((1, n)), shape((1, n)),
            shape((half, n), BF16),
        ),
        [vmem((slots, half, TILE), F32)],
        limit, points_x.T, y_mine,
    )
    yt_other, kept_mine, kept_other, b_term, omega, mu, lse = call(
        first_kernel,
        (
            shape((depth, half), BF16), shape((half, n), BF16), shape((half, n), BF16), shape((1, n)),
            shape((1, n)), shape((1, ny)), shape((2 * rows, count, LANES)),
        ),
        [vmem((depth, n), BF16), vmem((slots, half, TILE), F32), vmem((1, n), F32), vmem((1, ny), F32), pltpu.SemaphoreType.DMA],
        limit, xa, log_a, y_mine, y_other, base, total, kept_mine,
    )
    lse = lax.all_to_all(lse, AXES, 0, 0, tiled=True)
    r, wr, v, c_term, xs, sums, send = call(
        run(second_kernel, log_ny),
        (
            shape((1, n)), shape((1, n)), shape((1, ny)), shape((count, LANES)),
            shape((2 * width + PAD, n), BF16), shape((1, ny)), shape((width + PAD, half), BF16),
        ),
        [], limit, xa, log_a, omega, mu, lse, yt_mine, yt_other, kept_mine, kept_other,
    )
    got = swap(send)
    keep, norm, q = call(
        run(keep_kernel, log_nx), (shape((width, half)), shape((1, n)), shape((1, ny))), [],
        limit, xa, xs, v, sums, yt_mine, yt_other, kept_mine,
    )
    part = call(
        add_kernel, shape((rows, yd * width // LANES + extra, LANES), BF16), [], limit, keep, sums, got
    )
    part = lax.all_to_all(part, "row", 0, 0, tiled=True)
    f_pot, g_pot, grad_xt, grad_y = call(
        last_kernel,
        (shape((1, n)), shape((1, yd)), shape((width, n)), shape((yd, width))),
        [
            vmem((1, n), F32), vmem((1, yd), F32), vmem((width, n), F32), vmem((yd, width), F32),
            vmem((2 * width + PAD, ny), BF16), vmem((count, LANES), F32),
            pltpu.SemaphoreType.DMA((3 + n // TILE,)),
        ],
        limit, xa, log_a, norm, b_term, r, wr, q, c_term, part, yt_mine, yt_other, kept_mine, kept_other, y_own,
        out_space=pl.ANY,
    )
    return f_pot.reshape(n), g_pot.reshape(yd), grad_xt.T, grad_y


def solution(mesh):
    in_specs = (
        P(("groups", "row", "col"), None),
        P(("groups", "col", "row"), None),
        P(("groups", "row", "col")),
        P(("groups", "col", "row")),
    )
    out_specs = (
        P(("groups", "row", "col")),
        P(("groups", "col", "row")),
        P(("groups", "row", "col"), None),
        P(("groups", "col", "row"), None),
    )
    return jax.shard_map(
        on_device, mesh=mesh, in_specs=in_specs, out_specs=out_specs, check_vma=False
    )
```

```python
import functools
import math

import jax
import jax.numpy as jnp
from jax import lax
from jax.experimental import pallas as pl
from jax.experimental.pallas import tpu as pltpu
from jax.sharding import PartitionSpec as P

ITERS = 2
EPSILON = 0.02
LOG2E = math.log2(math.e)
TILE = 512
STEP = 16
EXT = 32
PAD = 16
LANES = 128
LIFT = 52.0
TINY = 1e-24
HUGE = 5e33
ACROSS = (((1,), (1,)), ((), ()))
AXES = ("row", "col")
F32 = jnp.float32
BF16 = jnp.bfloat16


def kappa_of(width):
    return 2.0 / (width * EPSILON)


def pieces(value):
    high = value.astype(BF16).astype(F32)
    rest = value - high
    mid = rest.astype(BF16).astype(F32)
    return high, mid, rest - mid


def select(index, values):
    out = jnp.zeros(index.shape, F32)
    for k, value in values.items():
        out = jnp.where(index == k, value, out)
    return out


def extras_x(index, b_term):
    high, mid, low = pieces(b_term)
    return select(index, {0: 1.0, 1: 1.0, 2: 1.0, 3: high, 4: mid, 5: low})


def rows_index(columns):
    return lax.broadcasted_iota(jnp.int32, (EXT, columns), 0)


def to_column(row):
    size = row.shape[1]
    eye = lax.broadcasted_iota(jnp.int32, (size, size), 0) == lax.broadcasted_iota(jnp.int32, (size, size), 1)
    return jnp.sum(jnp.where(eye, row, 0.0), axis=1, keepdims=True)


def to_row(column):
    size = column.shape[0]
    eye = lax.broadcasted_iota(jnp.int32, (size, size), 0) == lax.broadcasted_iota(jnp.int32, (size, size), 1)
    return jnp.sum(jnp.where(eye, column, 0.0), axis=0, keepdims=True)


def for_tiles(total, product, z_ref, use):
    count = total // TILE
    slots = z_ref.shape[0]
    if count <= slots:
        for t in range(count):
            z_ref[t] = product(pl.ds(t * TILE, TILE))
        for t in range(count):
            use(pl.ds(t * TILE, TILE), z_ref.at[t])
    else:

        @pl.loop(0, count)
        def _(t):
            tile = pl.ds(pl.multiple_of(t * TILE, TILE), TILE)
            z_ref[0] = product(tile)
            use(tile, z_ref.at[0])


def max_down(z_ref, rows):
    peak = z_ref[0:STEP, :]
    for r in range(STEP, rows, STEP):
        peak = jnp.maximum(peak, z_ref[r : r + STEP, :])
    return jnp.max(peak, axis=0, keepdims=True)


def exp_sum_down(z_ref, rows, scale, shift, keep=None):
    total = jnp.zeros((STEP, TILE), F32)
    for r in range(0, rows, STEP):
        value = jnp.exp2((z_ref[r : r + STEP, :] - shift) * scale)
        total = total + value
        if keep is not None:
            keep(r, value)
    return jnp.sum(total, axis=0, keepdims=True)


def to_lanes(row):
    return jnp.concatenate([row[:, k : k + LANES] for k in range(0, row.shape[1], LANES)], axis=0)


def from_lanes(block):
    return jnp.concatenate([block[k : k + 1] for k in range(block.shape[0])], axis=1)


def sums_rows(ny):
    return -(-2 * ny // LANES // 16) * 16


def sums_out(sums):
    high = sums.astype(BF16).astype(F32)
    spare = sums_rows(sums.size) - 2 * sums.shape[0]
    return jnp.concatenate([high, sums - high] + [jnp.zeros((spare, LANES), F32)] * (spare > 0), axis=0)


def pack(block):
    width, yd = block.shape
    base = width * yd // LANES
    return jnp.concatenate([block[k : k + base] for k in range(0, width, base)], axis=1)


def unpack(block, yd):
    return jnp.concatenate([block[:, k : k + yd] for k in range(0, LANES, yd)], axis=0)


def ones_kernel(ext_ref):
    index = lax.broadcasted_iota(jnp.int32, ext_ref.shape, 1)
    ext_ref[...] = select(index, {3: 1.0, 4: 1.0, 5: 1.0})


def prep_kernel(log_nx, log_ny, y_ref, my_ref, mx_ref, ones_ref, ya_ref, la_ref):
    la_ref[...] = from_lanes(mx_ref[...].astype(F32)) - log_nx
    width = y_ref.shape[1]
    y = y_ref[...]
    yf = y.astype(F32)
    norm = jnp.sum(yf * yf, axis=1, keepdims=True)
    mass = to_column(my_ref[...].astype(F32))
    c_term = (mass - log_ny) / kappa_of(width) - 0.5 * norm
    high, mid, low = pieces(c_term)
    index = lax.broadcasted_iota(jnp.int32, ones_ref.shape, 1)
    ext = (ones_ref[...] + select(index, {0: high, 1: mid, 2: low, 6: mass})).astype(BF16)
    for k in range(ya_ref.shape[0]):
        ya_ref[k, :, :width] = y
        ya_ref[k, :, width:] = ext


def halves(row):
    half = row.shape[1] // 2
    return row[:, :half], row[:, half:]


def other_order(row):
    mine, other = halves(row)
    return jnp.where(lax.axis_index("col") == 0, row, jnp.concatenate([other, mine], axis=1))


def piece_rows(row):
    one, two, three = pieces(row)
    index = lax.broadcasted_iota(jnp.int32, (PAD, row.shape[1]), 0)
    return select(index, {0: one, 1: two, 2: three}).astype(BF16)


def sum_pieces(block):
    return (block[0:1] + block[1:2]) + block[2:3]


def half_kernel(xt_ref, mine_ref, xa_ref, yt_ref, base_ref, total_ref, k_ref, z_ref):
    rows, yd, depth = mine_ref.shape
    width, n = xt_ref.shape
    half = rows * yd
    scale = kappa_of(width) * LOG2E
    xa_ref[:width, :] = xt_ref[...]
    xa_ref[width:, :] = extras_x(rows_index(n), jnp.zeros((1, n), F32)).astype(BF16)
    mine = mine_ref[...].reshape(half, depth)

    def product(t):
        return jnp.dot(mine, xa_ref[:, t], preferred_element_type=F32)

    def use(t, z):
        def keep(r, value):
            k_ref[r : r + STEP, t] = value.astype(BF16)

        base = max_down(z, half) - LIFT / scale
        base_ref[:, t] = base
        total_ref[:, t] = exp_sum_down(z, half, scale, base, keep)

    for_tiles(n, product, z_ref, use)
    yt_ref[...] = mine.T


def first_kernel(
    xa_ref, la_ref, mine_ref, other_ref, base_ref, total_ref, km0_ref,
    yt_ref, km_ref, ko_ref, b_ref, omega_ref, mu_ref, l_ref, xb_ref, z_ref, sum_ref, lse_ref, sem,
):
    rows, yd, depth = other_ref.shape
    n = xa_ref.shape[1]
    width = depth - EXT
    half = rows * yd
    scale = kappa_of(width) * LOG2E
    other = other_ref[...].reshape(half, depth)
    move = pltpu.make_async_copy(km0_ref, km_ref, sem)
    move.start()

    def product(t):
        return jnp.dot(other, xa_ref[:, t], preferred_element_type=F32)

    def use(t, z):
        def keep(r, value):
            ko_ref[r : r + STEP, t] = value.astype(BF16)

        sum_ref[:, t] = exp_sum_down(z, half, scale, base_ref[:, t], keep) + total_ref[:, t]

    for_tiles(n, product, z_ref, use)
    yt_ref[...] = other.T
    log_a = la_ref[...]
    total = sum_ref[...]
    b_ref[...] = (log_a - jnp.log(total)) * (LOG2E / scale) - base_ref[...]
    omega = jnp.exp(log_a) * (2.0**LIFT / total)
    omega_ref[...] = omega
    left = piece_rows(omega)
    move.wait()
    sums = jnp.concatenate(
        [
            sum_pieces(lax.dot_general(left, ref[...], ACROSS, preferred_element_type=F32))
            for ref in (km_ref, ko_ref)
        ],
        axis=1,
    )
    lse_ref[...] = jnp.log(sums) * LOG2E - LIFT
    mu_ref[...] = jnp.full(mu_ref.shape, -LIFT, F32)

    @pl.when(jnp.logical_not((jnp.max(total) < HUGE) & (jnp.min(sums) > TINY)))
    def _():
        step = LANES // yd
        sides = ((0, mine_ref, km_ref), (1, other_ref, ko_ref))

        def scores(y_ref, x_ref, t):
            y = y_ref[pl.ds(t * step, step)].reshape(LANES, depth)
            return jnp.dot(y, x_ref[...], preferred_element_type=F32)

        b_ref[...] = jnp.full((1, n), -jnp.inf, F32)
        for k, y_ref, k_ref in sides:

            @pl.loop(0, rows // step)
            def _(t):
                b_ref[...] = jnp.maximum(b_ref[...], jnp.max(scores(y_ref, xa_ref, t), axis=0, keepdims=True))

        sum_ref[...] = jnp.zeros((1, n), F32)
        for k, y_ref, k_ref in sides:

            @pl.loop(0, rows // step)
            def _(t):
                value = jnp.exp2((scores(y_ref, xa_ref, t) - b_ref[...]) * scale)
                sum_ref[...] = sum_ref[...] + jnp.sum(value, axis=0, keepdims=True)

        b_ref[...] = (log_a - jnp.log(sum_ref[...])) * (LOG2E / scale) - b_ref[...]
        xb_ref[:width, :] = xa_ref[:width, :]
        xb_ref[width:, :] = extras_x(rows_index(n), b_ref[...]).astype(BF16)
        omega_ref[...] = jnp.ones((1, n), F32)
        for k, y_ref, k_ref in sides:

            @pl.loop(0, rows // step)
            def _(t):
                z = scores(y_ref, xb_ref, t)
                peak = jnp.max(z, axis=1, keepdims=True)
                value = jnp.exp2((z - peak) * scale)
                k_ref[pl.ds(pl.multiple_of(t * LANES, LANES), LANES), :] = value.astype(BF16)
                place = pl.ds(pl.multiple_of(k * half + t * LANES, LANES), LANES)
                mu_ref[:, place] = to_row(scale * peak)
                lse_ref[:, place] = to_row(scale * peak + jnp.log(jnp.sum(value, axis=1, keepdims=True)) * LOG2E)

    lse = to_lanes(other_order(lse_ref[...]))
    for k in range(2 * rows):
        l_ref[k] = lse


def stack(out_ref, width, points, factor):
    moved = points.astype(F32) * factor
    high = moved.astype(BF16)
    out_ref[:width, :] = high
    out_ref[width : 2 * width, :] = (moved - high.astype(F32)).astype(BF16)
    one, two, three = pieces(factor)
    index = lax.broadcasted_iota(jnp.int32, (PAD, factor.shape[1]), 0)
    out_ref[2 * width :, :] = select(index, {0: one, 1: two, 2: three}).astype(BF16)


def unstack(product, width):
    ext = product[2 * width :]
    return product[:width] + product[width : 2 * width], (ext[0:1] + ext[1:2]) + ext[2:3]


def second_kernel(
    log_ny, xa_ref, la_ref, omega_ref, mu_ref, l_ref, ym_ref, yo_ref, km_ref, ko_ref,
    r_ref, wr_ref, v_ref, c_ref, xs_ref, sum_ref, send_ref,
):
    width = xa_ref.shape[0] - EXT
    half = ym_ref.shape[1]
    kappa = kappa_of(width)
    scale = kappa * LOG2E
    l_all = l_ref[...]
    peak = jnp.max(l_all, axis=0)
    total = jnp.sum(jnp.exp2(l_all - peak[None]), axis=0)
    lse2 = other_order(from_lanes(peak + jnp.log(total) * LOG2E))
    old = jnp.concatenate([ym_ref[width:, :], yo_ref[width:, :]], axis=1).astype(F32)
    lb2 = (old[6:7] - log_ny) * LOG2E
    c_ref[...] = to_lanes(sum_pieces(old) + (lb2 - lse2) / scale)
    v = jnp.exp2(mu_ref[...] + (lb2 - lse2))
    v_ref[...] = v
    v_mine, v_other = halves(v)
    left = piece_rows(v)
    rowsum = jnp.dot(left[:, :half], km_ref[...], preferred_element_type=F32) + jnp.dot(
        left[:, half:], ko_ref[...], preferred_element_type=F32
    )
    omega = omega_ref[...]
    rowsum = sum_pieces(rowsum) * omega
    r = jnp.exp(la_ref[...]) / rowsum
    r_ref[...] = r
    wr_ref[...] = r * omega
    stack(xs_ref, width, xa_ref[:width, :], r * omega)
    totals = []
    for k in range(half // TILE):
        t = slice(k * TILE, (k + 1) * TILE)
        product = lax.dot_general(xs_ref[...], ko_ref[t, :], ACROSS, preferred_element_type=F32)
        moment, total = unstack(product, width)
        total = total * v_other[:, t]
        totals.append(total)
        part = yo_ref[:width, t].astype(F32) * total - moment * v_other[:, t]
        send_ref[:width, t] = part
    s_other = jnp.concatenate(totals, axis=1)
    ext = lax.dot_general(xs_ref[2 * width :, :], km_ref[...], ACROSS, preferred_element_type=F32)
    s_mine = sum_pieces(ext) * v_mine
    sum_ref[...] = jnp.concatenate([s_mine, s_other], axis=1)
    index = lax.broadcasted_iota(jnp.int32, (8, half), 0)
    send_ref[width:, :] = select(index, {0: s_mine, 1: s_other})


def keep_kernel(log_nx, xa_ref, xs_ref, v_ref, sum_ref, ym_ref, yo_ref, km_ref, keep_ref, norm_ref, q_ref):
    width, half = keep_ref.shape
    for k in range(half // TILE):
        t = slice(k * TILE, (k + 1) * TILE)
        product = lax.dot_general(xs_ref[: 2 * width, :], km_ref[t, :], ACROSS, preferred_element_type=F32)
        moment = product[:width] + product[width:]
        keep_ref[:, t] = ym_ref[:width, t].astype(F32) * sum_ref[:, t] - moment * v_ref[:, t]
    xf = xa_ref[:width, :].astype(F32)
    norm_ref[...] = jnp.sum(xf * xf, axis=0, keepdims=True)
    mass = jnp.concatenate([ym_ref[width:, :], yo_ref[width:, :]], axis=1).astype(F32)[6:7]
    q_ref[...] = v_ref[...] * jnp.exp(mass + log_nx)


def add_kernel(keep_ref, sum_ref, got_ref, out_ref):
    width, half = keep_ref.shape
    rows = out_ref.shape[0]
    yd = half // rows
    base = yd * width // LANES
    other = jnp.concatenate([got_ref[width + 1 : width + 2, :], got_ref[width : width + 1, :]], axis=1)
    sums = sums_out(to_lanes(sum_ref[...] + other)).astype(BF16)
    total = keep_ref[...] + got_ref[:width, :]
    for r in range(rows):
        out_ref[r, :base, :] = pack(total[:, r * yd : (r + 1) * yd]).astype(BF16)
        out_ref[r, base:, :] = sums


def own_part(ref, yd):
    block = lax.axis_index("row")
    fit = LANES // yd
    row = ref[pl.ds(block // fit, 1), :]
    out = row[:, :yd]
    for k in range(1, fit):
        out = jnp.where(block % fit == k, row[:, k * yd : (k + 1) * yd], out)
    return out


def last_kernel(
    xa_ref, la_ref, norm_ref, b_ref, r_ref, wr_ref, q_ref, c_ref, got_ref, ym_ref, yo_ref, km_ref, ko_ref, y_ref,
    f_hbm, pot_hbm, gx_hbm, gy_hbm, f_ref, pot_ref, gx_ref, gy_ref, ys_ref, sum_ref, sems,
):
    width, n = gx_ref.shape
    ny = q_ref.shape[1]
    yd = y_ref.shape[1]
    base = yd * width // LANES
    count = ny // LANES
    kappa = kappa_of(width)
    moves = []

    def leave(source, target):
        move = pltpu.make_async_copy(source, target, sems.at[len(moves)])
        move.start()
        moves.append(move)

    log_row = la_ref[...] - jnp.log(r_ref[...])
    f_ref[...] = norm_ref[...] / width + EPSILON * (kappa * b_ref[...] - log_row)
    leave(f_ref, f_hbm)
    total = got_ref[0].astype(F32)
    for k in range(1, got_ref.shape[0]):
        total = total + got_ref[k].astype(F32)
    sums = total[base : base + count] + total[base + count : base + 2 * count]
    sum_ref[...] = sums
    colsum = own_part(sum_ref, yd)
    c_term = own_part(c_ref, yd)
    own = y_ref[0].astype(F32)
    gy_ref[...] = unpack(total[:base], yd).T * (
        jnp.exp(own[:, width + 6 : width + 7]) * to_column(1.0 / colsum)
    )
    leave(gy_ref, gy_hbm)
    norm = to_row(jnp.sum(own[:, :width] * own[:, :width], axis=1, keepdims=True))
    pot_ref[...] = norm / width - EPSILON * (jnp.log(colsum) - kappa * c_term)
    leave(pot_ref, pot_hbm)
    half = ny // 2
    yt = jnp.concatenate([ym_ref[:width, :], yo_ref[:width, :]], axis=1)
    stack(ys_ref, width, yt, q_ref[...] / from_lanes(sums))
    for k in range(n // TILE):
        t = slice(k * TILE, (k + 1) * TILE)
        product = jnp.dot(ys_ref[:, :half], km_ref[:, t], preferred_element_type=F32) + jnp.dot(
            ys_ref[:, half:], ko_ref[:, t], preferred_element_type=F32
        )
        moved, weight = unstack(product, width)
        gx_ref[:, t] = (xa_ref[:width, t].astype(F32) * weight - moved) * (wr_ref[:, t] * (1.0 / ny))
        leave(gx_ref.at[:, t], gx_hbm.at[:, t])
    for move in moves:
        move.wait()


def call(kernel, outs, scratch, limit, *args, space=pltpu.VMEM, out_space=pltpu.VMEM, cost=None):
    return pl.pallas_call(
        kernel,
        out_shape=outs,
        in_specs=[pl.BlockSpec(memory_space=space)] * len(args),
        out_specs=jax.tree.map(lambda _: pl.BlockSpec(memory_space=out_space), outs),
        scratch_shapes=scratch,
        cost_estimate=cost,
        compiler_params=pltpu.CompilerParams(vmem_limit_bytes=limit),
    )(*args)


def shape(dims, dtype=F32):
    return jax.ShapeDtypeStruct(dims, dtype)


def swap(value):
    return lax.ppermute(value, "col", [(0, 1), (1, 0)])


def on_device(points_x, points_y, mass_x, mass_y):
    n, width = points_x.shape
    yd = points_y.shape[0]
    rows = lax.axis_size("row")
    ny = 2 * rows * yd
    half = ny // 2
    count = ny // LANES
    log_nx, log_ny = math.log(n * 2 * rows), math.log(ny)
    depth = width + EXT
    limit = (20 if ny <= 1024 else 56) * 1024 * 1024
    extra = sums_rows(ny)
    run = functools.partial
    vmem = pltpu.VMEM
    slots = 4 if ny <= 1024 else 1
    ones = call(
        ones_kernel, shape((yd, EXT)), [], limit,
        cost=pl.CostEstimate(flops=4 * 10**9, bytes_accessed=10000, transcendentals=0),
    )
    y_own, log_a = call(
        run(prep_kernel, log_nx, log_ny), (shape((rows, yd, depth), BF16), shape((1, n))), [], limit,
        points_y, mass_y.reshape(1, yd), mass_x.reshape(n // LANES, LANES), ones,
        cost=pl.CostEstimate(flops=4 * 10**9, bytes_accessed=400000, transcendentals=0),
    )
    y_mine = lax.all_to_all(y_own, "row", 0, 0, tiled=True)
    y_other = swap(y_mine)
    xa, yt_mine, base, total, kept_mine = call(
        half_kernel,
        (
            shape((depth, n), BF16), shape((depth, half), BF16), shape((1, n)), shape((1, n)),
            shape((half, n), BF16),
        ),
        [vmem((slots, half, TILE), F32)],
        limit, points_x.T, y_mine,
    )
    yt_other, kept_mine, kept_other, b_term, omega, mu, lse = call(
        first_kernel,
        (
            shape((depth, half), BF16), shape((half, n), BF16), shape((half, n), BF16), shape((1, n)),
            shape((1, n)), shape((1, ny)), shape((2 * rows, count, LANES)),
        ),
        [vmem((depth, n), BF16), vmem((slots, half, TILE), F32), vmem((1, n), F32), vmem((1, ny), F32), pltpu.SemaphoreType.DMA],
        limit, xa, log_a, y_mine, y_other, base, total, kept_mine,
    )
    lse = lax.all_to_all(lse, AXES, 0, 0, tiled=True)
    r, wr, v, c_term, xs, sums, send = call(
        run(second_kernel, log_ny),
        (
            shape((1, n)), shape((1, n)), shape((1, ny)), shape((count, LANES)),
            shape((2 * width + PAD, n), BF16), shape((1, ny)), shape((width + 8, half)),
        ),
        [], limit, xa, log_a, omega, mu, lse, yt_mine, yt_other, kept_mine, kept_other,
    )
    got = swap(send)
    keep, norm, q = call(
        run(keep_kernel, log_nx), (shape((width, half)), shape((1, n)), shape((1, ny))), [],
        limit, xa, xs, v, sums, yt_mine, yt_other, kept_mine,
    )
    part = call(
        add_kernel, shape((rows, yd * width // LANES + extra, LANES), BF16), [], limit, keep, sums, got
    )
    part = lax.all_to_all(part, "row", 0, 0, tiled=True)
    f_pot, g_pot, grad_xt, grad_y = call(
        last_kernel,
        (shape((1, n)), shape((1, yd)), shape((width, n)), shape((yd, width))),
        [
            vmem((1, n), F32), vmem((1, yd), F32), vmem((width, n), F32), vmem((yd, width), F32),
            vmem((2 * width + PAD, ny), BF16), vmem((count, LANES), F32),
            pltpu.SemaphoreType.DMA((3 + n // TILE,)),
        ],
        limit, xa, log_a, norm, b_term, r, wr, q, c_term, part, yt_mine, yt_other, kept_mine, kept_other, y_own,
        out_space=pl.ANY,
    )
    return f_pot.reshape(n), g_pot.reshape(yd), grad_xt.T, grad_y


def solution(mesh):
    in_specs = (
        P(("groups", "row", "col"), None),
        P(("groups", "col", "row"), None),
        P(("groups", "row", "col")),
        P(("groups", "col", "row")),
    )
    out_specs = (
        P(("groups", "row", "col")),
        P(("groups", "col", "row")),
        P(("groups", "row", "col"), None),
        P(("groups", "col", "row"), None),
    )
    return jax.shard_map(
        on_device, mesh=mesh, in_specs=in_specs, out_specs=out_specs, check_vma=False
    )
```

```python
import functools
import math

import jax
import jax.numpy as jnp
from jax import lax
from jax.experimental import pallas as pl
from jax.experimental.pallas import tpu as pltpu
from jax.sharding import PartitionSpec as P

ITERS = 2
EPSILON = 0.02
LOG2E = math.log2(math.e)
TILE = 512
STEP = 16
EXT = 32
PAD = 16
LANES = 128
LIFT = 52.0
TINY = 1e-24
HUGE = 5e33
ACROSS = (((1,), (1,)), ((), ()))
AXES = ("row", "col")
F32 = jnp.float32
BF16 = jnp.bfloat16


def kappa_of(width):
    return 2.0 / (width * EPSILON)


def pieces(value):
    high = value.astype(BF16).astype(F32)
    rest = value - high
    mid = rest.astype(BF16).astype(F32)
    return high, mid, rest - mid


def select(index, values):
    out = jnp.zeros(index.shape, F32)
    for k, value in values.items():
        out = jnp.where(index == k, value, out)
    return out


def extras_x(index, b_term):
    high, mid, low = pieces(b_term)
    return select(index, {0: 1.0, 1: 1.0, 2: 1.0, 3: high, 4: mid, 5: low})


def rows_index(columns):
    return lax.broadcasted_iota(jnp.int32, (EXT, columns), 0)


def to_column(row):
    size = row.shape[1]
    eye = lax.broadcasted_iota(jnp.int32, (size, size), 0) == lax.broadcasted_iota(jnp.int32, (size, size), 1)
    return jnp.sum(jnp.where(eye, row, 0.0), axis=1, keepdims=True)


def to_row(column):
    size = column.shape[0]
    eye = lax.broadcasted_iota(jnp.int32, (size, size), 0) == lax.broadcasted_iota(jnp.int32, (size, size), 1)
    return jnp.sum(jnp.where(eye, column, 0.0), axis=0, keepdims=True)


def for_tiles(total, product, z_ref, use):
    count = total // TILE
    slots = z_ref.shape[0]
    if count <= slots:
        for t in range(count):
            z_ref[t] = product(pl.ds(t * TILE, TILE))
        for t in range(count):
            use(pl.ds(t * TILE, TILE), z_ref.at[t])
    else:

        @pl.loop(0, count)
        def _(t):
            tile = pl.ds(pl.multiple_of(t * TILE, TILE), TILE)
            z_ref[0] = product(tile)
            use(tile, z_ref.at[0])


def max_down(z_ref, rows):
    peak = z_ref[0:STEP, :]
    for r in range(STEP, rows, STEP):
        peak = jnp.maximum(peak, z_ref[r : r + STEP, :])
    return jnp.max(peak, axis=0, keepdims=True)


def exp_sum_down(z_ref, rows, scale, shift, keep=None):
    total = jnp.zeros((STEP, TILE), F32)
    for r in range(0, rows, STEP):
        value = jnp.exp2((z_ref[r : r + STEP, :] - shift) * scale)
        total = total + value
        if keep is not None:
            keep(r, value)
    return jnp.sum(total, axis=0, keepdims=True)


def to_lanes(row):
    return jnp.concatenate([row[:, k : k + LANES] for k in range(0, row.shape[1], LANES)], axis=0)


def from_lanes(block):
    return jnp.concatenate([block[k : k + 1] for k in range(block.shape[0])], axis=1)


def sums_rows(ny):
    return -(-2 * ny // LANES // 16) * 16


def sums_out(sums):
    high = sums.astype(BF16).astype(F32)
    spare = sums_rows(sums.size) - 2 * sums.shape[0]
    return jnp.concatenate([high, sums - high] + [jnp.zeros((spare, LANES), F32)] * (spare > 0), axis=0)


def pack(block):
    width, yd = block.shape
    base = width * yd // LANES
    return jnp.concatenate([block[k : k + base] for k in range(0, width, base)], axis=1)


def unpack(block, yd):
    return jnp.concatenate([block[:, k : k + yd] for k in range(0, LANES, yd)], axis=0)


def ones_kernel(ext_ref):
    index = lax.broadcasted_iota(jnp.int32, ext_ref.shape, 1)
    ext_ref[...] = select(index, {3: 1.0, 4: 1.0, 5: 1.0})


def prep_kernel(log_nx, log_ny, y_ref, my_ref, mx_ref, ones_ref, ya_ref, la_ref):
    la_ref[...] = from_lanes(mx_ref[...].astype(F32)) - log_nx
    width = y_ref.shape[1]
    y = y_ref[...]
    yf = y.astype(F32)
    norm = jnp.sum(yf * yf, axis=1, keepdims=True)
    mass = to_column(my_ref[...].astype(F32))
    c_term = (mass - log_ny) / kappa_of(width) - 0.5 * norm
    high, mid, low = pieces(c_term)
    index = lax.broadcasted_iota(jnp.int32, ones_ref.shape, 1)
    ext = (ones_ref[...] + select(index, {0: high, 1: mid, 2: low, 6: mass})).astype(BF16)
    for k in range(ya_ref.shape[0]):
        ya_ref[k, :, :width] = y
        ya_ref[k, :, width:] = ext


def halves(row):
    half = row.shape[1] // 2
    return row[:, :half], row[:, half:]


def other_order(row):
    mine, other = halves(row)
    return jnp.where(lax.axis_index("col") == 0, row, jnp.concatenate([other, mine], axis=1))


def piece_rows(row):
    one, two, three = pieces(row)
    index = lax.broadcasted_iota(jnp.int32, (PAD, row.shape[1]), 0)
    return select(index, {0: one, 1: two, 2: three}).astype(BF16)


def sum_pieces(block):
    return (block[0:1] + block[1:2]) + block[2:3]


def half_kernel(xt_ref, mine_ref, xa_ref, yt_ref, base_ref, total_ref, k_ref, z_ref):
    rows, yd, depth = mine_ref.shape
    width, n = xt_ref.shape
    half = rows * yd
    scale = kappa_of(width) * LOG2E
    xa_ref[:width, :] = xt_ref[...]
    xa_ref[width:, :] = extras_x(rows_index(n), jnp.zeros((1, n), F32)).astype(BF16)
    mine = mine_ref[...].reshape(half, depth)

    def product(t):
        return jnp.dot(mine, xa_ref[:, t], preferred_element_type=F32)

    def use(t, z):
        def keep(r, value):
            k_ref[r : r + STEP, t] = value.astype(BF16)

        base = max_down(z, half) - LIFT / scale
        base_ref[:, t] = base
        total_ref[:, t] = exp_sum_down(z, half, scale, base, keep)

    for_tiles(n, product, z_ref, use)
    yt_ref[...] = mine.T


def first_kernel(
    xa_ref, la_ref, mine_ref, other_ref, base_ref, total_ref, km0_ref,
    yt_ref, km_ref, ko_ref, b_ref, omega_ref, mu_ref, l_ref, xb_ref, z_ref, sum_ref, lse_ref, sem,
):
    rows, yd, depth = other_ref.shape
    n = xa_ref.shape[1]
    width = depth - EXT
    half = rows * yd
    scale = kappa_of(width) * LOG2E
    other = other_ref[...].reshape(half, depth)
    move = pltpu.make_async_copy(km0_ref, km_ref, sem)
    move.start()

    def product(t):
        return jnp.dot(other, xa_ref[:, t], preferred_element_type=F32)

    def use(t, z):
        def keep(r, value):
            ko_ref[r : r + STEP, t] = value.astype(BF16)

        sum_ref[:, t] = exp_sum_down(z, half, scale, base_ref[:, t], keep) + total_ref[:, t]

    for_tiles(n, product, z_ref, use)
    yt_ref[...] = other.T
    log_a = la_ref[...]
    total = sum_ref[...]
    b_ref[...] = (log_a - jnp.log(total)) * (LOG2E / scale) - base_ref[...]
    omega = jnp.exp(log_a) * (2.0**LIFT / total)
    omega_ref[...] = omega
    left = piece_rows(omega)
    move.wait()
    sums = jnp.concatenate(
        [
            sum_pieces(lax.dot_general(left, ref[...], ACROSS, preferred_element_type=F32))
            for ref in (km_ref, ko_ref)
        ],
        axis=1,
    )
    lse_ref[...] = jnp.log(sums) * LOG2E - LIFT
    mu_ref[...] = jnp.full(mu_ref.shape, -LIFT, F32)

    @pl.when(jnp.logical_not((jnp.max(total) < HUGE) & (jnp.min(sums) > TINY)))
    def _():
        step = LANES // yd
        sides = ((0, mine_ref, km_ref), (1, other_ref, ko_ref))

        def scores(y_ref, x_ref, t):
            y = y_ref[pl.ds(t * step, step)].reshape(LANES, depth)
            return jnp.dot(y, x_ref[...], preferred_element_type=F32)

        b_ref[...] = jnp.full((1, n), -jnp.inf, F32)
        for k, y_ref, k_ref in sides:

            @pl.loop(0, rows // step)
            def _(t):
                b_ref[...] = jnp.maximum(b_ref[...], jnp.max(scores(y_ref, xa_ref, t), axis=0, keepdims=True))

        sum_ref[...] = jnp.zeros((1, n), F32)
        for k, y_ref, k_ref in sides:

            @pl.loop(0, rows // step)
            def _(t):
                value = jnp.exp2((scores(y_ref, xa_ref, t) - b_ref[...]) * scale)
                sum_ref[...] = sum_ref[...] + jnp.sum(value, axis=0, keepdims=True)

        b_ref[...] = (log_a - jnp.log(sum_ref[...])) * (LOG2E / scale) - b_ref[...]
        xb_ref[:width, :] = xa_ref[:width, :]
        xb_ref[width:, :] = extras_x(rows_index(n), b_ref[...]).astype(BF16)
        omega_ref[...] = jnp.ones((1, n), F32)
        for k, y_ref, k_ref in sides:

            @pl.loop(0, rows // step)
            def _(t):
                z = scores(y_ref, xb_ref, t)
                peak = jnp.max(z, axis=1, keepdims=True)
                value = jnp.exp2((z - peak) * scale)
                k_ref[pl.ds(pl.multiple_of(t * LANES, LANES), LANES), :] = value.astype(BF16)
                place = pl.ds(pl.multiple_of(k * half + t * LANES, LANES), LANES)
                mu_ref[:, place] = to_row(scale * peak)
                lse_ref[:, place] = to_row(scale * peak + jnp.log(jnp.sum(value, axis=1, keepdims=True)) * LOG2E)

    lse = to_lanes(other_order(lse_ref[...]))
    for k in range(2 * rows):
        l_ref[k] = lse


def stack(out_ref, width, points, factor):
    moved = points.astype(F32) * factor
    high = moved.astype(BF16)
    out_ref[:width, :] = high
    out_ref[width : 2 * width, :] = (moved - high.astype(F32)).astype(BF16)
    one, two, three = pieces(factor)
    index = lax.broadcasted_iota(jnp.int32, (PAD, factor.shape[1]), 0)
    out_ref[2 * width :, :] = select(index, {0: one, 1: two, 2: three}).astype(BF16)


def unstack(product, width):
    ext = product[2 * width :]
    return product[:width] + product[width : 2 * width], (ext[0:1] + ext[1:2]) + ext[2:3]


def second_kernel(
    log_ny, xa_ref, la_ref, omega_ref, mu_ref, l_ref, ym_ref, yo_ref, km_ref, ko_ref,
    r_ref, wr_ref, v_ref, c_ref, xs_ref, sum_ref, send_ref,
):
    width = xa_ref.shape[0] - EXT
    half = ym_ref.shape[1]
    kappa = kappa_of(width)
    scale = kappa * LOG2E
    l_all = l_ref[...]
    peak = jnp.max(l_all, axis=0)
    total = jnp.sum(jnp.exp2(l_all - peak[None]), axis=0)
    lse2 = other_order(from_lanes(peak + jnp.log(total) * LOG2E))
    old = jnp.concatenate([ym_ref[width:, :], yo_ref[width:, :]], axis=1).astype(F32)
    lb2 = (old[6:7] - log_ny) * LOG2E
    c_ref[...] = to_lanes(sum_pieces(old) + (lb2 - lse2) / scale)
    v = jnp.exp2(mu_ref[...] + (lb2 - lse2))
    v_ref[...] = v
    v_mine, v_other = halves(v)
    left = piece_rows(v)
    rowsum = jnp.dot(left[:, :half], km_ref[...], preferred_element_type=F32) + jnp.dot(
        left[:, half:], ko_ref[...], preferred_element_type=F32
    )
    omega = omega_ref[...]
    rowsum = sum_pieces(rowsum) * omega
    r = jnp.exp(la_ref[...]) / rowsum
    r_ref[...] = r
    wr_ref[...] = r * omega
    stack(xs_ref, width, xa_ref[:width, :], r * omega)
    totals = []
    for k in range(half // TILE):
        t = slice(k * TILE, (k + 1) * TILE)
        product = lax.dot_general(xs_ref[...], ko_ref[t, :], ACROSS, preferred_element_type=F32)
        moment, total = unstack(product, width)
        total = total * v_other[:, t]
        totals.append(total)
        part = yo_ref[:width, t].astype(F32) * total - moment * v_other[:, t]
        send_ref[:width, t] = part
    s_other = jnp.concatenate(totals, axis=1)
    ext = lax.dot_general(xs_ref[2 * width :, :], km_ref[...], ACROSS, preferred_element_type=F32)
    s_mine = sum_pieces(ext) * v_mine
    sum_ref[...] = jnp.concatenate([s_mine, s_other], axis=1)
    index = lax.broadcasted_iota(jnp.int32, (8, half), 0)
    send_ref[width:, :] = select(index, {0: s_mine, 1: s_other})


def keep_kernel(log_nx, xa_ref, xs_ref, v_ref, sum_ref, ym_ref, yo_ref, km_ref, keep_ref, norm_ref, q_ref):
    width, half = keep_ref.shape
    for k in range(half // TILE):
        t = slice(k * TILE, (k + 1) * TILE)
        product = lax.dot_general(xs_ref[: 2 * width, :], km_ref[t, :], ACROSS, preferred_element_type=F32)
        moment = product[:width] + product[width:]
        keep_ref[:, t] = ym_ref[:width, t].astype(F32) * sum_ref[:, t] - moment * v_ref[:, t]
    xf = xa_ref[:width, :].astype(F32)
    norm_ref[...] = jnp.sum(xf * xf, axis=0, keepdims=True)
    mass = jnp.concatenate([ym_ref[width:, :], yo_ref[width:, :]], axis=1).astype(F32)[6:7]
    q_ref[...] = v_ref[...] * jnp.exp(mass + log_nx)


def add_kernel(keep_ref, sum_ref, got_ref, out_ref):
    width, half = keep_ref.shape
    rows = out_ref.shape[0]
    yd = half // rows
    base = yd * width // LANES
    other = jnp.concatenate([got_ref[width + 1 : width + 2, :], got_ref[width : width + 1, :]], axis=1)
    sums = sums_out(to_lanes(sum_ref[...] + other)).astype(BF16)
    total = keep_ref[...] + got_ref[:width, :]
    for r in range(rows):
        out_ref[r, :base, :] = pack(total[:, r * yd : (r + 1) * yd]).astype(BF16)
        out_ref[r, base:, :] = sums


def own_part(ref, yd):
    block = lax.axis_index("row")
    fit = LANES // yd
    row = ref[pl.ds(block // fit, 1), :]
    out = row[:, :yd]
    for k in range(1, fit):
        out = jnp.where(block % fit == k, row[:, k * yd : (k + 1) * yd], out)
    return out


def last_kernel(
    xa_ref, la_ref, norm_ref, b_ref, r_ref, wr_ref, q_ref, c_ref, got_ref, ym_ref, yo_ref, km_ref, ko_ref, y_ref,
    f_hbm, pot_hbm, gx_hbm, gy_hbm, f_ref, pot_ref, gx_ref, gy_ref, ys_ref, sum_ref, sems,
):
    width, n = gx_ref.shape
    ny = q_ref.shape[1]
    half = ny // 2
    yd = y_ref.shape[1]
    base = yd * width // LANES
    count = ny // LANES
    kappa = kappa_of(width)
    moves = []

    def leave(source, target):
        move = pltpu.make_async_copy(source, target, sems.at[len(moves)])
        move.start()
        moves.append(move)

    total = got_ref[0].astype(F32)
    for k in range(1, got_ref.shape[0]):
        total = total + got_ref[k].astype(F32)
    sums = total[base : base + count] + total[base + count : base + 2 * count]
    sum_ref[...] = sums
    yt = jnp.concatenate([ym_ref[:width, :], yo_ref[:width, :]], axis=1)
    stack(ys_ref, width, yt, q_ref[...] / from_lanes(sums))

    def tile(k):
        t = slice(k * TILE, (k + 1) * TILE)
        product = jnp.dot(ys_ref[:, :half], km_ref[:, t], preferred_element_type=F32) + jnp.dot(
            ys_ref[:, half:], ko_ref[:, t], preferred_element_type=F32
        )
        moved, weight = unstack(product, width)
        gx_ref[:, t] = (xa_ref[:width, t].astype(F32) * weight - moved) * (wr_ref[:, t] * (1.0 / ny))
        leave(gx_ref.at[:, t], gx_hbm.at[:, t])

    tile(0)
    log_row = la_ref[...] - jnp.log(r_ref[...])
    f_ref[...] = norm_ref[...] / width + EPSILON * (kappa * b_ref[...] - log_row)
    leave(f_ref, f_hbm)
    colsum = own_part(sum_ref, yd)
    c_term = own_part(c_ref, yd)
    own = y_ref[0].astype(F32)
    gy_ref[...] = unpack(total[:base], yd).T * (
        jnp.exp(own[:, width + 6 : width + 7]) * to_column(1.0 / colsum)
    )
    leave(gy_ref, gy_hbm)
    norm = to_row(jnp.sum(own[:, :width] * own[:, :width], axis=1, keepdims=True))
    pot_ref[...] = norm / width - EPSILON * (jnp.log(colsum) - kappa * c_term)
    leave(pot_ref, pot_hbm)
    for k in range(1, n // TILE):
        tile(k)
    for move in moves:
        move.wait()


def call(kernel, outs, scratch, limit, *args, space=pltpu.VMEM, out_space=pltpu.VMEM, cost=None):
    return pl.pallas_call(
        kernel,
        out_shape=outs,
        in_specs=[pl.BlockSpec(memory_space=space)] * len(args),
        out_specs=jax.tree.map(lambda _: pl.BlockSpec(memory_space=out_space), outs),
        scratch_shapes=scratch,
        cost_estimate=cost,
        compiler_params=pltpu.CompilerParams(vmem_limit_bytes=limit),
    )(*args)


def shape(dims, dtype=F32):
    return jax.ShapeDtypeStruct(dims, dtype)


def swap(value):
    return lax.ppermute(value, "col", [(0, 1), (1, 0)])


def on_device(points_x, points_y, mass_x, mass_y):
    n, width = points_x.shape
    yd = points_y.shape[0]
    rows = lax.axis_size("row")
    ny = 2 * rows * yd
    half = ny // 2
    count = ny // LANES
    log_nx, log_ny = math.log(n * 2 * rows), math.log(ny)
    depth = width + EXT
    limit = (20 if ny <= 1024 else 56) * 1024 * 1024
    extra = sums_rows(ny)
    run = functools.partial
    vmem = pltpu.VMEM
    slots = 4 if ny <= 1024 else 1
    ones = call(
        ones_kernel, shape((yd, EXT)), [], limit,
        cost=pl.CostEstimate(flops=4 * 10**9, bytes_accessed=10000, transcendentals=0),
    )
    y_own, log_a = call(
        run(prep_kernel, log_nx, log_ny), (shape((rows, yd, depth), BF16), shape((1, n))), [], limit,
        points_y, mass_y.reshape(1, yd), mass_x.reshape(n // LANES, LANES), ones,
        cost=pl.CostEstimate(flops=4 * 10**9, bytes_accessed=400000, transcendentals=0),
    )
    y_mine = lax.all_to_all(y_own, "row", 0, 0, tiled=True)
    y_other = swap(y_mine)
    xa, yt_mine, base, total, kept_mine = call(
        half_kernel,
        (
            shape((depth, n), BF16), shape((depth, half), BF16), shape((1, n)), shape((1, n)),
            shape((half, n), BF16),
        ),
        [vmem((slots, half, TILE), F32)],
        limit, points_x.T, y_mine,
    )
    yt_other, kept_mine, kept_other, b_term, omega, mu, lse = call(
        first_kernel,
        (
            shape((depth, half), BF16), shape((half, n), BF16), shape((half, n), BF16), shape((1, n)),
            shape((1, n)), shape((1, ny)), shape((2 * rows, count, LANES)),
        ),
        [vmem((depth, n), BF16), vmem((slots, half, TILE), F32), vmem((1, n), F32), vmem((1, ny), F32), pltpu.SemaphoreType.DMA],
        limit, xa, log_a, y_mine, y_other, base, total, kept_mine,
    )
    lse = lax.all_to_all(lse, AXES, 0, 0, tiled=True)
    r, wr, v, c_term, xs, sums, send = call(
        run(second_kernel, log_ny),
        (
            shape((1, n)), shape((1, n)), shape((1, ny)), shape((count, LANES)),
            shape((2 * width + PAD, n), BF16), shape((1, ny)), shape((width + 8, half)),
        ),
        [], limit, xa, log_a, omega, mu, lse, yt_mine, yt_other, kept_mine, kept_other,
    )
    got = swap(send)
    keep, norm, q = call(
        run(keep_kernel, log_nx), (shape((width, half)), shape((1, n)), shape((1, ny))), [],
        limit, xa, xs, v, sums, yt_mine, yt_other, kept_mine,
    )
    part = call(
        add_kernel, shape((rows, yd * width // LANES + extra, LANES), BF16), [], limit, keep, sums, got
    )
    part = lax.all_to_all(part, "row", 0, 0, tiled=True)
    f_pot, g_pot, grad_xt, grad_y = call(
        last_kernel,
        (shape((1, n)), shape((1, yd)), shape((width, n)), shape((yd, width))),
        [
            vmem((1, n), F32), vmem((1, yd), F32), vmem((width, n), F32), vmem((yd, width), F32),
            vmem((2 * width + PAD, ny), BF16), vmem((count, LANES), F32),
            pltpu.SemaphoreType.DMA((3 + n // TILE,)),
        ],
        limit, xa, log_a, norm, b_term, r, wr, q, c_term, part, yt_mine, yt_other, kept_mine, kept_other, y_own,
        out_space=pl.ANY,
    )
    return f_pot.reshape(n), g_pot.reshape(yd), grad_xt.T, grad_y


def solution(mesh):
    in_specs = (
        P(("groups", "row", "col"), None),
        P(("groups", "col", "row"), None),
        P(("groups", "row", "col")),
        P(("groups", "col", "row")),
    )
    out_specs = (
        P(("groups", "row", "col")),
        P(("groups", "col", "row")),
        P(("groups", "row", "col"), None),
        P(("groups", "col", "row"), None),
    )
    return jax.shard_map(
        on_device, mesh=mesh, in_specs=in_specs, out_specs=out_specs, check_vma=False
    )
```

```python
import functools
import math

import jax
import jax.numpy as jnp
from jax import lax
from jax.experimental import pallas as pl
from jax.experimental.pallas import tpu as pltpu
from jax.sharding import PartitionSpec as P

ITERS = 2
EPSILON = 0.02
LOG2E = math.log2(math.e)
TILE = 512
STEP = 16
EXT = 32
PAD = 16
LANES = 128
LIFT = 52.0
TINY = 1e-24
HUGE = 5e33
ACROSS = (((1,), (1,)), ((), ()))
AXES = ("row", "col")
F32 = jnp.float32
BF16 = jnp.bfloat16


def kappa_of(width):
    return 2.0 / (width * EPSILON)


def pieces(value):
    high = value.astype(BF16).astype(F32)
    rest = value - high
    mid = rest.astype(BF16).astype(F32)
    return high, mid, rest - mid


def select(index, values):
    out = jnp.zeros(index.shape, F32)
    for k, value in values.items():
        out = jnp.where(index == k, value, out)
    return out


def extras_x(index, b_term):
    high, mid, low = pieces(b_term)
    return select(index, {0: 1.0, 1: 1.0, 2: 1.0, 3: high, 4: mid, 5: low})


def rows_index(columns):
    return lax.broadcasted_iota(jnp.int32, (EXT, columns), 0)


def to_column(row):
    size = row.shape[1]
    eye = lax.broadcasted_iota(jnp.int32, (size, size), 0) == lax.broadcasted_iota(jnp.int32, (size, size), 1)
    return jnp.sum(jnp.where(eye, row, 0.0), axis=1, keepdims=True)


def to_row(column):
    size = column.shape[0]
    eye = lax.broadcasted_iota(jnp.int32, (size, size), 0) == lax.broadcasted_iota(jnp.int32, (size, size), 1)
    return jnp.sum(jnp.where(eye, column, 0.0), axis=0, keepdims=True)


def for_tiles(total, product, z_ref, use):
    count = total // TILE
    slots = z_ref.shape[0]
    if count <= slots:
        for t in range(count):
            z_ref[t] = product(pl.ds(t * TILE, TILE))
        for t in range(count):
            use(pl.ds(t * TILE, TILE), z_ref.at[t])
    else:

        @pl.loop(0, count)
        def _(t):
            tile = pl.ds(pl.multiple_of(t * TILE, TILE), TILE)
            z_ref[0] = product(tile)
            use(tile, z_ref.at[0])


def max_down(z_ref, rows):
    peak = z_ref[0:STEP, :]
    for r in range(STEP, rows, STEP):
        peak = jnp.maximum(peak, z_ref[r : r + STEP, :])
    return jnp.max(peak, axis=0, keepdims=True)


def exp_sum_down(z_ref, rows, scale, shift, keep=None):
    total = jnp.zeros((STEP, TILE), F32)
    for r in range(0, rows, STEP):
        z = z_ref[r : r + STEP, :]
        value = jnp.exp2((z if shift is None else z - shift) * scale)
        total = total + value
        if keep is not None:
            keep(r, value)
    return jnp.sum(total, axis=0, keepdims=True)


def to_lanes(row):
    return jnp.concatenate([row[:, k : k + LANES] for k in range(0, row.shape[1], LANES)], axis=0)


def from_lanes(block):
    return jnp.concatenate([block[k : k + 1] for k in range(block.shape[0])], axis=1)


def sums_rows(ny):
    return -(-2 * ny // LANES // 16) * 16


def sums_out(sums):
    high = sums.astype(BF16).astype(F32)
    spare = sums_rows(sums.size) - 2 * sums.shape[0]
    return jnp.concatenate([high, sums - high] + [jnp.zeros((spare, LANES), F32)] * (spare > 0), axis=0)


def pack(block):
    width, yd = block.shape
    base = width * yd // LANES
    return jnp.concatenate([block[k : k + base] for k in range(0, width, base)], axis=1)


def unpack(block, yd):
    return jnp.concatenate([block[:, k : k + yd] for k in range(0, LANES, yd)], axis=0)


def ones_kernel(ext_ref):
    index = lax.broadcasted_iota(jnp.int32, ext_ref.shape, 1)
    ext_ref[...] = select(index, {3: 1.0, 4: 1.0, 5: 1.0})


def prep_kernel(log_nx, log_ny, y_ref, my_ref, mx_ref, ones_ref, ya_ref, la_ref):
    la_ref[...] = from_lanes(mx_ref[...].astype(F32)) - log_nx
    width = y_ref.shape[1]
    y = y_ref[...]
    yf = y.astype(F32)
    norm = jnp.sum(yf * yf, axis=1, keepdims=True)
    mass = to_column(my_ref[...].astype(F32))
    c_term = (mass - log_ny) / kappa_of(width) - 0.5 * norm
    high, mid, low = pieces(c_term)
    index = lax.broadcasted_iota(jnp.int32, ones_ref.shape, 1)
    ext = (ones_ref[...] + select(index, {0: high, 1: mid, 2: low, 6: mass})).astype(BF16)
    for k in range(ya_ref.shape[0]):
        ya_ref[k, :, :width] = y
        ya_ref[k, :, width:] = ext


def halves(row):
    half = row.shape[1] // 2
    return row[:, :half], row[:, half:]


def other_order(row):
    mine, other = halves(row)
    return jnp.where(lax.axis_index("col") == 0, row, jnp.concatenate([other, mine], axis=1))


def piece_rows(row):
    one, two, three = pieces(row)
    index = lax.broadcasted_iota(jnp.int32, (PAD, row.shape[1]), 0)
    return select(index, {0: one, 1: two, 2: three}).astype(BF16)


def sum_pieces(block):
    return (block[0:1] + block[1:2]) + block[2:3]


def half_kernel(xt_ref, mine_ref, xa_ref, yt_ref, base_ref, total_ref, k_ref, z_ref):
    rows, yd, depth = mine_ref.shape
    width, n = xt_ref.shape
    half = rows * yd
    scale = kappa_of(width) * LOG2E
    xa_ref[:width, :] = xt_ref[...]
    xa_ref[width:, :] = extras_x(rows_index(n), jnp.zeros((1, n), F32)).astype(BF16)
    mine = mine_ref[...].reshape(half, depth)

    def product(t):
        return jnp.dot(mine, xa_ref[:, t], preferred_element_type=F32)

    def use(t, z):
        def keep(r, value):
            k_ref[r : r + STEP, t] = value.astype(BF16)

        base = max_down(z, half) - LIFT / scale
        base_ref[:, t] = base
        total_ref[:, t] = exp_sum_down(z, half, scale, base, keep)

    for_tiles(n, product, z_ref, use)
    xa_ref[width:, :] = extras_x(rows_index(n), -base_ref[...]).astype(BF16)
    yt_ref[...] = mine.T


def first_kernel(
    xa_ref, la_ref, mine_ref, other_ref, base_ref, total_ref, km0_ref,
    yt_ref, km_ref, ko_ref, b_ref, omega_ref, mu_ref, l_ref, xb_ref, z_ref, sum_ref, lse_ref, sem,
):
    rows, yd, depth = other_ref.shape
    n = xa_ref.shape[1]
    width = depth - EXT
    half = rows * yd
    scale = kappa_of(width) * LOG2E
    other = other_ref[...].reshape(half, depth)
    move = pltpu.make_async_copy(km0_ref, km_ref, sem)
    move.start()

    def product(t):
        return jnp.dot(other, xa_ref[:, t], preferred_element_type=F32)

    def use(t, z):
        def keep(r, value):
            ko_ref[r : r + STEP, t] = value.astype(BF16)

        sum_ref[:, t] = exp_sum_down(z, half, scale, None, keep) + total_ref[:, t]

    for_tiles(n, product, z_ref, use)
    yt_ref[...] = other.T
    log_a = la_ref[...]
    total = sum_ref[...]
    b_ref[...] = (log_a - jnp.log(total)) * (LOG2E / scale) - base_ref[...]
    omega = jnp.exp(log_a) * (2.0**LIFT / total)
    omega_ref[...] = omega
    left = piece_rows(omega)
    move.wait()
    sums = jnp.concatenate(
        [
            sum_pieces(lax.dot_general(left, ref[...], ACROSS, preferred_element_type=F32))
            for ref in (km_ref, ko_ref)
        ],
        axis=1,
    )
    lse_ref[...] = jnp.log(sums) * LOG2E - LIFT
    mu_ref[...] = jnp.full(mu_ref.shape, -LIFT, F32)

    @pl.when(jnp.logical_not((jnp.max(total) < HUGE) & (jnp.min(sums) > TINY)))
    def _():
        step = LANES // yd
        sides = ((0, mine_ref, km_ref), (1, other_ref, ko_ref))

        def scores(y_ref, x_ref, t):
            y = y_ref[pl.ds(t * step, step)].reshape(LANES, depth)
            return jnp.dot(y, x_ref[...], preferred_element_type=F32)

        b_ref[...] = jnp.full((1, n), -jnp.inf, F32)
        for k, y_ref, k_ref in sides:

            @pl.loop(0, rows // step)
            def _(t):
                b_ref[...] = jnp.maximum(b_ref[...], jnp.max(scores(y_ref, xa_ref, t), axis=0, keepdims=True))

        sum_ref[...] = jnp.zeros((1, n), F32)
        for k, y_ref, k_ref in sides:

            @pl.loop(0, rows // step)
            def _(t):
                value = jnp.exp2((scores(y_ref, xa_ref, t) - b_ref[...]) * scale)
                sum_ref[...] = sum_ref[...] + jnp.sum(value, axis=0, keepdims=True)

        b_ref[...] = (log_a - jnp.log(sum_ref[...])) * (LOG2E / scale) - b_ref[...] - base_ref[...]
        xb_ref[:width, :] = xa_ref[:width, :]
        xb_ref[width:, :] = extras_x(rows_index(n), b_ref[...]).astype(BF16)
        omega_ref[...] = jnp.ones((1, n), F32)
        for k, y_ref, k_ref in sides:

            @pl.loop(0, rows // step)
            def _(t):
                z = scores(y_ref, xb_ref, t)
                peak = jnp.max(z, axis=1, keepdims=True)
                value = jnp.exp2((z - peak) * scale)
                k_ref[pl.ds(pl.multiple_of(t * LANES, LANES), LANES), :] = value.astype(BF16)
                place = pl.ds(pl.multiple_of(k * half + t * LANES, LANES), LANES)
                mu_ref[:, place] = to_row(scale * peak)
                lse_ref[:, place] = to_row(scale * peak + jnp.log(jnp.sum(value, axis=1, keepdims=True)) * LOG2E)

    lse = to_lanes(other_order(lse_ref[...]))
    for k in range(2 * rows):
        l_ref[k] = lse


def stack(out_ref, width, points, factor):
    moved = points.astype(F32) * factor
    high = moved.astype(BF16)
    out_ref[:width, :] = high
    out_ref[width : 2 * width, :] = (moved - high.astype(F32)).astype(BF16)
    one, two, three = pieces(factor)
    index = lax.broadcasted_iota(jnp.int32, (PAD, factor.shape[1]), 0)
    out_ref[2 * width :, :] = select(index, {0: one, 1: two, 2: three}).astype(BF16)


def unstack(product, width):
    ext = product[2 * width :]
    return product[:width] + product[width : 2 * width], (ext[0:1] + ext[1:2]) + ext[2:3]


def second_kernel(
    log_ny, xa_ref, la_ref, omega_ref, mu_ref, l_ref, ym_ref, yo_ref, km_ref, ko_ref,
    r_ref, wr_ref, v_ref, c_ref, xs_ref, sum_ref, send_ref,
):
    width = xa_ref.shape[0] - EXT
    half = ym_ref.shape[1]
    kappa = kappa_of(width)
    scale = kappa * LOG2E
    l_all = l_ref[...]
    peak = jnp.max(l_all, axis=0)
    total = jnp.sum(jnp.exp2(l_all - peak[None]), axis=0)
    lse2 = other_order(from_lanes(peak + jnp.log(total) * LOG2E))
    old = jnp.concatenate([ym_ref[width:, :], yo_ref[width:, :]], axis=1).astype(F32)
    lb2 = (old[6:7] - log_ny) * LOG2E
    c_ref[...] = to_lanes(sum_pieces(old) + (lb2 - lse2) / scale)
    v = jnp.exp2(mu_ref[...] + (lb2 - lse2))
    v_ref[...] = v
    v_mine, v_other = halves(v)
    left = piece_rows(v)
    rowsum = jnp.dot(left[:, :half], km_ref[...], preferred_element_type=F32) + jnp.dot(
        left[:, half:], ko_ref[...], preferred_element_type=F32
    )
    omega = omega_ref[...]
    rowsum = sum_pieces(rowsum) * omega
    r = jnp.exp(la_ref[...]) / rowsum
    r_ref[...] = r
    wr_ref[...] = r * omega
    stack(xs_ref, width, xa_ref[:width, :], r * omega)
    totals = []
    for k in range(half // TILE):
        t = slice(k * TILE, (k + 1) * TILE)
        product = lax.dot_general(xs_ref[...], ko_ref[t, :], ACROSS, preferred_element_type=F32)
        moment, total = unstack(product, width)
        total = total * v_other[:, t]
        totals.append(total)
        part = yo_ref[:width, t].astype(F32) * total - moment * v_other[:, t]
        send_ref[:width, t] = part
    s_other = jnp.concatenate(totals, axis=1)
    ext = lax.dot_general(xs_ref[2 * width :, :], km_ref[...], ACROSS, preferred_element_type=F32)
    s_mine = sum_pieces(ext) * v_mine
    sum_ref[...] = jnp.concatenate([s_mine, s_other], axis=1)
    index = lax.broadcasted_iota(jnp.int32, (8, half), 0)
    send_ref[width:, :] = select(index, {0: s_mine, 1: s_other})


def keep_kernel(log_nx, xa_ref, xs_ref, v_ref, sum_ref, ym_ref, yo_ref, km_ref, keep_ref, norm_ref, q_ref):
    width, half = keep_ref.shape
    for k in range(half // TILE):
        t = slice(k * TILE, (k + 1) * TILE)
        product = lax.dot_general(xs_ref[: 2 * width, :], km_ref[t, :], ACROSS, preferred_element_type=F32)
        moment = product[:width] + product[width:]
        keep_ref[:, t] = ym_ref[:width, t].astype(F32) * sum_ref[:, t] - moment * v_ref[:, t]
    xf = xa_ref[:width, :].astype(F32)
    norm_ref[...] = jnp.sum(xf * xf, axis=0, keepdims=True)
    mass = jnp.concatenate([ym_ref[width:, :], yo_ref[width:, :]], axis=1).astype(F32)[6:7]
    q_ref[...] = v_ref[...] * jnp.exp(mass + log_nx)


def add_kernel(keep_ref, sum_ref, got_ref, out_ref):
    width, half = keep_ref.shape
    rows = out_ref.shape[0]
    yd = half // rows
    base = yd * width // LANES
    other = jnp.concatenate([got_ref[width + 1 : width + 2, :], got_ref[width : width + 1, :]], axis=1)
    sums = sums_out(to_lanes(sum_ref[...] + other)).astype(BF16)
    total = keep_ref[...] + got_ref[:width, :]
    for r in range(rows):
        out_ref[r, :base, :] = pack(total[:, r * yd : (r + 1) * yd]).astype(BF16)
        out_ref[r, base:, :] = sums


def own_part(ref, yd):
    block = lax.axis_index("row")
    fit = LANES // yd
    row = ref[pl.ds(block // fit, 1), :]
    out = row[:, :yd]
    for k in range(1, fit):
        out = jnp.where(block % fit == k, row[:, k * yd : (k + 1) * yd], out)
    return out


def last_kernel(
    xa_ref, la_ref, norm_ref, b_ref, r_ref, wr_ref, q_ref, c_ref, got_ref, ym_ref, yo_ref, km_ref, ko_ref, y_ref,
    f_hbm, pot_hbm, gx_hbm, gy_hbm, f_ref, pot_ref, gx_ref, gy_ref, ys_ref, sum_ref, sems,
):
    width, n = gx_ref.shape
    ny = q_ref.shape[1]
    yd = y_ref.shape[1]
    base = yd * width // LANES
    count = ny // LANES
    kappa = kappa_of(width)
    moves = []

    def leave(source, target):
        move = pltpu.make_async_copy(source, target, sems.at[len(moves)])
        move.start()
        moves.append(move)

    log_row = la_ref[...] - jnp.log(r_ref[...])
    f_ref[...] = norm_ref[...] / width + EPSILON * (kappa * b_ref[...] - log_row)
    leave(f_ref, f_hbm)
    total = got_ref[0].astype(F32)
    for k in range(1, got_ref.shape[0]):
        total = total + got_ref[k].astype(F32)
    sums = total[base : base + count] + total[base + count : base + 2 * count]
    sum_ref[...] = sums
    colsum = own_part(sum_ref, yd)
    c_term = own_part(c_ref, yd)
    own = y_ref[0].astype(F32)
    gy_ref[...] = unpack(total[:base], yd).T * (
        jnp.exp(own[:, width + 6 : width + 7]) * to_column(1.0 / colsum)
    )
    leave(gy_ref, gy_hbm)
    norm = to_row(jnp.sum(own[:, :width] * own[:, :width], axis=1, keepdims=True))
    pot_ref[...] = norm / width - EPSILON * (jnp.log(colsum) - kappa * c_term)
    leave(pot_ref, pot_hbm)
    half = ny // 2
    yt = jnp.concatenate([ym_ref[:width, :], yo_ref[:width, :]], axis=1)
    stack(ys_ref, width, yt, q_ref[...] / from_lanes(sums))
    for k in range(n // TILE):
        t = slice(k * TILE, (k + 1) * TILE)
        product = jnp.dot(ys_ref[:, :half], km_ref[:, t], preferred_element_type=F32) + jnp.dot(
            ys_ref[:, half:], ko_ref[:, t], preferred_element_type=F32
        )
        moved, weight = unstack(product, width)
        gx_ref[:, t] = (xa_ref[:width, t].astype(F32) * weight - moved) * (wr_ref[:, t] * (1.0 / ny))
        leave(gx_ref.at[:, t], gx_hbm.at[:, t])
    for move in moves:
        move.wait()


def call(kernel, outs, scratch, limit, *args, space=pltpu.VMEM, out_space=pltpu.VMEM, cost=None):
    return pl.pallas_call(
        kernel,
        out_shape=outs,
        in_specs=[pl.BlockSpec(memory_space=space)] * len(args),
        out_specs=jax.tree.map(lambda _: pl.BlockSpec(memory_space=out_space), outs),
        scratch_shapes=scratch,
        cost_estimate=cost,
        compiler_params=pltpu.CompilerParams(vmem_limit_bytes=limit),
    )(*args)


def shape(dims, dtype=F32):
    return jax.ShapeDtypeStruct(dims, dtype)


def swap(value):
    return lax.ppermute(value, "col", [(0, 1), (1, 0)])


def on_device(points_x, points_y, mass_x, mass_y):
    n, width = points_x.shape
    yd = points_y.shape[0]
    rows = lax.axis_size("row")
    ny = 2 * rows * yd
    half = ny // 2
    count = ny // LANES
    log_nx, log_ny = math.log(n * 2 * rows), math.log(ny)
    depth = width + EXT
    limit = (20 if ny <= 1024 else 56) * 1024 * 1024
    extra = sums_rows(ny)
    run = functools.partial
    vmem = pltpu.VMEM
    slots = 4 if ny <= 1024 else 1
    ones = call(
        ones_kernel, shape((yd, EXT)), [], limit,
        cost=pl.CostEstimate(flops=4 * 10**9, bytes_accessed=10000, transcendentals=0),
    )
    y_own, log_a = call(
        run(prep_kernel, log_nx, log_ny), (shape((rows, yd, depth), BF16), shape((1, n))), [], limit,
        points_y, mass_y.reshape(1, yd), mass_x.reshape(n // LANES, LANES), ones,
        cost=pl.CostEstimate(flops=4 * 10**9, bytes_accessed=400000, transcendentals=0),
    )
    y_mine = lax.all_to_all(y_own, "row", 0, 0, tiled=True)
    y_other = swap(y_mine)
    xa, yt_mine, base, total, kept_mine = call(
        half_kernel,
        (
            shape((depth, n), BF16), shape((depth, half), BF16), shape((1, n)), shape((1, n)),
            shape((half, n), BF16),
        ),
        [vmem((slots, half, TILE), F32)],
        limit, points_x.T, y_mine,
    )
    yt_other, kept_mine, kept_other, b_term, omega, mu, lse = call(
        first_kernel,
        (
            shape((depth, half), BF16), shape((half, n), BF16), shape((half, n), BF16), shape((1, n)),
            shape((1, n)), shape((1, ny)), shape((2 * rows, count, LANES)),
        ),
        [vmem((depth, n), BF16), vmem((slots, half, TILE), F32), vmem((1, n), F32), vmem((1, ny), F32), pltpu.SemaphoreType.DMA],
        limit, xa, log_a, y_mine, y_other, base, total, kept_mine,
    )
    lse = lax.all_to_all(lse, AXES, 0, 0, tiled=True)
    r, wr, v, c_term, xs, sums, send = call(
        run(second_kernel, log_ny),
        (
            shape((1, n)), shape((1, n)), shape((1, ny)), shape((count, LANES)),
            shape((2 * width + PAD, n), BF16), shape((1, ny)), shape((width + 8, half)),
        ),
        [], limit, xa, log_a, omega, mu, lse, yt_mine, yt_other, kept_mine, kept_other,
    )
    got = swap(send)
    keep, norm, q = call(
        run(keep_kernel, log_nx), (shape((width, half)), shape((1, n)), shape((1, ny))), [],
        limit, xa, xs, v, sums, yt_mine, yt_other, kept_mine,
    )
    part = call(
        add_kernel, shape((rows, yd * width // LANES + extra, LANES), BF16), [], limit, keep, sums, got
    )
    part = lax.all_to_all(part, "row", 0, 0, tiled=True)
    f_pot, g_pot, grad_xt, grad_y = call(
        last_kernel,
        (shape((1, n)), shape((1, yd)), shape((width, n)), shape((yd, width))),
        [
            vmem((1, n), F32), vmem((1, yd), F32), vmem((width, n), F32), vmem((yd, width), F32),
            vmem((2 * width + PAD, ny), BF16), vmem((count, LANES), F32),
            pltpu.SemaphoreType.DMA((3 + n // TILE,)),
        ],
        limit, xa, log_a, norm, b_term, r, wr, q, c_term, part, yt_mine, yt_other, kept_mine, kept_other, y_own,
        out_space=pl.ANY,
    )
    return f_pot.reshape(n), g_pot.reshape(yd), grad_xt.T, grad_y


def solution(mesh):
    in_specs = (
        P(("groups", "row", "col"), None),
        P(("groups", "col", "row"), None),
        P(("groups", "row", "col")),
        P(("groups", "col", "row")),
    )
    out_specs = (
        P(("groups", "row", "col")),
        P(("groups", "col", "row")),
        P(("groups", "row", "col"), None),
        P(("groups", "col", "row"), None),
    )
    return jax.shard_map(
        on_device, mesh=mesh, in_specs=in_specs, out_specs=out_specs, check_vma=False
    )
```

```python
import functools
import math

import jax
import jax.numpy as jnp
from jax import lax
from jax.experimental import pallas as pl
from jax.experimental.pallas import tpu as pltpu
from jax.sharding import PartitionSpec as P

ITERS = 2
EPSILON = 0.02
LOG2E = math.log2(math.e)
TILE = 512
STEP = 16
EXT = 32
PAD = 16
LANES = 128
LIFT = 52.0
TINY = 1e-24
HUGE = 5e33
ACROSS = (((1,), (1,)), ((), ()))
AXES = ("row", "col")
F32 = jnp.float32
BF16 = jnp.bfloat16


def kappa_of(width):
    return 2.0 / (width * EPSILON)


def pieces(value):
    high = value.astype(BF16).astype(F32)
    rest = value - high
    mid = rest.astype(BF16).astype(F32)
    return high, mid, rest - mid


def select(index, values):
    out = jnp.zeros(index.shape, F32)
    for k, value in values.items():
        out = jnp.where(index == k, value, out)
    return out


def extras_x(index, b_term):
    high, mid, low = pieces(b_term)
    return select(index, {0: 1.0, 1: 1.0, 2: 1.0, 3: high, 4: mid, 5: low})


def rows_index(columns):
    return lax.broadcasted_iota(jnp.int32, (EXT, columns), 0)


def to_column(row):
    size = row.shape[1]
    eye = lax.broadcasted_iota(jnp.int32, (size, size), 0) == lax.broadcasted_iota(jnp.int32, (size, size), 1)
    return jnp.sum(jnp.where(eye, row, 0.0), axis=1, keepdims=True)


def to_row(column):
    size = column.shape[0]
    eye = lax.broadcasted_iota(jnp.int32, (size, size), 0) == lax.broadcasted_iota(jnp.int32, (size, size), 1)
    return jnp.sum(jnp.where(eye, column, 0.0), axis=0, keepdims=True)


def for_tiles(total, product, z_ref, use):
    count = total // TILE
    slots = z_ref.shape[0]
    if count <= slots:
        for t in range(count):
            z_ref[t] = product(pl.ds(t * TILE, TILE))
        for t in range(count):
            use(pl.ds(t * TILE, TILE), z_ref.at[t])
    else:

        @pl.loop(0, count)
        def _(t):
            tile = pl.ds(pl.multiple_of(t * TILE, TILE), TILE)
            z_ref[0] = product(tile)
            use(tile, z_ref.at[0])


def max_down(z_ref, rows):
    peak = z_ref[0:STEP, :]
    for r in range(STEP, rows, STEP):
        peak = jnp.maximum(peak, z_ref[r : r + STEP, :])
    return jnp.max(peak, axis=0, keepdims=True)


def exp_sum_down(z_ref, rows, scale, shift, keep=None):
    total = jnp.zeros((STEP, TILE), F32)
    for r in range(0, rows, STEP):
        z = z_ref[r : r + STEP, :]
        value = jnp.exp2((z if shift is None else z - shift) * scale)
        total = total + value
        if keep is not None:
            keep(r, value)
    return jnp.sum(total, axis=0, keepdims=True)


def to_lanes(row):
    return jnp.concatenate([row[:, k : k + LANES] for k in range(0, row.shape[1], LANES)], axis=0)


def from_lanes(block):
    return jnp.concatenate([block[k : k + 1] for k in range(block.shape[0])], axis=1)


def sums_rows(ny):
    return -(-2 * ny // LANES // 16) * 16


def sums_out(sums):
    high = sums.astype(BF16).astype(F32)
    spare = sums_rows(sums.size) - 2 * sums.shape[0]
    return jnp.concatenate([high, sums - high] + [jnp.zeros((spare, LANES), F32)] * (spare > 0), axis=0)


def pack(block):
    width, yd = block.shape
    base = width * yd // LANES
    return jnp.concatenate([block[k : k + base] for k in range(0, width, base)], axis=1)


def unpack(block, yd):
    return jnp.concatenate([block[:, k : k + yd] for k in range(0, LANES, yd)], axis=0)


def ones_kernel(ext_ref):
    index = lax.broadcasted_iota(jnp.int32, ext_ref.shape, 1)
    ext_ref[...] = select(index, {3: 1.0, 4: 1.0, 5: 1.0})


def prep_kernel(log_nx, log_ny, y_ref, my_ref, mx_ref, ones_ref, ya_ref, la_ref):
    la_ref[...] = from_lanes(mx_ref[...].astype(F32)) - log_nx
    width = y_ref.shape[1]
    y = y_ref[...]
    yf = y.astype(F32)
    norm = jnp.sum(yf * yf, axis=1, keepdims=True)
    mass = to_column(my_ref[...].astype(F32))
    c_term = (mass - log_ny) / kappa_of(width) - 0.5 * norm
    high, mid, low = pieces(c_term)
    index = lax.broadcasted_iota(jnp.int32, ones_ref.shape, 1)
    ext = (ones_ref[...] + select(index, {0: high, 1: mid, 2: low, 6: mass})).astype(BF16)
    for k in range(ya_ref.shape[0]):
        ya_ref[k, :, :width] = y
        ya_ref[k, :, width:] = ext


def halves(row):
    half = row.shape[1] // 2
    return row[:, :half], row[:, half:]


def other_order(row):
    mine, other = halves(row)
    return jnp.where(lax.axis_index("col") == 0, row, jnp.concatenate([other, mine], axis=1))


def piece_rows(row):
    one, two, three = pieces(row)
    index = lax.broadcasted_iota(jnp.int32, (PAD, row.shape[1]), 0)
    return select(index, {0: one, 1: two, 2: three}).astype(BF16)


def sum_pieces(block):
    return (block[0:1] + block[1:2]) + block[2:3]


def half_kernel(xt_ref, mine_ref, xa_ref, yt_ref, base_ref, total_ref, k_ref, z_ref):
    rows, yd, depth = mine_ref.shape
    width, n = xt_ref.shape
    half = rows * yd
    scale = kappa_of(width) * LOG2E
    xa_ref[:width, :] = xt_ref[...]
    xa_ref[width:, :] = extras_x(rows_index(n), jnp.zeros((1, n), F32)).astype(BF16)
    mine = mine_ref[...].reshape(half, depth)

    def product(t):
        return jnp.dot(mine, xa_ref[:, t], preferred_element_type=F32)

    def use(t, z):
        def keep(r, value):
            k_ref[r : r + STEP, t] = value.astype(BF16)

        base = max_down(z, half) - LIFT / scale
        base_ref[:, t] = base
        total_ref[:, t] = exp_sum_down(z, half, scale, base, keep)

    for_tiles(n, product, z_ref, use)
    xa_ref[width:, :] = extras_x(rows_index(n), -base_ref[...]).astype(BF16)
    yt_ref[...] = mine.T


def first_kernel(
    xa_ref, la_ref, mine_ref, other_ref, base_ref, total_ref, km0_ref,
    yt_ref, km_ref, ko_ref, b_ref, omega_ref, mu_ref, l_ref, xb_ref, z_ref, sum_ref, lse_ref,
):
    rows, yd, depth = other_ref.shape
    n = xa_ref.shape[1]
    width = depth - EXT
    half = rows * yd
    scale = kappa_of(width) * LOG2E
    other = other_ref[...].reshape(half, depth)

    def product(t):
        return jnp.dot(other, xa_ref[:, t], preferred_element_type=F32)

    def use(t, z):
        def keep(r, value):
            ko_ref[r : r + STEP, t] = value.astype(BF16)

        sum_ref[:, t] = exp_sum_down(z, half, scale, None, keep) + total_ref[:, t]

    for_tiles(n, product, z_ref, use)
    yt_ref[...] = other.T
    log_a = la_ref[...]
    total = sum_ref[...]
    b_ref[...] = (log_a - jnp.log(total)) * (LOG2E / scale) - base_ref[...]
    omega = jnp.exp(log_a) * (2.0**LIFT / total)
    omega_ref[...] = omega
    left = piece_rows(omega)
    km_ref[...] = km0_ref[...]
    sums = jnp.concatenate(
        [
            sum_pieces(lax.dot_general(left, ref[...], ACROSS, preferred_element_type=F32))
            for ref in (km0_ref, ko_ref)
        ],
        axis=1,
    )
    lse_ref[...] = jnp.log(sums) * LOG2E - LIFT
    mu_ref[...] = jnp.full(mu_ref.shape, -LIFT, F32)

    @pl.when(jnp.logical_not((jnp.max(total) < HUGE) & (jnp.min(sums) > TINY)))
    def _():
        step = LANES // yd
        sides = ((0, mine_ref, km_ref), (1, other_ref, ko_ref))

        def scores(y_ref, x_ref, t):
            y = y_ref[pl.ds(t * step, step)].reshape(LANES, depth)
            return jnp.dot(y, x_ref[...], preferred_element_type=F32)

        b_ref[...] = jnp.full((1, n), -jnp.inf, F32)
        for k, y_ref, k_ref in sides:

            @pl.loop(0, rows // step)
            def _(t):
                b_ref[...] = jnp.maximum(b_ref[...], jnp.max(scores(y_ref, xa_ref, t), axis=0, keepdims=True))

        sum_ref[...] = jnp.zeros((1, n), F32)
        for k, y_ref, k_ref in sides:

            @pl.loop(0, rows // step)
            def _(t):
                value = jnp.exp2((scores(y_ref, xa_ref, t) - b_ref[...]) * scale)
                sum_ref[...] = sum_ref[...] + jnp.sum(value, axis=0, keepdims=True)

        b_ref[...] = (log_a - jnp.log(sum_ref[...])) * (LOG2E / scale) - b_ref[...] - base_ref[...]
        xb_ref[:width, :] = xa_ref[:width, :]
        xb_ref[width:, :] = extras_x(rows_index(n), b_ref[...]).astype(BF16)
        omega_ref[...] = jnp.ones((1, n), F32)
        for k, y_ref, k_ref in sides:

            @pl.loop(0, rows // step)
            def _(t):
                z = scores(y_ref, xb_ref, t)
                peak = jnp.max(z, axis=1, keepdims=True)
                value = jnp.exp2((z - peak) * scale)
                k_ref[pl.ds(pl.multiple_of(t * LANES, LANES), LANES), :] = value.astype(BF16)
                place = pl.ds(pl.multiple_of(k * half + t * LANES, LANES), LANES)
                mu_ref[:, place] = to_row(scale * peak)
                lse_ref[:, place] = to_row(scale * peak + jnp.log(jnp.sum(value, axis=1, keepdims=True)) * LOG2E)

    lse = to_lanes(other_order(lse_ref[...]))
    for k in range(2 * rows):
        l_ref[k] = lse


def stack(out_ref, width, points, factor):
    moved = points.astype(F32) * factor
    high = moved.astype(BF16)
    out_ref[:width, :] = high
    out_ref[width : 2 * width, :] = (moved - high.astype(F32)).astype(BF16)
    one, two, three = pieces(factor)
    index = lax.broadcasted_iota(jnp.int32, (PAD, factor.shape[1]), 0)
    out_ref[2 * width :, :] = select(index, {0: one, 1: two, 2: three}).astype(BF16)


def unstack(product, width):
    ext = product[2 * width :]
    return product[:width] + product[width : 2 * width], (ext[0:1] + ext[1:2]) + ext[2:3]


def second_kernel(
    log_ny, xa_ref, la_ref, omega_ref, mu_ref, l_ref, ym_ref, yo_ref, km_ref, ko_ref,
    r_ref, wr_ref, v_ref, c_ref, xs_ref, sum_ref, send_ref,
):
    width = xa_ref.shape[0] - EXT
    half = ym_ref.shape[1]
    kappa = kappa_of(width)
    scale = kappa * LOG2E
    l_all = l_ref[...]
    peak = jnp.max(l_all, axis=0)
    total = jnp.sum(jnp.exp2(l_all - peak[None]), axis=0)
    lse2 = other_order(from_lanes(peak + jnp.log(total) * LOG2E))
    old = jnp.concatenate([ym_ref[width:, :], yo_ref[width:, :]], axis=1).astype(F32)
    lb2 = (old[6:7] - log_ny) * LOG2E
    c_ref[...] = to_lanes(sum_pieces(old) + (lb2 - lse2) / scale)
    v = jnp.exp2(mu_ref[...] + (lb2 - lse2))
    v_ref[...] = v
    v_mine, v_other = halves(v)
    left = piece_rows(v)
    rowsum = jnp.dot(left[:, :half], km_ref[...], preferred_element_type=F32) + jnp.dot(
        left[:, half:], ko_ref[...], preferred_element_type=F32
    )
    omega = omega_ref[...]
    rowsum = sum_pieces(rowsum) * omega
    r = jnp.exp(la_ref[...]) / rowsum
    r_ref[...] = r
    wr_ref[...] = r * omega
    stack(xs_ref, width, xa_ref[:width, :], r * omega)
    totals = []
    for k in range(half // TILE):
        t = slice(k * TILE, (k + 1) * TILE)
        product = lax.dot_general(xs_ref[...], ko_ref[t, :], ACROSS, preferred_element_type=F32)
        moment, total = unstack(product, width)
        total = total * v_other[:, t]
        totals.append(total)
        part = yo_ref[:width, t].astype(F32) * total - moment * v_other[:, t]
        send_ref[:width, t] = part
    s_other = jnp.concatenate(totals, axis=1)
    ext = lax.dot_general(xs_ref[2 * width :, :], km_ref[...], ACROSS, preferred_element_type=F32)
    s_mine = sum_pieces(ext) * v_mine
    sum_ref[...] = jnp.concatenate([s_mine, s_other], axis=1)
    index = lax.broadcasted_iota(jnp.int32, (8, half), 0)
    send_ref[width:, :] = select(index, {0: s_mine, 1: s_other})


def keep_kernel(log_nx, xa_ref, xs_ref, v_ref, sum_ref, ym_ref, yo_ref, km_ref, keep_ref, norm_ref, q_ref):
    width, half = keep_ref.shape
    for k in range(half // TILE):
        t = slice(k * TILE, (k + 1) * TILE)
        product = lax.dot_general(xs_ref[: 2 * width, :], km_ref[t, :], ACROSS, preferred_element_type=F32)
        moment = product[:width] + product[width:]
        keep_ref[:, t] = ym_ref[:width, t].astype(F32) * sum_ref[:, t] - moment * v_ref[:, t]
    xf = xa_ref[:width, :].astype(F32)
    norm_ref[...] = jnp.sum(xf * xf, axis=0, keepdims=True)
    mass = jnp.concatenate([ym_ref[width:, :], yo_ref[width:, :]], axis=1).astype(F32)[6:7]
    q_ref[...] = v_ref[...] * jnp.exp(mass + log_nx)


def add_kernel(keep_ref, sum_ref, got_ref, out_ref):
    width, half = keep_ref.shape
    rows = out_ref.shape[0]
    yd = half // rows
    base = yd * width // LANES
    other = jnp.concatenate([got_ref[width + 1 : width + 2, :], got_ref[width : width + 1, :]], axis=1)
    sums = sums_out(to_lanes(sum_ref[...] + other)).astype(BF16)
    total = keep_ref[...] + got_ref[:width, :]
    for r in range(rows):
        out_ref[r, :base, :] = pack(total[:, r * yd : (r + 1) * yd]).astype(BF16)
        out_ref[r, base:, :] = sums


def own_part(ref, yd):
    block = lax.axis_index("row")
    fit = LANES // yd
    row = ref[pl.ds(block // fit, 1), :]
    out = row[:, :yd]
    for k in range(1, fit):
        out = jnp.where(block % fit == k, row[:, k * yd : (k + 1) * yd], out)
    return out


def last_kernel(
    xa_ref, la_ref, norm_ref, b_ref, r_ref, wr_ref, q_ref, c_ref, got_ref, ym_ref, yo_ref, km_ref, ko_ref, y_ref,
    f_hbm, pot_hbm, gx_hbm, gy_hbm, f_ref, pot_ref, gx_ref, gy_ref, ys_ref, sum_ref, sems,
):
    width, n = gx_ref.shape
    ny = q_ref.shape[1]
    yd = y_ref.shape[1]
    base = yd * width // LANES
    count = ny // LANES
    kappa = kappa_of(width)
    moves = []

    def leave(source, target):
        move = pltpu.make_async_copy(source, target, sems.at[len(moves)])
        move.start()
        moves.append(move)

    log_row = la_ref[...] - jnp.log(r_ref[...])
    f_ref[...] = norm_ref[...] / width + EPSILON * (kappa * b_ref[...] - log_row)
    leave(f_ref, f_hbm)
    total = got_ref[0].astype(F32)
    for k in range(1, got_ref.shape[0]):
        total = total + got_ref[k].astype(F32)
    sums = total[base : base + count] + total[base + count : base + 2 * count]
    sum_ref[...] = sums
    colsum = own_part(sum_ref, yd)
    c_term = own_part(c_ref, yd)
    own = y_ref[0].astype(F32)
    gy_ref[...] = unpack(total[:base], yd).T * (
        jnp.exp(own[:, width + 6 : width + 7]) * to_column(1.0 / colsum)
    )
    leave(gy_ref, gy_hbm)
    norm = to_row(jnp.sum(own[:, :width] * own[:, :width], axis=1, keepdims=True))
    pot_ref[...] = norm / width - EPSILON * (jnp.log(colsum) - kappa * c_term)
    leave(pot_ref, pot_hbm)
    half = ny // 2
    yt = jnp.concatenate([ym_ref[:width, :], yo_ref[:width, :]], axis=1)
    stack(ys_ref, width, yt, q_ref[...] / from_lanes(sums))
    for k in range(n // TILE):
        t = slice(k * TILE, (k + 1) * TILE)
        product = jnp.dot(ys_ref[:, :half], km_ref[:, t], preferred_element_type=F32) + jnp.dot(
            ys_ref[:, half:], ko_ref[:, t], preferred_element_type=F32
        )
        moved, weight = unstack(product, width)
        gx_ref[:, t] = (xa_ref[:width, t].astype(F32) * weight - moved) * (wr_ref[:, t] * (1.0 / ny))
        leave(gx_ref.at[:, t], gx_hbm.at[:, t])
    for move in moves:
        move.wait()


def call(kernel, outs, scratch, limit, *args, space=pltpu.VMEM, out_space=pltpu.VMEM, cost=None):
    return pl.pallas_call(
        kernel,
        out_shape=outs,
        in_specs=[pl.BlockSpec(memory_space=space)] * len(args),
        out_specs=jax.tree.map(lambda _: pl.BlockSpec(memory_space=out_space), outs),
        scratch_shapes=scratch,
        cost_estimate=cost,
        compiler_params=pltpu.CompilerParams(vmem_limit_bytes=limit),
    )(*args)


def shape(dims, dtype=F32):
    return jax.ShapeDtypeStruct(dims, dtype)


def swap(value):
    return lax.ppermute(value, "col", [(0, 1), (1, 0)])


def on_device(points_x, points_y, mass_x, mass_y):
    n, width = points_x.shape
    yd = points_y.shape[0]
    rows = lax.axis_size("row")
    ny = 2 * rows * yd
    half = ny // 2
    count = ny // LANES
    log_nx, log_ny = math.log(n * 2 * rows), math.log(ny)
    depth = width + EXT
    limit = (20 if ny <= 1024 else 56) * 1024 * 1024
    extra = sums_rows(ny)
    run = functools.partial
    vmem = pltpu.VMEM
    slots = 4 if ny <= 1024 else 1
    ones = call(
        ones_kernel, shape((yd, EXT)), [], limit,
        cost=pl.CostEstimate(flops=4 * 10**9, bytes_accessed=10000, transcendentals=0),
    )
    y_own, log_a = call(
        run(prep_kernel, log_nx, log_ny), (shape((rows, yd, depth), BF16), shape((1, n))), [], limit,
        points_y, mass_y.reshape(1, yd), mass_x.reshape(n // LANES, LANES), ones,
        cost=pl.CostEstimate(flops=4 * 10**9, bytes_accessed=400000, transcendentals=0),
    )
    y_mine = lax.all_to_all(y_own, "row", 0, 0, tiled=True)
    y_other = swap(y_mine)
    xa, yt_mine, base, total, kept_mine = call(
        half_kernel,
        (
            shape((depth, n), BF16), shape((depth, half), BF16), shape((1, n)), shape((1, n)),
            shape((half, n), BF16),
        ),
        [vmem((slots, half, TILE), F32)],
        limit, points_x.T, y_mine,
    )
    yt_other, kept_mine, kept_other, b_term, omega, mu, lse = call(
        first_kernel,
        (
            shape((depth, half), BF16), shape((half, n), BF16), shape((half, n), BF16), shape((1, n)),
            shape((1, n)), shape((1, ny)), shape((2 * rows, count, LANES)),
        ),
        [vmem((depth, n), BF16), vmem((slots, half, TILE), F32), vmem((1, n), F32), vmem((1, ny), F32)],
        limit, xa, log_a, y_mine, y_other, base, total, kept_mine,
    )
    lse = lax.all_to_all(lse, AXES, 0, 0, tiled=True)
    r, wr, v, c_term, xs, sums, send = call(
        run(second_kernel, log_ny),
        (
            shape((1, n)), shape((1, n)), shape((1, ny)), shape((count, LANES)),
            shape((2 * width + PAD, n), BF16), shape((1, ny)), shape((width + 8, half)),
        ),
        [], limit, xa, log_a, omega, mu, lse, yt_mine, yt_other, kept_mine, kept_other,
    )
    got = swap(send)
    keep, norm, q = call(
        run(keep_kernel, log_nx), (shape((width, half)), shape((1, n)), shape((1, ny))), [],
        limit, xa, xs, v, sums, yt_mine, yt_other, kept_mine,
    )
    part = call(
        add_kernel, shape((rows, yd * width // LANES + extra, LANES), BF16), [], limit, keep, sums, got
    )
    part = lax.all_to_all(part, "row", 0, 0, tiled=True)
    f_pot, g_pot, grad_xt, grad_y = call(
        last_kernel,
        (shape((1, n)), shape((1, yd)), shape((width, n)), shape((yd, width))),
        [
            vmem((1, n), F32), vmem((1, yd), F32), vmem((width, n), F32), vmem((yd, width), F32),
            vmem((2 * width + PAD, ny), BF16), vmem((count, LANES), F32),
            pltpu.SemaphoreType.DMA((3 + n // TILE,)),
        ],
        limit, xa, log_a, norm, b_term, r, wr, q, c_term, part, yt_mine, yt_other, kept_mine, kept_other, y_own,
        out_space=pl.ANY,
    )
    return f_pot.reshape(n), g_pot.reshape(yd), grad_xt.T, grad_y


def solution(mesh):
    in_specs = (
        P(("groups", "row", "col"), None),
        P(("groups", "col", "row"), None),
        P(("groups", "row", "col")),
        P(("groups", "col", "row")),
    )
    out_specs = (
        P(("groups", "row", "col")),
        P(("groups", "col", "row")),
        P(("groups", "row", "col"), None),
        P(("groups", "col", "row"), None),
    )
    return jax.shard_map(
        on_device, mesh=mesh, in_specs=in_specs, out_specs=out_specs, check_vma=False
    )
```
